32 devices in a mesh: dp: 2 (over core), row: 4 (over y, x), col: 4 (over z).
Axes of the slice: x: 2, y: 2, z: 4, core: 2. Of those that a mesh axis runs over, the one named last changes fastest.
Arguments:
- hidden_in: bfloat16 [8192, 2048], P(('dp', 'col'), 'row'), may hold values from -6 to 6
- teacher: bfloat16 [8192, 2048], P(('dp', 'col'), 'row'), may hold values from -6 to 6
- valid: int32 [8192], P(('dp', 'col')), may hold values from 0 to 1, as said below
- segment_ids: int32 [2, 4096], P('dp'), may hold values from 0 to 8, as said below
- query_weight: bfloat16 [2048, 2048], P('row', 'col'), may hold values from -0.1875 to 0.1875
- key_weight: bfloat16 [2048, 2048], P('row', 'col'), may hold values from -0.1875 to 0.1875
- value_weight: bfloat16 [2048, 2048], P('row', 'col'), may hold values from -0.125 to 0.125
- output_weight: bfloat16 [2048, 2048], P('col', 'row'), may hold values from -1 to 1
- gate_weight: bfloat16 [2048, 8192], P('row', 'col'), may hold values from -0.125 to 0.125
- up_weight: bfloat16 [2048, 8192], P('row', 'col'), may hold values from -0.125 to 0.125
- down_weight: bfloat16 [8192, 2048], P('col', 'row'), may hold values from -0.09375 to 0.09375
Outputs:
- layer_output: bfloat16 [8192, 2048], P(('dp', 'col'), 'row')
- mean_loss: float32 [1], replicated
- input_gradient: float32 [8192, 2048], P(('dp', 'col'), 'row')
- query_gradient: float32 [2048, 2048], P('row', 'col')
- key_gradient: float32 [2048, 2048], P('row', 'col')
- value_gradient: float32 [2048, 2048], P('row', 'col')
- output_gradient: float32 [2048, 2048], P('col', 'row')
- gate_gradient: float32 [2048, 8192], P('row', 'col')
- up_gradient: float32 [2048, 8192], P('row', 'col')
- down_gradient: float32 [8192, 2048], P('col', 'row')
The draws below stay inside these ranges and needn't reach their ends.
Inputs may be any that keep to these rules, and one draw needn't show every extreme that they name: `valid`: 1 marks a token that counts in the loss. `segment_ids`: along each group's row the ids never fall: segment 0, the prompt, holds at least 2048 tokens at the start, then continuations 1 to 8 follow in order, each of 128 to 256 tokens.
All inputs are finite; a program needn't handle non-finite values.
Results may differ from the reference program's by a relative error of at most 0.014.
The reference program's roundings to bfloat16 on the way count: a program that leaves them out, or rounds other values in their place, can miss the bound.
Values may be sent and summed in bfloat16 or wider, within the bound.
No kernel may reach another device: no remote copies, remote signals or barrier semaphores. Data moves between devices by JAX's collectives and lax.ppermute only.
A program may use at most 448 MiB of HBM per device.

```python
import math
import jax
import jax.numpy as jnp
from jax import lax

D = 2048
HEADS = 16
HD = 128
FF = 8192
CONT_LEN = 256
CONT = 8
G_TOK = 4096
GROUPS = 2
TOKENS = 8192


def draw_valid(key, part):
    key = jax.random.fold_in(key, 11)
    indices = jnp.arange(TOKENS, dtype=jnp.int32)
    levels = 20 + 75 * indices // TOKENS
    return (jax.random.randint(key, (TOKENS,), 0, 100) < levels).astype(jnp.int32)


def draw_segment_ids(key, part):
    key = jax.random.fold_in(key, 7)
    lengths = jax.random.randint(key, (GROUPS, CONT), CONT_LEN // 2, CONT_LEN + 1).astype(jnp.int32)
    tails = jnp.cumsum(lengths[:, ::-1], axis=1)[:, ::-1].astype(jnp.int32)
    starts = G_TOK - tails
    indices = jnp.arange(G_TOK, dtype=jnp.int32)
    return jnp.sum((indices[None, :, None] >= starts[:, None, :]).astype(jnp.int32), axis=2).astype(jnp.int32)


def steps_of(own_key, shape, split, least, top_value):
    level = 1.0
    for axis_at, parts in split:
        draws = jax.random.uniform(jax.random.fold_in(jax.random.fold_in(own_key, 6), axis_at), (parts,), jnp.float32, least / len(split), top_value / len(split))
        level = level * jnp.repeat(jnp.exp(draws), shape[axis_at] // parts).reshape((-1,) + (1,) * (len(shape) - 1 - axis_at))
    return level


def bell_draw(key, shape, scale, bound, split=(), kind=jnp.bfloat16):
    array = jax.random.normal(key, shape, jnp.float32) * scale
    if len(split) > 0:
        array = steps_of(key, shape, split, -0.22, 0.18) * array
    return jnp.clip(array, min=-bound, max=bound).astype(kind)


def setup_inputs(seed: int = 0) -> dict:
    arg_keys = jax.random.split(jax.random.key(seed), 12)
    return {
        "hidden_in": bell_draw(arg_keys[0], (TOKENS, D), 1.0, 6.0, ((0, 8), (1, 4))),
        "teacher": bell_draw(arg_keys[1], (TOKENS, D), 1.0, 6.0, ((0, 8), (1, 4))),
        "valid": draw_valid(jax.random.fold_in(arg_keys[11], 71), 0),
        "segment_ids": draw_segment_ids(jax.random.fold_in(arg_keys[11], 71), 0),
        "query_weight": bell_draw(arg_keys[4], (D, D), (D // 2) ** -0.5, 0.1875, ((0, 4), (1, 4))),
        "key_weight": bell_draw(arg_keys[5], (D, D), (D // 2) ** -0.5, 0.1875, ((0, 4), (1, 4))),
        "value_weight": bell_draw(arg_keys[6], (D, D), D ** -0.5, 0.125, ((0, 4), (1, 4))),
        "output_weight": bell_draw(arg_keys[7], (D, D), (max(8, D // 64)) ** -0.5, 1.0, ((0, 4), (1, 4))),
        "gate_weight": bell_draw(arg_keys[8], (D, FF), D ** -0.5, 0.125, ((0, 4), (1, 4))),
        "up_weight": bell_draw(arg_keys[9], (D, FF), D ** -0.5, 0.125, ((0, 4), (1, 4))),
        "down_weight": bell_draw(arg_keys[10], (FF, D), (FF // 2) ** -0.5, 0.09375, ((0, 4), (1, 4))),
    }


@jax.custom_vjp
def low(v):
    return lax.optimization_barrier(v.astype(jnp.bfloat16)).astype(jnp.float32)

@jax.custom_vjp
def low_back(v):
    return v

def low_keep(v):
    return (low(v), None)

def low_pass(kept, grad):
    return (grad,)

def back_keep(v):
    return (v, None)

def back_low(kept, grad):
    return (low(grad),)
low.defvjp(low_keep, low_pass)
low_back.defvjp(back_keep, back_low)
EPSILON = 1e-05
MASKED_SCORE = -1e+30
HIGHEST = lax.Precision.HIGHEST

def positions(segment):
    labels = jnp.arange(CONT + 1, dtype=jnp.int32)
    onehot = (segment[:, None] == labels[None, :]).astype(jnp.int32)
    counts = lax.optimization_barrier(jnp.sum(onehot, axis=0)).astype(jnp.int32)
    starts = (jnp.cumsum(counts) - counts).astype(jnp.int32)
    leading = lax.optimization_barrier(jnp.sum(onehot * starts[None, :], axis=1)).astype(jnp.int32)
    indices = jnp.arange(segment.shape[0], dtype=jnp.int32)
    return indices - leading + jnp.where(segment > 0, counts[0], 0).astype(jnp.int32)

def rotary(offsets):
    half_width = HD // 2
    frequency = jnp.power(10000.0, jnp.arange(half_width, dtype=jnp.float32) * (-2.0 / HD))
    angles = offsets.astype(jnp.float32)[:, None] * frequency[None, :]
    return (jnp.cos(angles), jnp.sin(angles))

def rotate(values, cosine, sine_table):
    half_width = values.shape[-1] // 2
    leading, trailing = (values[..., :half_width], values[..., half_width:])
    cos_wide = cosine[:, None, :]
    sin_wide = sine_table[:, None, :]
    return jnp.concatenate((leading * cos_wide - trailing * sin_wide, trailing * cos_wide + leading * sin_wide), axis=-1)

def layer_norm(values):
    average = lax.optimization_barrier(jnp.mean(values, axis=1, keepdims=True))
    square = lax.optimization_barrier(jnp.mean(values * values, axis=1, keepdims=True))
    return (values - average) * lax.rsqrt(square - average * average + EPSILON)

def attention(queries, key_rows, value_rows, segment):
    length = queries.shape[0]
    block = math.gcd(length, 512)
    scale = 1.0 / math.sqrt(HD)
    indices = jnp.arange(length, dtype=jnp.int32)

    def one_block(offset):
        query_block = lax.dynamic_slice_in_dim(queries, offset, block, 0)
        query_segment = lax.dynamic_slice_in_dim(segment, offset, block, 0)
        query_index = offset + jnp.arange(block, dtype=jnp.int32)
        allowed = (indices[None, :] <= query_index[:, None]) & ((segment[None, :] == 0) | (segment[None, :] == query_segment[:, None]))
        scores = low_back(jnp.einsum('qhd,khd->hqk', query_block, key_rows, precision=HIGHEST) * scale)
        scores = jnp.where(allowed[None, :, :], scores, MASKED_SCORE)
        probability = low(jax.nn.softmax(scores, axis=-1))
        mixed_block = jnp.einsum('hqk,khd->qhd', probability, value_rows, precision=HIGHEST)
        return mixed_block.reshape(block, HEADS * HD)
    offsets = jnp.arange(length // block, dtype=jnp.int32) * block
    return lax.map(jax.checkpoint(one_block), offsets).reshape(length, HEADS * HD)

def group_forward(matrices, hidden, target, counted, segment):
    query_weight, key_weight, value_weight, output_weight, gate_weight, up_weight, down_weight = matrices
    length = hidden.shape[0]
    cosine, sine_table = rotary(positions(segment))
    normed = low(layer_norm(hidden))
    queries = low_back(jnp.dot(normed, query_weight, precision=HIGHEST)).reshape(length, HEADS, HD)
    key_rows = low_back(jnp.dot(normed, key_weight, precision=HIGHEST)).reshape(length, HEADS, HD)
    value_rows = low(low_back(jnp.dot(normed, value_weight, precision=HIGHEST))).reshape(length, HEADS, HD)
    queries = low(rotate(queries, cosine, sine_table))
    key_rows = low(rotate(key_rows, cosine, sine_table))
    attended = low(low_back(attention(queries, key_rows, value_rows, segment)))
    after_attention = hidden + low_back(jnp.dot(attended, output_weight, precision=HIGHEST))
    normed_two = low(layer_norm(after_attention))
    gating = low_back(jnp.dot(normed_two, gate_weight, precision=HIGHEST))
    upward = low_back(jnp.dot(normed_two, up_weight, precision=HIGHEST))
    hidden_units = low(jax.nn.silu(gating) * upward)
    output = after_attention + low_back(jnp.dot(hidden_units, down_weight, precision=HIGHEST))
    differ = output - target
    return (output, jnp.sum(counted * lax.optimization_barrier(jnp.mean(differ * differ, axis=1))))

def reference(hidden_in, teacher, valid, segment_ids, query_weight, key_weight, value_weight, output_weight, gate_weight, up_weight, down_weight):
    weights = tuple((matrix.astype(jnp.float32) for matrix in (query_weight, key_weight, value_weight, output_weight, gate_weight, up_weight, down_weight)))
    hidden = hidden_in.astype(jnp.float32).reshape(GROUPS, G_TOK, D)
    target = teacher.astype(jnp.float32).reshape(GROUPS, G_TOK, D)
    counted = valid.astype(jnp.float32).reshape(GROUPS, G_TOK)
    total_count = jnp.maximum(jnp.sum(counted), 1.0)

    def objective(matrices, inputs):

        def one_group(carry, group):
            group_hidden, group_target, group_counted, group_segment = group
            output, partial_loss = group_forward(matrices, group_hidden, group_target, group_counted, group_segment)
            return (carry + partial_loss, output)
        summed, outputs = lax.scan(one_group, jnp.zeros((), jnp.float32), (inputs, target, counted, segment_ids))
        return (summed / total_count, outputs)
    mean_loss, pullback, outputs = jax.vjp(objective, weights, hidden, has_aux=True)
    weight_grads, input_grad = pullback(jnp.ones_like(mean_loss) * (TOKENS * D / 2.0))
    return (outputs.reshape(TOKENS, D).astype(jnp.bfloat16), mean_loss.reshape(1), input_grad.reshape(TOKENS, D), weight_grads[0], weight_grads[1], weight_grads[2], weight_grads[3], weight_grads[4], weight_grads[5], weight_grads[6])
```

```python
import math

import jax
import jax.numpy as jnp
from jax import lax
from jax.experimental import pallas as pl
from jax.experimental.pallas import tpu as pltpu
from jax.sharding import PartitionSpec as P

D = 2048
HD = 128
CONT = 8


EPSILON = 1e-05
MASKED_SCORE = -1e30


def positions(segment):
    labels = jnp.arange(CONT + 1, dtype=jnp.int32)
    onehot = (segment[:, None] == labels[None, :]).astype(jnp.int32)
    counts = jnp.sum(onehot, axis=0)
    starts = jnp.cumsum(counts) - counts
    leading = jnp.sum(onehot * starts[None, :], axis=1)
    indices = jnp.arange(segment.shape[0], dtype=jnp.int32)
    return indices - leading + jnp.where(segment > 0, counts[0], 0)


def rotary(offsets):
    half_width = HD // 2
    frequency = jnp.power(10000.0, jnp.arange(half_width, dtype=jnp.float32) * (-2.0 / HD))
    angles = offsets.astype(jnp.float32)[:, None] * frequency[None, :]
    return (jnp.cos(angles), jnp.sin(angles))


def rotate(values, cosine, sine_table):
    half_width = values.shape[-1] // 2
    leading, trailing = (values[..., :half_width], values[..., half_width:])
    cos_wide = cosine[:, None, :]
    sin_wide = sine_table[:, None, :]
    return jnp.concatenate(
        (leading * cos_wide - trailing * sin_wide, trailing * cos_wide + leading * sin_wide),
        axis=-1,
    )


def unrotate(gradient, cosine, sine_table):
    half_width = gradient.shape[-1] // 2
    leading, trailing = (gradient[..., :half_width], gradient[..., half_width:])
    cos_wide = cosine[:, None, :]
    sin_wide = sine_table[:, None, :]
    return jnp.concatenate(
        (leading * cos_wide + trailing * sin_wide, trailing * cos_wide - leading * sin_wide),
        axis=-1,
    )


def feature_sums(left, right):
    return lax.psum((jnp.sum(left, axis=1), jnp.sum(right, axis=1)), "row")


def normalize(values):
    summed, squared = feature_sums(values, values * values)
    average = (summed / D)[:, None]
    inverse = lax.rsqrt(squared[:, None] / D - average * average + EPSILON)
    return ((values - average) * inverse, inverse)


def norm_backward(gradient, normed, inverse):
    summed, crossed = feature_sums(gradient, gradient * normed)
    return inverse * (gradient - summed[:, None] / D - normed * (crossed[:, None] / D))


def widen(values):
    return lax.all_gather(values, "col", axis=0, tiled=True)


def collect(values):
    return lax.all_gather(values, "row", axis=0, tiled=True)


def row_product(full, matrix, contract):
    return lax.psum_scatter(
        lax.dot_general(
            full, matrix, (((1,), (contract,)), ((), ())), preferred_element_type=jnp.float32
        ),
        "row",
        scatter_dimension=0,
        tiled=True,
    )


def column_product(full, matrix, contract):
    return lax.psum_scatter(
        lax.dot_general(
            full, matrix, (((1,), (contract,)), ((), ())), preferred_element_type=jnp.float32
        ),
        "col",
        scatter_dimension=0,
        tiled=True,
    )


def project_in(gathered, matrix):
    result = row_product(gathered, matrix, 0)
    return result


def project_back(gathered, matrix):
    result = row_product(gathered, matrix, 1)
    return result


def weight_product(left, right):
    return lax.dot_general(
        left, right, (((0,), (0,)), ((), ())), preferred_element_type=jnp.float32
    )


def block_layout(tok_rows):
    blocks = max(1, tok_rows // 512)
    return (blocks, tok_rows // blocks)


def score_maker(key_rows, segment, block):
    key_index = jnp.arange(key_rows.shape[0], dtype=jnp.int32)
    scale = 1.0 / math.sqrt(HD)

    def scores_for(query_block, offset):
        query_index = offset + jnp.arange(block, dtype=jnp.int32)
        query_segment = lax.dynamic_slice_in_dim(segment, offset, block, 0)
        allowed = (key_index[None, :] <= query_index[:, None]) & (
            (segment[None, :] == 0) | (segment[None, :] == query_segment[:, None])
        )
        scores = (
            jnp.einsum("qhd,khd->hqk", query_block, key_rows, preferred_element_type=jnp.float32)
            * scale
        )
        return jnp.where(allowed[None, :, :], scores, MASKED_SCORE)

    return scores_for


def attend(queries, key_rows, value_rows, segment, row_offset):
    tok_rows, heads_here = (queries.shape[0], queries.shape[1])
    blocks, block = block_layout(tok_rows)
    scores_for = score_maker(key_rows, segment, block)
    offsets = row_offset + jnp.arange(blocks, dtype=jnp.int32) * block

    def forward_block(inputs):
        query_block, offset = inputs
        scores = scores_for(query_block, offset)
        highest = jnp.max(scores, axis=-1, keepdims=True)
        exponent = jnp.exp(scores - highest)
        summed = jnp.sum(exponent, axis=-1, keepdims=True)
        probability = (exponent / summed).astype(jnp.bfloat16)
        mixed_block = jnp.einsum(
            "hqk,khd->qhd", probability, value_rows, preferred_element_type=jnp.float32
        )
        return (mixed_block, highest + jnp.log(summed))

    mixed_blocks, log_total = lax.map(
        forward_block, (queries.reshape(blocks, block, heads_here, HD), offsets)
    )
    return (mixed_blocks.reshape(tok_rows, heads_here * HD), log_total)


def attend_back(queries, key_rows, value_rows, segment, row_offset, log_total, attended_grad):
    tok_rows, heads_here = (queries.shape[0], queries.shape[1])
    blocks, block = block_layout(tok_rows)
    scores_for = score_maker(key_rows, segment, block)
    offsets = row_offset + jnp.arange(blocks, dtype=jnp.int32) * block
    scale = 1.0 / math.sqrt(HD)

    def backward_block(carry, inputs):
        key_sum, value_sum = carry
        query_block, grad_block, log_block, offset = inputs
        scores = scores_for(query_block, offset)
        probability = jnp.exp(scores - log_block)
        rounded = probability.astype(jnp.bfloat16)
        prob_grad = jnp.einsum(
            "qhd,khd->hqk", grad_block, value_rows, preferred_element_type=jnp.float32
        )
        row_dot = jnp.sum(probability * prob_grad, axis=-1, keepdims=True)
        score_grad = (probability * (prob_grad - row_dot)).astype(jnp.bfloat16)
        query_grad = (
            jnp.einsum("hqk,khd->qhd", score_grad, key_rows, preferred_element_type=jnp.float32)
            * scale
        )
        key_sum = (
            key_sum
            + jnp.einsum(
                "hqk,qhd->khd", score_grad, query_block, preferred_element_type=jnp.float32
            )
            * scale
        )
        value_sum = value_sum + jnp.einsum(
            "hqk,qhd->khd", rounded, grad_block, preferred_element_type=jnp.float32
        )
        return ((key_sum, value_sum), query_grad)

    empty = jnp.zeros(key_rows.shape, jnp.float32)
    inputs = (
        queries.reshape(blocks, block, heads_here, HD),
        attended_grad.reshape(blocks, block, heads_here, HD),
        log_total,
        offsets,
    )
    (key_sum, value_sum), query_grads = lax.scan(backward_block, (empty, empty), inputs)
    return (query_grads.reshape(tok_rows, heads_here, HD), key_sum, value_sum)


def shards(
    hidden_in,
    teacher,
    valid,
    segment_ids,
    query_weight,
    key_weight,
    value_weight,
    output_weight,
    gate_weight,
    up_weight,
    down_weight,
):
    row_devices = lax.axis_size("row")
    col_devices = lax.axis_size("col")
    tok_cols = hidden_in.shape[0]
    group_tokens = tok_cols * col_devices
    tok_rows = group_tokens // row_devices
    query_width = query_weight.shape[1]
    heads_here = query_width // HD
    unit_width = gate_weight.shape[1]
    segment = segment_ids[0]
    row_offset = lax.axis_index("row") * tok_rows
    cosine_all, sine_all = rotary(positions(segment))
    cosine = lax.dynamic_slice_in_dim(cosine_all, row_offset, tok_rows, 0)
    sine_table = lax.dynamic_slice_in_dim(sine_all, row_offset, tok_rows, 0)
    counted = valid.astype(jnp.float32)
    total_count = jnp.maximum(lax.psum(jnp.sum(counted), ("dp", "col")), 1.0)
    hidden = hidden_in.astype(jnp.float32)
    normed, inverse_one = normalize(hidden)
    normed_wide = widen(normed.astype(jnp.bfloat16))
    attn_weights = jnp.concatenate((query_weight, key_weight, value_weight), axis=1)
    projected = project_in(normed_wide, attn_weights)
    queries = rotate(
        projected[:, :query_width].reshape(tok_rows, heads_here, HD), cosine, sine_table
    ).astype(jnp.bfloat16)
    key_local = rotate(
        projected[:, query_width : 2 * query_width].reshape(tok_rows, heads_here, HD),
        cosine,
        sine_table,
    )
    key_local = key_local.reshape(tok_rows, query_width).astype(jnp.bfloat16)
    value_local = projected[:, 2 * query_width :].astype(jnp.bfloat16)
    key_flat, value_flat = (
        lax.all_gather(key_local, "row", axis=0, tiled=True),
        lax.all_gather(value_local, "row", axis=0, tiled=True),
    )
    key_rows = key_flat.reshape(group_tokens, heads_here, HD)
    value_rows = value_flat.reshape(group_tokens, heads_here, HD)
    attended, log_total = attend(queries, key_rows, value_rows, segment, row_offset)
    attended_wide = collect(attended.astype(jnp.bfloat16))
    after_attention = hidden + column_product(attended_wide, output_weight, 0)
    normed_two, inverse_two = normalize(after_attention)
    normed_two_wide = widen(normed_two.astype(jnp.bfloat16))
    mlp_weights = jnp.concatenate((gate_weight, up_weight), axis=1)
    gated = project_in(normed_two_wide, mlp_weights)
    gating = gated[:, :unit_width]
    upward = gated[:, unit_width:]
    sigmoid = jax.nn.sigmoid(gating)
    activated = gating * sigmoid
    units_wide = collect((activated * upward).astype(jnp.bfloat16))
    output = after_attention + column_product(units_wide, down_weight, 0)
    differ = output - teacher.astype(jnp.float32)
    local_loss = jnp.sum(counted[:, None] * (differ * differ)) / D
    all_tokens = group_tokens * lax.axis_size("dp")
    out_grad = counted[:, None] * differ * (all_tokens / total_count)
    out_wide = widen(out_grad.astype(jnp.bfloat16))
    units_grad = project_back(out_wide, down_weight)
    down_grad = weight_product(units_wide, out_wide)
    gating_grad = units_grad * upward * sigmoid * (1.0 + gating * (1.0 - sigmoid))
    upward_grad = units_grad * activated
    gated_wide = collect(jnp.concatenate((gating_grad, upward_grad), axis=1).astype(jnp.bfloat16))
    mlp_grads = weight_product(normed_two_wide, gated_wide)
    normed_two_grad = column_product(gated_wide, mlp_weights, 1)
    middle_grad = out_grad + norm_backward(normed_two_grad, normed_two, inverse_two)
    middle_wide = widen(middle_grad.astype(jnp.bfloat16))
    attended_grad = project_back(middle_wide, output_weight).astype(jnp.bfloat16)
    output_grad_sum = weight_product(attended_wide, middle_wide)
    query_grad, key_sum, value_sum = attend_back(
        queries, key_rows, value_rows, segment, row_offset, log_total, attended_grad
    )
    key_grad, value_grad = (
        lax.psum_scatter(
            key_sum.reshape(group_tokens, query_width), "row", scatter_dimension=0, tiled=True
        ),
        lax.psum_scatter(
            value_sum.reshape(group_tokens, query_width), "row", scatter_dimension=0, tiled=True
        ),
    )
    query_pre = unrotate(query_grad, cosine, sine_table).reshape(tok_rows, query_width)
    key_pre = unrotate(key_grad.reshape(tok_rows, heads_here, HD), cosine, sine_table).reshape(
        tok_rows, query_width
    )
    projected_wide = collect(
        jnp.concatenate((query_pre, key_pre, value_grad), axis=1).astype(jnp.bfloat16)
    )
    attn_grads = weight_product(normed_wide, projected_wide)
    normed_grad = column_product(projected_wide, attn_weights, 1)
    input_gradient = middle_grad + norm_backward(normed_grad, normed, inverse_one)
    summed_grads = (
        lax.psum(attn_grads[:, :query_width].astype(jnp.bfloat16), "dp").astype(jnp.float32),
        lax.psum(attn_grads[:, query_width : 2 * query_width].astype(jnp.bfloat16), "dp").astype(
            jnp.float32
        ),
        lax.psum(attn_grads[:, 2 * query_width :].astype(jnp.bfloat16), "dp").astype(jnp.float32),
        lax.psum(output_grad_sum.astype(jnp.bfloat16), "dp").astype(jnp.float32),
        lax.psum(mlp_grads[:, :unit_width].astype(jnp.bfloat16), "dp").astype(jnp.float32),
        lax.psum(mlp_grads[:, unit_width:].astype(jnp.bfloat16), "dp").astype(jnp.float32),
        lax.psum(down_grad.astype(jnp.bfloat16), "dp").astype(jnp.float32),
    )
    mean_loss = lax.psum(local_loss, ("dp", "row", "col")) / total_count
    return (
        output.astype(jnp.bfloat16),
        mean_loss.reshape(1),
        input_gradient,
        summed_grads[0],
        summed_grads[1],
        summed_grads[2],
        summed_grads[3],
        summed_grads[4],
        summed_grads[5],
        summed_grads[6],
    )


BF = jnp.bfloat16
F32 = jnp.float32
LOG2E = 1.4426950408889634
SIDE = 4


def fits_square(mesh):
    return mesh.shape["dp"] == 2 and mesh.shape["row"] == SIDE and mesh.shape["col"] == SIDE


def flip(values, axis, bit):
    return lax.ppermute(values, axis, [(i, i ^ bit) for i in range(SIDE)])


def flip_x(values):
    return flip(values, "row", 1)


def flip_y(values):
    return flip(values, "row", 2)


def flip_zl(values):
    return flip(values, "col", 1)


def flip_zh(values):
    return flip(values, "col", 2)


def flip_y_zh(values):
    pairs = [
        (r * SIDE + c, (r ^ 2) * SIDE + (c ^ 2)) for r in range(SIDE) for c in range(SIDE)
    ]
    return lax.ppermute(values, ("row", "col"), pairs)


def flip_dp(values):
    return lax.ppermute(values, "dp", [(0, 1), (1, 0)])


def sum_all(value, with_row):
    value = value + flip_dp(value)
    value = value + flip_zl(value)
    value = value + flip_zh(value)
    if with_row:
        value = value + flip_x(value)
        value = value + flip_y(value)
    return value


def square_gather(block):
    half = block.shape[0] // 2
    top, bottom = block[:half], block[half:]
    x_top, z_bottom = flip_x(top), flip_zl(bottom)
    x_bottom, z_top = flip_x(bottom), flip_zl(top)
    d_top, d_bottom = flip_zl(x_top), flip_x(z_bottom)
    join = lambda a, b: jnp.concatenate((a, b), axis=0)
    return [block, join(x_top, x_bottom), join(z_top, z_bottom), join(d_top, d_bottom)]


def square_reduce(make):
    far = make(3)
    half = far.shape[0] // 2
    far = far.astype(BF)
    far_top, far_bottom = flip_zl(far[:half]), flip_x(far[half:])
    by_x, by_z = make(1), make(2)
    x_bottom = flip_x(by_x[half:].astype(BF))
    z_top = flip_zl(by_z[:half].astype(BF))
    x_top = flip_x((by_x[:half] + far_top.astype(F32)).astype(BF))
    z_bottom = flip_zl((by_z[half:] + far_bottom.astype(F32)).astype(BF))
    own = make(0)
    top = own[:half] + x_top.astype(F32) + z_top.astype(F32)
    bottom = own[half:] + x_bottom.astype(F32) + z_bottom.astype(F32)
    return jnp.concatenate((top, bottom), axis=0)


def ordered(flag, own, other, axis):
    return jnp.where(
        flag == 0,
        jnp.concatenate((own, other), axis=axis),
        jnp.concatenate((other, own), axis=axis),
    )


def pick(values, index, axis):
    return lax.dynamic_index_in_dim(values, index, axis, keepdims=False)


def gather_weights(matrices, place, lead):
    x, y, dp = place
    m, rows, n = matrices.shape
    cut = matrices.reshape(m, rows, 2, 2, n // 4)
    cut = pick(cut, dp, 3)
    own, send = pick(cut, x, 2), pick(cut, 1 - x, 2)
    tall = ordered(x, own, flip_x(send), 1)
    pair = jnp.stack((tall, flip_zh(tall)), axis=2)
    full = ordered(y, pair, flip_y(pair), 1)
    other = flip_dp(full)
    slots = ordered(lead, full[:, :, :, None], other[:, :, :, None], 3)
    return slots.reshape(m, 4 * rows, n)


def scatter_grads(grads, place, lead):
    x, y, dp = place
    m, depth, n = grads.shape
    rows = depth // 4
    cut = grads.astype(BF).reshape(m, depth, 2, 2, n // 4)
    keep, send = pick(cut, lead, 3), pick(cut, 1 - lead, 3)
    total = (keep.astype(F32) + flip_dp(send).astype(F32)).astype(BF)
    total = total.reshape(m, 2, 2 * rows, 2, n // 4)
    keep, send = pick(total, y, 1), pick(total, 1 - y, 1)
    total = (keep.astype(F32) + flip_y(send).astype(F32)).astype(BF)
    keep, send = total[:, :, 0], total[:, :, 1]
    total = (keep.astype(F32) + flip_zh(send).astype(F32)).astype(BF)
    total = total.reshape(m, 2, rows, n // 4)
    keep, send = pick(total, x, 1), pick(total, 1 - x, 1)
    both = ordered(x, keep[:, :, None], flip_x(send)[:, :, None], 2)
    whole = ordered(dp, both[:, :, :, None], flip_dp(both)[:, :, :, None], 3)
    return whole.reshape(m, rows, n).astype(F32)


def local_norm(values):
    average = jnp.mean(values, axis=1, keepdims=True)
    square = jnp.mean(values * values, axis=1, keepdims=True)
    inverse = lax.rsqrt(square - average * average + EPSILON)
    return ((values - average) * inverse, inverse)


def local_norm_backward(gradient, normed, inverse):
    average = jnp.mean(gradient, axis=1, keepdims=True)
    crossed = jnp.mean(gradient * normed, axis=1, keepdims=True)
    return inverse * (gradient - average - normed * crossed)


def dot(left, right, a, b):
    return lax.dot_general(left, right, (((a,), (b,)), ((), ())), preferred_element_type=F32)


BLOCK = 512
PIECE = 256


def allowed_pairs(starts, query0, key0, shape, query_axis):
    query = query0 + lax.broadcasted_iota(jnp.int32, shape, query_axis)
    key = key0 + lax.broadcasted_iota(jnp.int32, shape, 1 - query_axis)
    first = jnp.zeros(shape, jnp.int32)
    for s in range(CONT):
        first = jnp.where(query >= starts[s], starts[s], first)
    return (key <= query) & ((key < starts[0]) | (key >= first))


def block_bounds(starts, n):
    full = jnp.minimum(n, starts[0] // BLOCK)
    first = jnp.int32(0)
    for s in range(CONT):
        first = jnp.where(n * BLOCK >= starts[s], starts[s], first)
    return full, first


def block_used(starts, first, m):
    return (m * BLOCK < starts[0]) | ((m + 1) * BLOCK > first)


def attention_forward(place_ref, starts_ref, *refs):
    messages, refs = refs[:4], refs[4:]
    outs, refs = refs[:4], refs[4:]
    wide_ref, log_ref, q_s, k_s, v_s, score_s, acc_s, sum_s, max_s = refs
    scale = LOG2E / math.sqrt(HD)
    starts = [starts_ref[s] for s in range(CONT)]
    for b in range(4):
        for a in range(4):
            rows = pl.ds(pl.multiple_of(place_ref[4 * b + a] * PIECE, PIECE), PIECE)
            q_s[rows, :] = messages[b][0, a]
            k_s[rows, :] = messages[b][1, a]
            v_s[rows, :] = messages[b][2, a]

    def one_block(n, carry):
        rows = pl.ds(pl.multiple_of(n * BLOCK, BLOCK), BLOCK)
        full, first = block_bounds(starts, n)
        max_s[...] = jnp.full(max_s.shape, -1e30, F32)
        acc_s[...] = jnp.zeros(acc_s.shape, F32)
        sum_s[...] = jnp.zeros(sum_s.shape, F32)

        def note(scores, m):
            score_s[m] = scores
            top = max_s[...]
            for part in range(BLOCK // HD):
                top = jnp.maximum(top, scores[:, part * HD : (part + 1) * HD])
            max_s[...] = top

        def product(m):
            keys = pl.ds(pl.multiple_of(m * BLOCK, BLOCK), BLOCK)
            return dot(q_s[rows, :], k_s[keys, :], 1, 1)

        @pl.loop(0, full)
        def _(m):
            note(product(m), m)

        @pl.loop(full, n + 1)
        def _(m):
            @pl.when(block_used(starts, first, m))
            def _():
                allowed = allowed_pairs(starts, n * BLOCK, m * BLOCK, (BLOCK, BLOCK), 0)
                note(jnp.where(allowed, product(m), MASKED_SCORE), m)

        highest = jnp.max(max_s[...], axis=1, keepdims=True) * scale

        @pl.loop(0, n + 1)
        def _(m):
            @pl.when(block_used(starts, first, m))
            def _():
                keys = pl.ds(pl.multiple_of(m * BLOCK, BLOCK), BLOCK)
                exponent = jnp.exp2(score_s[m] * scale - highest)
                total = sum_s[...]
                for part in range(BLOCK // HD):
                    total = total + exponent[:, part * HD : (part + 1) * HD]
                sum_s[...] = total
                acc_s[...] += dot(exponent.astype(BF), v_s[keys, :], 1, 0)

        total = jnp.sum(sum_s[...], axis=1, keepdims=True)
        wide_ref[rows, :] = acc_s[...] / total
        log_total = jnp.broadcast_to(highest + jnp.log2(total), (BLOCK, HD))
        log_ref[n] = log_total.T[:8]
        return carry

    lax.fori_loop(0, k_s.shape[0] // BLOCK, one_block, 0)
    for b in range(4):
        for a in range(4):
            rows = pl.ds(pl.multiple_of(place_ref[4 * b + a] * PIECE, PIECE), PIECE)
            outs[b][a] = wide_ref[rows, :].astype(BF)


def attention_backward(place_ref, starts_ref, *refs):
    messages, refs = refs[:4], refs[4:]
    grads, refs = refs[:4], refs[4:]
    wide_ref, log_ref, cos_ref, sin_ref, *refs = refs
    outs, refs = refs[:4], refs[4:]
    q_s, k_s, v_s, g_s, dq_s, dk_s, dv_s = refs
    scale = LOG2E / math.sqrt(HD)
    starts = [starts_ref[s] for s in range(CONT)]
    for b in range(4):
        for a in range(4):
            rows = pl.ds(pl.multiple_of(place_ref[4 * b + a] * PIECE, PIECE), PIECE)
            q_s[rows, :] = messages[b][0, a]
            k_s[rows, :] = messages[b][1, a]
            v_s[rows, :] = messages[b][2, a]
            g_s[rows, :] = grads[b][a]
    dq_s[...] = jnp.zeros(dq_s.shape, F32)
    dk_s[...] = jnp.zeros(dk_s.shape, F32)
    dv_s[...] = jnp.zeros(dv_s.shape, F32)

    def one_block(n, carry):
        rows = pl.ds(pl.multiple_of(n * BLOCK, BLOCK), BLOCK)
        full, first = block_bounds(starts, n)
        crossed = g_s[rows, :].astype(F32) * wide_ref[rows, :]
        row_dot = jnp.sum(crossed.T, axis=0, keepdims=True)
        log_total = log_ref[n][:1]

        def step(m, masked):
            keys = pl.ds(pl.multiple_of(m * BLOCK, BLOCK), BLOCK)
            query, key = q_s[rows, :], k_s[keys, :]
            probability = jnp.exp2(dot(key, query, 1, 1) * scale - log_total)
            if masked:
                allowed = allowed_pairs(starts, n * BLOCK, m * BLOCK, (BLOCK, BLOCK), 1)
                probability = jnp.where(allowed, probability, 0.0)
            prob_grad = dot(v_s[keys, :], g_s[rows, :], 1, 1)
            score_grad = (probability * (prob_grad - row_dot)).astype(BF)
            dv_s[keys, :] += dot(probability.astype(BF), g_s[rows, :], 1, 0)
            dk_s[keys, :] += dot(score_grad, query, 1, 0)
            dq_s[rows, :] += dot(score_grad, key, 0, 0)

        @pl.loop(0, full)
        def _(m):
            step(m, False)

        @pl.loop(full, n + 1)
        def _(m):
            @pl.when(block_used(starts, first, m))
            def _():
                step(m, True)

        return carry

    lax.fori_loop(0, k_s.shape[0] // BLOCK, one_block, 0)
    for b in range(4):
        for a in range(4):
            rows = pl.ds(pl.multiple_of(place_ref[4 * b + a] * PIECE, PIECE), PIECE)
            for which, grad in ((0, dq_s), (1, dk_s)):
                value = grad[rows, :] * (1.0 / math.sqrt(HD))
                turned = value * cos_ref[rows, :] - pltpu.roll(value, HD // 2, 1) * sin_ref[rows, :]
                outs[b][which, a] = turned.astype(BF)
            outs[b][2, a] = dv_s[rows, :].astype(BF)


SMEM_SPEC = pl.BlockSpec(memory_space=pltpu.SMEM)
VMEM_SPEC = pl.BlockSpec(memory_space=pltpu.VMEM)


def run_forward(place, starts, messages):
    tokens = 16 * PIECE
    blocks = tokens // BLOCK
    out_shape = [jax.ShapeDtypeStruct((4, PIECE, HD), BF)] * 4
    out_shape += [
        jax.ShapeDtypeStruct((tokens, HD), F32),
        jax.ShapeDtypeStruct((blocks, 8, BLOCK), F32),
    ]
    return pl.pallas_call(
        attention_forward,
        out_shape=out_shape,
        in_specs=[SMEM_SPEC] * 2 + [VMEM_SPEC] * 4,
        out_specs=[VMEM_SPEC] * 6,
        scratch_shapes=[
            pltpu.VMEM((tokens, HD), BF),
            pltpu.VMEM((tokens, HD), BF),
            pltpu.VMEM((tokens, HD), BF),
            pltpu.VMEM((blocks, BLOCK, BLOCK), F32),
            pltpu.VMEM((BLOCK, HD), F32),
            pltpu.VMEM((BLOCK, HD), F32),
            pltpu.VMEM((BLOCK, HD), F32),
        ],
        compiler_params=pltpu.CompilerParams(vmem_limit_bytes=48 * 2**20),
        cost_estimate=pl.CostEstimate(
            flops=2 * tokens * tokens * HD * 2,
            bytes_accessed=8 * 2**20,
            transcendentals=tokens * tokens // 2,
        ),
    )(place, starts, *messages)


def run_backward(place, starts, messages, grads, wide, log_total, cosine, sine_table):
    tokens = 16 * PIECE
    return pl.pallas_call(
        attention_backward,
        out_shape=[jax.ShapeDtypeStruct((3, 4, PIECE, HD), BF)] * 4,
        in_specs=[SMEM_SPEC] * 2 + [VMEM_SPEC] * 12,
        out_specs=[VMEM_SPEC] * 4,
        scratch_shapes=[pltpu.VMEM((tokens, HD), BF)] * 4 + [pltpu.VMEM((tokens, HD), F32)] * 3,
        compiler_params=pltpu.CompilerParams(vmem_limit_bytes=52 * 2**20),
        cost_estimate=pl.CostEstimate(
            flops=5 * tokens * tokens * HD * 2,
            bytes_accessed=16 * 2**20,
            transcendentals=tokens * tokens // 2,
        ),
    )(place, starts, *messages, *grads, wide, log_total, cosine, sine_table)


def swap_slots(messages):
    return [messages[0], flip_y(messages[1]), flip_zh(messages[2]), flip_y_zh(messages[3])]


def to_tokens(values):
    return lax.all_to_all(values, "row", split_axis=0, concat_axis=1, tiled=True)


def to_width(values):
    return lax.all_to_all(values, "row", split_axis=1, concat_axis=0, tiled=True)


def square_shards(
    hidden_in,
    teacher,
    valid,
    segment_ids,
    query_weight,
    key_weight,
    value_weight,
    output_weight,
    gate_weight,
    up_weight,
    down_weight,
):
    row, col, dp = lax.axis_index("row"), lax.axis_index("col"), lax.axis_index("dp")
    x, y = row % 2, row // 2
    place = (x, y, dp)
    own_piece = col * SIDE + row
    segment = segment_ids[0]
    group_tokens = segment.shape[0]
    home_tokens = group_tokens // (SIDE * SIDE)
    unit_width = gate_weight.shape[1]

    hidden = to_tokens(hidden_in).astype(F32)
    normed, inverse_one = local_norm(hidden)
    normed_blocks = square_gather(normed.astype(BF))

    lead = (dp + y) % 2
    attn_weights = gather_weights(
        jnp.stack((query_weight, key_weight, value_weight, output_weight.T)), place, lead
    )
    qkv_weight = jnp.concatenate((attn_weights[0], attn_weights[1], attn_weights[2]), axis=1)
    out_weight = attn_weights[3]
    mlp_weights = gather_weights(jnp.stack((gate_weight, up_weight)), place, 0)
    gate_full, up_full = mlp_weights[0], mlp_weights[1]
    down_full = gather_weights(down_weight.T[None], place, 0)[0]

    labels = jnp.arange(1, CONT + 1, dtype=jnp.int32)
    starts = jnp.sum((segment[None, :] < labels[:, None]).astype(jnp.int32), axis=1)
    codes = jnp.arange(16, dtype=jnp.int32)
    relative = (
        (codes & 1) + ((codes >> 2) & 1) * 2 + ((codes >> 1) & 1) * 4 + ((codes >> 3) & 1) * 8
    )
    pieces = relative ^ own_piece
    cosine, sine_table = rotary(positions(segment))
    cos_wide = jnp.concatenate((cosine, cosine), axis=1)
    sin_wide = jnp.concatenate((-sine_table, sine_table), axis=1)

    def turn(values, cos_block, sin_block):
        heads = values.reshape(home_tokens, 4, HD)
        swapped = jnp.concatenate((heads[..., HD // 2 :], heads[..., : HD // 2]), axis=-1)
        return heads * cos_block[:, None] + swapped * sin_block[:, None]

    query_blocks, key_blocks, value_blocks = [], [], []
    for a in range(4):
        projected = dot(normed_blocks[a], qkv_weight, 1, 0)
        cos_block = lax.dynamic_slice_in_dim(cos_wide, pieces[a] * home_tokens, home_tokens, 0)
        sin_block = lax.dynamic_slice_in_dim(sin_wide, pieces[a] * home_tokens, home_tokens, 0)
        width = 4 * HD
        query_blocks.append(turn(projected[:, :width], cos_block, sin_block).astype(BF))
        key_blocks.append(turn(projected[:, width : 2 * width], cos_block, sin_block).astype(BF))
        value_blocks.append(projected[:, 2 * width :].reshape(home_tokens, 4, HD).astype(BF))
    messages = [
        jnp.stack(
            [
                jnp.stack([blocks[a][:, slot] for a in range(4)])
                for blocks in (query_blocks, key_blocks, value_blocks)
            ]
        )
        for slot in range(4)
    ]
    messages = swap_slots(messages)
    *mixed, wide, log_total = run_forward(pieces, starts, messages)
    mixed = swap_slots(mixed)
    attended = [jnp.concatenate([mixed[b][a] for b in range(4)], axis=1) for a in range(4)]
    after_attention = hidden + square_reduce(lambda a: dot(attended[a], out_weight, 1, 1))

    normed_two, inverse_two = local_norm(after_attention)
    normed_two_blocks = square_gather(normed_two.astype(BF))
    gating = [dot(normed_two_blocks[a], gate_full, 1, 0) for a in range(4)]
    upward = [dot(normed_two_blocks[a], up_full, 1, 0) for a in range(4)]
    units = [(gating[a] * jax.nn.sigmoid(gating[a]) * upward[a]).astype(BF) for a in range(4)]
    output = after_attention + square_reduce(lambda a: dot(units[a], down_full, 1, 1))

    counted = valid.astype(F32)
    total_count = jnp.maximum(sum_all(jnp.sum(counted).reshape(1), False), 1.0)
    counted_home = lax.dynamic_slice_in_dim(counted, row * home_tokens, home_tokens, 0)[:, None]
    differ = output - to_tokens(teacher).astype(F32)
    local_loss = jnp.sum(counted_home * (differ * differ)) / D
    mean_loss = sum_all(local_loss.reshape(1), True) / total_count
    all_tokens = group_tokens * lax.axis_size("dp")
    out_grad = counted_home * differ * (all_tokens / total_count)

    out_blocks = square_gather(out_grad.astype(BF))
    gate_low, up_low = [], []
    for a in range(4):
        units_grad = dot(out_blocks[a], down_full, 1, 0)
        sigmoid = jax.nn.sigmoid(gating[a])
        gate_low.append(
            (units_grad * upward[a] * sigmoid * (1.0 + gating[a] * (1.0 - sigmoid))).astype(BF)
        )
        up_low.append((units_grad * (gating[a] * sigmoid)).astype(BF))
    normed_two_grad = square_reduce(
        lambda a: dot(gate_low[a], gate_full, 1, 1) + dot(up_low[a], up_full, 1, 1)
    )
    middle_grad = out_grad + local_norm_backward(normed_two_grad, normed_two, inverse_two)

    join = lambda blocks: jnp.concatenate(blocks, axis=0)
    out_wide = join(out_blocks)
    down_grad = scatter_grads(dot(out_wide, join(units), 0, 0)[None], place, 0)
    normed_two_wide = join(normed_two_blocks)
    mlp_grads = scatter_grads(
        jnp.stack(
            (dot(normed_two_wide, join(gate_low), 0, 0), dot(normed_two_wide, join(up_low), 0, 0))
        ),
        place,
        0,
    )

    middle_blocks = square_gather(middle_grad.astype(BF))
    attended_grad = [dot(middle_blocks[a], out_weight, 1, 0).astype(BF) for a in range(4)]
    grad_messages = [
        jnp.stack([attended_grad[a][:, slot * HD : (slot + 1) * HD] for a in range(4)])
        for slot in range(4)
    ]
    grad_messages = swap_slots(grad_messages)
    back = run_backward(
        pieces, starts, messages, grad_messages, wide, log_total, cos_wide, sin_wide
    )
    back = swap_slots(back)
    projected_low = [
        jnp.concatenate([back[b][which, a] for which in range(3) for b in range(4)], axis=1)
        for a in range(4)
    ]
    normed_grad = square_reduce(lambda a: dot(projected_low[a], qkv_weight, 1, 1))
    input_gradient = middle_grad + local_norm_backward(normed_grad, normed, inverse_one)

    width = 4 * HD
    qkv_grad = dot(join(normed_blocks), join(projected_low), 0, 0)
    out_weight_grad = dot(join(middle_blocks), join(attended), 0, 0)
    attn_grads = scatter_grads(
        jnp.stack(
            (
                qkv_grad[:, :width],
                qkv_grad[:, width : 2 * width],
                qkv_grad[:, 2 * width :],
                out_weight_grad,
            )
        ),
        place,
        lead,
    )
    return (
        to_width(output.astype(BF)),
        mean_loss,
        to_width(input_gradient),
        attn_grads[0],
        attn_grads[1],
        attn_grads[2],
        attn_grads[3].T,
        mlp_grads[0],
        mlp_grads[1],
        down_grad[0].T,
    )


def solution(mesh):
    body = square_shards if fits_square(mesh) else shards
    in_specs = (
        P(("dp", "col"), "row"),
        P(("dp", "col"), "row"),
        P(("dp", "col")),
        P("dp", None),
        P("row", "col"),
        P("row", "col"),
        P("row", "col"),
        P("col", "row"),
        P("row", "col"),
        P("row", "col"),
        P("col", "row"),
    )
    out_specs = (
        P(("dp", "col"), "row"),
        P(),
        P(("dp", "col"), "row"),
        P("row", "col"),
        P("row", "col"),
        P("row", "col"),
        P("col", "row"),
        P("row", "col"),
        P("row", "col"),
        P("col", "row"),
    )
    return jax.shard_map(body, mesh=mesh, in_specs=in_specs, out_specs=out_specs, check_vma=False)
```

```python
import math

import jax
import jax.numpy as jnp
from jax import lax
from jax.experimental import pallas as pl
from jax.experimental.pallas import tpu as pltpu
from jax.sharding import PartitionSpec as P

D = 2048
HD = 128
CONT = 8


EPSILON = 1e-05
MASKED_SCORE = -1e30


def positions(segment):
    labels = jnp.arange(CONT + 1, dtype=jnp.int32)
    onehot = (segment[:, None] == labels[None, :]).astype(jnp.int32)
    counts = jnp.sum(onehot, axis=0)
    starts = jnp.cumsum(counts) - counts
    leading = jnp.sum(onehot * starts[None, :], axis=1)
    indices = jnp.arange(segment.shape[0], dtype=jnp.int32)
    return indices - leading + jnp.where(segment > 0, counts[0], 0)


def rotary(offsets):
    half_width = HD // 2
    frequency = jnp.power(10000.0, jnp.arange(half_width, dtype=jnp.float32) * (-2.0 / HD))
    angles = offsets.astype(jnp.float32)[:, None] * frequency[None, :]
    return (jnp.cos(angles), jnp.sin(angles))


def rotate(values, cosine, sine_table):
    half_width = values.shape[-1] // 2
    leading, trailing = (values[..., :half_width], values[..., half_width:])
    cos_wide = cosine[:, None, :]
    sin_wide = sine_table[:, None, :]
    return jnp.concatenate(
        (leading * cos_wide - trailing * sin_wide, trailing * cos_wide + leading * sin_wide),
        axis=-1,
    )


def unrotate(gradient, cosine, sine_table):
    half_width = gradient.shape[-1] // 2
    leading, trailing = (gradient[..., :half_width], gradient[..., half_width:])
    cos_wide = cosine[:, None, :]
    sin_wide = sine_table[:, None, :]
    return jnp.concatenate(
        (leading * cos_wide + trailing * sin_wide, trailing * cos_wide - leading * sin_wide),
        axis=-1,
    )


def feature_sums(left, right):
    return lax.psum((jnp.sum(left, axis=1), jnp.sum(right, axis=1)), "row")


def normalize(values):
    summed, squared = feature_sums(values, values * values)
    average = (summed / D)[:, None]
    inverse = lax.rsqrt(squared[:, None] / D - average * average + EPSILON)
    return ((values - average) * inverse, inverse)


def norm_backward(gradient, normed, inverse):
    summed, crossed = feature_sums(gradient, gradient * normed)
    return inverse * (gradient - summed[:, None] / D - normed * (crossed[:, None] / D))


def widen(values):
    return lax.all_gather(values, "col", axis=0, tiled=True)


def collect(values):
    return lax.all_gather(values, "row", axis=0, tiled=True)


def row_product(full, matrix, contract):
    return lax.psum_scatter(
        lax.dot_general(
            full, matrix, (((1,), (contract,)), ((), ())), preferred_element_type=jnp.float32
        ),
        "row",
        scatter_dimension=0,
        tiled=True,
    )


def column_product(full, matrix, contract):
    return lax.psum_scatter(
        lax.dot_general(
            full, matrix, (((1,), (contract,)), ((), ())), preferred_element_type=jnp.float32
        ),
        "col",
        scatter_dimension=0,
        tiled=True,
    )


def project_in(gathered, matrix):
    result = row_product(gathered, matrix, 0)
    return result


def project_back(gathered, matrix):
    result = row_product(gathered, matrix, 1)
    return result


def weight_product(left, right):
    return lax.dot_general(
        left, right, (((0,), (0,)), ((), ())), preferred_element_type=jnp.float32
    )


def block_layout(tok_rows):
    blocks = max(1, tok_rows // 512)
    return (blocks, tok_rows // blocks)


def score_maker(key_rows, segment, block):
    key_index = jnp.arange(key_rows.shape[0], dtype=jnp.int32)
    scale = 1.0 / math.sqrt(HD)

    def scores_for(query_block, offset):
        query_index = offset + jnp.arange(block, dtype=jnp.int32)
        query_segment = lax.dynamic_slice_in_dim(segment, offset, block, 0)
        allowed = (key_index[None, :] <= query_index[:, None]) & (
            (segment[None, :] == 0) | (segment[None, :] == query_segment[:, None])
        )
        scores = (
            jnp.einsum("qhd,khd->hqk", query_block, key_rows, preferred_element_type=jnp.float32)
            * scale
        )
        return jnp.where(allowed[None, :, :], scores, MASKED_SCORE)

    return scores_for


def attend(queries, key_rows, value_rows, segment, row_offset):
    tok_rows, heads_here = (queries.shape[0], queries.shape[1])
    blocks, block = block_layout(tok_rows)
    scores_for = score_maker(key_rows, segment, block)
    offsets = row_offset + jnp.arange(blocks, dtype=jnp.int32) * block

    def forward_block(inputs):
        query_block, offset = inputs
        scores = scores_for(query_block, offset)
        highest = jnp.max(scores, axis=-1, keepdims=True)
        exponent = jnp.exp(scores - highest)
        summed = jnp.sum(exponent, axis=-1, keepdims=True)
        probability = (exponent / summed).astype(jnp.bfloat16)
        mixed_block = jnp.einsum(
            "hqk,khd->qhd", probability, value_rows, preferred_element_type=jnp.float32
        )
        return (mixed_block, highest + jnp.log(summed))

    mixed_blocks, log_total = lax.map(
        forward_block, (queries.reshape(blocks, block, heads_here, HD), offsets)
    )
    return (mixed_blocks.reshape(tok_rows, heads_here * HD), log_total)


def attend_back(queries, key_rows, value_rows, segment, row_offset, log_total, attended_grad):
    tok_rows, heads_here = (queries.shape[0], queries.shape[1])
    blocks, block = block_layout(tok_rows)
    scores_for = score_maker(key_rows, segment, block)
    offsets = row_offset + jnp.arange(blocks, dtype=jnp.int32) * block
    scale = 1.0 / math.sqrt(HD)

    def backward_block(carry, inputs):
        key_sum, value_sum = carry
        query_block, grad_block, log_block, offset = inputs
        scores = scores_for(query_block, offset)
        probability = jnp.exp(scores - log_block)
        rounded = probability.astype(jnp.bfloat16)
        prob_grad = jnp.einsum(
            "qhd,khd->hqk", grad_block, value_rows, preferred_element_type=jnp.float32
        )
        row_dot = jnp.sum(probability * prob_grad, axis=-1, keepdims=True)
        score_grad = (probability * (prob_grad - row_dot)).astype(jnp.bfloat16)
        query_grad = (
            jnp.einsum("hqk,khd->qhd", score_grad, key_rows, preferred_element_type=jnp.float32)
            * scale
        )
        key_sum = (
            key_sum
            + jnp.einsum(
                "hqk,qhd->khd", score_grad, query_block, preferred_element_type=jnp.float32
            )
            * scale
        )
        value_sum = value_sum + jnp.einsum(
            "hqk,qhd->khd", rounded, grad_block, preferred_element_type=jnp.float32
        )
        return ((key_sum, value_sum), query_grad)

    empty = jnp.zeros(key_rows.shape, jnp.float32)
    inputs = (
        queries.reshape(blocks, block, heads_here, HD),
        attended_grad.reshape(blocks, block, heads_here, HD),
        log_total,
        offsets,
    )
    (key_sum, value_sum), query_grads = lax.scan(backward_block, (empty, empty), inputs)
    return (query_grads.reshape(tok_rows, heads_here, HD), key_sum, value_sum)


def shards(
    hidden_in,
    teacher,
    valid,
    segment_ids,
    query_weight,
    key_weight,
    value_weight,
    output_weight,
    gate_weight,
    up_weight,
    down_weight,
):
    row_devices = lax.axis_size("row")
    col_devices = lax.axis_size("col")
    tok_cols = hidden_in.shape[0]
    group_tokens = tok_cols * col_devices
    tok_rows = group_tokens // row_devices
    query_width = query_weight.shape[1]
    heads_here = query_width // HD
    unit_width = gate_weight.shape[1]
    segment = segment_ids[0]
    row_offset = lax.axis_index("row") * tok_rows
    cosine_all, sine_all = rotary(positions(segment))
    cosine = lax.dynamic_slice_in_dim(cosine_all, row_offset, tok_rows, 0)
    sine_table = lax.dynamic_slice_in_dim(sine_all, row_offset, tok_rows, 0)
    counted = valid.astype(jnp.float32)
    total_count = jnp.maximum(lax.psum(jnp.sum(counted), ("dp", "col")), 1.0)
    hidden = hidden_in.astype(jnp.float32)
    normed, inverse_one = normalize(hidden)
    normed_wide = widen(normed.astype(jnp.bfloat16))
    attn_weights = jnp.concatenate((query_weight, key_weight, value_weight), axis=1)
    projected = project_in(normed_wide, attn_weights)
    queries = rotate(
        projected[:, :query_width].reshape(tok_rows, heads_here, HD), cosine, sine_table
    ).astype(jnp.bfloat16)
    key_local = rotate(
        projected[:, query_width : 2 * query_width].reshape(tok_rows, heads_here, HD),
        cosine,
        sine_table,
    )
    key_local = key_local.reshape(tok_rows, query_width).astype(jnp.bfloat16)
    value_local = projected[:, 2 * query_width :].astype(jnp.bfloat16)
    key_flat, value_flat = (
        lax.all_gather(key_local, "row", axis=0, tiled=True),
        lax.all_gather(value_local, "row", axis=0, tiled=True),
    )
    key_rows = key_flat.reshape(group_tokens, heads_here, HD)
    value_rows = value_flat.reshape(group_tokens, heads_here, HD)
    attended, log_total = attend(queries, key_rows, value_rows, segment, row_offset)
    attended_wide = collect(attended.astype(jnp.bfloat16))
    after_attention = hidden + column_product(attended_wide, output_weight, 0)
    normed_two, inverse_two = normalize(after_attention)
    normed_two_wide = widen(normed_two.astype(jnp.bfloat16))
    mlp_weights = jnp.concatenate((gate_weight, up_weight), axis=1)
    gated = project_in(normed_two_wide, mlp_weights)
    gating = gated[:, :unit_width]
    upward = gated[:, unit_width:]
    sigmoid = jax.nn.sigmoid(gating)
    activated = gating * sigmoid
    units_wide = collect((activated * upward).astype(jnp.bfloat16))
    output = after_attention + column_product(units_wide, down_weight, 0)
    differ = output - teacher.astype(jnp.float32)
    local_loss = jnp.sum(counted[:, None] * (differ * differ)) / D
    all_tokens = group_tokens * lax.axis_size("dp")
    out_grad = counted[:, None] * differ * (all_tokens / total_count)
    out_wide = widen(out_grad.astype(jnp.bfloat16))
    units_grad = project_back(out_wide, down_weight)
    down_grad = weight_product(units_wide, out_wide)
    gating_grad = units_grad * upward * sigmoid * (1.0 + gating * (1.0 - sigmoid))
    upward_grad = units_grad * activated
    gated_wide = collect(jnp.concatenate((gating_grad, upward_grad), axis=1).astype(jnp.bfloat16))
    mlp_grads = weight_product(normed_two_wide, gated_wide)
    normed_two_grad = column_product(gated_wide, mlp_weights, 1)
    middle_grad = out_grad + norm_backward(normed_two_grad, normed_two, inverse_two)
    middle_wide = widen(middle_grad.astype(jnp.bfloat16))
    attended_grad = project_back(middle_wide, output_weight).astype(jnp.bfloat16)
    output_grad_sum = weight_product(attended_wide, middle_wide)
    query_grad, key_sum, value_sum = attend_back(
        queries, key_rows, value_rows, segment, row_offset, log_total, attended_grad
    )
    key_grad, value_grad = (
        lax.psum_scatter(
            key_sum.reshape(group_tokens, query_width), "row", scatter_dimension=0, tiled=True
        ),
        lax.psum_scatter(
            value_sum.reshape(group_tokens, query_width), "row", scatter_dimension=0, tiled=True
        ),
    )
    query_pre = unrotate(query_grad, cosine, sine_table).reshape(tok_rows, query_width)
    key_pre = unrotate(key_grad.reshape(tok_rows, heads_here, HD), cosine, sine_table).reshape(
        tok_rows, query_width
    )
    projected_wide = collect(
        jnp.concatenate((query_pre, key_pre, value_grad), axis=1).astype(jnp.bfloat16)
    )
    attn_grads = weight_product(normed_wide, projected_wide)
    normed_grad = column_product(projected_wide, attn_weights, 1)
    input_gradient = middle_grad + norm_backward(normed_grad, normed, inverse_one)
    summed_grads = (
        lax.psum(attn_grads[:, :query_width].astype(jnp.bfloat16), "dp").astype(jnp.float32),
        lax.psum(attn_grads[:, query_width : 2 * query_width].astype(jnp.bfloat16), "dp").astype(
            jnp.float32
        ),
        lax.psum(attn_grads[:, 2 * query_width :].astype(jnp.bfloat16), "dp").astype(jnp.float32),
        lax.psum(output_grad_sum.astype(jnp.bfloat16), "dp").astype(jnp.float32),
        lax.psum(mlp_grads[:, :unit_width].astype(jnp.bfloat16), "dp").astype(jnp.float32),
        lax.psum(mlp_grads[:, unit_width:].astype(jnp.bfloat16), "dp").astype(jnp.float32),
        lax.psum(down_grad.astype(jnp.bfloat16), "dp").astype(jnp.float32),
    )
    mean_loss = lax.psum(local_loss, ("dp", "row", "col")) / total_count
    return (
        output.astype(jnp.bfloat16),
        mean_loss.reshape(1),
        input_gradient,
        summed_grads[0],
        summed_grads[1],
        summed_grads[2],
        summed_grads[3],
        summed_grads[4],
        summed_grads[5],
        summed_grads[6],
    )


BF = jnp.bfloat16
F32 = jnp.float32
LOG2E = 1.4426950408889634
SIDE = 4
HALF = D // 2
PIECE = 256
BLOCK = 512
SLOTS = [(d, h) for h in range(2) for d in range(2)]


def fits_square(mesh):
    return mesh.shape["dp"] == 2 and mesh.shape["row"] == SIDE and mesh.shape["col"] == SIDE


def flip(values, axis, bit):
    return lax.ppermute(values, axis, [(i, i ^ bit) for i in range(SIDE)])


def flip_x(values):
    return flip(values, "row", 1)


def flip_y(values):
    return flip(values, "row", 2)


def flip_zl(values):
    return flip(values, "col", 1)


def flip_zh(values):
    return flip(values, "col", 2)


def flip_y_zh(values):
    pairs = [
        (r * SIDE + c, (r ^ 2) * SIDE + (c ^ 2)) for r in range(SIDE) for c in range(SIDE)
    ]
    return lax.ppermute(values, ("row", "col"), pairs)


def flip_dp(values):
    return lax.ppermute(values, "dp", [(0, 1), (1, 0)])


def flip_dp_y(values):
    pairs = [(g * SIDE + r, (1 - g) * SIDE + (r ^ 2)) for g in range(2) for r in range(SIDE)]
    return lax.ppermute(values, ("dp", "row"), pairs)


def square_gather(block, *events):
    half = block.shape[0] // 2
    by_x, by_z = flip_x(block), flip_zl(block)
    next_x, next_z = after((by_x, by_z), *events) if events else (by_x, by_z)
    return [block, by_x, by_z, flip_zl(next_x[:half]), flip_x(next_z[half:])]


def square_reduce(far, sides, own, *events):
    x_top, x_bottom, z_top, z_bottom = sides
    far_top, far_bottom = flip_zl(far[0]), flip_x(far[1])
    got_x_bottom, got_z_top = flip_x(x_bottom), flip_zl(z_top)
    if events:
        far_top, far_bottom = after((far_top, far_bottom), *events)
    got_x_top = flip_x((x_top + far_top.astype(F32)).astype(BF))
    got_z_bottom = flip_zl((z_bottom + far_bottom.astype(F32)).astype(BF))
    half = far_top.shape[0]
    top = own[:half] + got_x_top.astype(F32) + got_z_top.astype(F32)
    bottom = own[half:] + got_x_bottom.astype(F32) + got_z_bottom.astype(F32)
    return jnp.concatenate((top, bottom), axis=0)


def ordered(flag, own, other, axis):
    return jnp.where(
        flag == 0,
        jnp.concatenate((own, other), axis=axis),
        jnp.concatenate((other, own), axis=axis),
    )


def after(values, *events):
    return lax.optimization_barrier((values, events))[0]


def other_core(quarter):
    return [flip_dp(piece) for piece in quarter]


def piece_list(tall, high, by_y, by_y_high, others):
    other_tall, other_y, other_high, other_y_high = others
    return [tall, by_y, other_tall, other_y, high, by_y_high, other_high, other_y_high]


def wide(values):
    return values.astype(F32)


class Spread:
    def __init__(self, grads):
        self.keep, self.send = grads

    def to_core(self, *events):
        self.got = flip_dp(after(self.send, *events))
        return self.got

    def here(self, y, h):
        return wide(self.keep[y, h]) + wide(self.got[y, h])

    def to_y(self, h, *events):
        by_y = flip_dp_y(after(self.here(1, h).astype(BF), *events))
        setattr(self, "by_y%d" % h, by_y)
        return by_y

    def to_high(self, *events):
        send = (self.here(0, 1) + wide(self.by_y1)).astype(BF)
        self.high = flip_zh(after(send, *events))
        return self.high

    def to_x(self, x, axis, *events):
        total = self.here(0, 0) + wide(self.by_y0) + wide(self.high)
        total = after(total.astype(BF), *events)
        size = total.shape[axis] // 2
        own = lax.dynamic_slice_in_dim(total, x * size, size, axis)
        other = flip_x(lax.dynamic_slice_in_dim(total, (1 - x) * size, size, axis))
        self.parts = (own, other)
        return self.parts


def unite(own, by_x, x, q, axis):
    other_own, other_x = flip_dp(own), flip_dp(by_x)
    first = jnp.where(x == 0, own, by_x), jnp.where(x == 0, other_own, other_x)
    second = jnp.where(x == 0, by_x, own), jnp.where(x == 0, other_x, other_own)
    parts = []
    for mine, theirs in (first, second):
        parts += [jnp.where(q == 0, mine, theirs), jnp.where(q == 0, theirs, mine)]
    return jnp.concatenate(parts, axis=axis).astype(F32)


def local_norm(values):
    average = jnp.mean(values, axis=1, keepdims=True)
    square = jnp.mean(values * values, axis=1, keepdims=True)
    inverse = lax.rsqrt(square - average * average + EPSILON)
    return ((values - average) * inverse, inverse)


def local_norm_backward(gradient, normed, inverse):
    average = jnp.mean(gradient, axis=1, keepdims=True)
    crossed = jnp.mean(gradient * normed, axis=1, keepdims=True)
    return inverse * (gradient - average - normed * crossed)


def dot(left, right, a, b):
    return lax.dot_general(left, right, (((a,), (b,)), ((), ())), preferred_element_type=F32)


SMEM_SPEC = pl.BlockSpec(memory_space=pltpu.SMEM)
VMEM_SPEC = pl.BlockSpec(memory_space=pltpu.VMEM)


def shape(dims, kind):
    return jax.ShapeDtypeStruct(dims, kind)


def params(megabytes):
    return pltpu.CompilerParams(vmem_limit_bytes=megabytes * 2**20)


def cost(flops, moved, transcendentals=0):
    return pl.CostEstimate(
        flops=int(flops), bytes_accessed=int(moved), transcendentals=int(transcendentals)
    )


def y_half(y):
    return slice(y * HALF, (y + 1) * HALF)


def columns(index, width):
    return slice(index * width, (index + 1) * width)


FAR_SHAPES = [shape((PIECE // 2, D), BF)] * 2
SIDE_SHAPES = [
    shape((PIECE // 2, D), F32),
    shape((PIECE // 2, D), BF),
    shape((PIECE // 2, D), BF),
    shape((PIECE // 2, D), F32),
]
OWN_SHAPES = [shape((PIECE, D), F32)]
SUM_SHAPES = {"far": FAR_SHAPES, "sides": SIDE_SHAPES, "own": OWN_SHAPES}
SUM_BLOCKS = {"far": (3,), "sides": (1, 2), "own": (0,)}


def store_sum(kind, index, part, value, outs):
    half = PIECE // 2
    if kind == "own":
        outs[0][:, y_half(part)] = value
        return
    for low in range(2):
        out = outs[2 * index + low]
        out[:, y_half(part)] = value[low * half : (low + 1) * half].astype(out.dtype)


def qkv_kernel(place_ref, *refs):
    acts, refs = refs[:5], refs[5:]
    weights, refs = refs[:8], refs[8:]
    cos_ref, sin_ref, *refs = refs
    outs, weight_s = refs[:4], refs[4]
    for b in range(4):
        for y in range(2):
            for which in range(3):
                weight_s[y_half(y), columns(which * 4 + b, HD)] = weights[2 * b + y][which]
    for a in range(4):
        rows = pl.ds(pl.multiple_of(place_ref[a] * PIECE, PIECE), PIECE)
        cos_block, sin_block = cos_ref[rows, :], sin_ref[rows, :]
        act = acts[a][...] if a < 3 else jnp.concatenate((acts[3][...], acts[4][...]), axis=0)
        projected = dot(act, weight_s[...], 1, 0)
        for which in range(3):
            for b in range(4):
                tile = projected[:, columns(which * 4 + b, HD)]
                if which < 2:
                    tile = tile * cos_block + pltpu.roll(tile, HD // 2, 1) * sin_block
                outs[b][which, a] = tile.astype(BF)


def run_qkv(place, acts, weights, cos_wide, sin_wide):
    return pl.pallas_call(
        qkv_kernel,
        out_shape=[shape((3, 4, PIECE, HD), BF)] * 4,
        in_specs=[SMEM_SPEC] + [VMEM_SPEC] * 15,
        out_specs=[VMEM_SPEC] * 4,
        scratch_shapes=[pltpu.VMEM((D, 12 * HD), BF)],
        compiler_params=params(40),
        cost_estimate=cost(2 * 4 * PIECE * D * 12 * HD, 20 * 2**20),
    )(place, *acts, *weights, cos_wide, sin_wide)


def out_kernel(*refs):
    mixed, refs = refs[:4], refs[4:]
    weights, refs = refs[:8], refs[8:]
    outs, weight_s = refs[:7], refs[7]
    for b in range(4):
        for y in range(2):
            weight_s[y_half(y), columns(b, HD)] = weights[2 * b + y][...]
    at = 0
    for kind in ("far", "sides", "own"):
        for index, a in enumerate(SUM_BLOCKS[kind]):
            act = jnp.concatenate([mixed[b][a] for b in range(4)], axis=1)
            for y in range(2):
                value = dot(act, weight_s[y_half(y), :], 1, 1)
                store_sum(kind, index, y, value, outs[at:])
        at += len(SUM_SHAPES[kind])


def run_out(mixed, weights):
    outs = pl.pallas_call(
        out_kernel,
        out_shape=FAR_SHAPES + SIDE_SHAPES + OWN_SHAPES,
        in_specs=[VMEM_SPEC] * 12,
        out_specs=[VMEM_SPEC] * 7,
        scratch_shapes=[pltpu.VMEM((D, 4 * HD), BF)],
        compiler_params=params(36),
        cost_estimate=cost(2 * 4 * PIECE * D * 4 * HD, 16 * 2**20),
    )(*mixed, *weights)
    return outs[:2], outs[2:6], outs[6]


def input_kernel(*refs):
    back, refs = refs[:4], refs[4:]
    weights, refs = refs[:8], refs[8:]
    outs, weight_s = refs[:7], refs[7]
    for b in range(4):
        for y in range(2):
            for which in range(3):
                weight_s[y_half(y), columns(which * 4 + b, HD)] = weights[2 * b + y][which]
    at = 0
    for kind in ("far", "sides", "own"):
        for index, a in enumerate(SUM_BLOCKS[kind]):
            act = jnp.concatenate(
                [back[b][which, a] for which in range(3) for b in range(4)], axis=1
            )
            for y in range(2):
                value = dot(act, weight_s[y_half(y), :], 1, 1)
                store_sum(kind, index, y, value, outs[at:])
        at += len(SUM_SHAPES[kind])


def run_input(back, weights):
    outs = pl.pallas_call(
        input_kernel,
        out_shape=FAR_SHAPES + SIDE_SHAPES + OWN_SHAPES,
        in_specs=[VMEM_SPEC] * 12,
        out_specs=[VMEM_SPEC] * 7,
        scratch_shapes=[pltpu.VMEM((D, 12 * HD), BF)],
        compiler_params=params(40),
        cost_estimate=cost(2 * 4 * PIECE * D * 12 * HD, 20 * 2**20),
    )(*back, *weights)
    return outs[:2], outs[2:6], outs[6]


def attended_grad_kernel(*refs):
    acts, refs = refs[:5], refs[5:]
    weights, refs = refs[:8], refs[8:]
    outs, weight_s = refs[:4], refs[4]
    for b in range(4):
        for y in range(2):
            weight_s[y_half(y), columns(b, HD)] = weights[2 * b + y][...]
    for a in range(4):
        act = acts[a][...] if a < 3 else jnp.concatenate((acts[3][...], acts[4][...]), axis=0)
        value = dot(act, weight_s[...], 1, 0)
        for b in range(4):
            outs[b][a] = value[:, columns(b, HD)].astype(BF)


def run_attended_grad(acts, weights):
    return pl.pallas_call(
        attended_grad_kernel,
        out_shape=[shape((4, PIECE, HD), BF)] * 4,
        in_specs=[VMEM_SPEC] * 13,
        out_specs=[VMEM_SPEC] * 4,
        scratch_shapes=[pltpu.VMEM((D, 4 * HD), BF)],
        compiler_params=params(36),
        cost_estimate=cost(2 * 4 * PIECE * D * 4 * HD, 16 * 2**20),
    )(*acts, *weights)


CHUNK = 256


def up_kernel(count, *refs):
    acts, refs = refs[:count], refs[count:]
    gates, refs = refs[:8], refs[8:]
    ups, refs = refs[:8], refs[8:]
    gating_ref, upward_ref, units_ref = refs
    start = 0
    for act_ref in acts:
        size = act_ref.shape[0]
        rows = slice(start, start + size)
        start += size
        low, high = act_ref[:, y_half(0)], act_ref[:, y_half(1)]
        for b in range(4):
            gate = dot(low, gates[2 * b][...], 1, 0) + dot(high, gates[2 * b + 1][...], 1, 0)
            up = dot(low, ups[2 * b][...], 1, 0) + dot(high, ups[2 * b + 1][...], 1, 0)
            gating_ref[b, rows] = gate
            upward_ref[b, rows] = up
            units_ref[b, rows] = (gate * jax.nn.sigmoid(gate) * up).astype(BF)


def run_up(acts, gates, ups):
    rows = sum(act.shape[0] for act in acts)
    width = gates[0].shape[1]
    whole = lambda act: pl.BlockSpec(act.shape, lambda j: (0, 0))
    piece = pl.BlockSpec((HALF, CHUNK), lambda j: (0, j))
    out = pl.BlockSpec((4, rows, CHUNK), lambda j: (0, 0, j))
    return pl.pallas_call(
        lambda *refs: up_kernel(len(acts), *refs),
        grid=(width // CHUNK,),
        out_shape=[shape((4, rows, width), kind) for kind in (F32, F32, BF)],
        in_specs=[whole(act) for act in acts] + [piece] * 16,
        out_specs=[out] * 3,
        compiler_params=params(48),
        cost_estimate=cost(2 * rows * D * 8 * width, 16 * 2**20, 4 * rows * width),
    )(*acts, *gates, *ups)


def down_kernel(kind, units_ref, *refs):
    weights, outs = refs[:8], refs[8:]
    for index in range(len(SUM_BLOCKS[kind])):
        rows = slice(index * PIECE, (index + 1) * PIECE)
        for y in range(2):
            value = dot(units_ref[0, rows], weights[y][...], 1, 0)
            for b in range(1, 4):
                value += dot(units_ref[b, rows], weights[2 * b + y][...], 1, 0)
            store_sum(kind, index, y, value, outs)


def run_down(kind, units, weights):
    rows, width = units.shape[1], units.shape[2]
    shapes = SUM_SHAPES[kind]
    return pl.pallas_call(
        lambda *refs: down_kernel(kind, *refs),
        out_shape=shapes,
        in_specs=[VMEM_SPEC] * 9,
        out_specs=[VMEM_SPEC] * len(shapes),
        compiler_params=params(36),
        cost_estimate=cost(2 * rows * D * 4 * width, 12 * 2**20),
    )(units, *weights)


def gated_kernel(count, *refs):
    acts, refs = refs[:count], refs[count:]
    gating_ref, upward_ref, *refs = refs
    weights, refs = refs[:8], refs[8:]
    gate_ref, up_ref = refs
    start = 0
    for act_ref in acts:
        size = act_ref.shape[0]
        rows = slice(start, start + size)
        start += size
        low, high = act_ref[:, y_half(0)], act_ref[:, y_half(1)]
        for b in range(4):
            grad = dot(low, weights[2 * b][...], 1, 1) + dot(high, weights[2 * b + 1][...], 1, 1)
            gate = gating_ref[b, rows]
            sigmoid = jax.nn.sigmoid(gate)
            gate_ref[b, rows] = (
                grad * upward_ref[b, rows] * sigmoid * (1.0 + gate * (1.0 - sigmoid))
            ).astype(BF)
            up_ref[b, rows] = (grad * (gate * sigmoid)).astype(BF)


def run_gated(acts, gating, upward, weights):
    rows, width = gating.shape[1], gating.shape[2]
    return pl.pallas_call(
        lambda *refs: gated_kernel(len(acts), *refs),
        out_shape=[shape((4, rows, width), BF)] * 2,
        in_specs=[VMEM_SPEC] * (len(acts) + 10),
        out_specs=[VMEM_SPEC] * 2,
        compiler_params=params(44),
        cost_estimate=cost(2 * rows * D * 4 * width, 16 * 2**20, 4 * rows * width),
    )(*acts, gating, upward, *weights)


def normed_two_kernel(kind, gate_ref, up_ref, *refs):
    gates, refs = refs[:8], refs[8:]
    ups, refs = refs[:8], refs[8:]
    outs, total_s = refs[:-1], refs[-1]
    step, last = pl.program_id(0), pl.num_programs(0) - 1
    for y in range(2):
        value = dot(gate_ref[0], gates[y][...], 1, 1)
        for b in range(4):
            if b > 0:
                value += dot(gate_ref[b], gates[2 * b + y][...], 1, 1)
            value += dot(up_ref[b], ups[2 * b + y][...], 1, 1)

        @pl.when(step == 0)
        def _():
            total_s[:, y_half(y)] = value

        @pl.when(step == last)
        def _():
            whole = total_s[:, y_half(y)] + value
            for index in range(len(SUM_BLOCKS[kind])):
                rows = slice(index * PIECE, (index + 1) * PIECE)
                store_sum(kind, index, y, whole[rows], outs)


def run_normed_two(kind, gate_low, up_low, gates, ups):
    rows, width = gate_low.shape[1], gate_low.shape[2]
    shapes = SUM_SHAPES[kind]
    low = pl.BlockSpec((4, rows, width // 2), lambda j: (0, 0, j))
    piece = pl.BlockSpec((HALF, width // 2), lambda j: (0, j))
    return pl.pallas_call(
        lambda *refs: normed_two_kernel(kind, *refs),
        grid=(2,),
        out_shape=shapes,
        in_specs=[low] * 2 + [piece] * 16,
        out_specs=[pl.BlockSpec(s.shape, lambda j: (0, 0)) for s in shapes],
        scratch_shapes=[pltpu.VMEM((rows, D), F32)],
        compiler_params=params(48),
        cost_estimate=cost(2 * rows * D * 8 * width, 18 * 2**20),
    )(gate_low, up_low, *gates, *ups)


def wide_grad_kernel(*refs):
    acts, refs = refs[:5], refs[5:]
    lows, refs = refs[:3], refs[3:]
    outs, turned_s = refs[:2], refs[2]

    @pl.when(pl.program_id(1) == 0)
    def _():
        start = 0
        for act_ref in acts:
            size = act_ref.shape[0]
            turned_s[:, start : start + size] = act_ref[...].T
            start += size

    for d in range(2):
        total, start = None, 0
        for low_ref in lows:
            size = low_ref.shape[1]
            value = dot(turned_s[:, start : start + size], low_ref[d], 1, 0)
            total = value if total is None else total + value
            start += size
        outs[d][0, 0] = total.astype(BF)


def run_wide_grad(acts, lows):
    width = lows[0].shape[2]
    return pl.pallas_call(
        wide_grad_kernel,
        grid=(2, 2),
        out_shape=[shape((2, 2, HALF, width), BF)] * 2,
        in_specs=[pl.BlockSpec((act.shape[0], HALF), lambda y, h: (0, y)) for act in acts]
        + [pl.BlockSpec((2, low.shape[1], width), lambda y, h: (h, 0, 0)) for low in lows],
        out_specs=[pl.BlockSpec((1, 1, HALF, width), lambda y, h: (y, h, 0, 0))] * 2,
        scratch_shapes=[pltpu.VMEM((HALF, 4 * PIECE), BF)],
        compiler_params=params(36),
        cost_estimate=cost(2 * 4 * PIECE * D * 4 * width, 16 * 2**20),
    )(*acts, *lows)


def down_grad_kernel(*refs):
    units, refs = refs[:3], refs[3:]
    acts, refs = refs[:5], refs[5:]
    outs, turned_s = refs[:2], refs[2]

    @pl.when(pl.program_id(1) == 0)
    def _():
        start = 0
        for unit_ref in units:
            size = unit_ref.shape[1]
            for d in range(2):
                turned_s[d, :, start : start + size] = unit_ref[d].T
            start += size

    for d in range(2):
        total, start = None, 0
        for act_ref in acts:
            size = act_ref.shape[0]
            value = dot(turned_s[d, :, start : start + size], act_ref[...], 1, 0)
            total = value if total is None else total + value
            start += size
        outs[d][0, 0] = total.astype(BF)


def run_down_grad(units, acts):
    width = units[0].shape[2]
    return pl.pallas_call(
        down_grad_kernel,
        grid=(2, 2),
        out_shape=[shape((2, 2, width, HALF), BF)] * 2,
        in_specs=[pl.BlockSpec((2, unit.shape[1], width), lambda h, y: (h, 0, 0)) for unit in units]
        + [pl.BlockSpec((act.shape[0], HALF), lambda h, y: (0, y)) for act in acts],
        out_specs=[pl.BlockSpec((1, 1, width, HALF), lambda h, y: (y, h, 0, 0))] * 2,
        scratch_shapes=[pltpu.VMEM((2, width, 4 * PIECE), BF)],
        compiler_params=params(36),
        cost_estimate=cost(2 * 4 * PIECE * D * 4 * width, 16 * 2**20),
    )(*units, *acts)


def head_grad_kernel(kinds, *refs):
    acts, refs = refs[:5], refs[5:]
    messages, refs = refs[:4], refs[4:]
    outs, turned_s, right_s = refs[:2], refs[2], refs[3]
    start = 0
    for act_ref in acts:
        size = act_ref.shape[0]
        turned_s[:, start : start + size] = act_ref[...].T
        start += size

    @pl.when(pl.program_id(0) == 0)
    def _():
        for which in range(kinds):
            for b in range(4):
                for a in range(4):
                    value = messages[b][which, a] if kinds > 1 else messages[b][a]
                    right_s[columns(a, PIECE), columns(which * 4 + b, HD)] = value

    for which in range(kinds):
        value = dot(turned_s[...], right_s[:, columns(which, 4 * HD)], 1, 0)
        for b, (d, h) in enumerate(SLOTS):
            outs[d][0, h, which] = value[:, columns(b, HD)].astype(BF)


def run_head_grad(kinds, acts, messages):
    whole = lambda dims: pl.BlockSpec(dims, lambda y: (0,) * len(dims))
    return pl.pallas_call(
        lambda *refs: head_grad_kernel(kinds, *refs),
        grid=(2,),
        out_shape=[shape((2, 2, kinds, HALF, HD), BF)] * 2,
        in_specs=[pl.BlockSpec((act.shape[0], HALF), lambda y: (0, y)) for act in acts]
        + [whole(message.shape) for message in messages],
        out_specs=[pl.BlockSpec((1, 2, kinds, HALF, HD), lambda y: (y, 0, 0, 0, 0))] * 2,
        scratch_shapes=[
            pltpu.VMEM((HALF, 4 * PIECE), BF),
            pltpu.VMEM((4 * PIECE, kinds * 4 * HD), BF),
        ],
        compiler_params=params(40),
        cost_estimate=cost(2 * 4 * PIECE * D * kinds * 4 * HD, 12 * 2**20),
    )(*acts, *messages)


def allowed_pairs(starts, query0, key0, shape, query_axis):
    query = query0 + lax.broadcasted_iota(jnp.int32, shape, query_axis)
    key = key0 + lax.broadcasted_iota(jnp.int32, shape, 1 - query_axis)
    first = jnp.zeros(shape, jnp.int32)
    for s in range(CONT):
        first = jnp.where(query >= starts[s], starts[s], first)
    return (key <= query) & ((key < starts[0]) | (key >= first))


def block_bounds(starts, n):
    full = jnp.minimum(n, starts[0] // BLOCK)
    first = jnp.int32(0)
    for s in range(CONT):
        first = jnp.where(n * BLOCK >= starts[s], starts[s], first)
    return full, first


def block_used(starts, first, m):
    return (m * BLOCK < starts[0]) | ((m + 1) * BLOCK > first)


def attention_forward(place_ref, starts_ref, *refs):
    messages, refs = refs[:4], refs[4:]
    outs, refs = refs[:4], refs[4:]
    wide_ref, log_ref, q_s, k_s, v_s, score_s, acc_s, sum_s, max_s = refs
    scale = LOG2E / math.sqrt(HD)
    starts = [starts_ref[s] for s in range(CONT)]
    for b in range(4):
        for a in range(4):
            rows = pl.ds(pl.multiple_of(place_ref[4 * b + a] * PIECE, PIECE), PIECE)
            q_s[rows, :] = messages[b][0, a]
            k_s[rows, :] = messages[b][1, a]
            v_s[rows, :] = messages[b][2, a]

    def one_block(n, carry):
        rows = pl.ds(pl.multiple_of(n * BLOCK, BLOCK), BLOCK)
        full, first = block_bounds(starts, n)
        max_s[...] = jnp.full(max_s.shape, -1e30, F32)
        acc_s[...] = jnp.zeros(acc_s.shape, F32)
        sum_s[...] = jnp.zeros(sum_s.shape, F32)

        def note(scores, m):
            score_s[m] = scores
            top = max_s[...]
            for part in range(BLOCK // HD):
                top = jnp.maximum(top, scores[:, part * HD : (part + 1) * HD])
            max_s[...] = top

        def product(m):
            keys = pl.ds(pl.multiple_of(m * BLOCK, BLOCK), BLOCK)
            return dot(q_s[rows, :], k_s[keys, :], 1, 1)

        @pl.loop(0, full)
        def _(m):
            note(product(m), m)

        @pl.loop(full, n + 1)
        def _(m):
            @pl.when(block_used(starts, first, m))
            def _():
                allowed = allowed_pairs(starts, n * BLOCK, m * BLOCK, (BLOCK, BLOCK), 0)
                note(jnp.where(allowed, product(m), MASKED_SCORE), m)

        highest = jnp.max(max_s[...], axis=1, keepdims=True) * scale

        @pl.loop(0, n + 1)
        def _(m):
            @pl.when(block_used(starts, first, m))
            def _():
                keys = pl.ds(pl.multiple_of(m * BLOCK, BLOCK), BLOCK)
                exponent = jnp.exp2(score_s[m] * scale - highest)
                total = sum_s[...]
                for part in range(BLOCK // HD):
                    total = total + exponent[:, part * HD : (part + 1) * HD]
                sum_s[...] = total
                acc_s[...] += dot(exponent.astype(BF), v_s[keys, :], 1, 0)

        total = jnp.sum(sum_s[...], axis=1, keepdims=True)
        wide_ref[rows, :] = acc_s[...] / total
        log_total = jnp.broadcast_to(highest + jnp.log2(total), (BLOCK, HD))
        log_ref[n] = log_total.T[:8]
        return carry

    lax.fori_loop(0, k_s.shape[0] // BLOCK, one_block, 0)
    for b in range(4):
        for a in range(4):
            rows = pl.ds(pl.multiple_of(place_ref[4 * b + a] * PIECE, PIECE), PIECE)
            outs[b][a] = wide_ref[rows, :].astype(BF)


def attention_backward(place_ref, starts_ref, *refs):
    messages, refs = refs[:4], refs[4:]
    grads, refs = refs[:4], refs[4:]
    wide_ref, log_ref, cos_ref, sin_ref, *refs = refs
    outs, refs = refs[:4], refs[4:]
    q_s, k_s, v_s, g_s, dq_s, dk_s, dv_s = refs
    scale = LOG2E / math.sqrt(HD)
    starts = [starts_ref[s] for s in range(CONT)]
    for b in range(4):
        for a in range(4):
            rows = pl.ds(pl.multiple_of(place_ref[4 * b + a] * PIECE, PIECE), PIECE)
            q_s[rows, :] = messages[b][0, a]
            k_s[rows, :] = messages[b][1, a]
            v_s[rows, :] = messages[b][2, a]
            g_s[rows, :] = grads[b][a]
    dq_s[...] = jnp.zeros(dq_s.shape, F32)
    dk_s[...] = jnp.zeros(dk_s.shape, F32)
    dv_s[...] = jnp.zeros(dv_s.shape, F32)

    def one_block(n, carry):
        rows = pl.ds(pl.multiple_of(n * BLOCK, BLOCK), BLOCK)
        full, first = block_bounds(starts, n)
        crossed = g_s[rows, :].astype(F32) * wide_ref[rows, :]
        row_dot = jnp.sum(crossed.T, axis=0, keepdims=True)
        log_total = log_ref[n][:1]

        def step(m, masked):
            keys = pl.ds(pl.multiple_of(m * BLOCK, BLOCK), BLOCK)
            query, key = q_s[rows, :], k_s[keys, :]
            probability = jnp.exp2(dot(key, query, 1, 1) * scale - log_total)
            if masked:
                allowed = allowed_pairs(starts, n * BLOCK, m * BLOCK, (BLOCK, BLOCK), 1)
                probability = jnp.where(allowed, probability, 0.0)
            prob_grad = dot(v_s[keys, :], g_s[rows, :], 1, 1)
            score_grad = (probability * (prob_grad - row_dot)).astype(BF)
            dv_s[keys, :] += dot(probability.astype(BF), g_s[rows, :], 1, 0)
            dk_s[keys, :] += dot(score_grad, query, 1, 0)
            dq_s[rows, :] += dot(score_grad, key, 0, 0)

        @pl.loop(0, full)
        def _(m):
            step(m, False)

        @pl.loop(full, n + 1)
        def _(m):
            @pl.when(block_used(starts, first, m))
            def _():
                step(m, True)

        return carry

    lax.fori_loop(0, k_s.shape[0] // BLOCK, one_block, 0)
    for b in range(4):
        for a in range(4):
            rows = pl.ds(pl.multiple_of(place_ref[4 * b + a] * PIECE, PIECE), PIECE)
            for which, grad in ((0, dq_s), (1, dk_s)):
                value = grad[rows, :] * (1.0 / math.sqrt(HD))
                turned = value * cos_ref[rows, :] - pltpu.roll(value, HD // 2, 1) * sin_ref[rows, :]
                outs[b][which, a] = turned.astype(BF)
            outs[b][2, a] = dv_s[rows, :].astype(BF)


def run_forward(place, starts, messages):
    tokens = 16 * PIECE
    blocks = tokens // BLOCK
    out_shape = [jax.ShapeDtypeStruct((4, PIECE, HD), BF)] * 4
    out_shape += [
        jax.ShapeDtypeStruct((tokens, HD), F32),
        jax.ShapeDtypeStruct((blocks, 8, BLOCK), F32),
    ]
    return pl.pallas_call(
        attention_forward,
        out_shape=out_shape,
        in_specs=[SMEM_SPEC] * 2 + [VMEM_SPEC] * 4,
        out_specs=[VMEM_SPEC] * 6,
        scratch_shapes=[
            pltpu.VMEM((tokens, HD), BF),
            pltpu.VMEM((tokens, HD), BF),
            pltpu.VMEM((tokens, HD), BF),
            pltpu.VMEM((blocks, BLOCK, BLOCK), F32),
            pltpu.VMEM((BLOCK, HD), F32),
            pltpu.VMEM((BLOCK, HD), F32),
            pltpu.VMEM((BLOCK, HD), F32),
        ],
        compiler_params=pltpu.CompilerParams(vmem_limit_bytes=48 * 2**20),
        cost_estimate=pl.CostEstimate(
            flops=2 * tokens * tokens * HD * 2,
            bytes_accessed=8 * 2**20,
            transcendentals=tokens * tokens // 2,
        ),
    )(place, starts, *messages)


def run_backward(place, starts, messages, grads, wide, log_total, cosine, sine_table):
    tokens = 16 * PIECE
    return pl.pallas_call(
        attention_backward,
        out_shape=[jax.ShapeDtypeStruct((3, 4, PIECE, HD), BF)] * 4,
        in_specs=[SMEM_SPEC] * 2 + [VMEM_SPEC] * 12,
        out_specs=[VMEM_SPEC] * 4,
        scratch_shapes=[pltpu.VMEM((tokens, HD), BF)] * 4 + [pltpu.VMEM((tokens, HD), F32)] * 3,
        compiler_params=pltpu.CompilerParams(vmem_limit_bytes=52 * 2**20),
        cost_estimate=pl.CostEstimate(
            flops=5 * tokens * tokens * HD * 2,
            bytes_accessed=16 * 2**20,
            transcendentals=tokens * tokens // 2,
        ),
    )(place, starts, *messages, *grads, wide, log_total, cosine, sine_table)


def swap_slots(messages):
    return [messages[0], flip_y(messages[1]), flip_zh(messages[2]), flip_y_zh(messages[3])]


def to_tokens(values):
    return lax.all_to_all(values, "row", split_axis=0, concat_axis=1, tiled=True)


def to_width(values):
    return lax.all_to_all(values, "row", split_axis=1, concat_axis=0, tiled=True)


def square_shards(
    hidden_in,
    teacher,
    valid,
    segment_ids,
    query_weight,
    key_weight,
    value_weight,
    output_weight,
    gate_weight,
    up_weight,
    down_weight,
):
    row, col, dp = lax.axis_index("row"), lax.axis_index("col"), lax.axis_index("dp")
    x, y = row % 2, row // 2
    q = (dp + y) % 2
    own_piece = col * SIDE + row
    segment = segment_ids[0]
    group_tokens = segment.shape[0]
    home_tokens = group_tokens // (SIDE * SIDE)

    def swap_y(values):
        return jnp.where(
            y == 0, values, jnp.concatenate((values[:, HALF:], values[:, :HALF]), axis=1)
        )

    def cut(matrix, at, axis):
        size = matrix.shape[axis] // 4
        return lax.dynamic_slice_in_dim(matrix, (2 * at + q) * size, size, axis)

    def head_cut(at):
        parts = [cut(matrix, at, 1) for matrix in (query_weight, key_weight, value_weight)]
        return jnp.stack(parts + [cut(output_weight, at, 0).T])

    labels = jnp.arange(1, CONT + 1, dtype=jnp.int32)
    starts = jnp.sum((segment[None, :] < labels[:, None]).astype(jnp.int32), axis=1)
    codes = jnp.arange(16, dtype=jnp.int32)
    relative = (
        (codes & 1) + ((codes >> 1) & 1) * 4 + ((codes >> 2) & 1) * 2 + ((codes >> 3) & 1) * 8
    )
    pieces = relative ^ own_piece
    frequency = jnp.power(10000.0, jnp.arange(HD // 2, dtype=F32) * (-2.0 / HD))
    angles = positions(segment).astype(F32)[:, None] * jnp.tile(frequency, 2)[None, :]
    sign = jnp.where(jnp.arange(HD) < HD // 2, -1.0, 1.0)
    cos_wide, sin_wide = jnp.cos(angles), jnp.sin(angles) * sign[None, :]

    heads_x = after(flip_x(head_cut(1 - x)), cos_wide, sin_wide)
    gates_x = flip_x(after(cut(gate_weight, 1 - x, 1), heads_x))
    hidden = swap_y(to_tokens(after(hidden_in, heads_x))).astype(F32)
    all_heads = ordered(x, head_cut(x), heads_x, 1)
    heads_tall, outs_tall = all_heads[:3], all_heads[3]
    heads_high = flip_zh(heads_tall)
    heads_y = flip_dp_y(heads_tall)
    hidden = after(hidden, gates_x)
    gates_tall = ordered(x, cut(gate_weight, x, 1), gates_x, 0)
    row_half = gates_tall.shape[0] // 2
    normed, inverse_one = local_norm(hidden)
    normed_acts = square_gather(normed.astype(BF), heads_high)
    gates_first = flip_zh(after(gates_tall[:row_half], heads_high))
    heads_y_high = flip_dp_y(heads_high)
    gates_second = flip_zh(after(gates_tall[row_half:], gates_first))
    heads_other = other_core(
        (heads_tall, heads_y, heads_high, after(heads_y_high, gates_first))
    )
    heads = piece_list(heads_tall, heads_high, heads_y, heads_y_high, heads_other)

    heads, normed_acts = after((heads, normed_acts), gates_second)
    gates_high = jnp.concatenate((gates_first, gates_second), axis=0)
    messages = run_qkv(pieces, normed_acts, heads, cos_wide, sin_wide)
    ups_x = flip_x(after(cut(up_weight, 1 - x, 1), messages[0]))
    downs_x = flip_x(after(cut(down_weight, 1 - x, 0), messages[0]))
    outs_high = flip_zh(after(outs_tall, messages[0]))
    outs_y = flip_dp_y(after(outs_tall, messages[0]))
    gates_y = flip_dp_y(after(gates_tall, outs_y))
    messages = swap_slots(messages)
    messages = after(messages, ups_x, downs_x, outs_high, outs_y, gates_y)

    ups_tall = ordered(x, cut(up_weight, x, 1), after(ups_x, messages), 0)
    ups_high = flip_zh(ups_tall)
    outs_y_high = flip_dp_y(after(outs_high, messages))
    gates_y_high = flip_dp_y(after(gates_high, messages))
    *mixed, wide_mixed, log_total = run_forward(pieces, starts, messages)
    mixed = after(mixed, ups_high, outs_y_high, gates_y_high)
    outs_other = other_core(after((outs_tall, outs_y, outs_high, outs_y_high), mixed))
    outs = piece_list(outs_tall, outs_high, outs_y, outs_y_high, outs_other)
    mixed = swap_slots(mixed)

    downs_tall = ordered(x, cut(down_weight, x, 0), after(downs_x, mixed), 1)
    middle_row = downs_tall.shape[0] // 2
    downs_first = flip_zh(downs_tall[:middle_row])
    downs_second = flip_zh(after(downs_tall[middle_row:], downs_first))
    ups_y = flip_dp_y(after(ups_tall, mixed))
    ups_y_high = flip_dp_y(after(ups_high, ups_y))
    gates_other = other_core(after((gates_tall, gates_y, gates_high, gates_y_high), mixed))
    gates = piece_list(gates_tall, gates_high, gates_y, gates_y_high, gates_other)
    sums = run_out(mixed, outs)
    after_attention = hidden + square_reduce(*sums, downs_first, ups_y)
    after_attention = after(after_attention, downs_second, ups_y_high, gates_other)

    normed_two, inverse_two = local_norm(after_attention)
    ups_other = other_core(after((ups_tall, ups_y, ups_high, ups_y_high), normed_two))
    ups = piece_list(ups_tall, ups_high, ups_y, ups_y_high, ups_other)
    downs_high = jnp.concatenate((downs_first, downs_second), axis=0)
    low_two = normed_two.astype(BF)
    downs_y = flip_dp_y(after(downs_tall, normed_two))
    up_own = run_up([low_two], gates, ups)
    two_acts = square_gather(low_two, up_own)
    downs_y_high = flip_dp_y(after(downs_high, downs_y))
    count = jnp.sum(valid.astype(F32)).reshape(1)
    count = count + flip_dp(after(count, low_two))
    up_sides = run_up(after(two_acts[1:3], up_own[2], downs_y, count), gates, ups)
    downs_other = other_core(
        after((downs_tall, downs_y, downs_high, downs_y_high), up_own[2])
    )
    count = count + flip_zh(after(count, two_acts[1:3]))
    up_far = run_up(after(two_acts[3:], up_sides[2], downs_y_high, count), gates, ups)
    count = count + flip_zl(after(count, two_acts))
    downs = piece_list(downs_tall, downs_high, downs_y, downs_y_high, downs_other)
    ups_out = [up_own, up_sides, up_far]
    units = [out[2] for out in ups_out]
    down_far = run_down("far", after(units[2], count), downs)
    down_sides = run_down("sides", after(units[1], down_far), downs)
    down_own = run_down("own", after(units[0], down_sides), downs)
    output = after_attention + square_reduce(down_far, down_sides, down_own[0])

    total_count = jnp.maximum(count, 1.0)
    counted_home = lax.dynamic_slice_in_dim(
        valid.astype(F32), row * home_tokens, home_tokens, 0
    )[:, None]
    target = swap_y(to_tokens(after(teacher, mixed)))
    differ = output - target.astype(F32)
    local_loss = jnp.sum(counted_home * (differ * differ)) / D
    all_tokens = group_tokens * lax.axis_size("dp")
    out_grad = counted_home * differ * (all_tokens / total_count)

    low_out = out_grad.astype(BF)
    loss = local_loss.reshape(1)
    loss = loss + flip_dp(after(loss, low_out))
    low_own = run_gated([low_out], up_own[0], up_own[1], downs)
    out_acts = square_gather(low_out, low_own)
    low_sides = run_gated(after(out_acts[1:3], low_own, loss), up_sides[0], up_sides[1], downs)
    loss = loss + flip_y(after(loss, out_acts[1:3]))
    low_far = run_gated(after(out_acts[3:], low_sides, loss), up_far[0], up_far[1], downs)
    loss = loss + flip_zl(after(loss, low_sides))
    lows = [low_own, low_sides, low_far]
    two_far = run_normed_two("far", *after(low_far, loss), gates, ups)
    loss = loss + flip_x(after(loss, low_far))
    two_sides = run_normed_two("sides", *after(low_sides, two_far, loss), gates, ups)
    loss = loss + flip_zh(after(loss, two_far))

    down_grads = Spread(run_down_grad(after(units, two_sides), after(out_acts, loss)))
    down_core = down_grads.to_core()
    two_own = run_normed_two("own", *after(low_own, down_grads.keep), gates, ups)
    gate_pair = run_wide_grad(two_acts, after([low[0] for low in lows], two_own, down_core))
    gate_grads = Spread(gate_pair)
    down_y1 = down_grads.to_y(1)
    normed_two_grad = square_reduce(two_far, two_sides, two_own[0])
    normed_two_grad = after(normed_two_grad, down_y1, gate_pair)
    middle_grad = out_grad + local_norm_backward(normed_two_grad, normed_two, inverse_two)
    low_middle = middle_grad.astype(BF)
    gate_core = gate_grads.to_core(low_middle)
    down_y0 = down_grads.to_y(0, low_middle)
    up_pair = run_wide_grad(two_acts, after([low[1] for low in lows], gate_pair))
    up_grads = Spread(up_pair)
    middle_acts = square_gather(low_middle, down_y0, gate_core)
    down_grads.to_high(down_y0)
    gate_y1 = gate_grads.to_y(1, down_y0)
    middle_acts = after(middle_acts, up_pair, gate_y1)
    grad_messages = run_attended_grad(middle_acts, outs)
    grad_messages = after(grad_messages, down_grads.high)
    up_core = up_grads.to_core(grad_messages)
    gate_y0 = gate_grads.to_y(0, grad_messages)
    out_grads = Spread(run_head_grad(1, after(middle_acts, grad_messages), mixed))
    grad_messages = swap_slots(grad_messages)
    grad_messages = after(grad_messages, up_core, out_grads.keep, gate_y0)
    gate_grads.to_high(grad_messages)
    up_y1 = up_grads.to_y(1, grad_messages)
    up_y0 = up_grads.to_y(0, grad_messages)
    back = run_backward(
        pieces, starts, messages, grad_messages, wide_mixed, log_total, cos_wide, sin_wide
    )
    back = after(back, gate_grads.high, up_y1, up_y0)
    layer_output = to_width(swap_y(after(output, back).astype(BF)))
    gate_grads.to_x(x, 0, back)
    down_grads.to_x(x, 1, back)
    out_core = out_grads.to_core(back)
    out_y1 = out_grads.to_y(1, back)
    out_y0 = out_grads.to_y(0, back)
    back = swap_slots(back)
    back = after(back, out_y1, out_y0, gate_grads.parts, down_grads.parts, layer_output)
    up_grads.to_high(back)
    head_pair = run_head_grad(3, normed_acts, back)
    head_grads = Spread(head_pair)
    head_core = head_grads.to_core()
    input_sums = run_input(after(back, head_pair), heads)
    input_sums = after(input_sums, head_core)
    head_y1 = head_grads.to_y(1)
    normed_grad = square_reduce(*input_sums, head_y1)
    head_y0 = head_grads.to_y(0, head_y1)
    out_grads.to_high(up_grads.high)
    head_grads.to_high(head_y1)
    normed_grad = after(normed_grad, head_y0, up_grads.high)
    up_grads.to_x(x, 0, normed_grad)
    out_grads.to_x(x, 1, normed_grad)
    input_gradient = middle_grad + local_norm_backward(normed_grad, normed, inverse_one)
    head_grads.to_x(x, 1, normed_grad)
    mean_loss = loss / total_count

    down_grad = unite(*down_grads.parts, x, q, 0)
    gate_grad = unite(*gate_grads.parts, x, q, 1)
    up_grad = unite(*up_grads.parts, x, q, 1)
    out_weight_grad = unite(*out_grads.parts, x, q, 2)
    head_grads = unite(*head_grads.parts, x, q, 2)
    return (
        layer_output,
        mean_loss,
        to_width(swap_y(input_gradient)),
        head_grads[0],
        head_grads[1],
        head_grads[2],
        out_weight_grad[0].T,
        gate_grad,
        up_grad,
        down_grad,
    )


def solution(mesh):
    body = square_shards if fits_square(mesh) else shards
    in_specs = (
        P(("dp", "col"), "row"),
        P(("dp", "col"), "row"),
        P(("dp", "col")),
        P("dp", None),
        P("row", "col"),
        P("row", "col"),
        P("row", "col"),
        P("col", "row"),
        P("row", "col"),
        P("row", "col"),
        P("col", "row"),
    )
    out_specs = (
        P(("dp", "col"), "row"),
        P(),
        P(("dp", "col"), "row"),
        P("row", "col"),
        P("row", "col"),
        P("row", "col"),
        P("col", "row"),
        P("row", "col"),
        P("row", "col"),
        P("col", "row"),
    )
    return jax.shard_map(body, mesh=mesh, in_specs=in_specs, out_specs=out_specs, check_vma=False)
```

```python
import math

import jax
import jax.numpy as jnp
from jax import lax
from jax.experimental import pallas as pl
from jax.experimental.pallas import tpu as pltpu
from jax.sharding import PartitionSpec as P

D = 2048
HD = 128
CONT = 8


EPSILON = 1e-05
MASKED_SCORE = -1e30


def positions(segment):
    labels = jnp.arange(CONT + 1, dtype=jnp.int32)
    onehot = (segment[:, None] == labels[None, :]).astype(jnp.int32)
    counts = jnp.sum(onehot, axis=0)
    starts = jnp.cumsum(counts) - counts
    leading = jnp.sum(onehot * starts[None, :], axis=1)
    indices = jnp.arange(segment.shape[0], dtype=jnp.int32)
    return indices - leading + jnp.where(segment > 0, counts[0], 0)


def rotary(offsets):
    half_width = HD // 2
    frequency = jnp.power(10000.0, jnp.arange(half_width, dtype=jnp.float32) * (-2.0 / HD))
    angles = offsets.astype(jnp.float32)[:, None] * frequency[None, :]
    return (jnp.cos(angles), jnp.sin(angles))


def rotate(values, cosine, sine_table):
    half_width = values.shape[-1] // 2
    leading, trailing = (values[..., :half_width], values[..., half_width:])
    cos_wide = cosine[:, None, :]
    sin_wide = sine_table[:, None, :]
    return jnp.concatenate(
        (leading * cos_wide - trailing * sin_wide, trailing * cos_wide + leading * sin_wide),
        axis=-1,
    )


def unrotate(gradient, cosine, sine_table):
    half_width = gradient.shape[-1] // 2
    leading, trailing = (gradient[..., :half_width], gradient[..., half_width:])
    cos_wide = cosine[:, None, :]
    sin_wide = sine_table[:, None, :]
    return jnp.concatenate(
        (leading * cos_wide + trailing * sin_wide, trailing * cos_wide - leading * sin_wide),
        axis=-1,
    )


def feature_sums(left, right):
    return lax.psum((jnp.sum(left, axis=1), jnp.sum(right, axis=1)), "row")


def normalize(values):
    summed, squared = feature_sums(values, values * values)
    average = (summed / D)[:, None]
    inverse = lax.rsqrt(squared[:, None] / D - average * average + EPSILON)
    return ((values - average) * inverse, inverse)


def norm_backward(gradient, normed, inverse):
    summed, crossed = feature_sums(gradient, gradient * normed)
    return inverse * (gradient - summed[:, None] / D - normed * (crossed[:, None] / D))


def widen(values):
    return lax.all_gather(values, "col", axis=0, tiled=True)


def collect(values):
    return lax.all_gather(values, "row", axis=0, tiled=True)


def row_product(full, matrix, contract):
    return lax.psum_scatter(
        lax.dot_general(
            full, matrix, (((1,), (contract,)), ((), ())), preferred_element_type=jnp.float32
        ),
        "row",
        scatter_dimension=0,
        tiled=True,
    )


def column_product(full, matrix, contract):
    return lax.psum_scatter(
        lax.dot_general(
            full, matrix, (((1,), (contract,)), ((), ())), preferred_element_type=jnp.float32
        ),
        "col",
        scatter_dimension=0,
        tiled=True,
    )


def project_in(gathered, matrix):
    result = row_product(gathered, matrix, 0)
    return result


def project_back(gathered, matrix):
    result = row_product(gathered, matrix, 1)
    return result


def weight_product(left, right):
    return lax.dot_general(
        left, right, (((0,), (0,)), ((), ())), preferred_element_type=jnp.float32
    )


def block_layout(tok_rows):
    blocks = max(1, tok_rows // 512)
    return (blocks, tok_rows // blocks)


def score_maker(key_rows, segment, block):
    key_index = jnp.arange(key_rows.shape[0], dtype=jnp.int32)
    scale = 1.0 / math.sqrt(HD)

    def scores_for(query_block, offset):
        query_index = offset + jnp.arange(block, dtype=jnp.int32)
        query_segment = lax.dynamic_slice_in_dim(segment, offset, block, 0)
        allowed = (key_index[None, :] <= query_index[:, None]) & (
            (segment[None, :] == 0) | (segment[None, :] == query_segment[:, None])
        )
        scores = (
            jnp.einsum("qhd,khd->hqk", query_block, key_rows, preferred_element_type=jnp.float32)
            * scale
        )
        return jnp.where(allowed[None, :, :], scores, MASKED_SCORE)

    return scores_for


def attend(queries, key_rows, value_rows, segment, row_offset):
    tok_rows, heads_here = (queries.shape[0], queries.shape[1])
    blocks, block = block_layout(tok_rows)
    scores_for = score_maker(key_rows, segment, block)
    offsets = row_offset + jnp.arange(blocks, dtype=jnp.int32) * block

    def forward_block(inputs):
        query_block, offset = inputs
        scores = scores_for(query_block, offset)
        highest = jnp.max(scores, axis=-1, keepdims=True)
        exponent = jnp.exp(scores - highest)
        summed = jnp.sum(exponent, axis=-1, keepdims=True)
        probability = (exponent / summed).astype(jnp.bfloat16)
        mixed_block = jnp.einsum(
            "hqk,khd->qhd", probability, value_rows, preferred_element_type=jnp.float32
        )
        return (mixed_block, highest + jnp.log(summed))

    mixed_blocks, log_total = lax.map(
        forward_block, (queries.reshape(blocks, block, heads_here, HD), offsets)
    )
    return (mixed_blocks.reshape(tok_rows, heads_here * HD), log_total)


def attend_back(queries, key_rows, value_rows, segment, row_offset, log_total, attended_grad):
    tok_rows, heads_here = (queries.shape[0], queries.shape[1])
    blocks, block = block_layout(tok_rows)
    scores_for = score_maker(key_rows, segment, block)
    offsets = row_offset + jnp.arange(blocks, dtype=jnp.int32) * block
    scale = 1.0 / math.sqrt(HD)

    def backward_block(carry, inputs):
        key_sum, value_sum = carry
        query_block, grad_block, log_block, offset = inputs
        scores = scores_for(query_block, offset)
        probability = jnp.exp(scores - log_block)
        rounded = probability.astype(jnp.bfloat16)
        prob_grad = jnp.einsum(
            "qhd,khd->hqk", grad_block, value_rows, preferred_element_type=jnp.float32
        )
        row_dot = jnp.sum(probability * prob_grad, axis=-1, keepdims=True)
        score_grad = (probability * (prob_grad - row_dot)).astype(jnp.bfloat16)
        query_grad = (
            jnp.einsum("hqk,khd->qhd", score_grad, key_rows, preferred_element_type=jnp.float32)
            * scale
        )
        key_sum = (
            key_sum
            + jnp.einsum(
                "hqk,qhd->khd", score_grad, query_block, preferred_element_type=jnp.float32
            )
            * scale
        )
        value_sum = value_sum + jnp.einsum(
            "hqk,qhd->khd", rounded, grad_block, preferred_element_type=jnp.float32
        )
        return ((key_sum, value_sum), query_grad)

    empty = jnp.zeros(key_rows.shape, jnp.float32)
    inputs = (
        queries.reshape(blocks, block, heads_here, HD),
        attended_grad.reshape(blocks, block, heads_here, HD),
        log_total,
        offsets,
    )
    (key_sum, value_sum), query_grads = lax.scan(backward_block, (empty, empty), inputs)
    return (query_grads.reshape(tok_rows, heads_here, HD), key_sum, value_sum)


def shards(
    hidden_in,
    teacher,
    valid,
    segment_ids,
    query_weight,
    key_weight,
    value_weight,
    output_weight,
    gate_weight,
    up_weight,
    down_weight,
):
    row_devices = lax.axis_size("row")
    col_devices = lax.axis_size("col")
    tok_cols = hidden_in.shape[0]
    group_tokens = tok_cols * col_devices
    tok_rows = group_tokens // row_devices
    query_width = query_weight.shape[1]
    heads_here = query_width // HD
    unit_width = gate_weight.shape[1]
    segment = segment_ids[0]
    row_offset = lax.axis_index("row") * tok_rows
    cosine_all, sine_all = rotary(positions(segment))
    cosine = lax.dynamic_slice_in_dim(cosine_all, row_offset, tok_rows, 0)
    sine_table = lax.dynamic_slice_in_dim(sine_all, row_offset, tok_rows, 0)
    counted = valid.astype(jnp.float32)
    total_count = jnp.maximum(lax.psum(jnp.sum(counted), ("dp", "col")), 1.0)
    hidden = hidden_in.astype(jnp.float32)
    normed, inverse_one = normalize(hidden)
    normed_wide = widen(normed.astype(jnp.bfloat16))
    attn_weights = jnp.concatenate((query_weight, key_weight, value_weight), axis=1)
    projected = project_in(normed_wide, attn_weights)
    queries = rotate(
        projected[:, :query_width].reshape(tok_rows, heads_here, HD), cosine, sine_table
    ).astype(jnp.bfloat16)
    key_local = rotate(
        projected[:, query_width : 2 * query_width].reshape(tok_rows, heads_here, HD),
        cosine,
        sine_table,
    )
    key_local = key_local.reshape(tok_rows, query_width).astype(jnp.bfloat16)
    value_local = projected[:, 2 * query_width :].astype(jnp.bfloat16)
    key_flat, value_flat = (
        lax.all_gather(key_local, "row", axis=0, tiled=True),
        lax.all_gather(value_local, "row", axis=0, tiled=True),
    )
    key_rows = key_flat.reshape(group_tokens, heads_here, HD)
    value_rows = value_flat.reshape(group_tokens, heads_here, HD)
    attended, log_total = attend(queries, key_rows, value_rows, segment, row_offset)
    attended_wide = collect(attended.astype(jnp.bfloat16))
    after_attention = hidden + column_product(attended_wide, output_weight, 0)
    normed_two, inverse_two = normalize(after_attention)
    normed_two_wide = widen(normed_two.astype(jnp.bfloat16))
    mlp_weights = jnp.concatenate((gate_weight, up_weight), axis=1)
    gated = project_in(normed_two_wide, mlp_weights)
    gating = gated[:, :unit_width]
    upward = gated[:, unit_width:]
    sigmoid = jax.nn.sigmoid(gating)
    activated = gating * sigmoid
    units_wide = collect((activated * upward).astype(jnp.bfloat16))
    output = after_attention + column_product(units_wide, down_weight, 0)
    differ = output - teacher.astype(jnp.float32)
    local_loss = jnp.sum(counted[:, None] * (differ * differ)) / D
    all_tokens = group_tokens * lax.axis_size("dp")
    out_grad = counted[:, None] * differ * (all_tokens / total_count)
    out_wide = widen(out_grad.astype(jnp.bfloat16))
    units_grad = project_back(out_wide, down_weight)
    down_grad = weight_product(units_wide, out_wide)
    gating_grad = units_grad * upward * sigmoid * (1.0 + gating * (1.0 - sigmoid))
    upward_grad = units_grad * activated
    gated_wide = collect(jnp.concatenate((gating_grad, upward_grad), axis=1).astype(jnp.bfloat16))
    mlp_grads = weight_product(normed_two_wide, gated_wide)
    normed_two_grad = column_product(gated_wide, mlp_weights, 1)
    middle_grad = out_grad + norm_backward(normed_two_grad, normed_two, inverse_two)
    middle_wide = widen(middle_grad.astype(jnp.bfloat16))
    attended_grad = project_back(middle_wide, output_weight).astype(jnp.bfloat16)
    output_grad_sum = weight_product(attended_wide, middle_wide)
    query_grad, key_sum, value_sum = attend_back(
        queries, key_rows, value_rows, segment, row_offset, log_total, attended_grad
    )
    key_grad, value_grad = (
        lax.psum_scatter(
            key_sum.reshape(group_tokens, query_width), "row", scatter_dimension=0, tiled=True
        ),
        lax.psum_scatter(
            value_sum.reshape(group_tokens, query_width), "row", scatter_dimension=0, tiled=True
        ),
    )
    query_pre = unrotate(query_grad, cosine, sine_table).reshape(tok_rows, query_width)
    key_pre = unrotate(key_grad.reshape(tok_rows, heads_here, HD), cosine, sine_table).reshape(
        tok_rows, query_width
    )
    projected_wide = collect(
        jnp.concatenate((query_pre, key_pre, value_grad), axis=1).astype(jnp.bfloat16)
    )
    attn_grads = weight_product(normed_wide, projected_wide)
    normed_grad = column_product(projected_wide, attn_weights, 1)
    input_gradient = middle_grad + norm_backward(normed_grad, normed, inverse_one)
    summed_grads = (
        lax.psum(attn_grads[:, :query_width].astype(jnp.bfloat16), "dp").astype(jnp.float32),
        lax.psum(attn_grads[:, query_width : 2 * query_width].astype(jnp.bfloat16), "dp").astype(
            jnp.float32
        ),
        lax.psum(attn_grads[:, 2 * query_width :].astype(jnp.bfloat16), "dp").astype(jnp.float32),
        lax.psum(output_grad_sum.astype(jnp.bfloat16), "dp").astype(jnp.float32),
        lax.psum(mlp_grads[:, :unit_width].astype(jnp.bfloat16), "dp").astype(jnp.float32),
        lax.psum(mlp_grads[:, unit_width:].astype(jnp.bfloat16), "dp").astype(jnp.float32),
        lax.psum(down_grad.astype(jnp.bfloat16), "dp").astype(jnp.float32),
    )
    mean_loss = lax.psum(local_loss, ("dp", "row", "col")) / total_count
    return (
        output.astype(jnp.bfloat16),
        mean_loss.reshape(1),
        input_gradient,
        summed_grads[0],
        summed_grads[1],
        summed_grads[2],
        summed_grads[3],
        summed_grads[4],
        summed_grads[5],
        summed_grads[6],
    )


BF = jnp.bfloat16
F32 = jnp.float32
LOG2E = 1.4426950408889634
SIDE = 4
HALF = D // 2
PIECE = 256
BLOCK = 512
SLOTS = [(d, h) for h in range(2) for d in range(2)]


def fits_square(mesh):
    return mesh.shape["dp"] == 2 and mesh.shape["row"] == SIDE and mesh.shape["col"] == SIDE


def flip(values, axis, bit):
    return lax.ppermute(values, axis, [(i, i ^ bit) for i in range(SIDE)])


def flip_x(values):
    return flip(values, "row", 1)


def flip_y(values):
    return flip(values, "row", 2)


def flip_far(values):
    return flip(values, "col", 2)


def flip_near(values):
    return flip(values, "col", 1)


def flip_y_near(values):
    pairs = [
        (r * SIDE + c, (r ^ 2) * SIDE + (c ^ 1)) for r in range(SIDE) for c in range(SIDE)
    ]
    return lax.ppermute(values, ("row", "col"), pairs)


def flip_z(values):
    return flip(values, "col", 3)


def flip_dp(values):
    return lax.ppermute(values, "dp", [(0, 1), (1, 0)])


def flip_dp_y(values):
    pairs = [(g * SIDE + r, (1 - g) * SIDE + (r ^ 2)) for g in range(2) for r in range(SIDE)]
    return lax.ppermute(values, ("dp", "row"), pairs)


def near_gather(block, *events):
    half = block.shape[0] // 2
    by_x, by_z = flip_x(block), flip_near(block)
    next_x, next_z = after((by_x, by_z), *events)
    return [block, by_x, by_z, flip_near(next_x[:half]), flip_x(next_z[half:])]


def near_reduce(far, sides, own):
    first = near_reduce_far(far)
    return near_reduce_end(near_reduce_sides(first, sides), own)


def near_reduce_far(far):
    return flip_near(far[0]), flip_x(far[1])


def near_reduce_sides(first, sides):
    far_top, far_bottom = first
    x_top, x_bottom, z_top, z_bottom = sides
    return (
        flip_x((x_top + wide(far_top)).astype(BF)),
        flip_x(x_bottom),
        flip_near(z_top),
        flip_near((z_bottom + wide(far_bottom)).astype(BF)),
    )


def near_reduce_end(got, own):
    x_top, x_bottom, z_top, z_bottom = got
    half = x_top.shape[0]
    top = own[:half] + wide(x_top) + wide(z_top)
    bottom = own[half:] + wide(x_bottom) + wide(z_bottom)
    return jnp.concatenate((top, bottom), axis=0)


def square_gather(block, *events):
    by_z, by_x = flip_far(block), flip_x(block)
    return [block, by_x, by_z, flip_x(after(by_z, *events) if events else by_z)]


def square_reduce(far, by_x, by_z, own):
    got_far = flip_x(far)
    got_x = flip_x(after(by_x, got_far))
    got_z = flip_far((by_z + wide(got_far)).astype(BF))
    return own + wide(got_x) + wide(got_z)


def ordered(flag, own, other, axis):
    return jnp.where(
        flag == 0,
        jnp.concatenate((own, other), axis=axis),
        jnp.concatenate((other, own), axis=axis),
    )


def after(values, *events):
    return lax.optimization_barrier((values, events))[0]


def both_cores(tall, by_y, high, by_y_high, *events):
    own = jnp.stack((tall, by_y, high, by_y_high))
    return own, flip_dp(after(own, *events) if events else own)


def piece(pair, slot, y):
    return pair[slot % 2].at[2 * (slot // 2) + y]


def wide(values):
    return values.astype(F32)


class Spread:
    def __init__(self, grads):
        self.keep, self.send = grads

    def to_core(self, *events):
        self.got = flip_dp(after(self.send, *events))
        return self.got

    def here(self, y, h):
        return wide(self.keep[y, h]) + wide(self.got[y, h])

    def to_y(self, h, *events):
        by_y = flip_dp_y(after(self.here(1, h).astype(BF), *events))
        setattr(self, "by_y%d" % h, by_y)
        return by_y

    def to_high(self, flip_z, *events):
        send = (self.here(0, 1) + wide(self.by_y1)).astype(BF)
        self.high = flip_z(after(send, *events))
        return self.high

    def total(self, *events):
        value = self.here(0, 0) + wide(self.by_y0) + wide(self.high)
        return after(value.astype(BF), *events) if events else value.astype(BF)


def to_x(total, x, axis):
    size = total.shape[axis] // 2
    own = lax.dynamic_slice_in_dim(total, x * size, size, axis)
    return own, lax.dynamic_slice_in_dim(total, (1 - x) * size, size, axis)


def pair_up(own, by_x, x):
    return jnp.where(x == 0, jnp.stack((own, by_x)), jnp.stack((by_x, own)))


def unite(mine, theirs, q, axis):
    parts = []
    for at in range(2):
        parts += [jnp.where(q == 0, mine[at], theirs[at]), jnp.where(q == 0, theirs[at], mine[at])]
    return jnp.concatenate(parts, axis=axis).astype(F32)


def exchanged_sum(value, axes, count):
    tiles = jnp.broadcast_to(value, (count, 8, HD))
    tiles = lax.all_to_all(tiles, axes, split_axis=0, concat_axis=0, tiled=True)
    return jnp.sum(tiles[:, 0, 0]).reshape(1)


def local_norm(values):
    average = jnp.mean(values, axis=1, keepdims=True)
    square = jnp.mean(values * values, axis=1, keepdims=True)
    inverse = lax.rsqrt(square - average * average + EPSILON)
    return ((values - average) * inverse, inverse)


def local_norm_backward(gradient, normed, inverse):
    average = jnp.mean(gradient, axis=1, keepdims=True)
    crossed = jnp.mean(gradient * normed, axis=1, keepdims=True)
    return inverse * (gradient - average - normed * crossed)


def dot(left, right, a, b):
    return lax.dot_general(left, right, (((a,), (b,)), ((), ())), preferred_element_type=F32)


SMEM_SPEC = pl.BlockSpec(memory_space=pltpu.SMEM)
VMEM_SPEC = pl.BlockSpec(memory_space=pltpu.VMEM)


def shape(dims, kind):
    return jax.ShapeDtypeStruct(dims, kind)


def params(megabytes):
    return pltpu.CompilerParams(vmem_limit_bytes=megabytes * 2**20)


def cost(flops, moved, transcendentals=0):
    return pl.CostEstimate(
        flops=int(flops), bytes_accessed=int(moved), transcendentals=int(transcendentals)
    )


def y_half(y):
    return slice(y * HALF, (y + 1) * HALF)


def columns(index, width):
    return slice(index * width, (index + 1) * width)


FAR_SHAPES = [shape((PIECE // 2, D), BF)] * 2
SIDE_SHAPES = [
    shape((PIECE, D), BF),
    shape((PIECE // 2, D), F32),
    shape((PIECE // 2, D), F32),
]
OWN_SHAPES = [shape((PIECE, D), F32)]
NEAR_SHAPES = [
    shape((PIECE // 2, D), F32),
    shape((PIECE // 2, D), BF),
    shape((PIECE // 2, D), BF),
    shape((PIECE // 2, D), F32),
]
SUM_SHAPES = {"far": FAR_SHAPES, "sides": NEAR_SHAPES, "own": OWN_SHAPES}
SUM_BLOCKS = {"far": (3,), "sides": (1, 2), "own": (0,)}


def store_halves(part, value, outs):
    half = PIECE // 2
    for low in range(2):
        rows = value[low * half : (low + 1) * half]
        outs[low][:, y_half(part)] = rows.astype(outs[low].dtype)


def store_sum(kind, index, part, value, outs):
    if kind == "own":
        outs[0][:, y_half(part)] = value
    else:
        store_halves(part, value, outs[2 * index : 2 * index + 2])


ALL_SHAPES = [shape((PIECE, D), kind) for kind in (F32, BF, F32, BF)]


def store_any(a, part, value, outs):
    outs[a][:, y_half(part)] = value.astype(outs[a].dtype)


def qkv_kernel(place_ref, *refs):
    acts, refs = refs[:4], refs[4:]
    weights, refs = refs[:2], refs[2:]
    cos_ref, sin_ref, *refs = refs
    outs, weight_s = refs[:4], refs[4]
    for b in range(4):
        for y in range(2):
            for which in range(3):
                weight_s[y_half(y), columns(which * 4 + b, HD)] = piece(weights, b, y)[which]
    for a in range(4):
        rows = pl.ds(pl.multiple_of(place_ref[a] * PIECE, PIECE), PIECE)
        cos_block, sin_block = cos_ref[rows, :], sin_ref[rows, :]
        act = acts[a][...]
        projected = dot(act, weight_s[...], 1, 0)
        for which in range(3):
            for b in range(4):
                tile = projected[:, columns(which * 4 + b, HD)]
                if which < 2:
                    tile = tile * cos_block + pltpu.roll(tile, HD // 2, 1) * sin_block
                outs[b][which, a] = tile.astype(BF)


def run_qkv(place, acts, weights, cos_wide, sin_wide):
    return pl.pallas_call(
        qkv_kernel,
        out_shape=[shape((3, 4, PIECE, HD), BF)] * 4,
        in_specs=[SMEM_SPEC] + [VMEM_SPEC] * 8,
        out_specs=[VMEM_SPEC] * 4,
        scratch_shapes=[pltpu.VMEM((D, 12 * HD), BF)],
        compiler_params=params(40),
        cost_estimate=cost(2 * 4 * PIECE * D * 12 * HD, 20 * 2**20),
    )(place, *acts, *weights, cos_wide, sin_wide)


def out_kernel(*refs):
    mixed, refs = refs[:4], refs[4:]
    weights, refs = refs[:2], refs[2:]
    outs, weight_s = refs[:4], refs[4]
    for b in range(4):
        for y in range(2):
            weight_s[y_half(y), columns(b, HD)] = piece(weights, b, y)[3]
    for a in range(4):
        act = jnp.concatenate([mixed[b][a] for b in range(4)], axis=1)
        for y in range(2):
            store_any(a, y, dot(act, weight_s[y_half(y), :], 1, 1), outs)


def run_out(mixed, weights):
    outs = pl.pallas_call(
        out_kernel,
        out_shape=ALL_SHAPES,
        in_specs=[VMEM_SPEC] * 6,
        out_specs=[VMEM_SPEC] * 4,
        scratch_shapes=[pltpu.VMEM((D, 4 * HD), BF)],
        compiler_params=params(36),
        cost_estimate=cost(2 * 4 * PIECE * D * 4 * HD, 16 * 2**20),
    )(*mixed, *weights)
    return outs[3], outs[1], outs[2], outs[0]


def input_kernel(*refs):
    back, refs = refs[:4], refs[4:]
    weights, refs = refs[:2], refs[2:]
    outs, weight_s = refs[:4], refs[4]
    for b in range(4):
        for y in range(2):
            for which in range(3):
                weight_s[y_half(y), columns(which * 4 + b, HD)] = piece(weights, b, y)[which]
    for a in range(4):
        act = jnp.concatenate(
            [back[b][which, a] for which in range(3) for b in range(4)], axis=1
        )
        for y in range(2):
            store_any(a, y, dot(act, weight_s[y_half(y), :], 1, 1), outs)


def run_input(back, weights):
    outs = pl.pallas_call(
        input_kernel,
        out_shape=ALL_SHAPES,
        in_specs=[VMEM_SPEC] * 6,
        out_specs=[VMEM_SPEC] * 4,
        scratch_shapes=[pltpu.VMEM((D, 12 * HD), BF)],
        compiler_params=params(40),
        cost_estimate=cost(2 * 4 * PIECE * D * 12 * HD, 20 * 2**20),
    )(*back, *weights)
    return outs[3], outs[1], outs[2], outs[0]


def attended_grad_kernel(*refs):
    acts, refs = refs[:4], refs[4:]
    weights, refs = refs[:2], refs[2:]
    outs, weight_s = refs[:4], refs[4]
    for b in range(4):
        for y in range(2):
            weight_s[y_half(y), columns(b, HD)] = piece(weights, b, y)[3]
    for a in range(4):
        act = acts[a][...]
        value = dot(act, weight_s[...], 1, 0)
        for b in range(4):
            outs[b][a] = value[:, columns(b, HD)].astype(BF)


def run_attended_grad(acts, weights):
    return pl.pallas_call(
        attended_grad_kernel,
        out_shape=[shape((4, PIECE, HD), BF)] * 4,
        in_specs=[VMEM_SPEC] * 6,
        out_specs=[VMEM_SPEC] * 4,
        scratch_shapes=[pltpu.VMEM((D, 4 * HD), BF)],
        compiler_params=params(36),
        cost_estimate=cost(2 * 4 * PIECE * D * 4 * HD, 16 * 2**20),
    )(*acts, *weights)


CHUNK = 256


def up_kernel(count, *refs):
    acts, refs = refs[:count], refs[count:]
    gates, refs = refs[:2], refs[2:]
    ups, refs = refs[:2], refs[2:]
    gating_ref, upward_ref, units_ref = refs
    start = 0
    for act_ref in acts:
        size = act_ref.shape[0]
        rows = slice(start, start + size)
        start += size
        low, high = act_ref[:, y_half(0)], act_ref[:, y_half(1)]
        for b in range(4):
            gate = dot(low, piece(gates, b, 0)[...], 1, 0)
            gate += dot(high, piece(gates, b, 1)[...], 1, 0)
            up = dot(low, piece(ups, b, 0)[...], 1, 0) + dot(high, piece(ups, b, 1)[...], 1, 0)
            gating_ref[b, rows] = gate
            upward_ref[b, rows] = up
            units_ref[b, rows] = (gate * jax.nn.sigmoid(gate) * up).astype(BF)


def run_up(acts, gates, ups):
    rows = sum(act.shape[0] for act in acts)
    width = gates[0].shape[2]
    whole = lambda act: pl.BlockSpec(act.shape, lambda j: (0, 0))
    part = pl.BlockSpec((4, HALF, CHUNK), lambda j: (0, 0, j))
    out = pl.BlockSpec((4, rows, CHUNK), lambda j: (0, 0, j))
    return pl.pallas_call(
        lambda *refs: up_kernel(len(acts), *refs),
        grid=(width // CHUNK,),
        out_shape=[shape((4, rows, width), kind) for kind in (F32, F32, BF)],
        in_specs=[whole(act) for act in acts] + [part] * 4,
        out_specs=[out] * 3,
        compiler_params=params(48),
        cost_estimate=cost(2 * rows * D * 8 * width, 16 * 2**20, 4 * rows * width),
    )(*acts, *gates, *ups)


def down_kernel(kind, units_ref, *refs):
    weights, outs = refs[:2], refs[2:]
    for index in range(len(SUM_BLOCKS[kind])):
        rows = slice(index * PIECE, (index + 1) * PIECE)
        for y in range(2):
            value = dot(units_ref[0, rows], piece(weights, 0, y)[...], 1, 0)
            for b in range(1, 4):
                value += dot(units_ref[b, rows], piece(weights, b, y)[...], 1, 0)
            store_sum(kind, index, y, value, outs)


def run_down(kind, units, weights):
    rows, width = units.shape[1], units.shape[2]
    shapes = SUM_SHAPES[kind]
    return pl.pallas_call(
        lambda *refs: down_kernel(kind, *refs),
        out_shape=shapes,
        in_specs=[VMEM_SPEC] * 3,
        out_specs=[VMEM_SPEC] * len(shapes),
        compiler_params=params(36),
        cost_estimate=cost(2 * rows * D * 4 * width, 12 * 2**20),
    )(units, *weights)


def gated_kernel(count, *refs):
    acts, refs = refs[:count], refs[count:]
    gating_ref, upward_ref, *refs = refs
    weights, refs = refs[:2], refs[2:]
    gate_ref, up_ref = refs
    start = 0
    for act_ref in acts:
        size = act_ref.shape[0]
        rows = slice(start, start + size)
        start += size
        low, high = act_ref[:, y_half(0)], act_ref[:, y_half(1)]
        for b in range(4):
            grad = dot(low, piece(weights, b, 0)[...], 1, 1)
            grad += dot(high, piece(weights, b, 1)[...], 1, 1)
            gate = gating_ref[b, rows]
            sigmoid = jax.nn.sigmoid(gate)
            gate_ref[b, rows] = (
                grad * upward_ref[b, rows] * sigmoid * (1.0 + gate * (1.0 - sigmoid))
            ).astype(BF)
            up_ref[b, rows] = (grad * (gate * sigmoid)).astype(BF)


def run_gated(acts, gating, upward, weights):
    rows, width = gating.shape[1], gating.shape[2]
    return pl.pallas_call(
        lambda *refs: gated_kernel(len(acts), *refs),
        out_shape=[shape((4, rows, width), BF)] * 2,
        in_specs=[VMEM_SPEC] * (len(acts) + 4),
        out_specs=[VMEM_SPEC] * 2,
        compiler_params=params(44),
        cost_estimate=cost(2 * rows * D * 4 * width, 16 * 2**20, 4 * rows * width),
    )(*acts, gating, upward, *weights)


def normed_two_kernel(kind, gate_ref, up_ref, *refs):
    gates, refs = refs[:2], refs[2:]
    ups, refs = refs[:2], refs[2:]
    outs, total_s = refs[:-1], refs[-1]
    step, last = pl.program_id(0), pl.num_programs(0) - 1
    for y in range(2):
        value = dot(gate_ref[0], piece(gates, 0, y)[...], 1, 1)
        for b in range(4):
            if b > 0:
                value += dot(gate_ref[b], piece(gates, b, y)[...], 1, 1)
            value += dot(up_ref[b], piece(ups, b, y)[...], 1, 1)

        @pl.when(step == 0)
        def _():
            total_s[:, y_half(y)] = value

        @pl.when(step == last)
        def _():
            whole = total_s[:, y_half(y)] + value
            for index in range(len(SUM_BLOCKS[kind])):
                rows = slice(index * PIECE, (index + 1) * PIECE)
                store_sum(kind, index, y, whole[rows], outs)


def run_normed_two(kind, gate_low, up_low, gates, ups):
    rows, width = gate_low.shape[1], gate_low.shape[2]
    shapes = SUM_SHAPES[kind]
    low = pl.BlockSpec((4, rows, width // 2), lambda j: (0, 0, j))
    part = pl.BlockSpec((4, HALF, width // 2), lambda j: (0, 0, j))
    return pl.pallas_call(
        lambda *refs: normed_two_kernel(kind, *refs),
        grid=(2,),
        out_shape=shapes,
        in_specs=[low] * 2 + [part] * 4,
        out_specs=[pl.BlockSpec(s.shape, lambda j: (0, 0)) for s in shapes],
        scratch_shapes=[pltpu.VMEM((rows, D), F32)],
        compiler_params=params(48),
        cost_estimate=cost(2 * rows * D * 8 * width, 18 * 2**20),
    )(gate_low, up_low, *gates, *ups)


def wide_grad_kernel(*refs):
    acts, refs = refs[:5], refs[5:]
    lows, refs = refs[:3], refs[3:]
    outs, turned_s = refs[:2], refs[2]

    @pl.when(pl.program_id(1) == 0)
    def _():
        start = 0
        for act_ref in acts:
            size = act_ref.shape[0]
            turned_s[:, start : start + size] = act_ref[...].T
            start += size

    for d in range(2):
        total, start = None, 0
        for low_ref in lows:
            size = low_ref.shape[1]
            value = dot(turned_s[:, start : start + size], low_ref[d], 1, 0)
            total = value if total is None else total + value
            start += size
        outs[d][0, 0] = total.astype(BF)


def run_wide_grad(acts, lows):
    width = lows[0].shape[2]
    return pl.pallas_call(
        wide_grad_kernel,
        grid=(2, 2),
        out_shape=[shape((2, 2, HALF, width), BF)] * 2,
        in_specs=[pl.BlockSpec((act.shape[0], HALF), lambda y, h: (0, y)) for act in acts]
        + [pl.BlockSpec((2, low.shape[1], width), lambda y, h: (h, 0, 0)) for low in lows],
        out_specs=[pl.BlockSpec((1, 1, HALF, width), lambda y, h: (y, h, 0, 0))] * 2,
        scratch_shapes=[pltpu.VMEM((HALF, 4 * PIECE), BF)],
        compiler_params=params(36),
        cost_estimate=cost(2 * 4 * PIECE * D * 4 * width, 16 * 2**20),
    )(*acts, *lows)


def down_grad_kernel(*refs):
    units, refs = refs[:3], refs[3:]
    acts, refs = refs[:5], refs[5:]
    outs, turned_s = refs[:2], refs[2]

    @pl.when(pl.program_id(1) == 0)
    def _():
        start = 0
        for unit_ref in units:
            size = unit_ref.shape[1]
            for d in range(2):
                turned_s[d, :, start : start + size] = unit_ref[d].T
            start += size

    for d in range(2):
        total, start = None, 0
        for act_ref in acts:
            size = act_ref.shape[0]
            value = dot(turned_s[d, :, start : start + size], act_ref[...], 1, 0)
            total = value if total is None else total + value
            start += size
        outs[d][0, 0] = total.astype(BF)


def run_down_grad(units, acts):
    width = units[0].shape[2]
    return pl.pallas_call(
        down_grad_kernel,
        grid=(2, 2),
        out_shape=[shape((2, 2, width, HALF), BF)] * 2,
        in_specs=[pl.BlockSpec((2, unit.shape[1], width), lambda h, y: (h, 0, 0)) for unit in units]
        + [pl.BlockSpec((act.shape[0], HALF), lambda h, y: (0, y)) for act in acts],
        out_specs=[pl.BlockSpec((1, 1, width, HALF), lambda h, y: (y, h, 0, 0))] * 2,
        scratch_shapes=[pltpu.VMEM((2, width, 4 * PIECE), BF)],
        compiler_params=params(36),
        cost_estimate=cost(2 * 4 * PIECE * D * 4 * width, 16 * 2**20),
    )(*units, *acts)


def head_grad_kernel(kinds, *refs):
    acts, refs = refs[:4], refs[4:]
    messages, refs = refs[:4], refs[4:]
    passed, refs = (refs[:2], refs[2:]) if kinds > 1 else (None, refs)
    outs, turned_s, right_s = refs[:2], refs[2], refs[3]
    start = 0
    for act_ref in acts:
        size = act_ref.shape[0]
        turned_s[:, start : start + size] = act_ref[...].T
        start += size

    @pl.when(pl.program_id(0) == 0)
    def _():
        for which in range(kinds):
            for b in range(4):
                for a in range(4):
                    value = messages[b][which, a] if kinds > 1 else messages[b][a]
                    right_s[columns(a, PIECE), columns(which * 4 + b, HD)] = value

    for which in range(kinds):
        value = dot(turned_s[...], right_s[:, columns(which, 4 * HD)], 1, 0)
        for b, (d, h) in enumerate(SLOTS):
            outs[d][0, h, which] = value[:, columns(b, HD)].astype(BF)
    if passed:
        for d in range(2):
            outs[d][0, :, kinds] = passed[d][0, :, 0]


def run_head_grad(kinds, acts, messages, passed=()):
    whole = lambda dims: pl.BlockSpec(dims, lambda y: (0,) * len(dims))
    rows = lambda count: pl.BlockSpec((1, 2, count, HALF, HD), lambda y: (y, 0, 0, 0, 0))
    made = kinds + 1 if passed else kinds
    return pl.pallas_call(
        lambda *refs: head_grad_kernel(kinds, *refs),
        grid=(2,),
        out_shape=[shape((2, 2, made, HALF, HD), BF)] * 2,
        in_specs=[pl.BlockSpec((act.shape[0], HALF), lambda y: (0, y)) for act in acts]
        + [whole(message.shape) for message in messages]
        + [rows(1)] * len(passed),
        out_specs=[rows(made)] * 2,
        scratch_shapes=[
            pltpu.VMEM((HALF, 4 * PIECE), BF),
            pltpu.VMEM((4 * PIECE, kinds * 4 * HD), BF),
        ],
        compiler_params=params(44),
        cost_estimate=cost(2 * 4 * PIECE * D * kinds * 4 * HD, 12 * 2**20),
    )(*acts, *messages, *passed)


def allowed_pairs(starts, query0, key0, shape, query_axis):
    query = query0 + lax.broadcasted_iota(jnp.int32, shape, query_axis)
    key = key0 + lax.broadcasted_iota(jnp.int32, shape, 1 - query_axis)
    first = jnp.zeros(shape, jnp.int32)
    for s in range(CONT):
        first = jnp.where(query >= starts[s], starts[s], first)
    return (key <= query) & ((key < starts[0]) | (key >= first))


def block_bounds(starts, n):
    full = jnp.minimum(n, starts[0] // BLOCK)
    first = jnp.int32(0)
    for s in range(CONT):
        first = jnp.where(n * BLOCK >= starts[s], starts[s], first)
    return full, first


def block_used(starts, first, m):
    return (m * BLOCK < starts[0]) | ((m + 1) * BLOCK > first)


def attention_forward(place_ref, starts_ref, *refs):
    messages, refs = refs[:4], refs[4:]
    outs, refs = refs[:4], refs[4:]
    wide_ref, log_ref, q_s, k_s, v_s, score_s, acc_s, sum_s, max_s = refs
    scale = LOG2E / math.sqrt(HD)
    starts = [starts_ref[s] for s in range(CONT)]
    for b in range(4):
        for a in range(4):
            rows = pl.ds(pl.multiple_of(place_ref[4 * b + a] * PIECE, PIECE), PIECE)
            q_s[rows, :] = messages[b][0, a]
            k_s[rows, :] = messages[b][1, a]
            v_s[rows, :] = messages[b][2, a]

    def one_block(n, carry):
        rows = pl.ds(pl.multiple_of(n * BLOCK, BLOCK), BLOCK)
        full, first = block_bounds(starts, n)
        max_s[...] = jnp.full(max_s.shape, -1e30, F32)
        acc_s[...] = jnp.zeros(acc_s.shape, F32)
        sum_s[...] = jnp.zeros(sum_s.shape, F32)

        def note(scores, m):
            score_s[m] = scores
            top = max_s[...]
            for part in range(BLOCK // HD):
                top = jnp.maximum(top, scores[:, part * HD : (part + 1) * HD])
            max_s[...] = top

        def product(m):
            keys = pl.ds(pl.multiple_of(m * BLOCK, BLOCK), BLOCK)
            return dot(q_s[rows, :], k_s[keys, :], 1, 1)

        @pl.loop(0, full)
        def _(m):
            note(product(m), m)

        @pl.loop(full, n + 1)
        def _(m):
            @pl.when(block_used(starts, first, m))
            def _():
                allowed = allowed_pairs(starts, n * BLOCK, m * BLOCK, (BLOCK, BLOCK), 0)
                note(jnp.where(allowed, product(m), MASKED_SCORE), m)

        highest = jnp.max(max_s[...], axis=1, keepdims=True) * scale

        @pl.loop(0, n + 1)
        def _(m):
            @pl.when(block_used(starts, first, m))
            def _():
                keys = pl.ds(pl.multiple_of(m * BLOCK, BLOCK), BLOCK)
                exponent = jnp.exp2(score_s[m] * scale - highest)
                total = sum_s[...]
                for part in range(BLOCK // HD):
                    total = total + exponent[:, part * HD : (part + 1) * HD]
                sum_s[...] = total
                acc_s[...] += dot(exponent.astype(BF), v_s[keys, :], 1, 0)

        total = jnp.sum(sum_s[...], axis=1, keepdims=True)
        wide_ref[rows, :] = acc_s[...] / total
        log_total = jnp.broadcast_to(highest + jnp.log2(total), (BLOCK, HD))
        log_ref[n] = log_total.T[:8]
        return carry

    lax.fori_loop(0, k_s.shape[0] // BLOCK, one_block, 0)
    for b in range(4):
        for a in range(4):
            rows = pl.ds(pl.multiple_of(place_ref[4 * b + a] * PIECE, PIECE), PIECE)
            outs[b][a] = wide_ref[rows, :].astype(BF)


def attention_backward(place_ref, starts_ref, *refs):
    messages, refs = refs[:4], refs[4:]
    grads, refs = refs[:4], refs[4:]
    wide_ref, log_ref, cos_ref, sin_ref, *refs = refs
    outs, refs = refs[:4], refs[4:]
    q_s, k_s, v_s, g_s, dq_s, dk_s, dv_s = refs
    scale = LOG2E / math.sqrt(HD)
    starts = [starts_ref[s] for s in range(CONT)]
    for b in range(4):
        for a in range(4):
            rows = pl.ds(pl.multiple_of(place_ref[4 * b + a] * PIECE, PIECE), PIECE)
            q_s[rows, :] = messages[b][0, a]
            k_s[rows, :] = messages[b][1, a]
            v_s[rows, :] = messages[b][2, a]
            g_s[rows, :] = grads[b][a]
    dq_s[...] = jnp.zeros(dq_s.shape, F32)
    dk_s[...] = jnp.zeros(dk_s.shape, F32)
    dv_s[...] = jnp.zeros(dv_s.shape, F32)

    def one_block(n, carry):
        rows = pl.ds(pl.multiple_of(n * BLOCK, BLOCK), BLOCK)
        full, first = block_bounds(starts, n)
        crossed = g_s[rows, :].astype(F32) * wide_ref[rows, :]
        row_dot = jnp.sum(crossed.T, axis=0, keepdims=True)
        log_total = log_ref[n][:1]

        def step(m, masked):
            keys = pl.ds(pl.multiple_of(m * BLOCK, BLOCK), BLOCK)
            query, key = q_s[rows, :], k_s[keys, :]
            probability = jnp.exp2(dot(key, query, 1, 1) * scale - log_total)
            if masked:
                allowed = allowed_pairs(starts, n * BLOCK, m * BLOCK, (BLOCK, BLOCK), 1)
                probability = jnp.where(allowed, probability, 0.0)
            prob_grad = dot(v_s[keys, :], g_s[rows, :], 1, 1)
            score_grad = (probability * (prob_grad - row_dot)).astype(BF)
            dv_s[keys, :] += dot(probability.astype(BF), g_s[rows, :], 1, 0)
            dk_s[keys, :] += dot(score_grad, query, 1, 0)
            dq_s[rows, :] += dot(score_grad, key, 0, 0)

        @pl.loop(0, full)
        def _(m):
            step(m, False)

        @pl.loop(full, n + 1)
        def _(m):
            @pl.when(block_used(starts, first, m))
            def _():
                step(m, True)

        return carry

    lax.fori_loop(0, k_s.shape[0] // BLOCK, one_block, 0)
    for b in range(4):
        for a in range(4):
            rows = pl.ds(pl.multiple_of(place_ref[4 * b + a] * PIECE, PIECE), PIECE)
            for which, grad in ((0, dq_s), (1, dk_s)):
                value = grad[rows, :] * (1.0 / math.sqrt(HD))
                turned = value * cos_ref[rows, :] - pltpu.roll(value, HD // 2, 1) * sin_ref[rows, :]
                outs[b][which, a] = turned.astype(BF)
            outs[b][2, a] = dv_s[rows, :].astype(BF)


def run_forward(place, starts, messages):
    tokens = 16 * PIECE
    blocks = tokens // BLOCK
    out_shape = [jax.ShapeDtypeStruct((4, PIECE, HD), BF)] * 4
    out_shape += [
        jax.ShapeDtypeStruct((tokens, HD), F32),
        jax.ShapeDtypeStruct((blocks, 8, BLOCK), F32),
    ]
    return pl.pallas_call(
        attention_forward,
        out_shape=out_shape,
        in_specs=[SMEM_SPEC] * 2 + [VMEM_SPEC] * 4,
        out_specs=[VMEM_SPEC] * 6,
        scratch_shapes=[
            pltpu.VMEM((tokens, HD), BF),
            pltpu.VMEM((tokens, HD), BF),
            pltpu.VMEM((tokens, HD), BF),
            pltpu.VMEM((blocks, BLOCK, BLOCK), F32),
            pltpu.VMEM((BLOCK, HD), F32),
            pltpu.VMEM((BLOCK, HD), F32),
            pltpu.VMEM((BLOCK, HD), F32),
        ],
        compiler_params=pltpu.CompilerParams(vmem_limit_bytes=48 * 2**20),
        cost_estimate=pl.CostEstimate(
            flops=2 * tokens * tokens * HD * 2,
            bytes_accessed=8 * 2**20,
            transcendentals=tokens * tokens // 2,
        ),
    )(place, starts, *messages)


def run_backward(place, starts, messages, grads, wide, log_total, cosine, sine_table):
    tokens = 16 * PIECE
    return pl.pallas_call(
        attention_backward,
        out_shape=[jax.ShapeDtypeStruct((3, 4, PIECE, HD), BF)] * 4,
        in_specs=[SMEM_SPEC] * 2 + [VMEM_SPEC] * 12,
        out_specs=[VMEM_SPEC] * 4,
        scratch_shapes=[pltpu.VMEM((tokens, HD), BF)] * 4 + [pltpu.VMEM((tokens, HD), F32)] * 3,
        compiler_params=pltpu.CompilerParams(vmem_limit_bytes=52 * 2**20),
        cost_estimate=pl.CostEstimate(
            flops=5 * tokens * tokens * HD * 2,
            bytes_accessed=16 * 2**20,
            transcendentals=tokens * tokens // 2,
        ),
    )(place, starts, *messages, *grads, wide, log_total, cosine, sine_table)


def swap_slots(messages):
    return [messages[0], flip_y(messages[1]), flip_near(messages[2]), flip_y_near(messages[3])]


def to_tokens(values):
    return lax.all_to_all(values, "row", split_axis=0, concat_axis=1, tiled=True)


def to_width(values):
    return lax.all_to_all(values, "row", split_axis=1, concat_axis=0, tiled=True)


def square_shards(
    hidden_in,
    teacher,
    valid,
    segment_ids,
    query_weight,
    key_weight,
    value_weight,
    output_weight,
    gate_weight,
    up_weight,
    down_weight,
):
    row, col, dp = lax.axis_index("row"), lax.axis_index("col"), lax.axis_index("dp")
    x, y = row % 2, row // 2
    q = (dp + y) % 2
    own_piece = col * SIDE + row
    segment = segment_ids[0]
    group_tokens = segment.shape[0]
    home_tokens = group_tokens // (SIDE * SIDE)

    def swap_y(values):
        return jnp.where(
            y == 0, values, jnp.concatenate((values[:, HALF:], values[:, :HALF]), axis=1)
        )

    def cut(matrix, at, axis):
        size = matrix.shape[axis] // 4
        return lax.dynamic_slice_in_dim(matrix, (2 * at + q) * size, size, axis)

    def head_cut(at):
        parts = [cut(matrix, at, 1) for matrix in (query_weight, key_weight, value_weight)]
        return jnp.stack(parts + [cut(output_weight, at, 0).T])

    labels = jnp.arange(1, CONT + 1, dtype=jnp.int32)
    starts = jnp.sum((segment[None, :] < labels[:, None]).astype(jnp.int32), axis=1)
    codes = jnp.arange(16, dtype=jnp.int32)
    relative = (
        (codes & 1) + ((codes >> 1) & 1) * 8 + ((codes >> 2) & 1) * 2 + ((codes >> 3) & 1) * 4
    )
    pieces = relative ^ own_piece
    frequency = jnp.power(10000.0, jnp.arange(HD // 2, dtype=F32) * (-2.0 / HD))
    angles = positions(segment).astype(F32)[:, None] * jnp.tile(frequency, 2)[None, :]
    sign = jnp.where(jnp.arange(HD) < HD // 2, -1.0, 1.0)
    cos_wide, sin_wide = jnp.cos(angles), jnp.sin(angles) * sign[None, :]

    heads_x = flip_x(head_cut(1 - x))
    count = exchanged_sum(jnp.sum(valid.astype(F32)), ("dp", "col"), 2 * SIDE)
    heads_x = after(heads_x, count)
    gates_x = flip_x(after(cut(gate_weight, 1 - x, 1), heads_x))
    hidden = swap_y(to_tokens(after(hidden_in, heads_x))).astype(F32)
    heads_tall = ordered(x, head_cut(x), heads_x, 1)
    heads_high = flip_near(heads_tall)
    heads_y = flip_dp_y(heads_tall)
    normed, inverse_one = local_norm(after(hidden, gates_x))
    low_normed = normed.astype(BF)
    normed_acts = square_gather(low_normed)
    heads_y_high = flip_dp_y(after(heads_high, low_normed))
    gates_tall = ordered(x, cut(gate_weight, x, 1), gates_x, 0)
    gates_high = flip_far(after(gates_tall, heads_high, normed_acts[1:3]))
    cos_wide, sin_wide = after((cos_wide, sin_wide), heads_tall)
    heads = both_cores(
        heads_tall, heads_y, heads_high, after(heads_y_high, normed_acts[1:3], cos_wide, sin_wide)
    )
    gates_y = flip_dp_y(after(gates_tall, normed_acts))

    messages = run_qkv(pieces, normed_acts, heads, cos_wide, sin_wide)
    mlp_x = jnp.stack((cut(up_weight, 1 - x, 1), cut(down_weight, 1 - x, 0)))
    mlp_x = flip_x(after(mlp_x, messages[0]))
    target = to_tokens(after(teacher, messages[0]))
    messages = swap_slots(messages)
    messages = after(messages, mlp_x, gates_high, gates_y, target)

    ups_tall = ordered(x, cut(up_weight, x, 1), after(mlp_x[0], messages), 0)
    ups_high = flip_far(after(ups_tall, gates_high))
    gates_y_high = flip_dp_y(after(gates_high, messages))
    ups_y = flip_dp_y(ups_tall)
    *mixed, wide_mixed, log_total = run_forward(pieces, starts, messages)
    mixed = after(mixed, gates_y_high)
    downs_tall = ordered(x, cut(down_weight, x, 0), after(mlp_x[1], mixed), 1)
    mixed = swap_slots(mixed)
    mixed = after(mixed, ups_high, ups_y)
    gates = both_cores(gates_tall, gates_y, gates_high, gates_y_high, mixed)

    ups_y_high = flip_dp_y(after(ups_high, mixed))
    downs_y = flip_dp_y(after(downs_tall, ups_y_high))
    after_attention = hidden + square_reduce(*run_out(mixed, heads))
    after_attention = after(after_attention, ups_y_high, gates, downs_y)

    normed_two, inverse_two = local_norm(after_attention)
    ups = both_cores(ups_tall, ups_y, ups_high, ups_y_high, normed_two)
    low_two = normed_two.astype(BF)
    up_own = run_up([low_two], gates, ups)
    two_acts = near_gather(low_two, up_own)
    downs_high = flip_far(after(downs_tall, low_two))
    downs_y_high = flip_dp_y(after(downs_high, two_acts[1:3], up_own[2]))
    up_sides = run_up(after(two_acts[1:3], up_own[2]), gates, ups)
    up_far = run_up(after(two_acts[3:], up_sides[2], downs_y_high), gates, ups)
    downs = both_cores(downs_tall, downs_y, downs_high, downs_y_high, two_acts, up_sides[2])
    ups_out = [up_own, up_sides, up_far]
    units = [out[2] for out in ups_out]
    down_far = run_down("far", units[2], downs)
    down_sides = run_down("sides", after(units[1], down_far), downs)
    down_own = run_down("own", after(units[0], down_sides), downs)
    output = after_attention + near_reduce(down_far, down_sides, down_own[0])

    total_count = jnp.maximum(count, 1.0)
    counted_home = lax.dynamic_slice_in_dim(
        valid.astype(F32), row * home_tokens, home_tokens, 0
    )[:, None]
    differ = output - swap_y(target).astype(F32)
    local_loss = jnp.sum(counted_home * (differ * differ)) / D
    all_tokens = group_tokens * lax.axis_size("dp")
    out_grad = counted_home * differ * (all_tokens / total_count)

    low_out = out_grad.astype(BF)
    loss = exchanged_sum(after(local_loss, low_out), ("dp", "row", "col"), 2 * SIDE * SIDE)
    low_own = run_gated([low_out], up_own[0], up_own[1], downs)
    out_acts = near_gather(low_out, low_own)
    low_sides = run_gated(after(out_acts[1:3], low_own), up_sides[0], up_sides[1], downs)
    low_far = run_gated(after(out_acts[3:], low_sides, loss), up_far[0], up_far[1], downs)
    lows = [low_own, low_sides, low_far]
    two_far = run_normed_two("far", *low_far, gates, ups)
    two_sides = run_normed_two("sides", *after(low_sides, two_far), gates, ups)

    first = near_reduce_far(two_far)
    down_grads = Spread(run_down_grad(after(units, two_sides, first), out_acts))
    got = near_reduce_sides(first, two_sides)
    down_core = down_grads.to_core()
    two_own = run_normed_two("own", *after(low_own, down_grads.keep, got[1:3]), gates, ups)
    normed_two_grad = near_reduce_end(got, two_own[0])
    gate_pair = run_wide_grad(two_acts, after([low[0] for low in lows], two_own, down_core))
    gate_grads = Spread(gate_pair)
    down_y1 = down_grads.to_y(1)
    middle_grad = out_grad + local_norm_backward(normed_two_grad, normed_two, inverse_two)
    low_middle = middle_grad.astype(BF)
    gate_core = gate_grads.to_core(low_middle)
    down_y0 = down_grads.to_y(0, low_middle)
    up_pair = run_wide_grad(two_acts, after([low[1] for low in lows], gate_pair))
    up_grads = Spread(up_pair)
    middle_acts = square_gather(low_middle, gate_pair, down_y1)
    gate_y1 = gate_grads.to_y(1, down_y0, middle_acts[1:3])
    middle_acts = after(middle_acts, up_pair, down_y0, gate_y1)
    grad_messages = run_attended_grad(middle_acts, heads)
    up_core = up_grads.to_core(grad_messages)
    gate_y0 = gate_grads.to_y(0, gate_y1)
    down_grads.to_high(flip_far, middle_acts[1:3])
    out_pair = run_head_grad(1, after(middle_acts, grad_messages), mixed)
    grad_messages = swap_slots(grad_messages)
    grad_messages = after(grad_messages, up_core, out_pair, gate_y0)
    layer_output = to_width(swap_y(after(output, grad_messages).astype(BF)))
    up_y0 = up_grads.to_y(0, grad_messages)
    up_y1 = up_grads.to_y(1, grad_messages)
    back = run_backward(
        pieces, starts, messages, grad_messages, wide_mixed, log_total, cos_wide, sin_wide
    )
    back = after(back, down_grads.high, up_y1, up_y0)
    gate_grads.to_high(flip_far, back)
    own_down, send_down = to_x(down_grads.total(back), x, 1)
    down_x = flip_x(send_down)
    back = swap_slots(back)
    back = after(back, down_x, gate_grads.high, layer_output)
    up_grads.to_high(flip_far, back)
    head_pair = run_head_grad(3, normed_acts, back, out_pair)
    head_grads = Spread(head_pair)
    head_core = head_grads.to_core()
    input_sums = run_input(after(back, head_pair), heads)
    input_sums = after(input_sums, head_core)
    head_y1 = head_grads.to_y(1)
    normed_grad = square_reduce(*input_sums)
    head_y0 = head_grads.to_y(0, head_y1)
    head_grads.to_high(flip_near, head_y1)
    down_mine = pair_up(own_down, down_x, x)
    down_theirs = flip_dp(after(down_mine, input_sums))
    normed_grad = after(normed_grad, head_y0, head_grads.high, down_theirs, up_grads.high)
    input_gradient = middle_grad + local_norm_backward(normed_grad, normed, inverse_one)
    own_head, send_head = to_x(head_grads.total(normed_grad), x, 1)
    own_gate, send_gate = to_x(gate_grads.total(input_sums), x, 0)
    own_up, send_up = to_x(up_grads.total(normed_grad), x, 0)
    head_x = flip_x(send_head)
    last_x = flip_x(jnp.stack((send_gate, send_up)))
    last_mine = jnp.stack((pair_up(own_gate, last_x[0], x), pair_up(own_up, last_x[1], x)))
    last_theirs = flip_dp(last_mine)
    head_mine = pair_up(own_head, head_x, x)
    head_theirs = flip_dp(head_mine)
    mean_loss = loss / total_count

    gate_grad = unite(last_mine[0], last_theirs[0], q, 1)
    down_grad = unite(down_mine, down_theirs, q, 0)
    up_grad = unite(last_mine[1], last_theirs[1], q, 1)
    head_grads = unite(head_mine, head_theirs, q, 2)
    return (
        layer_output,
        mean_loss,
        to_width(swap_y(input_gradient.astype(BF))).astype(F32),
        head_grads[0],
        head_grads[1],
        head_grads[2],
        head_grads[3].T,
        gate_grad,
        up_grad,
        down_grad,
    )


def solution(mesh):
    body = square_shards if fits_square(mesh) else shards
    in_specs = (
        P(("dp", "col"), "row"),
        P(("dp", "col"), "row"),
        P(("dp", "col")),
        P("dp", None),
        P("row", "col"),
        P("row", "col"),
        P("row", "col"),
        P("col", "row"),
        P("row", "col"),
        P("row", "col"),
        P("col", "row"),
    )
    out_specs = (
        P(("dp", "col"), "row"),
        P(),
        P(("dp", "col"), "row"),
        P("row", "col"),
        P("row", "col"),
        P("row", "col"),
        P("col", "row"),
        P("row", "col"),
        P("row", "col"),
        P("col", "row"),
    )
    return jax.shard_map(body, mesh=mesh, in_specs=in_specs, out_specs=out_specs, check_vma=False)
```

```python
import math

import jax
import jax.numpy as jnp
from jax import lax
from jax.experimental import pallas as pl
from jax.experimental.pallas import tpu as pltpu
from jax.sharding import PartitionSpec as P

D = 2048
HD = 128
CONT = 8


EPSILON = 1e-05
MASKED_SCORE = -1e30


def positions(segment):
    labels = jnp.arange(CONT + 1, dtype=jnp.int32)
    onehot = (segment[:, None] == labels[None, :]).astype(jnp.int32)
    counts = jnp.sum(onehot, axis=0)
    starts = jnp.cumsum(counts) - counts
    leading = jnp.sum(onehot * starts[None, :], axis=1)
    indices = jnp.arange(segment.shape[0], dtype=jnp.int32)
    return indices - leading + jnp.where(segment > 0, counts[0], 0)


def rotary(offsets):
    half_width = HD // 2
    frequency = jnp.power(10000.0, jnp.arange(half_width, dtype=jnp.float32) * (-2.0 / HD))
    angles = offsets.astype(jnp.float32)[:, None] * frequency[None, :]
    return (jnp.cos(angles), jnp.sin(angles))


def rotate(values, cosine, sine_table):
    half_width = values.shape[-1] // 2
    leading, trailing = (values[..., :half_width], values[..., half_width:])
    cos_wide = cosine[:, None, :]
    sin_wide = sine_table[:, None, :]
    return jnp.concatenate(
        (leading * cos_wide - trailing * sin_wide, trailing * cos_wide + leading * sin_wide),
        axis=-1,
    )


def unrotate(gradient, cosine, sine_table):
    half_width = gradient.shape[-1] // 2
    leading, trailing = (gradient[..., :half_width], gradient[..., half_width:])
    cos_wide = cosine[:, None, :]
    sin_wide = sine_table[:, None, :]
    return jnp.concatenate(
        (leading * cos_wide + trailing * sin_wide, trailing * cos_wide - leading * sin_wide),
        axis=-1,
    )


def feature_sums(left, right):
    return lax.psum((jnp.sum(left, axis=1), jnp.sum(right, axis=1)), "row")


def normalize(values):
    summed, squared = feature_sums(values, values * values)
    average = (summed / D)[:, None]
    inverse = lax.rsqrt(squared[:, None] / D - average * average + EPSILON)
    return ((values - average) * inverse, inverse)


def norm_backward(gradient, normed, inverse):
    summed, crossed = feature_sums(gradient, gradient * normed)
    return inverse * (gradient - summed[:, None] / D - normed * (crossed[:, None] / D))


def widen(values):
    return lax.all_gather(values, "col", axis=0, tiled=True)


def collect(values):
    return lax.all_gather(values, "row", axis=0, tiled=True)


def row_product(full, matrix, contract):
    return lax.psum_scatter(
        lax.dot_general(
            full, matrix, (((1,), (contract,)), ((), ())), preferred_element_type=jnp.float32
        ),
        "row",
        scatter_dimension=0,
        tiled=True,
    )


def column_product(full, matrix, contract):
    return lax.psum_scatter(
        lax.dot_general(
            full, matrix, (((1,), (contract,)), ((), ())), preferred_element_type=jnp.float32
        ),
        "col",
        scatter_dimension=0,
        tiled=True,
    )


def project_in(gathered, matrix):
    result = row_product(gathered, matrix, 0)
    return result


def project_back(gathered, matrix):
    result = row_product(gathered, matrix, 1)
    return result


def weight_product(left, right):
    return lax.dot_general(
        left, right, (((0,), (0,)), ((), ())), preferred_element_type=jnp.float32
    )


def block_layout(tok_rows):
    blocks = max(1, tok_rows // 512)
    return (blocks, tok_rows // blocks)


def score_maker(key_rows, segment, block):
    key_index = jnp.arange(key_rows.shape[0], dtype=jnp.int32)
    scale = 1.0 / math.sqrt(HD)

    def scores_for(query_block, offset):
        query_index = offset + jnp.arange(block, dtype=jnp.int32)
        query_segment = lax.dynamic_slice_in_dim(segment, offset, block, 0)
        allowed = (key_index[None, :] <= query_index[:, None]) & (
            (segment[None, :] == 0) | (segment[None, :] == query_segment[:, None])
        )
        scores = (
            jnp.einsum("qhd,khd->hqk", query_block, key_rows, preferred_element_type=jnp.float32)
            * scale
        )
        return jnp.where(allowed[None, :, :], scores, MASKED_SCORE)

    return scores_for


def attend(queries, key_rows, value_rows, segment, row_offset):
    tok_rows, heads_here = (queries.shape[0], queries.shape[1])
    blocks, block = block_layout(tok_rows)
    scores_for = score_maker(key_rows, segment, block)
    offsets = row_offset + jnp.arange(blocks, dtype=jnp.int32) * block

    def forward_block(inputs):
        query_block, offset = inputs
        scores = scores_for(query_block, offset)
        highest = jnp.max(scores, axis=-1, keepdims=True)
        exponent = jnp.exp(scores - highest)
        summed = jnp.sum(exponent, axis=-1, keepdims=True)
        probability = (exponent / summed).astype(jnp.bfloat16)
        mixed_block = jnp.einsum(
            "hqk,khd->qhd", probability, value_rows, preferred_element_type=jnp.float32
        )
        return (mixed_block, highest + jnp.log(summed))

    mixed_blocks, log_total = lax.map(
        forward_block, (queries.reshape(blocks, block, heads_here, HD), offsets)
    )
    return (mixed_blocks.reshape(tok_rows, heads_here * HD), log_total)


def attend_back(queries, key_rows, value_rows, segment, row_offset, log_total, attended_grad):
    tok_rows, heads_here = (queries.shape[0], queries.shape[1])
    blocks, block = block_layout(tok_rows)
    scores_for = score_maker(key_rows, segment, block)
    offsets = row_offset + jnp.arange(blocks, dtype=jnp.int32) * block
    scale = 1.0 / math.sqrt(HD)

    def backward_block(carry, inputs):
        key_sum, value_sum = carry
        query_block, grad_block, log_block, offset = inputs
        scores = scores_for(query_block, offset)
        probability = jnp.exp(scores - log_block)
        rounded = probability.astype(jnp.bfloat16)
        prob_grad = jnp.einsum(
            "qhd,khd->hqk", grad_block, value_rows, preferred_element_type=jnp.float32
        )
        row_dot = jnp.sum(probability * prob_grad, axis=-1, keepdims=True)
        score_grad = (probability * (prob_grad - row_dot)).astype(jnp.bfloat16)
        query_grad = (
            jnp.einsum("hqk,khd->qhd", score_grad, key_rows, preferred_element_type=jnp.float32)
            * scale
        )
        key_sum = (
            key_sum
            + jnp.einsum(
                "hqk,qhd->khd", score_grad, query_block, preferred_element_type=jnp.float32
            )
            * scale
        )
        value_sum = value_sum + jnp.einsum(
            "hqk,qhd->khd", rounded, grad_block, preferred_element_type=jnp.float32
        )
        return ((key_sum, value_sum), query_grad)

    empty = jnp.zeros(key_rows.shape, jnp.float32)
    inputs = (
        queries.reshape(blocks, block, heads_here, HD),
        attended_grad.reshape(blocks, block, heads_here, HD),
        log_total,
        offsets,
    )
    (key_sum, value_sum), query_grads = lax.scan(backward_block, (empty, empty), inputs)
    return (query_grads.reshape(tok_rows, heads_here, HD), key_sum, value_sum)


def shards(
    hidden_in,
    teacher,
    valid,
    segment_ids,
    query_weight,
    key_weight,
    value_weight,
    output_weight,
    gate_weight,
    up_weight,
    down_weight,
):
    row_devices = lax.axis_size("row")
    col_devices = lax.axis_size("col")
    tok_cols = hidden_in.shape[0]
    group_tokens = tok_cols * col_devices
    tok_rows = group_tokens // row_devices
    query_width = query_weight.shape[1]
    heads_here = query_width // HD
    unit_width = gate_weight.shape[1]
    segment = segment_ids[0]
    row_offset = lax.axis_index("row") * tok_rows
    cosine_all, sine_all = rotary(positions(segment))
    cosine = lax.dynamic_slice_in_dim(cosine_all, row_offset, tok_rows, 0)
    sine_table = lax.dynamic_slice_in_dim(sine_all, row_offset, tok_rows, 0)
    counted = valid.astype(jnp.float32)
    total_count = jnp.maximum(lax.psum(jnp.sum(counted), ("dp", "col")), 1.0)
    hidden = hidden_in.astype(jnp.float32)
    normed, inverse_one = normalize(hidden)
    normed_wide = widen(normed.astype(jnp.bfloat16))
    attn_weights = jnp.concatenate((query_weight, key_weight, value_weight), axis=1)
    projected = project_in(normed_wide, attn_weights)
    queries = rotate(
        projected[:, :query_width].reshape(tok_rows, heads_here, HD), cosine, sine_table
    ).astype(jnp.bfloat16)
    key_local = rotate(
        projected[:, query_width : 2 * query_width].reshape(tok_rows, heads_here, HD),
        cosine,
        sine_table,
    )
    key_local = key_local.reshape(tok_rows, query_width).astype(jnp.bfloat16)
    value_local = projected[:, 2 * query_width :].astype(jnp.bfloat16)
    key_flat, value_flat = (
        lax.all_gather(key_local, "row", axis=0, tiled=True),
        lax.all_gather(value_local, "row", axis=0, tiled=True),
    )
    key_rows = key_flat.reshape(group_tokens, heads_here, HD)
    value_rows = value_flat.reshape(group_tokens, heads_here, HD)
    attended, log_total = attend(queries, key_rows, value_rows, segment, row_offset)
    attended_wide = collect(attended.astype(jnp.bfloat16))
    after_attention = hidden + column_product(attended_wide, output_weight, 0)
    normed_two, inverse_two = normalize(after_attention)
    normed_two_wide = widen(normed_two.astype(jnp.bfloat16))
    mlp_weights = jnp.concatenate((gate_weight, up_weight), axis=1)
    gated = project_in(normed_two_wide, mlp_weights)
    gating = gated[:, :unit_width]
    upward = gated[:, unit_width:]
    sigmoid = jax.nn.sigmoid(gating)
    activated = gating * sigmoid
    units_wide = collect((activated * upward).astype(jnp.bfloat16))
    output = after_attention + column_product(units_wide, down_weight, 0)
    differ = output - teacher.astype(jnp.float32)
    local_loss = jnp.sum(counted[:, None] * (differ * differ)) / D
    all_tokens = group_tokens * lax.axis_size("dp")
    out_grad = counted[:, None] * differ * (all_tokens / total_count)
    out_wide = widen(out_grad.astype(jnp.bfloat16))
    units_grad = project_back(out_wide, down_weight)
    down_grad = weight_product(units_wide, out_wide)
    gating_grad = units_grad * upward * sigmoid * (1.0 + gating * (1.0 - sigmoid))
    upward_grad = units_grad * activated
    gated_wide = collect(jnp.concatenate((gating_grad, upward_grad), axis=1).astype(jnp.bfloat16))
    mlp_grads = weight_product(normed_two_wide, gated_wide)
    normed_two_grad = column_product(gated_wide, mlp_weights, 1)
    middle_grad = out_grad + norm_backward(normed_two_grad, normed_two, inverse_two)
    middle_wide = widen(middle_grad.astype(jnp.bfloat16))
    attended_grad = project_back(middle_wide, output_weight).astype(jnp.bfloat16)
    output_grad_sum = weight_product(attended_wide, middle_wide)
    query_grad, key_sum, value_sum = attend_back(
        queries, key_rows, value_rows, segment, row_offset, log_total, attended_grad
    )
    key_grad, value_grad = (
        lax.psum_scatter(
            key_sum.reshape(group_tokens, query_width), "row", scatter_dimension=0, tiled=True
        ),
        lax.psum_scatter(
            value_sum.reshape(group_tokens, query_width), "row", scatter_dimension=0, tiled=True
        ),
    )
    query_pre = unrotate(query_grad, cosine, sine_table).reshape(tok_rows, query_width)
    key_pre = unrotate(key_grad.reshape(tok_rows, heads_here, HD), cosine, sine_table).reshape(
        tok_rows, query_width
    )
    projected_wide = collect(
        jnp.concatenate((query_pre, key_pre, value_grad), axis=1).astype(jnp.bfloat16)
    )
    attn_grads = weight_product(normed_wide, projected_wide)
    normed_grad = column_product(projected_wide, attn_weights, 1)
    input_gradient = middle_grad + norm_backward(normed_grad, normed, inverse_one)
    summed_grads = (
        lax.psum(attn_grads[:, :query_width].astype(jnp.bfloat16), "dp").astype(jnp.float32),
        lax.psum(attn_grads[:, query_width : 2 * query_width].astype(jnp.bfloat16), "dp").astype(
            jnp.float32
        ),
        lax.psum(attn_grads[:, 2 * query_width :].astype(jnp.bfloat16), "dp").astype(jnp.float32),
        lax.psum(output_grad_sum.astype(jnp.bfloat16), "dp").astype(jnp.float32),
        lax.psum(mlp_grads[:, :unit_width].astype(jnp.bfloat16), "dp").astype(jnp.float32),
        lax.psum(mlp_grads[:, unit_width:].astype(jnp.bfloat16), "dp").astype(jnp.float32),
        lax.psum(down_grad.astype(jnp.bfloat16), "dp").astype(jnp.float32),
    )
    mean_loss = lax.psum(local_loss, ("dp", "row", "col")) / total_count
    return (
        output.astype(jnp.bfloat16),
        mean_loss.reshape(1),
        input_gradient,
        summed_grads[0],
        summed_grads[1],
        summed_grads[2],
        summed_grads[3],
        summed_grads[4],
        summed_grads[5],
        summed_grads[6],
    )


BF = jnp.bfloat16
F32 = jnp.float32
LOG2E = 1.4426950408889634
SIDE = 4
HALF = D // 2
PIECE = 256
BLOCK = 512
SLOTS = [(d, h) for h in range(2) for d in range(2)]


def fits_square(mesh):
    return mesh.shape["dp"] == 2 and mesh.shape["row"] == SIDE and mesh.shape["col"] == SIDE


def flip(values, axis, bit):
    return lax.ppermute(values, axis, [(i, i ^ bit) for i in range(SIDE)])


def flip_x(values):
    return flip(values, "row", 1)


def flip_y(values):
    return flip(values, "row", 2)


def flip_far(values):
    return flip(values, "col", 2)


def flip_near(values):
    return flip(values, "col", 1)


def flip_y_near(values):
    pairs = [
        (r * SIDE + c, (r ^ 2) * SIDE + (c ^ 1)) for r in range(SIDE) for c in range(SIDE)
    ]
    return lax.ppermute(values, ("row", "col"), pairs)


def flip_z(values):
    return flip(values, "col", 3)


def flip_dp(values):
    return lax.ppermute(values, "dp", [(0, 1), (1, 0)])


def flip_dp_y(values):
    pairs = [(g * SIDE + r, (1 - g) * SIDE + (r ^ 2)) for g in range(2) for r in range(SIDE)]
    return lax.ppermute(values, ("dp", "row"), pairs)


def near_gather(block, *events):
    half = block.shape[0] // 2
    by_x, by_z = flip_x(block), flip_near(block)
    next_x, next_z = after((by_x, by_z), *events)
    return [block, by_x, by_z, flip_near(next_x[:half]), flip_x(next_z[half:])]


def near_reduce(far, sides, own):
    first = near_reduce_far(far)
    return near_reduce_end(near_reduce_sides(first, sides), own)


def near_reduce_far(far):
    return flip_near(far[0]), flip_x(far[1])


def near_reduce_sides(first, sides):
    far_top, far_bottom = first
    x_top, x_bottom, z_top, z_bottom = sides
    return (
        flip_x((x_top + wide(far_top)).astype(BF)),
        flip_x(x_bottom),
        flip_near(z_top),
        flip_near((z_bottom + wide(far_bottom)).astype(BF)),
    )


def near_reduce_end(got, own):
    x_top, x_bottom, z_top, z_bottom = got
    half = x_top.shape[0]
    top = own[:half] + wide(x_top) + wide(z_top)
    bottom = own[half:] + wide(x_bottom) + wide(z_bottom)
    return jnp.concatenate((top, bottom), axis=0)


def square_gather(block, *events):
    by_z, by_x = flip_far(block), flip_x(block)
    return [block, by_x, by_z, flip_x(after(by_z, *events) if events else by_z)]


def square_reduce(far, by_x, by_z, own, *events):
    got_far = flip_x(far)
    got_far = after(got_far, *events) if events else got_far
    got_x = flip_x(after(by_x, got_far))
    got_z = flip_far((by_z + wide(got_far)).astype(BF))
    return own + wide(got_x) + wide(got_z)


def ordered(flag, own, other, axis):
    return jnp.where(
        flag == 0,
        jnp.concatenate((own, other), axis=axis),
        jnp.concatenate((other, own), axis=axis),
    )


def after(values, *events):
    return lax.optimization_barrier((values, events))[0]


def both_cores(tall, by_y, high, by_y_high, *events):
    own = jnp.stack((tall, by_y, high, by_y_high))
    return own, flip_dp(after(own, *events) if events else own)


def piece(pair, slot, y):
    return pair[slot % 2].at[2 * (slot // 2) + y]


def wide(values):
    return values.astype(F32)


class Spread:
    def __init__(self, grads):
        self.keep, self.send = grads

    def to_core(self, *events):
        self.got = flip_dp(after(self.send, *events))
        return self.got

    def here(self, y, h):
        return wide(self.keep[y, h]) + wide(self.got[y, h])

    def to_y(self, h, *events):
        by_y = flip_dp_y(after(self.here(1, h).astype(BF), *events))
        setattr(self, "by_y%d" % h, by_y)
        return by_y

    def to_high(self, flip_z, *events):
        send = (self.here(0, 1) + wide(self.by_y1)).astype(BF)
        self.high = flip_z(after(send, *events))
        return self.high

    def total(self, *events):
        value = self.here(0, 0) + wide(self.by_y0) + wide(self.high)
        return after(value.astype(BF), *events) if events else value.astype(BF)


def to_x(total, x, axis):
    size = total.shape[axis] // 2
    own = lax.dynamic_slice_in_dim(total, x * size, size, axis)
    return own, lax.dynamic_slice_in_dim(total, (1 - x) * size, size, axis)


def pair_up(own, by_x, x):
    return jnp.where(x == 0, jnp.stack((own, by_x)), jnp.stack((by_x, own)))


def unite(mine, theirs, q, axis):
    parts = []
    for at in range(2):
        parts += [jnp.where(q == 0, mine[at], theirs[at]), jnp.where(q == 0, theirs[at], mine[at])]
    return jnp.concatenate(parts, axis=axis).astype(F32)


def exchanged_sum(value, axes, count):
    tiles = jnp.broadcast_to(value, (count, 8, HD))
    tiles = lax.all_to_all(tiles, axes, split_axis=0, concat_axis=0, tiled=True)
    return jnp.sum(tiles[:, 0, 0]).reshape(1)


def local_norm(values):
    average = jnp.mean(values, axis=1, keepdims=True)
    square = jnp.mean(values * values, axis=1, keepdims=True)
    inverse = lax.rsqrt(square - average * average + EPSILON)
    return ((values - average) * inverse, inverse)


def local_norm_backward(gradient, normed, inverse):
    average = jnp.mean(gradient, axis=1, keepdims=True)
    crossed = jnp.mean(gradient * normed, axis=1, keepdims=True)
    return inverse * (gradient - average - normed * crossed)


def dot(left, right, a, b):
    return lax.dot_general(left, right, (((a,), (b,)), ((), ())), preferred_element_type=F32)


SMEM_SPEC = pl.BlockSpec(memory_space=pltpu.SMEM)
VMEM_SPEC = pl.BlockSpec(memory_space=pltpu.VMEM)


def shape(dims, kind):
    return jax.ShapeDtypeStruct(dims, kind)


def params(megabytes):
    return pltpu.CompilerParams(vmem_limit_bytes=megabytes * 2**20)


def cost(flops, moved, transcendentals=0):
    return pl.CostEstimate(
        flops=int(flops), bytes_accessed=int(moved), transcendentals=int(transcendentals)
    )


def y_half(y):
    return slice(y * HALF, (y + 1) * HALF)


def columns(index, width):
    return slice(index * width, (index + 1) * width)


FAR_SHAPES = [shape((PIECE // 2, D), BF)] * 2
SIDE_SHAPES = [
    shape((PIECE, D), BF),
    shape((PIECE // 2, D), F32),
    shape((PIECE // 2, D), F32),
]
OWN_SHAPES = [shape((PIECE, D), F32)]
NEAR_SHAPES = [
    shape((PIECE // 2, D), F32),
    shape((PIECE // 2, D), BF),
    shape((PIECE // 2, D), BF),
    shape((PIECE // 2, D), F32),
]
SUM_SHAPES = {"far": FAR_SHAPES, "sides": NEAR_SHAPES, "own": OWN_SHAPES}
SUM_BLOCKS = {"far": (3,), "sides": (1, 2), "own": (0,)}


def store_halves(part, value, outs):
    half = PIECE // 2
    for low in range(2):
        rows = value[low * half : (low + 1) * half]
        outs[low][:, y_half(part)] = rows.astype(outs[low].dtype)


def store_sum(kind, index, part, value, outs):
    if kind == "own":
        outs[0][:, y_half(part)] = value
    else:
        store_halves(part, value, outs[2 * index : 2 * index + 2])


ALL_SHAPES = [shape((PIECE, D), kind) for kind in (F32, BF, F32, BF)]


def store_any(a, part, value, outs):
    outs[a][:, y_half(part)] = value.astype(outs[a].dtype)


def qkv_kernel(place_ref, *refs):
    acts, refs = refs[:4], refs[4:]
    weights, refs = refs[:2], refs[2:]
    cos_ref, sin_ref, *refs = refs
    outs, weight_s = refs[:4], refs[4]
    for b in range(4):
        for y in range(2):
            for which in range(3):
                weight_s[y_half(y), columns(which * 4 + b, HD)] = piece(weights, b, y)[which]
    for a in range(4):
        rows = pl.ds(pl.multiple_of(place_ref[a] * PIECE, PIECE), PIECE)
        cos_block, sin_block = cos_ref[rows, :], sin_ref[rows, :]
        act = acts[a][...]
        projected = dot(act, weight_s[...], 1, 0)
        for which in range(3):
            for b in range(4):
                tile = projected[:, columns(which * 4 + b, HD)]
                if which < 2:
                    tile = tile * cos_block + pltpu.roll(tile, HD // 2, 1) * sin_block
                outs[b][which, a] = tile.astype(BF)


def run_qkv(place, acts, weights, cos_wide, sin_wide):
    return pl.pallas_call(
        qkv_kernel,
        out_shape=[shape((3, 4, PIECE, HD), BF)] * 4,
        in_specs=[SMEM_SPEC] + [VMEM_SPEC] * 8,
        out_specs=[VMEM_SPEC] * 4,
        scratch_shapes=[pltpu.VMEM((D, 12 * HD), BF)],
        compiler_params=params(40),
        cost_estimate=cost(2 * 4 * PIECE * D * 12 * HD, 20 * 2**20),
    )(place, *acts, *weights, cos_wide, sin_wide)


def out_kernel(*refs):
    mixed, refs = refs[:4], refs[4:]
    weights, refs = refs[:2], refs[2:]
    outs, weight_s = refs[:4], refs[4]
    for b in range(4):
        for y in range(2):
            weight_s[y_half(y), columns(b, HD)] = piece(weights, b, y)[3]
    for a in range(4):
        act = jnp.concatenate([mixed[b][a] for b in range(4)], axis=1)
        for y in range(2):
            store_any(a, y, dot(act, weight_s[y_half(y), :], 1, 1), outs)


def run_out(mixed, weights):
    outs = pl.pallas_call(
        out_kernel,
        out_shape=ALL_SHAPES,
        in_specs=[VMEM_SPEC] * 6,
        out_specs=[VMEM_SPEC] * 4,
        scratch_shapes=[pltpu.VMEM((D, 4 * HD), BF)],
        compiler_params=params(36),
        cost_estimate=cost(2 * 4 * PIECE * D * 4 * HD, 16 * 2**20),
    )(*mixed, *weights)
    return outs[3], outs[1], outs[2], outs[0]


def input_kernel(*refs):
    back, refs = refs[:4], refs[4:]
    weights, refs = refs[:2], refs[2:]
    outs, weight_s = refs[:4], refs[4]
    for b in range(4):
        for y in range(2):
            for which in range(3):
                weight_s[y_half(y), columns(which * 4 + b, HD)] = piece(weights, b, y)[which]
    for a in range(4):
        act = jnp.concatenate(
            [back[b][which, a] for which in range(3) for b in range(4)], axis=1
        )
        for y in range(2):
            store_any(a, y, dot(act, weight_s[y_half(y), :], 1, 1), outs)


def run_input(back, weights):
    outs = pl.pallas_call(
        input_kernel,
        out_shape=ALL_SHAPES,
        in_specs=[VMEM_SPEC] * 6,
        out_specs=[VMEM_SPEC] * 4,
        scratch_shapes=[pltpu.VMEM((D, 12 * HD), BF)],
        compiler_params=params(40),
        cost_estimate=cost(2 * 4 * PIECE * D * 12 * HD, 20 * 2**20),
    )(*back, *weights)
    return outs[3], outs[1], outs[2], outs[0]


def attended_grad_kernel(*refs):
    acts, refs = refs[:4], refs[4:]
    weights, refs = refs[:2], refs[2:]
    outs, weight_s = refs[:4], refs[4]
    for b in range(4):
        for y in range(2):
            weight_s[y_half(y), columns(b, HD)] = piece(weights, b, y)[3]
    for a in range(4):
        act = acts[a][...]
        value = dot(act, weight_s[...], 1, 0)
        for b in range(4):
            outs[b][a] = value[:, columns(b, HD)].astype(BF)


def run_attended_grad(acts, weights):
    return pl.pallas_call(
        attended_grad_kernel,
        out_shape=[shape((4, PIECE, HD), BF)] * 4,
        in_specs=[VMEM_SPEC] * 6,
        out_specs=[VMEM_SPEC] * 4,
        scratch_shapes=[pltpu.VMEM((D, 4 * HD), BF)],
        compiler_params=params(36),
        cost_estimate=cost(2 * 4 * PIECE * D * 4 * HD, 16 * 2**20),
    )(*acts, *weights)


CHUNK = 256


def up_kernel(count, *refs):
    acts, refs = refs[:count], refs[count:]
    gates, refs = refs[:2], refs[2:]
    ups, refs = refs[:2], refs[2:]
    gating_ref, upward_ref, units_ref = refs
    start = 0
    for act_ref in acts:
        size = act_ref.shape[0]
        rows = slice(start, start + size)
        start += size
        low, high = act_ref[:, y_half(0)], act_ref[:, y_half(1)]
        for b in range(4):
            gate = dot(low, piece(gates, b, 0)[...], 1, 0)
            gate += dot(high, piece(gates, b, 1)[...], 1, 0)
            up = dot(low, piece(ups, b, 0)[...], 1, 0) + dot(high, piece(ups, b, 1)[...], 1, 0)
            gating_ref[b, rows] = gate
            upward_ref[b, rows] = up
            units_ref[b, rows] = (gate * jax.nn.sigmoid(gate) * up).astype(BF)


def run_up(acts, gates, ups):
    rows = sum(act.shape[0] for act in acts)
    width = gates[0].shape[2]
    whole = lambda act: pl.BlockSpec(act.shape, lambda j: (0, 0))
    part = pl.BlockSpec((4, HALF, CHUNK), lambda j: (0, 0, j))
    out = pl.BlockSpec((4, rows, CHUNK), lambda j: (0, 0, j))
    return pl.pallas_call(
        lambda *refs: up_kernel(len(acts), *refs),
        grid=(width // CHUNK,),
        out_shape=[shape((4, rows, width), kind) for kind in (F32, F32, BF)],
        in_specs=[whole(act) for act in acts] + [part] * 4,
        out_specs=[out] * 3,
        compiler_params=params(48),
        cost_estimate=cost(2 * rows * D * 8 * width, 16 * 2**20, 4 * rows * width),
    )(*acts, *gates, *ups)


def down_kernel(kind, units_ref, *refs):
    weights, outs = refs[:2], refs[2:]
    for index in range(len(SUM_BLOCKS[kind])):
        rows = slice(index * PIECE, (index + 1) * PIECE)
        for y in range(2):
            value = dot(units_ref[0, rows], piece(weights, 0, y)[...], 1, 0)
            for b in range(1, 4):
                value += dot(units_ref[b, rows], piece(weights, b, y)[...], 1, 0)
            store_sum(kind, index, y, value, outs)


def run_down(kind, units, weights):
    rows, width = units.shape[1], units.shape[2]
    shapes = SUM_SHAPES[kind]
    return pl.pallas_call(
        lambda *refs: down_kernel(kind, *refs),
        out_shape=shapes,
        in_specs=[VMEM_SPEC] * 3,
        out_specs=[VMEM_SPEC] * len(shapes),
        compiler_params=params(36),
        cost_estimate=cost(2 * rows * D * 4 * width, 12 * 2**20),
    )(units, *weights)


def gated_kernel(count, *refs):
    acts, refs = refs[:count], refs[count:]
    gating_ref, upward_ref, *refs = refs
    weights, refs = refs[:2], refs[2:]
    gate_ref, up_ref = refs
    start = 0
    for act_ref in acts:
        size = act_ref.shape[0]
        rows = slice(start, start + size)
        start += size
        low, high = act_ref[:, y_half(0)], act_ref[:, y_half(1)]
        for b in range(4):
            grad = dot(low, piece(weights, b, 0)[...], 1, 1)
            grad += dot(high, piece(weights, b, 1)[...], 1, 1)
            gate = gating_ref[b, rows]
            sigmoid = jax.nn.sigmoid(gate)
            gate_ref[b, rows] = (
                grad * upward_ref[b, rows] * sigmoid * (1.0 + gate * (1.0 - sigmoid))
            ).astype(BF)
            up_ref[b, rows] = (grad * (gate * sigmoid)).astype(BF)


def run_gated(acts, gating, upward, weights):
    rows, width = gating.shape[1], gating.shape[2]
    return pl.pallas_call(
        lambda *refs: gated_kernel(len(acts), *refs),
        out_shape=[shape((4, rows, width), BF)] * 2,
        in_specs=[VMEM_SPEC] * (len(acts) + 4),
        out_specs=[VMEM_SPEC] * 2,
        compiler_params=params(44),
        cost_estimate=cost(2 * rows * D * 4 * width, 16 * 2**20, 4 * rows * width),
    )(*acts, gating, upward, *weights)


def normed_two_kernel(kind, gate_ref, up_ref, *refs):
    gates, refs = refs[:2], refs[2:]
    ups, refs = refs[:2], refs[2:]
    outs, total_s = refs[:-1], refs[-1]
    step, last = pl.program_id(0), pl.num_programs(0) - 1
    for y in range(2):
        value = dot(gate_ref[0], piece(gates, 0, y)[...], 1, 1)
        for b in range(4):
            if b > 0:
                value += dot(gate_ref[b], piece(gates, b, y)[...], 1, 1)
            value += dot(up_ref[b], piece(ups, b, y)[...], 1, 1)

        @pl.when(step == 0)
        def _():
            total_s[:, y_half(y)] = value

        @pl.when(step == last)
        def _():
            whole = total_s[:, y_half(y)] + value
            for index in range(len(SUM_BLOCKS[kind])):
                rows = slice(index * PIECE, (index + 1) * PIECE)
                store_sum(kind, index, y, whole[rows], outs)


def run_normed_two(kind, gate_low, up_low, gates, ups):
    rows, width = gate_low.shape[1], gate_low.shape[2]
    shapes = SUM_SHAPES[kind]
    low = pl.BlockSpec((4, rows, width // 2), lambda j: (0, 0, j))
    part = pl.BlockSpec((4, HALF, width // 2), lambda j: (0, 0, j))
    return pl.pallas_call(
        lambda *refs: normed_two_kernel(kind, *refs),
        grid=(2,),
        out_shape=shapes,
        in_specs=[low] * 2 + [part] * 4,
        out_specs=[pl.BlockSpec(s.shape, lambda j: (0, 0)) for s in shapes],
        scratch_shapes=[pltpu.VMEM((rows, D), F32)],
        compiler_params=params(48),
        cost_estimate=cost(2 * rows * D * 8 * width, 18 * 2**20),
    )(gate_low, up_low, *gates, *ups)


def wide_grad_kernel(*refs):
    acts, refs = refs[:5], refs[5:]
    lows, refs = refs[:3], refs[3:]
    outs, turned_s = refs[:2], refs[2]

    @pl.when(pl.program_id(1) == 0)
    def _():
        start = 0
        for act_ref in acts:
            size = act_ref.shape[0]
            turned_s[:, start : start + size] = act_ref[...].T
            start += size

    for d in range(2):
        total, start = None, 0
        for low_ref in lows:
            size = low_ref.shape[1]
            value = dot(turned_s[:, start : start + size], low_ref[d], 1, 0)
            total = value if total is None else total + value
            start += size
        outs[d][0, 0] = total.astype(BF)


def run_wide_grad(acts, lows):
    width = lows[0].shape[2]
    return pl.pallas_call(
        wide_grad_kernel,
        grid=(2, 2),
        out_shape=[shape((2, 2, HALF, width), BF)] * 2,
        in_specs=[pl.BlockSpec((act.shape[0], HALF), lambda y, h: (0, y)) for act in acts]
        + [pl.BlockSpec((2, low.shape[1], width), lambda y, h: (h, 0, 0)) for low in lows],
        out_specs=[pl.BlockSpec((1, 1, HALF, width), lambda y, h: (y, h, 0, 0))] * 2,
        scratch_shapes=[pltpu.VMEM((HALF, 4 * PIECE), BF)],
        compiler_params=params(36),
        cost_estimate=cost(2 * 4 * PIECE * D * 4 * width, 16 * 2**20),
    )(*acts, *lows)


def down_grad_kernel(*refs):
    units, refs = refs[:3], refs[3:]
    acts, refs = refs[:5], refs[5:]
    outs, turned_s = refs[:2], refs[2]

    @pl.when(pl.program_id(1) == 0)
    def _():
        start = 0
        for unit_ref in units:
            size = unit_ref.shape[1]
            for d in range(2):
                turned_s[d, :, start : start + size] = unit_ref[d].T
            start += size

    for d in range(2):
        total, start = None, 0
        for act_ref in acts:
            size = act_ref.shape[0]
            value = dot(turned_s[d, :, start : start + size], act_ref[...], 1, 0)
            total = value if total is None else total + value
            start += size
        outs[d][0, 0] = total.astype(BF)


def run_down_grad(units, acts):
    width = units[0].shape[2]
    return pl.pallas_call(
        down_grad_kernel,
        grid=(2, 2),
        out_shape=[shape((2, 2, width, HALF), BF)] * 2,
        in_specs=[pl.BlockSpec((2, unit.shape[1], width), lambda h, y: (h, 0, 0)) for unit in units]
        + [pl.BlockSpec((act.shape[0], HALF), lambda h, y: (0, y)) for act in acts],
        out_specs=[pl.BlockSpec((1, 1, width, HALF), lambda h, y: (y, h, 0, 0))] * 2,
        scratch_shapes=[pltpu.VMEM((2, width, 4 * PIECE), BF)],
        compiler_params=params(36),
        cost_estimate=cost(2 * 4 * PIECE * D * 4 * width, 16 * 2**20),
    )(*units, *acts)


def head_grad_kernel(kinds, *refs):
    acts, refs = refs[:4], refs[4:]
    messages, refs = refs[:4], refs[4:]
    passed, refs = (refs[:2], refs[2:]) if kinds > 1 else (None, refs)
    outs, turned_s, right_s = refs[:2], refs[2], refs[3]
    start = 0
    for act_ref in acts:
        size = act_ref.shape[0]
        turned_s[:, start : start + size] = act_ref[...].T
        start += size

    @pl.when(pl.program_id(0) == 0)
    def _():
        for which in range(kinds):
            for b in range(4):
                for a in range(4):
                    value = messages[b][which, a] if kinds > 1 else messages[b][a]
                    right_s[columns(a, PIECE), columns(which * 4 + b, HD)] = value

    for which in range(kinds):
        value = dot(turned_s[...], right_s[:, columns(which, 4 * HD)], 1, 0)
        for b, (d, h) in enumerate(SLOTS):
            outs[d][0, h, which] = value[:, columns(b, HD)].astype(BF)
    if passed:
        for d in range(2):
            outs[d][0, :, kinds] = passed[d][0, :, 0]


def run_head_grad(kinds, acts, messages, passed=()):
    whole = lambda dims: pl.BlockSpec(dims, lambda y: (0,) * len(dims))
    rows = lambda count: pl.BlockSpec((1, 2, count, HALF, HD), lambda y: (y, 0, 0, 0, 0))
    made = kinds + 1 if passed else kinds
    return pl.pallas_call(
        lambda *refs: head_grad_kernel(kinds, *refs),
        grid=(2,),
        out_shape=[shape((2, 2, made, HALF, HD), BF)] * 2,
        in_specs=[pl.BlockSpec((act.shape[0], HALF), lambda y: (0, y)) for act in acts]
        + [whole(message.shape) for message in messages]
        + [rows(1)] * len(passed),
        out_specs=[rows(made)] * 2,
        scratch_shapes=[
            pltpu.VMEM((HALF, 4 * PIECE), BF),
            pltpu.VMEM((4 * PIECE, kinds * 4 * HD), BF),
        ],
        compiler_params=params(44),
        cost_estimate=cost(2 * 4 * PIECE * D * kinds * 4 * HD, 12 * 2**20),
    )(*acts, *messages, *passed)


def allowed_pairs(starts, query0, key0, shape, query_axis):
    query = query0 + lax.broadcasted_iota(jnp.int32, shape, query_axis)
    key = key0 + lax.broadcasted_iota(jnp.int32, shape, 1 - query_axis)
    first = jnp.zeros(shape, jnp.int32)
    for s in range(CONT):
        first = jnp.where(query >= starts[s], starts[s], first)
    return (key <= query) & ((key < starts[0]) | (key >= first))


def block_bounds(starts, n):
    full = jnp.minimum(n, starts[0] // BLOCK)
    first = jnp.int32(0)
    for s in range(CONT):
        first = jnp.where(n * BLOCK >= starts[s], starts[s], first)
    return full, first


def block_used(starts, first, m):
    return (m * BLOCK < starts[0]) | ((m + 1) * BLOCK > first)


def attention_forward(place_ref, starts_ref, *refs):
    messages, refs = refs[:4], refs[4:]
    outs, refs = refs[:4], refs[4:]
    wide_ref, log_ref, q_s, k_s, v_s, score_s, acc_s, sum_s, max_s = refs
    scale = LOG2E / math.sqrt(HD)
    starts = [starts_ref[s] for s in range(CONT)]
    for b in range(4):
        for a in range(4):
            rows = pl.ds(pl.multiple_of(place_ref[4 * b + a] * PIECE, PIECE), PIECE)
            q_s[rows, :] = messages[b][0, a]
            k_s[rows, :] = messages[b][1, a]
            v_s[rows, :] = messages[b][2, a]

    def one_block(n, carry):
        rows = pl.ds(pl.multiple_of(n * BLOCK, BLOCK), BLOCK)
        full, first = block_bounds(starts, n)
        max_s[...] = jnp.full(max_s.shape, -1e30, F32)
        acc_s[...] = jnp.zeros(acc_s.shape, F32)
        sum_s[...] = jnp.zeros(sum_s.shape, F32)

        def note(scores, m):
            score_s[m] = scores
            top = max_s[...]
            for part in range(BLOCK // HD):
                top = jnp.maximum(top, scores[:, part * HD : (part + 1) * HD])
            max_s[...] = top

        def product(m):
            keys = pl.ds(pl.multiple_of(m * BLOCK, BLOCK), BLOCK)
            return dot(q_s[rows, :], k_s[keys, :], 1, 1)

        @pl.loop(0, full)
        def _(m):
            note(product(m), m)

        @pl.loop(full, n + 1)
        def _(m):
            @pl.when(block_used(starts, first, m))
            def _():
                allowed = allowed_pairs(starts, n * BLOCK, m * BLOCK, (BLOCK, BLOCK), 0)
                note(jnp.where(allowed, product(m), MASKED_SCORE), m)

        highest = jnp.max(max_s[...], axis=1, keepdims=True) * scale

        @pl.loop(0, n + 1)
        def _(m):
            @pl.when(block_used(starts, first, m))
            def _():
                keys = pl.ds(pl.multiple_of(m * BLOCK, BLOCK), BLOCK)
                exponent = jnp.exp2(score_s[m] * scale - highest)
                total = sum_s[...]
                for part in range(BLOCK // HD):
                    total = total + exponent[:, part * HD : (part + 1) * HD]
                sum_s[...] = total
                acc_s[...] += dot(exponent.astype(BF), v_s[keys, :], 1, 0)

        total = jnp.sum(sum_s[...], axis=1, keepdims=True)
        wide_ref[rows, :] = acc_s[...] / total
        log_total = jnp.broadcast_to(highest + jnp.log2(total), (BLOCK, HD))
        log_ref[n] = log_total.T[:8]
        return carry

    lax.fori_loop(0, k_s.shape[0] // BLOCK, one_block, 0)
    for b in range(4):
        for a in range(4):
            rows = pl.ds(pl.multiple_of(place_ref[4 * b + a] * PIECE, PIECE), PIECE)
            outs[b][a] = wide_ref[rows, :].astype(BF)


def attention_backward(place_ref, starts_ref, *refs):
    messages, refs = refs[:4], refs[4:]
    grads, refs = refs[:4], refs[4:]
    wide_ref, log_ref, cos_ref, sin_ref, *refs = refs
    outs, refs = refs[:4], refs[4:]
    q_s, k_s, v_s, g_s, dq_s, dk_s, dv_s = refs
    scale = LOG2E / math.sqrt(HD)
    starts = [starts_ref[s] for s in range(CONT)]
    for b in range(4):
        for a in range(4):
            rows = pl.ds(pl.multiple_of(place_ref[4 * b + a] * PIECE, PIECE), PIECE)
            q_s[rows, :] = messages[b][0, a]
            k_s[rows, :] = messages[b][1, a]
            v_s[rows, :] = messages[b][2, a]
            g_s[rows, :] = grads[b][a]
    dq_s[...] = jnp.zeros(dq_s.shape, F32)
    dk_s[...] = jnp.zeros(dk_s.shape, F32)
    dv_s[...] = jnp.zeros(dv_s.shape, F32)

    def one_block(n, carry):
        rows = pl.ds(pl.multiple_of(n * BLOCK, BLOCK), BLOCK)
        full, first = block_bounds(starts, n)
        crossed = g_s[rows, :].astype(F32) * wide_ref[rows, :]
        row_dot = jnp.sum(crossed.T, axis=0, keepdims=True)
        log_total = log_ref[n][:1]

        def step(m, masked):
            keys = pl.ds(pl.multiple_of(m * BLOCK, BLOCK), BLOCK)
            query, key = q_s[rows, :], k_s[keys, :]
            probability = jnp.exp2(dot(key, query, 1, 1) * scale - log_total)
            if masked:
                allowed = allowed_pairs(starts, n * BLOCK, m * BLOCK, (BLOCK, BLOCK), 1)
                probability = jnp.where(allowed, probability, 0.0)
            prob_grad = dot(v_s[keys, :], g_s[rows, :], 1, 1)
            score_grad = (probability * (prob_grad - row_dot)).astype(BF)
            dv_s[keys, :] += dot(probability.astype(BF), g_s[rows, :], 1, 0)
            dk_s[keys, :] += dot(score_grad, query, 1, 0)
            dq_s[rows, :] += dot(score_grad, key, 0, 0)

        @pl.loop(0, full)
        def _(m):
            step(m, False)

        @pl.loop(full, n + 1)
        def _(m):
            @pl.when(block_used(starts, first, m))
            def _():
                step(m, True)

        return carry

    lax.fori_loop(0, k_s.shape[0] // BLOCK, one_block, 0)
    for b in range(4):
        for a in range(4):
            rows = pl.ds(pl.multiple_of(place_ref[4 * b + a] * PIECE, PIECE), PIECE)
            for which, grad in ((0, dq_s), (1, dk_s)):
                value = grad[rows, :] * (1.0 / math.sqrt(HD))
                turned = value * cos_ref[rows, :] - pltpu.roll(value, HD // 2, 1) * sin_ref[rows, :]
                outs[b][which, a] = turned.astype(BF)
            outs[b][2, a] = dv_s[rows, :].astype(BF)


def run_forward(place, starts, messages):
    tokens = 16 * PIECE
    blocks = tokens // BLOCK
    out_shape = [jax.ShapeDtypeStruct((4, PIECE, HD), BF)] * 4
    out_shape += [
        jax.ShapeDtypeStruct((tokens, HD), F32),
        jax.ShapeDtypeStruct((blocks, 8, BLOCK), F32),
    ]
    return pl.pallas_call(
        attention_forward,
        out_shape=out_shape,
        in_specs=[SMEM_SPEC] * 2 + [VMEM_SPEC] * 4,
        out_specs=[VMEM_SPEC] * 6,
        scratch_shapes=[
            pltpu.VMEM((tokens, HD), BF),
            pltpu.VMEM((tokens, HD), BF),
            pltpu.VMEM((tokens, HD), BF),
            pltpu.VMEM((blocks, BLOCK, BLOCK), F32),
            pltpu.VMEM((BLOCK, HD), F32),
            pltpu.VMEM((BLOCK, HD), F32),
            pltpu.VMEM((BLOCK, HD), F32),
        ],
        compiler_params=pltpu.CompilerParams(vmem_limit_bytes=48 * 2**20),
        cost_estimate=pl.CostEstimate(
            flops=2 * tokens * tokens * HD * 2,
            bytes_accessed=8 * 2**20,
            transcendentals=tokens * tokens // 2,
        ),
    )(place, starts, *messages)


def run_backward(place, starts, messages, grads, wide, log_total, cosine, sine_table):
    tokens = 16 * PIECE
    return pl.pallas_call(
        attention_backward,
        out_shape=[jax.ShapeDtypeStruct((3, 4, PIECE, HD), BF)] * 4,
        in_specs=[SMEM_SPEC] * 2 + [VMEM_SPEC] * 12,
        out_specs=[VMEM_SPEC] * 4,
        scratch_shapes=[pltpu.VMEM((tokens, HD), BF)] * 4 + [pltpu.VMEM((tokens, HD), F32)] * 3,
        compiler_params=pltpu.CompilerParams(vmem_limit_bytes=52 * 2**20),
        cost_estimate=pl.CostEstimate(
            flops=5 * tokens * tokens * HD * 2,
            bytes_accessed=16 * 2**20,
            transcendentals=tokens * tokens // 2,
        ),
    )(place, starts, *messages, *grads, wide, log_total, cosine, sine_table)


def swap_slots(messages):
    return [messages[0], flip_y(messages[1]), flip_near(messages[2]), flip_y_near(messages[3])]


def to_tokens(values):
    return lax.all_to_all(values, "row", split_axis=0, concat_axis=1, tiled=True)


def to_width(values):
    return lax.all_to_all(values, "row", split_axis=1, concat_axis=0, tiled=True)


def square_shards(
    hidden_in,
    teacher,
    valid,
    segment_ids,
    query_weight,
    key_weight,
    value_weight,
    output_weight,
    gate_weight,
    up_weight,
    down_weight,
):
    row, col, dp = lax.axis_index("row"), lax.axis_index("col"), lax.axis_index("dp")
    x, y = row % 2, row // 2
    q = (dp + y) % 2
    own_piece = col * SIDE + row
    segment = segment_ids[0]
    group_tokens = segment.shape[0]
    home_tokens = group_tokens // (SIDE * SIDE)

    def swap_y(values):
        return jnp.where(
            y == 0, values, jnp.concatenate((values[:, HALF:], values[:, :HALF]), axis=1)
        )

    def cut(matrix, at, axis):
        size = matrix.shape[axis] // 4
        return lax.dynamic_slice_in_dim(matrix, (2 * at + q) * size, size, axis)

    def head_cut(at):
        parts = [cut(matrix, at, 1) for matrix in (query_weight, key_weight, value_weight)]
        return jnp.stack(parts + [cut(output_weight, at, 0).T])

    labels = jnp.arange(1, CONT + 1, dtype=jnp.int32)
    starts = jnp.sum((segment[None, :] < labels[:, None]).astype(jnp.int32), axis=1)
    codes = jnp.arange(16, dtype=jnp.int32)
    relative = (
        (codes & 1) + ((codes >> 1) & 1) * 8 + ((codes >> 2) & 1) * 2 + ((codes >> 3) & 1) * 4
    )
    pieces = relative ^ own_piece
    frequency = jnp.power(10000.0, jnp.arange(HD // 2, dtype=F32) * (-2.0 / HD))
    angles = positions(segment).astype(F32)[:, None] * jnp.tile(frequency, 2)[None, :]
    sign = jnp.where(jnp.arange(HD) < HD // 2, -1.0, 1.0)
    cos_wide, sin_wide = jnp.cos(angles), jnp.sin(angles) * sign[None, :]

    heads_x = flip_x(head_cut(1 - x))
    gates_x = flip_x(after(cut(gate_weight, 1 - x, 1), heads_x))
    rows_y = hidden_in.shape[0] // 2
    kept = lax.dynamic_slice_in_dim(hidden_in, y * rows_y, rows_y, 0)
    sent = lax.dynamic_slice_in_dim(hidden_in, (1 - y) * rows_y, rows_y, 0)
    piece_here = jnp.concatenate((kept, flip_y(sent)), axis=1)
    piece_far = flip_far(piece_here)
    piece_x = flip_x(after(piece_here, heads_x))
    piece_far_x = flip_x(piece_far)

    count = after(jnp.sum(valid.astype(F32)), piece_here)
    count = exchanged_sum(count, ("dp", "col"), 2 * SIDE)
    target = to_tokens(after(teacher, piece_x))

    def whole_rows(own, other):
        width = own.shape[1] // 2
        first, second = jnp.where(x == 0, own, other), jnp.where(x == 0, other, own)
        return jnp.concatenate(
            (first[:, :width], second[:, :width], first[:, width:], second[:, width:]), axis=1
        )

    def own_and_x(rows):
        half = rows.shape[0] // 2
        return [lax.dynamic_slice_in_dim(rows, at * half, half, 0) for at in (x, 1 - x)]

    hidden_rows = whole_rows(piece_here, piece_x)
    hidden = own_and_x(hidden_rows)[0].astype(F32)
    acts_here = own_and_x(local_norm(hidden_rows.astype(F32))[0].astype(BF))
    far_rows = whole_rows(piece_far, piece_far_x)
    acts_far = own_and_x(local_norm(far_rows.astype(F32))[0].astype(BF))
    normed_acts = acts_here + acts_far
    heads_tall = ordered(x, head_cut(x), heads_x, 1)
    heads_high = flip_near(heads_tall)
    heads_y = flip_dp_y(heads_tall)
    normed, inverse_one = local_norm(hidden)
    heads_y_high = flip_dp_y(after(heads_high, piece_x, count))
    gates_tall = ordered(x, cut(gate_weight, x, 1), gates_x, 0)
    gates_high = flip_far(after(gates_tall, heads_high, piece_far))
    cos_wide, sin_wide = after((cos_wide, sin_wide), heads_tall)
    heads = both_cores(
        heads_tall, heads_y, heads_high, after(heads_y_high, piece_far, target, cos_wide, sin_wide)
    )
    gates_y = flip_dp_y(after(gates_tall, piece_far_x))

    messages = run_qkv(pieces, normed_acts, heads, cos_wide, sin_wide)
    mlp_x = jnp.stack((cut(up_weight, 1 - x, 1), cut(down_weight, 1 - x, 0)))
    mlp_x = flip_x(after(mlp_x, messages[0]))
    messages = swap_slots(messages)
    messages = after(messages, mlp_x, gates_high, gates_y)

    ups_tall = ordered(x, cut(up_weight, x, 1), after(mlp_x[0], messages), 0)
    ups_high = flip_far(after(ups_tall, gates_high))
    gates_y_high = flip_dp_y(after(gates_high, messages))
    ups_y = flip_dp_y(ups_tall)
    *mixed, wide_mixed, log_total = run_forward(pieces, starts, messages)
    mixed = after(mixed, gates_y_high)
    downs_tall = ordered(x, cut(down_weight, x, 0), after(mlp_x[1], mixed), 1)
    mixed = swap_slots(mixed)
    mixed = after(mixed, ups_high, ups_y)
    gates = both_cores(gates_tall, gates_y, gates_high, gates_y_high, mixed)

    ups_y_high = flip_dp_y(after(ups_high, mixed))
    downs_y = flip_dp_y(after(downs_tall, ups_y_high))
    after_attention = hidden + square_reduce(*run_out(mixed, heads))
    after_attention = after(after_attention, ups_y_high, gates, downs_y)

    normed_two, inverse_two = local_norm(after_attention)
    ups = both_cores(ups_tall, ups_y, ups_high, ups_y_high, normed_two)
    low_two = normed_two.astype(BF)
    up_own = run_up([low_two], gates, ups)
    two_acts = near_gather(low_two, up_own)
    downs_high = flip_far(after(downs_tall, low_two))
    downs_y_high = flip_dp_y(after(downs_high, two_acts[1:3], up_own[2]))
    up_sides = run_up(after(two_acts[1:3], up_own[2]), gates, ups)
    up_far = run_up(after(two_acts[3:], up_sides[2], downs_y_high), gates, ups)
    downs = both_cores(downs_tall, downs_y, downs_high, downs_y_high, two_acts, up_sides[2])
    ups_out = [up_own, up_sides, up_far]
    units = [out[2] for out in ups_out]
    down_far = run_down("far", units[2], downs)
    down_sides = run_down("sides", after(units[1], down_far), downs)
    down_own = run_down("own", after(units[0], down_sides), downs)
    output = after_attention + near_reduce(down_far, down_sides, down_own[0])

    total_count = jnp.maximum(count, 1.0)
    counted_home = lax.dynamic_slice_in_dim(
        valid.astype(F32), row * home_tokens, home_tokens, 0
    )[:, None]
    differ = output - swap_y(target).astype(F32)
    local_loss = jnp.sum(counted_home * (differ * differ)) / D
    all_tokens = group_tokens * lax.axis_size("dp")
    out_grad = counted_home * differ * (all_tokens / total_count)

    low_out = out_grad.astype(BF)
    loss = exchanged_sum(after(local_loss, low_out), ("dp", "row", "col"), 2 * SIDE * SIDE)
    low_own = run_gated([low_out], up_own[0], up_own[1], downs)
    out_acts = near_gather(low_out, low_own)
    low_sides = run_gated(after(out_acts[1:3], low_own), up_sides[0], up_sides[1], downs)
    low_far = run_gated(after(out_acts[3:], low_sides, loss), up_far[0], up_far[1], downs)
    lows = [low_own, low_sides, low_far]
    two_far = run_normed_two("far", *low_far, gates, ups)
    two_sides = run_normed_two("sides", *after(low_sides, two_far), gates, ups)

    first = near_reduce_far(two_far)
    down_grads = Spread(run_down_grad(after(units, two_sides, first), out_acts))
    got = near_reduce_sides(first, two_sides)
    down_core = down_grads.to_core()
    two_own = run_normed_two("own", *after(low_own, down_grads.keep, got[1:3]), gates, ups)
    normed_two_grad = near_reduce_end(got, two_own[0])
    gate_pair = run_wide_grad(two_acts, after([low[0] for low in lows], two_own, down_core))
    gate_grads = Spread(gate_pair)
    down_y1 = down_grads.to_y(1)
    middle_grad = out_grad + local_norm_backward(normed_two_grad, normed_two, inverse_two)
    low_middle = middle_grad.astype(BF)
    layer_output = to_width(swap_y(after(output, low_middle).astype(BF)))
    gate_core = gate_grads.to_core(low_middle)
    down_y0 = down_grads.to_y(0, low_middle)
    up_pair = run_wide_grad(two_acts, after([low[1] for low in lows], gate_pair))
    up_grads = Spread(up_pair)
    middle_acts = square_gather(low_middle, gate_pair, down_y1)
    gate_y1 = gate_grads.to_y(1, down_y0, middle_acts[1:3])
    middle_acts = after(middle_acts, up_pair, down_y0, gate_y1, layer_output)
    grad_messages = run_attended_grad(middle_acts, heads)
    up_core = up_grads.to_core(grad_messages)
    gate_y0 = gate_grads.to_y(0, gate_y1)
    down_grads.to_high(flip_far, middle_acts[1:3])
    out_pair = run_head_grad(1, after(middle_acts, grad_messages), mixed)
    grad_messages = swap_slots(grad_messages)
    grad_messages = after(grad_messages, up_core, out_pair, gate_y0)
    up_y0 = up_grads.to_y(0, grad_messages)
    up_y1 = up_grads.to_y(1, grad_messages)
    back = run_backward(
        pieces, starts, messages, grad_messages, wide_mixed, log_total, cos_wide, sin_wide
    )
    back = after(back, down_grads.high, up_y1, up_y0)
    gate_grads.to_high(flip_far, back)
    own_down, send_down = to_x(down_grads.total(back), x, 1)
    down_x = flip_x(send_down)
    back = swap_slots(back)
    back = after(back, down_x, gate_grads.high)
    up_grads.to_high(flip_far, back)
    own_gate, send_gate = to_x(gate_grads.total(back), x, 0)
    gate_x = flip_x(send_gate)
    head_pair = run_head_grad(3, normed_acts, back, out_pair)
    head_grads = Spread(head_pair)
    head_core = head_grads.to_core()
    input_sums = run_input(after(back, head_pair), heads)
    input_sums = after(input_sums, head_core)
    head_y1 = head_grads.to_y(1)
    normed_grad = square_reduce(*input_sums, up_grads.high)
    head_y0 = head_grads.to_y(0, head_y1)
    head_grads.to_high(flip_near, head_y1)
    first_mine = jnp.stack((pair_up(own_gate, gate_x, x), pair_up(own_down, down_x, x)))
    first_theirs = flip_dp(after(first_mine, head_y1))
    normed_grad = after(normed_grad, head_y0, head_grads.high, first_theirs)
    input_gradient = middle_grad + local_norm_backward(normed_grad, normed, inverse_one)
    own_head, send_head = to_x(head_grads.total(normed_grad), x, 1)
    own_up, send_up = to_x(up_grads.total(normed_grad), x, 0)
    head_x = flip_x(send_head)
    last_mine = pair_up(own_up, flip_x(send_up), x)
    input_out = to_width(swap_y(input_gradient.astype(BF)))
    last_theirs = flip_dp(after(last_mine, input_out))
    head_mine = pair_up(own_head, head_x, x)
    head_theirs = flip_dp(head_mine)
    mean_loss = loss / total_count

    gate_grad = unite(first_mine[0], first_theirs[0], q, 1)
    down_grad = unite(first_mine[1], first_theirs[1], q, 0)
    up_grad = unite(last_mine, last_theirs, q, 1)
    head_grads = unite(head_mine, head_theirs, q, 2)
    return (
        layer_output,
        mean_loss,
        input_out.astype(F32),
        head_grads[0],
        head_grads[1],
        head_grads[2],
        head_grads[3].T,
        gate_grad,
        up_grad,
        down_grad,
    )


def solution(mesh):
    body = square_shards if fits_square(mesh) else shards
    in_specs = (
        P(("dp", "col"), "row"),
        P(("dp", "col"), "row"),
        P(("dp", "col")),
        P("dp", None),
        P("row", "col"),
        P("row", "col"),
        P("row", "col"),
        P("col", "row"),
        P("row", "col"),
        P("row", "col"),
        P("col", "row"),
    )
    out_specs = (
        P(("dp", "col"), "row"),
        P(),
        P(("dp", "col"), "row"),
        P("row", "col"),
        P("row", "col"),
        P("row", "col"),
        P("col", "row"),
        P("row", "col"),
        P("row", "col"),
        P("col", "row"),
    )
    return jax.shard_map(body, mesh=mesh, in_specs=in_specs, out_specs=out_specs, check_vma=False)
```

```python
import math

import jax
import jax.numpy as jnp
from jax import lax
from jax.experimental import pallas as pl
from jax.experimental.pallas import tpu as pltpu
from jax.sharding import PartitionSpec as P

D = 2048
HD = 128
CONT = 8


EPSILON = 1e-05
MASKED_SCORE = -1e30


def positions(segment):
    labels = jnp.arange(CONT + 1, dtype=jnp.int32)
    onehot = (segment[:, None] == labels[None, :]).astype(jnp.int32)
    counts = jnp.sum(onehot, axis=0)
    starts = jnp.cumsum(counts) - counts
    leading = jnp.sum(onehot * starts[None, :], axis=1)
    indices = jnp.arange(segment.shape[0], dtype=jnp.int32)
    return indices - leading + jnp.where(segment > 0, counts[0], 0)


def rotary(offsets):
    half_width = HD // 2
    frequency = jnp.power(10000.0, jnp.arange(half_width, dtype=jnp.float32) * (-2.0 / HD))
    angles = offsets.astype(jnp.float32)[:, None] * frequency[None, :]
    return (jnp.cos(angles), jnp.sin(angles))


def rotate(values, cosine, sine_table):
    half_width = values.shape[-1] // 2
    leading, trailing = (values[..., :half_width], values[..., half_width:])
    cos_wide = cosine[:, None, :]
    sin_wide = sine_table[:, None, :]
    return jnp.concatenate(
        (leading * cos_wide - trailing * sin_wide, trailing * cos_wide + leading * sin_wide),
        axis=-1,
    )


def unrotate(gradient, cosine, sine_table):
    half_width = gradient.shape[-1] // 2
    leading, trailing = (gradient[..., :half_width], gradient[..., half_width:])
    cos_wide = cosine[:, None, :]
    sin_wide = sine_table[:, None, :]
    return jnp.concatenate(
        (leading * cos_wide + trailing * sin_wide, trailing * cos_wide - leading * sin_wide),
        axis=-1,
    )


def feature_sums(left, right):
    return lax.psum((jnp.sum(left, axis=1), jnp.sum(right, axis=1)), "row")


def normalize(values):
    summed, squared = feature_sums(values, values * values)
    average = (summed / D)[:, None]
    inverse = lax.rsqrt(squared[:, None] / D - average * average + EPSILON)
    return ((values - average) * inverse, inverse)


def norm_backward(gradient, normed, inverse):
    summed, crossed = feature_sums(gradient, gradient * normed)
    return inverse * (gradient - summed[:, None] / D - normed * (crossed[:, None] / D))


def widen(values):
    return lax.all_gather(values, "col", axis=0, tiled=True)


def collect(values):
    return lax.all_gather(values, "row", axis=0, tiled=True)


def row_product(full, matrix, contract):
    return lax.psum_scatter(
        lax.dot_general(
            full, matrix, (((1,), (contract,)), ((), ())), preferred_element_type=jnp.float32
        ),
        "row",
        scatter_dimension=0,
        tiled=True,
    )


def column_product(full, matrix, contract):
    return lax.psum_scatter(
        lax.dot_general(
            full, matrix, (((1,), (contract,)), ((), ())), preferred_element_type=jnp.float32
        ),
        "col",
        scatter_dimension=0,
        tiled=True,
    )


def project_in(gathered, matrix):
    result = row_product(gathered, matrix, 0)
    return result


def project_back(gathered, matrix):
    result = row_product(gathered, matrix, 1)
    return result


def weight_product(left, right):
    return lax.dot_general(
        left, right, (((0,), (0,)), ((), ())), preferred_element_type=jnp.float32
    )


def block_layout(tok_rows):
    blocks = max(1, tok_rows // 512)
    return (blocks, tok_rows // blocks)


def score_maker(key_rows, segment, block):
    key_index = jnp.arange(key_rows.shape[0], dtype=jnp.int32)
    scale = 1.0 / math.sqrt(HD)

    def scores_for(query_block, offset):
        query_index = offset + jnp.arange(block, dtype=jnp.int32)
        query_segment = lax.dynamic_slice_in_dim(segment, offset, block, 0)
        allowed = (key_index[None, :] <= query_index[:, None]) & (
            (segment[None, :] == 0) | (segment[None, :] == query_segment[:, None])
        )
        scores = (
            jnp.einsum("qhd,khd->hqk", query_block, key_rows, preferred_element_type=jnp.float32)
            * scale
        )
        return jnp.where(allowed[None, :, :], scores, MASKED_SCORE)

    return scores_for


def attend(queries, key_rows, value_rows, segment, row_offset):
    tok_rows, heads_here = (queries.shape[0], queries.shape[1])
    blocks, block = block_layout(tok_rows)
    scores_for = score_maker(key_rows, segment, block)
    offsets = row_offset + jnp.arange(blocks, dtype=jnp.int32) * block

    def forward_block(inputs):
        query_block, offset = inputs
        scores = scores_for(query_block, offset)
        highest = jnp.max(scores, axis=-1, keepdims=True)
        exponent = jnp.exp(scores - highest)
        summed = jnp.sum(exponent, axis=-1, keepdims=True)
        probability = (exponent / summed).astype(jnp.bfloat16)
        mixed_block = jnp.einsum(
            "hqk,khd->qhd", probability, value_rows, preferred_element_type=jnp.float32
        )
        return (mixed_block, highest + jnp.log(summed))

    mixed_blocks, log_total = lax.map(
        forward_block, (queries.reshape(blocks, block, heads_here, HD), offsets)
    )
    return (mixed_blocks.reshape(tok_rows, heads_here * HD), log_total)


def attend_back(queries, key_rows, value_rows, segment, row_offset, log_total, attended_grad):
    tok_rows, heads_here = (queries.shape[0], queries.shape[1])
    blocks, block = block_layout(tok_rows)
    scores_for = score_maker(key_rows, segment, block)
    offsets = row_offset + jnp.arange(blocks, dtype=jnp.int32) * block
    scale = 1.0 / math.sqrt(HD)

    def backward_block(carry, inputs):
        key_sum, value_sum = carry
        query_block, grad_block, log_block, offset = inputs
        scores = scores_for(query_block, offset)
        probability = jnp.exp(scores - log_block)
        rounded = probability.astype(jnp.bfloat16)
        prob_grad = jnp.einsum(
            "qhd,khd->hqk", grad_block, value_rows, preferred_element_type=jnp.float32
        )
        row_dot = jnp.sum(probability * prob_grad, axis=-1, keepdims=True)
        score_grad = (probability * (prob_grad - row_dot)).astype(jnp.bfloat16)
        query_grad = (
            jnp.einsum("hqk,khd->qhd", score_grad, key_rows, preferred_element_type=jnp.float32)
            * scale
        )
        key_sum = (
            key_sum
            + jnp.einsum(
                "hqk,qhd->khd", score_grad, query_block, preferred_element_type=jnp.float32
            )
            * scale
        )
        value_sum = value_sum + jnp.einsum(
            "hqk,qhd->khd", rounded, grad_block, preferred_element_type=jnp.float32
        )
        return ((key_sum, value_sum), query_grad)

    empty = jnp.zeros(key_rows.shape, jnp.float32)
    inputs = (
        queries.reshape(blocks, block, heads_here, HD),
        attended_grad.reshape(blocks, block, heads_here, HD),
        log_total,
        offsets,
    )
    (key_sum, value_sum), query_grads = lax.scan(backward_block, (empty, empty), inputs)
    return (query_grads.reshape(tok_rows, heads_here, HD), key_sum, value_sum)


def shards(
    hidden_in,
    teacher,
    valid,
    segment_ids,
    query_weight,
    key_weight,
    value_weight,
    output_weight,
    gate_weight,
    up_weight,
    down_weight,
):
    row_devices = lax.axis_size("row")
    col_devices = lax.axis_size("col")
    tok_cols = hidden_in.shape[0]
    group_tokens = tok_cols * col_devices
    tok_rows = group_tokens // row_devices
    query_width = query_weight.shape[1]
    heads_here = query_width // HD
    unit_width = gate_weight.shape[1]
    segment = segment_ids[0]
    row_offset = lax.axis_index("row") * tok_rows
    cosine_all, sine_all = rotary(positions(segment))
    cosine = lax.dynamic_slice_in_dim(cosine_all, row_offset, tok_rows, 0)
    sine_table = lax.dynamic_slice_in_dim(sine_all, row_offset, tok_rows, 0)
    counted = valid.astype(jnp.float32)
    total_count = jnp.maximum(lax.psum(jnp.sum(counted), ("dp", "col")), 1.0)
    hidden = hidden_in.astype(jnp.float32)
    normed, inverse_one = normalize(hidden)
    normed_wide = widen(normed.astype(jnp.bfloat16))
    attn_weights = jnp.concatenate((query_weight, key_weight, value_weight), axis=1)
    projected = project_in(normed_wide, attn_weights)
    queries = rotate(
        projected[:, :query_width].reshape(tok_rows, heads_here, HD), cosine, sine_table
    ).astype(jnp.bfloat16)
    key_local = rotate(
        projected[:, query_width : 2 * query_width].reshape(tok_rows, heads_here, HD),
        cosine,
        sine_table,
    )
    key_local = key_local.reshape(tok_rows, query_width).astype(jnp.bfloat16)
    value_local = projected[:, 2 * query_width :].astype(jnp.bfloat16)
    key_flat, value_flat = (
        lax.all_gather(key_local, "row", axis=0, tiled=True),
        lax.all_gather(value_local, "row", axis=0, tiled=True),
    )
    key_rows = key_flat.reshape(group_tokens, heads_here, HD)
    value_rows = value_flat.reshape(group_tokens, heads_here, HD)
    attended, log_total = attend(queries, key_rows, value_rows, segment, row_offset)
    attended_wide = collect(attended.astype(jnp.bfloat16))
    after_attention = hidden + column_product(attended_wide, output_weight, 0)
    normed_two, inverse_two = normalize(after_attention)
    normed_two_wide = widen(normed_two.astype(jnp.bfloat16))
    mlp_weights = jnp.concatenate((gate_weight, up_weight), axis=1)
    gated = project_in(normed_two_wide, mlp_weights)
    gating = gated[:, :unit_width]
    upward = gated[:, unit_width:]
    sigmoid = jax.nn.sigmoid(gating)
    activated = gating * sigmoid
    units_wide = collect((activated * upward).astype(jnp.bfloat16))
    output = after_attention + column_product(units_wide, down_weight, 0)
    differ = output - teacher.astype(jnp.float32)
    local_loss = jnp.sum(counted[:, None] * (differ * differ)) / D
    all_tokens = group_tokens * lax.axis_size("dp")
    out_grad = counted[:, None] * differ * (all_tokens / total_count)
    out_wide = widen(out_grad.astype(jnp.bfloat16))
    units_grad = project_back(out_wide, down_weight)
    down_grad = weight_product(units_wide, out_wide)
    gating_grad = units_grad * upward * sigmoid * (1.0 + gating * (1.0 - sigmoid))
    upward_grad = units_grad * activated
    gated_wide = collect(jnp.concatenate((gating_grad, upward_grad), axis=1).astype(jnp.bfloat16))
    mlp_grads = weight_product(normed_two_wide, gated_wide)
    normed_two_grad = column_product(gated_wide, mlp_weights, 1)
    middle_grad = out_grad + norm_backward(normed_two_grad, normed_two, inverse_two)
    middle_wide = widen(middle_grad.astype(jnp.bfloat16))
    attended_grad = project_back(middle_wide, output_weight).astype(jnp.bfloat16)
    output_grad_sum = weight_product(attended_wide, middle_wide)
    query_grad, key_sum, value_sum = attend_back(
        queries, key_rows, value_rows, segment, row_offset, log_total, attended_grad
    )
    key_grad, value_grad = (
        lax.psum_scatter(
            key_sum.reshape(group_tokens, query_width), "row", scatter_dimension=0, tiled=True
        ),
        lax.psum_scatter(
            value_sum.reshape(group_tokens, query_width), "row", scatter_dimension=0, tiled=True
        ),
    )
    query_pre = unrotate(query_grad, cosine, sine_table).reshape(tok_rows, query_width)
    key_pre = unrotate(key_grad.reshape(tok_rows, heads_here, HD), cosine, sine_table).reshape(
        tok_rows, query_width
    )
    projected_wide = collect(
        jnp.concatenate((query_pre, key_pre, value_grad), axis=1).astype(jnp.bfloat16)
    )
    attn_grads = weight_product(normed_wide, projected_wide)
    normed_grad = column_product(projected_wide, attn_weights, 1)
    input_gradient = middle_grad + norm_backward(normed_grad, normed, inverse_one)
    summed_grads = (
        lax.psum(attn_grads[:, :query_width].astype(jnp.bfloat16), "dp").astype(jnp.float32),
        lax.psum(attn_grads[:, query_width : 2 * query_width].astype(jnp.bfloat16), "dp").astype(
            jnp.float32
        ),
        lax.psum(attn_grads[:, 2 * query_width :].astype(jnp.bfloat16), "dp").astype(jnp.float32),
        lax.psum(output_grad_sum.astype(jnp.bfloat16), "dp").astype(jnp.float32),
        lax.psum(mlp_grads[:, :unit_width].astype(jnp.bfloat16), "dp").astype(jnp.float32),
        lax.psum(mlp_grads[:, unit_width:].astype(jnp.bfloat16), "dp").astype(jnp.float32),
        lax.psum(down_grad.astype(jnp.bfloat16), "dp").astype(jnp.float32),
    )
    mean_loss = lax.psum(local_loss, ("dp", "row", "col")) / total_count
    return (
        output.astype(jnp.bfloat16),
        mean_loss.reshape(1),
        input_gradient,
        summed_grads[0],
        summed_grads[1],
        summed_grads[2],
        summed_grads[3],
        summed_grads[4],
        summed_grads[5],
        summed_grads[6],
    )


BF = jnp.bfloat16
F32 = jnp.float32
LOG2E = 1.4426950408889634
SIDE = 4
HALF = D // 2
PIECE = 256
BLOCK = 512
SLOTS = [(d, h) for h in range(2) for d in range(2)]


def fits_square(mesh):
    return mesh.shape["dp"] == 2 and mesh.shape["row"] == SIDE and mesh.shape["col"] == SIDE


def flip(values, axis, bit):
    return lax.ppermute(values, axis, [(i, i ^ bit) for i in range(SIDE)])


def flip_x(values):
    return flip(values, "row", 1)


def flip_y(values):
    return flip(values, "row", 2)


def flip_far(values):
    return flip(values, "col", 2)


def flip_near(values):
    return flip(values, "col", 1)


def flip_y_near(values):
    pairs = [
        (r * SIDE + c, (r ^ 2) * SIDE + (c ^ 1)) for r in range(SIDE) for c in range(SIDE)
    ]
    return lax.ppermute(values, ("row", "col"), pairs)


def flip_z(values):
    return flip(values, "col", 3)


def flip_dp(values):
    return lax.ppermute(values, "dp", [(0, 1), (1, 0)])


def flip_dp_y(values):
    pairs = [(g * SIDE + r, (1 - g) * SIDE + (r ^ 2)) for g in range(2) for r in range(SIDE)]
    return lax.ppermute(values, ("dp", "row"), pairs)


def near_gather(block, *events):
    half = block.shape[0] // 2
    by_x, by_z = flip_x(block), flip_near(block)
    next_x, next_z = after((by_x, by_z), *events)
    return [block, by_x, by_z, flip_near(next_x[:half]), flip_x(next_z[half:])]


def near_reduce(far, sides, own):
    first = near_reduce_far(far)
    return near_reduce_end(near_reduce_sides(first, sides), own)


def near_reduce_far(far):
    return flip_near(far[0]), flip_x(far[1])


def near_reduce_sides(first, sides):
    far_top, far_bottom = first
    x_top, x_bottom, z_top, z_bottom = sides
    return (
        flip_x((x_top + wide(far_top)).astype(BF)),
        flip_x(x_bottom),
        flip_near(z_top),
        flip_near((z_bottom + wide(far_bottom)).astype(BF)),
    )


def near_reduce_end(got, own):
    x_top, x_bottom, z_top, z_bottom = got
    half = x_top.shape[0]
    top = own[:half] + wide(x_top) + wide(z_top)
    bottom = own[half:] + wide(x_bottom) + wide(z_bottom)
    return jnp.concatenate((top, bottom), axis=0)


def square_gather(block, *events):
    by_z, by_x = flip_far(block), flip_x(block)
    return [block, by_x, by_z, flip_x(after(by_z, *events) if events else by_z)]


def square_reduce(far, by_x, by_z, own, *events):
    got_far = flip_x(far)
    got_far = after(got_far, *events) if events else got_far
    got_x = flip_x(after(by_x, got_far))
    got_z = flip_far((by_z + wide(got_far)).astype(BF))
    return own + wide(got_x) + wide(got_z)


def ordered(flag, own, other, axis):
    return jnp.where(
        flag == 0,
        jnp.concatenate((own, other), axis=axis),
        jnp.concatenate((other, own), axis=axis),
    )


def after(values, *events):
    return lax.optimization_barrier((values, events))[0]


def both_cores(tall, by_y, high, by_y_high, *events):
    own = jnp.stack((tall, by_y, high, by_y_high))
    return own, flip_dp(after(own, *events) if events else own)


def piece(pair, slot, y):
    return pair[slot % 2].at[2 * (slot // 2) + y]


def wide(values):
    return values.astype(F32)


class Spread:
    def __init__(self, grads):
        self.keep, self.send = grads

    def to_core(self, *events):
        self.got = flip_dp(after(self.send, *events))
        return self.got

    def here(self, y, h):
        return wide(self.keep[y, h]) + wide(self.got[y, h])

    def to_y(self, h, *events):
        by_y = flip_dp_y(after(self.here(1, h).astype(BF), *events))
        setattr(self, "by_y%d" % h, by_y)
        return by_y

    def to_high(self, flip_z, *events):
        send = (self.here(0, 1) + wide(self.by_y1)).astype(BF)
        self.high = flip_z(after(send, *events))
        return self.high

    def total(self, *events):
        value = self.here(0, 0) + wide(self.by_y0) + wide(self.high)
        return after(value.astype(BF), *events) if events else value.astype(BF)


def to_x(total, x, axis):
    size = total.shape[axis] // 2
    own = lax.dynamic_slice_in_dim(total, x * size, size, axis)
    return own, lax.dynamic_slice_in_dim(total, (1 - x) * size, size, axis)


def pair_up(own, by_x, x):
    return jnp.where(x == 0, jnp.stack((own, by_x)), jnp.stack((by_x, own)))


def unite(mine, theirs, q, axis):
    parts = []
    for at in range(2):
        parts += [jnp.where(q == 0, mine[at], theirs[at]), jnp.where(q == 0, theirs[at], mine[at])]
    return jnp.concatenate(parts, axis=axis).astype(F32)


def exchanged_sum(value, axes, count):
    tiles = jnp.broadcast_to(value, (count, 8, HD))
    tiles = lax.all_to_all(tiles, axes, split_axis=0, concat_axis=0, tiled=True)
    return jnp.sum(tiles[:, 0, 0]).reshape(1)


def local_norm(values):
    average = jnp.mean(values, axis=1, keepdims=True)
    square = jnp.mean(values * values, axis=1, keepdims=True)
    inverse = lax.rsqrt(square - average * average + EPSILON)
    return ((values - average) * inverse, inverse)


def local_norm_backward(gradient, normed, inverse):
    average = jnp.mean(gradient, axis=1, keepdims=True)
    crossed = jnp.mean(gradient * normed, axis=1, keepdims=True)
    return inverse * (gradient - average - normed * crossed)


def dot(left, right, a, b):
    return lax.dot_general(left, right, (((a,), (b,)), ((), ())), preferred_element_type=F32)


SMEM_SPEC = pl.BlockSpec(memory_space=pltpu.SMEM)
VMEM_SPEC = pl.BlockSpec(memory_space=pltpu.VMEM)


def shape(dims, kind):
    return jax.ShapeDtypeStruct(dims, kind)


def params(megabytes):
    return pltpu.CompilerParams(vmem_limit_bytes=megabytes * 2**20)


def cost(flops, moved, transcendentals=0):
    return pl.CostEstimate(
        flops=int(flops), bytes_accessed=int(moved), transcendentals=int(transcendentals)
    )


def y_half(y):
    return slice(y * HALF, (y + 1) * HALF)


def columns(index, width):
    return slice(index * width, (index + 1) * width)


FAR_SHAPES = [shape((PIECE // 2, D), BF)] * 2
SIDE_SHAPES = [
    shape((PIECE, D), BF),
    shape((PIECE // 2, D), F32),
    shape((PIECE // 2, D), F32),
]
OWN_SHAPES = [shape((PIECE, D), F32)]
NEAR_SHAPES = [
    shape((PIECE // 2, D), F32),
    shape((PIECE // 2, D), BF),
    shape((PIECE // 2, D), BF),
    shape((PIECE // 2, D), F32),
]
SUM_SHAPES = {"far": FAR_SHAPES, "sides": NEAR_SHAPES, "own": OWN_SHAPES}
SUM_BLOCKS = {"far": (3,), "sides": (1, 2), "own": (0,)}


def store_halves(part, value, outs):
    half = PIECE // 2
    for low in range(2):
        rows = value[low * half : (low + 1) * half]
        outs[low][:, y_half(part)] = rows.astype(outs[low].dtype)


def store_sum(kind, index, part, value, outs):
    if kind == "own":
        outs[0][:, y_half(part)] = value
    else:
        store_halves(part, value, outs[2 * index : 2 * index + 2])


ALL_SHAPES = [shape((PIECE, D), kind) for kind in (F32, BF, F32, BF)]


def store_any(a, part, value, outs):
    outs[a][:, y_half(part)] = value.astype(outs[a].dtype)


def qkv_kernel(place_ref, *refs):
    acts, refs = refs[:4], refs[4:]
    weights, refs = refs[:2], refs[2:]
    cos_ref, sin_ref, *refs = refs
    outs, weight_s = refs[:4], refs[4]
    for b in range(4):
        for y in range(2):
            for which in range(3):
                weight_s[y_half(y), columns(which * 4 + b, HD)] = piece(weights, b, y)[which]
    for a in range(4):
        rows = pl.ds(pl.multiple_of(place_ref[a] * PIECE, PIECE), PIECE)
        cos_block, sin_block = cos_ref[rows, :], sin_ref[rows, :]
        act = acts[a][...]
        projected = dot(act, weight_s[...], 1, 0)
        for which in range(3):
            for b in range(4):
                tile = projected[:, columns(which * 4 + b, HD)]
                if which < 2:
                    tile = tile * cos_block + pltpu.roll(tile, HD // 2, 1) * sin_block
                outs[b][which, a] = tile.astype(BF)


def run_qkv(place, acts, weights, cos_wide, sin_wide):
    return pl.pallas_call(
        qkv_kernel,
        out_shape=[shape((3, 4, PIECE, HD), BF)] * 4,
        in_specs=[SMEM_SPEC] + [VMEM_SPEC] * 8,
        out_specs=[VMEM_SPEC] * 4,
        scratch_shapes=[pltpu.VMEM((D, 12 * HD), BF)],
        compiler_params=params(40),
        cost_estimate=cost(2 * 4 * PIECE * D * 12 * HD, 20 * 2**20),
    )(place, *acts, *weights, cos_wide, sin_wide)


def out_kernel(*refs):
    mixed, refs = refs[:4], refs[4:]
    weights, refs = refs[:2], refs[2:]
    outs, weight_s = refs[:4], refs[4]
    for b in range(4):
        for y in range(2):
            weight_s[y_half(y), columns(b, HD)] = piece(weights, b, y)[3]
    for a in range(4):
        act = jnp.concatenate([mixed[b][a] for b in range(4)], axis=1)
        for y in range(2):
            store_any(a, y, dot(act, weight_s[y_half(y), :], 1, 1), outs)


def run_out(mixed, weights):
    outs = pl.pallas_call(
        out_kernel,
        out_shape=ALL_SHAPES,
        in_specs=[VMEM_SPEC] * 6,
        out_specs=[VMEM_SPEC] * 4,
        scratch_shapes=[pltpu.VMEM((D, 4 * HD), BF)],
        compiler_params=params(36),
        cost_estimate=cost(2 * 4 * PIECE * D * 4 * HD, 16 * 2**20),
    )(*mixed, *weights)
    return outs[3], outs[1], outs[2], outs[0]


def input_kernel(*refs):
    back, refs = refs[:4], refs[4:]
    weights, refs = refs[:2], refs[2:]
    outs, weight_s = refs[:4], refs[4]
    for b in range(4):
        for y in range(2):
            for which in range(3):
                weight_s[y_half(y), columns(which * 4 + b, HD)] = piece(weights, b, y)[which]
    for a in range(4):
        act = jnp.concatenate(
            [back[b][which, a] for which in range(3) for b in range(4)], axis=1
        )
        for y in range(2):
            store_any(a, y, dot(act, weight_s[y_half(y), :], 1, 1), outs)


def run_input(back, weights):
    outs = pl.pallas_call(
        input_kernel,
        out_shape=ALL_SHAPES,
        in_specs=[VMEM_SPEC] * 6,
        out_specs=[VMEM_SPEC] * 4,
        scratch_shapes=[pltpu.VMEM((D, 12 * HD), BF)],
        compiler_params=params(40),
        cost_estimate=cost(2 * 4 * PIECE * D * 12 * HD, 20 * 2**20),
    )(*back, *weights)
    return outs[3], outs[1], outs[2], outs[0]


def attended_grad_kernel(*refs):
    acts, refs = refs[:4], refs[4:]
    weights, refs = refs[:2], refs[2:]
    outs, weight_s = refs[:4], refs[4]
    for b in range(4):
        for y in range(2):
            weight_s[y_half(y), columns(b, HD)] = piece(weights, b, y)[3]
    for a in range(4):
        act = acts[a][...]
        value = dot(act, weight_s[...], 1, 0)
        for b in range(4):
            outs[b][a] = value[:, columns(b, HD)].astype(BF)


def run_attended_grad(acts, weights):
    return pl.pallas_call(
        attended_grad_kernel,
        out_shape=[shape((4, PIECE, HD), BF)] * 4,
        in_specs=[VMEM_SPEC] * 6,
        out_specs=[VMEM_SPEC] * 4,
        scratch_shapes=[pltpu.VMEM((D, 4 * HD), BF)],
        compiler_params=params(36),
        cost_estimate=cost(2 * 4 * PIECE * D * 4 * HD, 16 * 2**20),
    )(*acts, *weights)


CHUNK = 256


def up_kernel(count, *refs):
    acts, refs = refs[:count], refs[count:]
    gates, refs = refs[:2], refs[2:]
    ups, refs = refs[:2], refs[2:]
    gating_ref, upward_ref, units_ref = refs
    start = 0
    for act_ref in acts:
        size = act_ref.shape[0]
        rows = slice(start, start + size)
        start += size
        low, high = act_ref[:, y_half(0)], act_ref[:, y_half(1)]
        for b in range(4):
            gate = dot(low, piece(gates, b, 0)[...], 1, 0)
            gate += dot(high, piece(gates, b, 1)[...], 1, 0)
            up = dot(low, piece(ups, b, 0)[...], 1, 0) + dot(high, piece(ups, b, 1)[...], 1, 0)
            gating_ref[b, rows] = gate
            upward_ref[b, rows] = up
            units_ref[b, rows] = (gate * jax.nn.sigmoid(gate) * up).astype(BF)


def run_up(acts, gates, ups):
    rows = sum(act.shape[0] for act in acts)
    width = gates[0].shape[2]
    whole = lambda act: pl.BlockSpec(act.shape, lambda j: (0, 0))
    part = pl.BlockSpec((4, HALF, CHUNK), lambda j: (0, 0, j))
    out = pl.BlockSpec((4, rows, CHUNK), lambda j: (0, 0, j))
    return pl.pallas_call(
        lambda *refs: up_kernel(len(acts), *refs),
        grid=(width // CHUNK,),
        out_shape=[shape((4, rows, width), kind) for kind in (F32, F32, BF)],
        in_specs=[whole(act) for act in acts] + [part] * 4,
        out_specs=[out] * 3,
        compiler_params=params(48),
        cost_estimate=cost(2 * rows * D * 8 * width, 16 * 2**20, 4 * rows * width),
    )(*acts, *gates, *ups)


def down_kernel(kind, units_ref, *refs):
    weights, outs = refs[:2], refs[2:]
    for index in range(len(SUM_BLOCKS[kind])):
        rows = slice(index * PIECE, (index + 1) * PIECE)
        for y in range(2):
            value = dot(units_ref[0, rows], piece(weights, 0, y)[...], 1, 0)
            for b in range(1, 4):
                value += dot(units_ref[b, rows], piece(weights, b, y)[...], 1, 0)
            store_sum(kind, index, y, value, outs)


def run_down(kind, units, weights):
    rows, width = units.shape[1], units.shape[2]
    shapes = SUM_SHAPES[kind]
    return pl.pallas_call(
        lambda *refs: down_kernel(kind, *refs),
        out_shape=shapes,
        in_specs=[VMEM_SPEC] * 3,
        out_specs=[VMEM_SPEC] * len(shapes),
        compiler_params=params(36),
        cost_estimate=cost(2 * rows * D * 4 * width, 12 * 2**20),
    )(units, *weights)


def gated_kernel(count, *refs):
    acts, refs = refs[:count], refs[count:]
    gating_ref, upward_ref, *refs = refs
    weights, refs = refs[:2], refs[2:]
    gate_ref, up_ref = refs
    start = 0
    for act_ref in acts:
        size = act_ref.shape[0]
        rows = slice(start, start + size)
        start += size
        low, high = act_ref[:, y_half(0)], act_ref[:, y_half(1)]
        for b in range(4):
            grad = dot(low, piece(weights, b, 0)[...], 1, 1)
            grad += dot(high, piece(weights, b, 1)[...], 1, 1)
            gate = gating_ref[b, rows]
            sigmoid = jax.nn.sigmoid(gate)
            gate_ref[b, rows] = (
                grad * upward_ref[b, rows] * sigmoid * (1.0 + gate * (1.0 - sigmoid))
            ).astype(BF)
            up_ref[b, rows] = (grad * (gate * sigmoid)).astype(BF)


def run_gated(acts, gating, upward, weights):
    rows, width = gating.shape[1], gating.shape[2]
    return pl.pallas_call(
        lambda *refs: gated_kernel(len(acts), *refs),
        out_shape=[shape((4, rows, width), BF)] * 2,
        in_specs=[VMEM_SPEC] * (len(acts) + 4),
        out_specs=[VMEM_SPEC] * 2,
        compiler_params=params(44),
        cost_estimate=cost(2 * rows * D * 4 * width, 16 * 2**20, 4 * rows * width),
    )(*acts, gating, upward, *weights)


def normed_two_kernel(kind, gate_ref, up_ref, *refs):
    gates, refs = refs[:2], refs[2:]
    ups, refs = refs[:2], refs[2:]
    outs, total_s = refs[:-1], refs[-1]
    step, last = pl.program_id(0), pl.num_programs(0) - 1
    for y in range(2):
        value = dot(gate_ref[0], piece(gates, 0, y)[...], 1, 1)
        for b in range(4):
            if b > 0:
                value += dot(gate_ref[b], piece(gates, b, y)[...], 1, 1)
            value += dot(up_ref[b], piece(ups, b, y)[...], 1, 1)

        @pl.when(step == 0)
        def _():
            total_s[:, y_half(y)] = value

        @pl.when(step == last)
        def _():
            whole = total_s[:, y_half(y)] + value
            for index in range(len(SUM_BLOCKS[kind])):
                rows = slice(index * PIECE, (index + 1) * PIECE)
                store_sum(kind, index, y, whole[rows], outs)


def run_normed_two(kind, gate_low, up_low, gates, ups):
    rows, width = gate_low.shape[1], gate_low.shape[2]
    shapes = SUM_SHAPES[kind]
    low = pl.BlockSpec((4, rows, width // 2), lambda j: (0, 0, j))
    part = pl.BlockSpec((4, HALF, width // 2), lambda j: (0, 0, j))
    return pl.pallas_call(
        lambda *refs: normed_two_kernel(kind, *refs),
        grid=(2,),
        out_shape=shapes,
        in_specs=[low] * 2 + [part] * 4,
        out_specs=[pl.BlockSpec(s.shape, lambda j: (0, 0)) for s in shapes],
        scratch_shapes=[pltpu.VMEM((rows, D), F32)],
        compiler_params=params(48),
        cost_estimate=cost(2 * rows * D * 8 * width, 18 * 2**20),
    )(gate_low, up_low, *gates, *ups)


def wide_grad_kernel(*refs):
    acts, refs = refs[:5], refs[5:]
    lows, refs = refs[:3], refs[3:]
    outs, turned_s = refs[:2], refs[2]

    @pl.when(pl.program_id(1) == 0)
    def _():
        start = 0
        for act_ref in acts:
            size = act_ref.shape[0]
            turned_s[:, start : start + size] = act_ref[...].T
            start += size

    for d in range(2):
        total, start = None, 0
        for low_ref in lows:
            size = low_ref.shape[1]
            value = dot(turned_s[:, start : start + size], low_ref[d], 1, 0)
            total = value if total is None else total + value
            start += size
        outs[d][0, 0] = total.astype(BF)


def run_wide_grad(acts, lows):
    width = lows[0].shape[2]
    return pl.pallas_call(
        wide_grad_kernel,
        grid=(2, 2),
        out_shape=[shape((2, 2, HALF, width), BF)] * 2,
        in_specs=[pl.BlockSpec((act.shape[0], HALF), lambda y, h: (0, y)) for act in acts]
        + [pl.BlockSpec((2, low.shape[1], width), lambda y, h: (h, 0, 0)) for low in lows],
        out_specs=[pl.BlockSpec((1, 1, HALF, width), lambda y, h: (y, h, 0, 0))] * 2,
        scratch_shapes=[pltpu.VMEM((HALF, 4 * PIECE), BF)],
        compiler_params=params(36),
        cost_estimate=cost(2 * 4 * PIECE * D * 4 * width, 16 * 2**20),
    )(*acts, *lows)


def down_grad_kernel(*refs):
    units, refs = refs[:3], refs[3:]
    acts, refs = refs[:5], refs[5:]
    outs, turned_s = refs[:2], refs[2]

    @pl.when(pl.program_id(1) == 0)
    def _():
        start = 0
        for unit_ref in units:
            size = unit_ref.shape[1]
            for d in range(2):
                turned_s[d, :, start : start + size] = unit_ref[d].T
            start += size

    for d in range(2):
        total, start = None, 0
        for act_ref in acts:
            size = act_ref.shape[0]
            value = dot(turned_s[d, :, start : start + size], act_ref[...], 1, 0)
            total = value if total is None else total + value
            start += size
        outs[d][0, 0] = total.astype(BF)


def run_down_grad(units, acts):
    width = units[0].shape[2]
    return pl.pallas_call(
        down_grad_kernel,
        grid=(2, 2),
        out_shape=[shape((2, 2, width, HALF), BF)] * 2,
        in_specs=[pl.BlockSpec((2, unit.shape[1], width), lambda h, y: (h, 0, 0)) for unit in units]
        + [pl.BlockSpec((act.shape[0], HALF), lambda h, y: (0, y)) for act in acts],
        out_specs=[pl.BlockSpec((1, 1, width, HALF), lambda h, y: (y, h, 0, 0))] * 2,
        scratch_shapes=[pltpu.VMEM((2, width, 4 * PIECE), BF)],
        compiler_params=params(36),
        cost_estimate=cost(2 * 4 * PIECE * D * 4 * width, 16 * 2**20),
    )(*units, *acts)


def head_grad_kernel(kinds, *refs):
    acts, refs = refs[:4], refs[4:]
    messages, refs = refs[:4], refs[4:]
    passed, refs = (refs[:2], refs[2:]) if kinds > 1 else (None, refs)
    outs, turned_s, right_s = refs[:2], refs[2], refs[3]
    start = 0
    for act_ref in acts:
        size = act_ref.shape[0]
        turned_s[:, start : start + size] = act_ref[...].T
        start += size

    @pl.when(pl.program_id(0) == 0)
    def _():
        for which in range(kinds):
            for b in range(4):
                for a in range(4):
                    value = messages[b][which, a] if kinds > 1 else messages[b][a]
                    right_s[columns(a, PIECE), columns(which * 4 + b, HD)] = value

    for which in range(kinds):
        value = dot(turned_s[...], right_s[:, columns(which, 4 * HD)], 1, 0)
        for b, (d, h) in enumerate(SLOTS):
            outs[d][0, h, which] = value[:, columns(b, HD)].astype(BF)
    if passed:
        for d in range(2):
            outs[d][0, :, kinds] = passed[d][0, :, 0]


def run_head_grad(kinds, acts, messages, passed=()):
    whole = lambda dims: pl.BlockSpec(dims, lambda y: (0,) * len(dims))
    rows = lambda count: pl.BlockSpec((1, 2, count, HALF, HD), lambda y: (y, 0, 0, 0, 0))
    made = kinds + 1 if passed else kinds
    return pl.pallas_call(
        lambda *refs: head_grad_kernel(kinds, *refs),
        grid=(2,),
        out_shape=[shape((2, 2, made, HALF, HD), BF)] * 2,
        in_specs=[pl.BlockSpec((act.shape[0], HALF), lambda y: (0, y)) for act in acts]
        + [whole(message.shape) for message in messages]
        + [rows(1)] * len(passed),
        out_specs=[rows(made)] * 2,
        scratch_shapes=[
            pltpu.VMEM((HALF, 4 * PIECE), BF),
            pltpu.VMEM((4 * PIECE, kinds * 4 * HD), BF),
        ],
        compiler_params=params(44),
        cost_estimate=cost(2 * 4 * PIECE * D * kinds * 4 * HD, 12 * 2**20),
    )(*acts, *messages, *passed)


def allowed_pairs(starts, query0, key0, shape, query_axis):
    query = query0 + lax.broadcasted_iota(jnp.int32, shape, query_axis)
    key = key0 + lax.broadcasted_iota(jnp.int32, shape, 1 - query_axis)
    first = jnp.zeros(shape, jnp.int32)
    for s in range(CONT):
        first = jnp.where(query >= starts[s], starts[s], first)
    return (key <= query) & ((key < starts[0]) | (key >= first))


def block_bounds(starts, n):
    full = jnp.minimum(n, starts[0] // BLOCK)
    first = jnp.int32(0)
    for s in range(CONT):
        first = jnp.where(n * BLOCK >= starts[s], starts[s], first)
    return full, first


def block_used(starts, first, m):
    return (m * BLOCK < starts[0]) | ((m + 1) * BLOCK > first)


def attention_forward(place_ref, starts_ref, *refs):
    messages, refs = refs[:4], refs[4:]
    outs, refs = refs[:4], refs[4:]
    wide_ref, log_ref, q_s, k_s, v_s, score_s, acc_s, sum_s, max_s = refs
    scale = LOG2E / math.sqrt(HD)
    starts = [starts_ref[s] for s in range(CONT)]
    for b in range(4):
        for a in range(4):
            rows = pl.ds(pl.multiple_of(place_ref[4 * b + a] * PIECE, PIECE), PIECE)
            q_s[rows, :] = messages[b][0, a]
            k_s[rows, :] = messages[b][1, a]
            v_s[rows, :] = messages[b][2, a]

    def one_block(n, carry):
        rows = pl.ds(pl.multiple_of(n * BLOCK, BLOCK), BLOCK)
        full, first = block_bounds(starts, n)
        max_s[...] = jnp.full(max_s.shape, -1e30, F32)
        acc_s[...] = jnp.zeros(acc_s.shape, F32)
        sum_s[...] = jnp.zeros(sum_s.shape, F32)

        def note(scores, m):
            score_s[m] = scores
            top = max_s[...]
            for part in range(BLOCK // HD):
                top = jnp.maximum(top, scores[:, part * HD : (part + 1) * HD])
            max_s[...] = top

        def product(m):
            keys = pl.ds(pl.multiple_of(m * BLOCK, BLOCK), BLOCK)
            return dot(q_s[rows, :], k_s[keys, :], 1, 1)

        @pl.loop(0, full)
        def _(m):
            note(product(m), m)

        @pl.loop(full, n + 1)
        def _(m):
            @pl.when(block_used(starts, first, m))
            def _():
                allowed = allowed_pairs(starts, n * BLOCK, m * BLOCK, (BLOCK, BLOCK), 0)
                note(jnp.where(allowed, product(m), MASKED_SCORE), m)

        highest = jnp.max(max_s[...], axis=1, keepdims=True) * scale

        @pl.loop(0, n + 1)
        def _(m):
            @pl.when(block_used(starts, first, m))
            def _():
                keys = pl.ds(pl.multiple_of(m * BLOCK, BLOCK), BLOCK)
                exponent = jnp.exp2(score_s[m] * scale - highest)
                total = sum_s[...]
                for part in range(BLOCK // HD):
                    total = total + exponent[:, part * HD : (part + 1) * HD]
                sum_s[...] = total
                acc_s[...] += dot(exponent.astype(BF), v_s[keys, :], 1, 0)

        total = jnp.sum(sum_s[...], axis=1, keepdims=True)
        wide_ref[rows, :] = acc_s[...] / total
        log_total = jnp.broadcast_to(highest + jnp.log2(total), (BLOCK, HD))
        log_ref[n] = log_total.T[:8]
        return carry

    lax.fori_loop(0, k_s.shape[0] // BLOCK, one_block, 0)
    for b in range(4):
        for a in range(4):
            rows = pl.ds(pl.multiple_of(place_ref[4 * b + a] * PIECE, PIECE), PIECE)
            outs[b][a] = wide_ref[rows, :].astype(BF)


def attention_backward(place_ref, starts_ref, *refs):
    messages, refs = refs[:4], refs[4:]
    grads, refs = refs[:4], refs[4:]
    wide_ref, log_ref, cos_ref, sin_ref, *refs = refs
    outs, refs = refs[:4], refs[4:]
    q_s, k_s, v_s, g_s, dq_s, dk_s, dv_s = refs
    scale = LOG2E / math.sqrt(HD)
    starts = [starts_ref[s] for s in range(CONT)]
    for b in range(4):
        for a in range(4):
            rows = pl.ds(pl.multiple_of(place_ref[4 * b + a] * PIECE, PIECE), PIECE)
            q_s[rows, :] = messages[b][0, a]
            k_s[rows, :] = messages[b][1, a]
            v_s[rows, :] = messages[b][2, a]
            g_s[rows, :] = grads[b][a]
    dq_s[...] = jnp.zeros(dq_s.shape, F32)
    dk_s[...] = jnp.zeros(dk_s.shape, F32)
    dv_s[...] = jnp.zeros(dv_s.shape, F32)

    def one_block(n, carry):
        rows = pl.ds(pl.multiple_of(n * BLOCK, BLOCK), BLOCK)
        full, first = block_bounds(starts, n)
        crossed = g_s[rows, :].astype(F32) * wide_ref[rows, :]
        row_dot = jnp.sum(crossed.T, axis=0, keepdims=True)
        log_total = log_ref[n][:1]

        def step(m, masked):
            keys = pl.ds(pl.multiple_of(m * BLOCK, BLOCK), BLOCK)
            query, key = q_s[rows, :], k_s[keys, :]
            probability = jnp.exp2(dot(key, query, 1, 1) * scale - log_total)
            if masked:
                allowed = allowed_pairs(starts, n * BLOCK, m * BLOCK, (BLOCK, BLOCK), 1)
                probability = jnp.where(allowed, probability, 0.0)
            prob_grad = dot(v_s[keys, :], g_s[rows, :], 1, 1)
            score_grad = (probability * (prob_grad - row_dot)).astype(BF)
            dv_s[keys, :] += dot(probability.astype(BF), g_s[rows, :], 1, 0)
            dk_s[keys, :] += dot(score_grad, query, 1, 0)
            dq_s[rows, :] += dot(score_grad, key, 0, 0)

        @pl.loop(0, full)
        def _(m):
            step(m, False)

        @pl.loop(full, n + 1)
        def _(m):
            @pl.when(block_used(starts, first, m))
            def _():
                step(m, True)

        return carry

    lax.fori_loop(0, k_s.shape[0] // BLOCK, one_block, 0)
    for b in range(4):
        for a in range(4):
            rows = pl.ds(pl.multiple_of(place_ref[4 * b + a] * PIECE, PIECE), PIECE)
            for which, grad in ((0, dq_s), (1, dk_s)):
                value = grad[rows, :] * (1.0 / math.sqrt(HD))
                turned = value * cos_ref[rows, :] - pltpu.roll(value, HD // 2, 1) * sin_ref[rows, :]
                outs[b][which, a] = turned.astype(BF)
            outs[b][2, a] = dv_s[rows, :].astype(BF)


def run_forward(place, starts, messages):
    tokens = 16 * PIECE
    blocks = tokens // BLOCK
    out_shape = [jax.ShapeDtypeStruct((4, PIECE, HD), BF)] * 4
    out_shape += [
        jax.ShapeDtypeStruct((tokens, HD), F32),
        jax.ShapeDtypeStruct((blocks, 8, BLOCK), F32),
    ]
    return pl.pallas_call(
        attention_forward,
        out_shape=out_shape,
        in_specs=[SMEM_SPEC] * 2 + [VMEM_SPEC] * 4,
        out_specs=[VMEM_SPEC] * 6,
        scratch_shapes=[
            pltpu.VMEM((tokens, HD), BF),
            pltpu.VMEM((tokens, HD), BF),
            pltpu.VMEM((tokens, HD), BF),
            pltpu.VMEM((blocks, BLOCK, BLOCK), F32),
            pltpu.VMEM((BLOCK, HD), F32),
            pltpu.VMEM((BLOCK, HD), F32),
            pltpu.VMEM((BLOCK, HD), F32),
        ],
        compiler_params=pltpu.CompilerParams(vmem_limit_bytes=48 * 2**20),
        cost_estimate=pl.CostEstimate(
            flops=2 * tokens * tokens * HD * 2,
            bytes_accessed=8 * 2**20,
            transcendentals=tokens * tokens // 2,
        ),
    )(place, starts, *messages)


def run_backward(place, starts, messages, grads, wide, log_total, cosine, sine_table):
    tokens = 16 * PIECE
    return pl.pallas_call(
        attention_backward,
        out_shape=[jax.ShapeDtypeStruct((3, 4, PIECE, HD), BF)] * 4,
        in_specs=[SMEM_SPEC] * 2 + [VMEM_SPEC] * 12,
        out_specs=[VMEM_SPEC] * 4,
        scratch_shapes=[pltpu.VMEM((tokens, HD), BF)] * 4 + [pltpu.VMEM((tokens, HD), F32)] * 3,
        compiler_params=pltpu.CompilerParams(vmem_limit_bytes=52 * 2**20),
        cost_estimate=pl.CostEstimate(
            flops=5 * tokens * tokens * HD * 2,
            bytes_accessed=16 * 2**20,
            transcendentals=tokens * tokens // 2,
        ),
    )(place, starts, *messages, *grads, wide, log_total, cosine, sine_table)


def swap_slots(messages):
    return [messages[0], flip_y(messages[1]), flip_near(messages[2]), flip_y_near(messages[3])]


def to_tokens(values):
    return lax.all_to_all(values, "row", split_axis=0, concat_axis=1, tiled=True)


def to_width(values):
    return lax.all_to_all(values, "row", split_axis=1, concat_axis=0, tiled=True)


def square_shards(
    hidden_in,
    teacher,
    valid,
    segment_ids,
    query_weight,
    key_weight,
    value_weight,
    output_weight,
    gate_weight,
    up_weight,
    down_weight,
):
    row, col, dp = lax.axis_index("row"), lax.axis_index("col"), lax.axis_index("dp")
    x, y = row % 2, row // 2
    q = (dp + y) % 2
    own_piece = col * SIDE + row
    segment = segment_ids[0]
    group_tokens = segment.shape[0]
    home_tokens = group_tokens // (SIDE * SIDE)

    def swap_y(values):
        return jnp.where(
            y == 0, values, jnp.concatenate((values[:, HALF:], values[:, :HALF]), axis=1)
        )

    def cut(matrix, at, axis):
        size = matrix.shape[axis] // 4
        return lax.dynamic_slice_in_dim(matrix, (2 * at + q) * size, size, axis)

    def head_cut(at):
        parts = [cut(matrix, at, 1) for matrix in (query_weight, key_weight, value_weight)]
        return jnp.stack(parts + [cut(output_weight, at, 0).T])

    labels = jnp.arange(1, CONT + 1, dtype=jnp.int32)
    starts = jnp.sum((segment[None, :] < labels[:, None]).astype(jnp.int32), axis=1)
    codes = jnp.arange(16, dtype=jnp.int32)
    relative = (
        (codes & 1) + ((codes >> 1) & 1) * 8 + ((codes >> 2) & 1) * 2 + ((codes >> 3) & 1) * 4
    )
    pieces = relative ^ own_piece
    frequency = jnp.power(10000.0, jnp.arange(HD // 2, dtype=F32) * (-2.0 / HD))
    angles = positions(segment).astype(F32)[:, None] * jnp.tile(frequency, 2)[None, :]
    sign = jnp.where(jnp.arange(HD) < HD // 2, -1.0, 1.0)
    cos_wide, sin_wide = jnp.cos(angles), jnp.sin(angles) * sign[None, :]

    heads_x = flip_x(head_cut(1 - x))
    gates_x = flip_x(after(cut(gate_weight, 1 - x, 1), heads_x))
    rows_y = hidden_in.shape[0] // 2
    kept = lax.dynamic_slice_in_dim(hidden_in, y * rows_y, rows_y, 0)
    sent = lax.dynamic_slice_in_dim(hidden_in, (1 - y) * rows_y, rows_y, 0)
    piece_here = jnp.concatenate((kept, flip_y(sent)), axis=1)
    piece_far = flip_far(piece_here)
    piece_x = flip_x(after(piece_here, heads_x))
    piece_far_x = flip_x(piece_far)

    count = after(jnp.sum(valid.astype(F32)), piece_here)
    count = exchanged_sum(count, ("dp", "col"), 2 * SIDE)
    target = to_tokens(after(teacher, piece_x))

    def whole_rows(own, other):
        width = own.shape[1] // 2
        first, second = jnp.where(x == 0, own, other), jnp.where(x == 0, other, own)
        return jnp.concatenate(
            (first[:, :width], second[:, :width], first[:, width:], second[:, width:]), axis=1
        )

    def own_and_x(rows):
        half = rows.shape[0] // 2
        return [lax.dynamic_slice_in_dim(rows, at * half, half, 0) for at in (x, 1 - x)]

    hidden_rows = whole_rows(piece_here, piece_x)
    hidden = own_and_x(hidden_rows)[0].astype(F32)
    acts_here = own_and_x(local_norm(hidden_rows.astype(F32))[0].astype(BF))
    far_rows = whole_rows(piece_far, piece_far_x)
    acts_far = own_and_x(local_norm(far_rows.astype(F32))[0].astype(BF))
    normed_acts = acts_here + acts_far
    heads_tall = ordered(x, head_cut(x), heads_x, 1)
    heads_high = flip_near(heads_tall)
    heads_y = flip_dp_y(heads_tall)
    normed, inverse_one = local_norm(hidden)
    heads_y_high = flip_dp_y(after(heads_high, piece_x, count))
    gates_tall = ordered(x, cut(gate_weight, x, 1), gates_x, 0)
    gates_high = flip_far(after(gates_tall, heads_high, piece_far))
    cos_wide, sin_wide = after((cos_wide, sin_wide), heads_tall)
    heads = both_cores(
        heads_tall, heads_y, heads_high, after(heads_y_high, piece_far, target, cos_wide, sin_wide)
    )
    gates_y = flip_dp_y(after(gates_tall, piece_far_x))

    messages = run_qkv(pieces, normed_acts, heads, cos_wide, sin_wide)
    mlp_x = jnp.stack((cut(up_weight, 1 - x, 1), cut(down_weight, 1 - x, 0)))
    mlp_x = flip_x(after(mlp_x, messages[0]))
    messages = swap_slots(messages)
    messages = after(messages, mlp_x, gates_high, gates_y)

    ups_tall = ordered(x, cut(up_weight, x, 1), after(mlp_x[0], messages), 0)
    ups_high = flip_far(after(ups_tall, gates_high))
    gates_y_high = flip_dp_y(after(gates_high, messages))
    ups_y = flip_dp_y(ups_tall)
    *mixed, wide_mixed, log_total = run_forward(pieces, starts, messages)
    mixed = after(mixed, gates_y_high)
    downs_tall = ordered(x, cut(down_weight, x, 0), after(mlp_x[1], mixed), 1)
    mixed = swap_slots(mixed)
    mixed = after(mixed, ups_high, ups_y)
    gates = both_cores(gates_tall, gates_y, gates_high, gates_y_high, mixed)

    ups_y_high = flip_dp_y(after(ups_high, mixed))
    downs_y = flip_dp_y(after(downs_tall, ups_y_high))
    after_attention = hidden + square_reduce(*run_out(mixed, heads))
    after_attention = after(after_attention, ups_y_high, gates, downs_y)

    normed_two, inverse_two = local_norm(after_attention)
    ups = both_cores(ups_tall, ups_y, ups_high, ups_y_high, normed_two)
    low_two = normed_two.astype(BF)
    up_own = run_up([low_two], gates, ups)
    two_acts = near_gather(low_two, up_own)
    downs_high = flip_far(after(downs_tall, low_two))
    downs_y_high = flip_dp_y(after(downs_high, two_acts[1:3], up_own[2]))
    up_sides = run_up(after(two_acts[1:3], up_own[2]), gates, ups)
    up_far = run_up(after(two_acts[3:], up_sides[2], downs_y_high), gates, ups)
    downs = both_cores(downs_tall, downs_y, downs_high, downs_y_high, two_acts, up_sides[2])
    ups_out = [up_own, up_sides, up_far]
    units = [out[2] for out in ups_out]
    down_far = run_down("far", units[2], downs)
    down_sides = run_down("sides", after(units[1], down_far), downs)
    down_own = run_down("own", after(units[0], down_sides), downs)
    output = after_attention + near_reduce(down_far, down_sides, down_own[0])

    total_count = jnp.maximum(count, 1.0)
    counted_home = lax.dynamic_slice_in_dim(
        valid.astype(F32), row * home_tokens, home_tokens, 0
    )[:, None]
    differ = output - swap_y(target).astype(F32)
    local_loss = jnp.sum(counted_home * (differ * differ)) / D
    all_tokens = group_tokens * lax.axis_size("dp")
    out_grad = counted_home * differ * (all_tokens / total_count)

    low_out = out_grad.astype(BF)
    loss = exchanged_sum(after(local_loss, low_out), ("dp", "row", "col"), 2 * SIDE * SIDE)
    low_own = run_gated([low_out], up_own[0], up_own[1], downs)
    out_acts = near_gather(low_out, low_own)
    low_sides = run_gated(after(out_acts[1:3], low_own), up_sides[0], up_sides[1], downs)
    low_far = run_gated(after(out_acts[3:], low_sides, loss), up_far[0], up_far[1], downs)
    lows = [low_own, low_sides, low_far]
    two_far = run_normed_two("far", *low_far, gates, ups)
    two_sides = run_normed_two("sides", *after(low_sides, two_far), gates, ups)

    first = near_reduce_far(two_far)
    got = near_reduce_sides(first, two_sides)
    two_own = run_normed_two("own", *after(low_own, two_sides, first), gates, ups)
    down_grads = Spread(run_down_grad(after(units, two_own, got[1:3]), out_acts))
    down_core = down_grads.to_core()
    normed_two_grad = near_reduce_end(got, two_own[0])
    middle_grad = out_grad + local_norm_backward(normed_two_grad, normed_two, inverse_two)
    low_middle = middle_grad.astype(BF)
    gate_pair = run_wide_grad(two_acts, after([low[0] for low in lows], low_middle, down_core))
    gate_grads = Spread(gate_pair)
    down_y1 = down_grads.to_y(1)
    layer_output = to_width(swap_y(after(output, low_middle).astype(BF)))
    gate_core = gate_grads.to_core(low_middle)
    down_y0 = down_grads.to_y(0, low_middle)
    up_pair = run_wide_grad(two_acts, after([low[1] for low in lows], gate_pair, down_y1))
    up_grads = Spread(up_pair)
    middle_acts = square_gather(low_middle, gate_pair, up_pair, layer_output)
    middle_acts = after(middle_acts, up_pair, down_y0, layer_output)
    grad_messages = run_attended_grad(middle_acts, heads)
    up_core = up_grads.to_core(grad_messages)
    down_grads.to_high(flip_far, middle_acts[1:3])
    out_pair = run_head_grad(1, after(middle_acts, grad_messages), mixed)
    grad_messages = swap_slots(grad_messages)
    grad_messages = after(grad_messages, up_core, out_pair)
    gate_y1 = gate_grads.to_y(1, grad_messages)
    gate_y0 = gate_grads.to_y(0, grad_messages)
    up_y0 = up_grads.to_y(0, grad_messages)
    up_y1 = up_grads.to_y(1, grad_messages)
    back = run_backward(
        pieces, starts, messages, grad_messages, wide_mixed, log_total, cos_wide, sin_wide
    )
    back = after(back, down_grads.high, gate_y1, gate_y0)
    gate_grads.to_high(flip_far, back)
    own_down, send_down = to_x(down_grads.total(back), x, 1)
    down_x = flip_x(send_down)
    back = swap_slots(back)
    back = after(back, down_x, gate_grads.high, up_y1, up_y0)
    up_grads.to_high(flip_far, back)
    own_gate, send_gate = to_x(gate_grads.total(back), x, 0)
    gate_x = flip_x(send_gate)
    head_pair = run_head_grad(3, normed_acts, back, out_pair)
    head_grads = Spread(head_pair)
    head_core = head_grads.to_core()
    input_sums = run_input(after(back, head_pair), heads)
    input_sums = after(input_sums, head_core)
    head_y1 = head_grads.to_y(1)
    normed_grad = square_reduce(*input_sums, up_grads.high)
    head_y0 = head_grads.to_y(0, head_y1)
    head_grads.to_high(flip_near, head_y1)
    first_mine = jnp.stack((pair_up(own_gate, gate_x, x), pair_up(own_down, down_x, x)))
    first_theirs = flip_dp(after(first_mine, head_y1))
    normed_grad = after(normed_grad, head_y0, head_grads.high, first_theirs)
    input_gradient = middle_grad + local_norm_backward(normed_grad, normed, inverse_one)
    own_head, send_head = to_x(head_grads.total(normed_grad), x, 1)
    own_up, send_up = to_x(up_grads.total(normed_grad), x, 0)
    head_x = flip_x(send_head)
    last_mine = pair_up(own_up, flip_x(send_up), x)
    input_out = to_width(swap_y(input_gradient.astype(BF)))
    last_theirs = flip_dp(after(last_mine, input_out))
    head_mine = pair_up(own_head, head_x, x)
    head_theirs = flip_dp(head_mine)
    mean_loss = loss / total_count

    gate_grad = unite(first_mine[0], first_theirs[0], q, 1)
    down_grad = unite(first_mine[1], first_theirs[1], q, 0)
    up_grad = unite(last_mine, last_theirs, q, 1)
    head_grads = unite(head_mine, head_theirs, q, 2)
    return (
        layer_output,
        mean_loss,
        input_out.astype(F32),
        head_grads[0],
        head_grads[1],
        head_grads[2],
        head_grads[3].T,
        gate_grad,
        up_grad,
        down_grad,
    )


def solution(mesh):
    body = square_shards if fits_square(mesh) else shards
    in_specs = (
        P(("dp", "col"), "row"),
        P(("dp", "col"), "row"),
        P(("dp", "col")),
        P("dp", None),
        P("row", "col"),
        P("row", "col"),
        P("row", "col"),
        P("col", "row"),
        P("row", "col"),
        P("row", "col"),
        P("col", "row"),
    )
    out_specs = (
        P(("dp", "col"), "row"),
        P(),
        P(("dp", "col"), "row"),
        P("row", "col"),
        P("row", "col"),
        P("row", "col"),
        P("col", "row"),
        P("row", "col"),
        P("row", "col"),
        P("col", "row"),
    )
    return jax.shard_map(body, mesh=mesh, in_specs=in_specs, out_specs=out_specs, check_vma=False)
```

```python
import math

import jax
import jax.numpy as jnp
from jax import lax
from jax.experimental import pallas as pl
from jax.experimental.pallas import tpu as pltpu
from jax.sharding import PartitionSpec as P

D = 2048
HD = 128
CONT = 8


EPSILON = 1e-05
MASKED_SCORE = -1e30


def positions(segment):
    labels = jnp.arange(CONT + 1, dtype=jnp.int32)
    onehot = (segment[:, None] == labels[None, :]).astype(jnp.int32)
    counts = jnp.sum(onehot, axis=0)
    starts = jnp.cumsum(counts) - counts
    leading = jnp.sum(onehot * starts[None, :], axis=1)
    indices = jnp.arange(segment.shape[0], dtype=jnp.int32)
    return indices - leading + jnp.where(segment > 0, counts[0], 0)


def rotary(offsets):
    half_width = HD // 2
    frequency = jnp.power(10000.0, jnp.arange(half_width, dtype=jnp.float32) * (-2.0 / HD))
    angles = offsets.astype(jnp.float32)[:, None] * frequency[None, :]
    return (jnp.cos(angles), jnp.sin(angles))


def rotate(values, cosine, sine_table):
    half_width = values.shape[-1] // 2
    leading, trailing = (values[..., :half_width], values[..., half_width:])
    cos_wide = cosine[:, None, :]
    sin_wide = sine_table[:, None, :]
    return jnp.concatenate(
        (leading * cos_wide - trailing * sin_wide, trailing * cos_wide + leading * sin_wide),
        axis=-1,
    )


def unrotate(gradient, cosine, sine_table):
    half_width = gradient.shape[-1] // 2
    leading, trailing = (gradient[..., :half_width], gradient[..., half_width:])
    cos_wide = cosine[:, None, :]
    sin_wide = sine_table[:, None, :]
    return jnp.concatenate(
        (leading * cos_wide + trailing * sin_wide, trailing * cos_wide - leading * sin_wide),
        axis=-1,
    )


def feature_sums(left, right):
    return lax.psum((jnp.sum(left, axis=1), jnp.sum(right, axis=1)), "row")


def normalize(values):
    summed, squared = feature_sums(values, values * values)
    average = (summed / D)[:, None]
    inverse = lax.rsqrt(squared[:, None] / D - average * average + EPSILON)
    return ((values - average) * inverse, inverse)


def norm_backward(gradient, normed, inverse):
    summed, crossed = feature_sums(gradient, gradient * normed)
    return inverse * (gradient - summed[:, None] / D - normed * (crossed[:, None] / D))


def widen(values):
    return lax.all_gather(values, "col", axis=0, tiled=True)


def collect(values):
    return lax.all_gather(values, "row", axis=0, tiled=True)


def row_product(full, matrix, contract):
    return lax.psum_scatter(
        lax.dot_general(
            full, matrix, (((1,), (contract,)), ((), ())), preferred_element_type=jnp.float32
        ),
        "row",
        scatter_dimension=0,
        tiled=True,
    )


def column_product(full, matrix, contract):
    return lax.psum_scatter(
        lax.dot_general(
            full, matrix, (((1,), (contract,)), ((), ())), preferred_element_type=jnp.float32
        ),
        "col",
        scatter_dimension=0,
        tiled=True,
    )


def project_in(gathered, matrix):
    result = row_product(gathered, matrix, 0)
    return result


def project_back(gathered, matrix):
    result = row_product(gathered, matrix, 1)
    return result


def weight_product(left, right):
    return lax.dot_general(
        left, right, (((0,), (0,)), ((), ())), preferred_element_type=jnp.float32
    )


def block_layout(tok_rows):
    blocks = max(1, tok_rows // 512)
    return (blocks, tok_rows // blocks)


def score_maker(key_rows, segment, block):
    key_index = jnp.arange(key_rows.shape[0], dtype=jnp.int32)
    scale = 1.0 / math.sqrt(HD)

    def scores_for(query_block, offset):
        query_index = offset + jnp.arange(block, dtype=jnp.int32)
        query_segment = lax.dynamic_slice_in_dim(segment, offset, block, 0)
        allowed = (key_index[None, :] <= query_index[:, None]) & (
            (segment[None, :] == 0) | (segment[None, :] == query_segment[:, None])
        )
        scores = (
            jnp.einsum("qhd,khd->hqk", query_block, key_rows, preferred_element_type=jnp.float32)
            * scale
        )
        return jnp.where(allowed[None, :, :], scores, MASKED_SCORE)

    return scores_for


def attend(queries, key_rows, value_rows, segment, row_offset):
    tok_rows, heads_here = (queries.shape[0], queries.shape[1])
    blocks, block = block_layout(tok_rows)
    scores_for = score_maker(key_rows, segment, block)
    offsets = row_offset + jnp.arange(blocks, dtype=jnp.int32) * block

    def forward_block(inputs):
        query_block, offset = inputs
        scores = scores_for(query_block, offset)
        highest = jnp.max(scores, axis=-1, keepdims=True)
        exponent = jnp.exp(scores - highest)
        summed = jnp.sum(exponent, axis=-1, keepdims=True)
        probability = (exponent / summed).astype(jnp.bfloat16)
        mixed_block = jnp.einsum(
            "hqk,khd->qhd", probability, value_rows, preferred_element_type=jnp.float32
        )
        return (mixed_block, highest + jnp.log(summed))

    mixed_blocks, log_total = lax.map(
        forward_block, (queries.reshape(blocks, block, heads_here, HD), offsets)
    )
    return (mixed_blocks.reshape(tok_rows, heads_here * HD), log_total)


def attend_back(queries, key_rows, value_rows, segment, row_offset, log_total, attended_grad):
    tok_rows, heads_here = (queries.shape[0], queries.shape[1])
    blocks, block = block_layout(tok_rows)
    scores_for = score_maker(key_rows, segment, block)
    offsets = row_offset + jnp.arange(blocks, dtype=jnp.int32) * block
    scale = 1.0 / math.sqrt(HD)

    def backward_block(carry, inputs):
        key_sum, value_sum = carry
        query_block, grad_block, log_block, offset = inputs
        scores = scores_for(query_block, offset)
        probability = jnp.exp(scores - log_block)
        rounded = probability.astype(jnp.bfloat16)
        prob_grad = jnp.einsum(
            "qhd,khd->hqk", grad_block, value_rows, preferred_element_type=jnp.float32
        )
        row_dot = jnp.sum(probability * prob_grad, axis=-1, keepdims=True)
        score_grad = (probability * (prob_grad - row_dot)).astype(jnp.bfloat16)
        query_grad = (
            jnp.einsum("hqk,khd->qhd", score_grad, key_rows, preferred_element_type=jnp.float32)
            * scale
        )
        key_sum = (
            key_sum
            + jnp.einsum(
                "hqk,qhd->khd", score_grad, query_block, preferred_element_type=jnp.float32
            )
            * scale
        )
        value_sum = value_sum + jnp.einsum(
            "hqk,qhd->khd", rounded, grad_block, preferred_element_type=jnp.float32
        )
        return ((key_sum, value_sum), query_grad)

    empty = jnp.zeros(key_rows.shape, jnp.float32)
    inputs = (
        queries.reshape(blocks, block, heads_here, HD),
        attended_grad.reshape(blocks, block, heads_here, HD),
        log_total,
        offsets,
    )
    (key_sum, value_sum), query_grads = lax.scan(backward_block, (empty, empty), inputs)
    return (query_grads.reshape(tok_rows, heads_here, HD), key_sum, value_sum)


def shards(
    hidden_in,
    teacher,
    valid,
    segment_ids,
    query_weight,
    key_weight,
    value_weight,
    output_weight,
    gate_weight,
    up_weight,
    down_weight,
):
    row_devices = lax.axis_size("row")
    col_devices = lax.axis_size("col")
    tok_cols = hidden_in.shape[0]
    group_tokens = tok_cols * col_devices
    tok_rows = group_tokens // row_devices
    query_width = query_weight.shape[1]
    heads_here = query_width // HD
    unit_width = gate_weight.shape[1]
    segment = segment_ids[0]
    row_offset = lax.axis_index("row") * tok_rows
    cosine_all, sine_all = rotary(positions(segment))
    cosine = lax.dynamic_slice_in_dim(cosine_all, row_offset, tok_rows, 0)
    sine_table = lax.dynamic_slice_in_dim(sine_all, row_offset, tok_rows, 0)
    counted = valid.astype(jnp.float32)
    total_count = jnp.maximum(lax.psum(jnp.sum(counted), ("dp", "col")), 1.0)
    hidden = hidden_in.astype(jnp.float32)
    normed, inverse_one = normalize(hidden)
    normed_wide = widen(normed.astype(jnp.bfloat16))
    attn_weights = jnp.concatenate((query_weight, key_weight, value_weight), axis=1)
    projected = project_in(normed_wide, attn_weights)
    queries = rotate(
        projected[:, :query_width].reshape(tok_rows, heads_here, HD), cosine, sine_table
    ).astype(jnp.bfloat16)
    key_local = rotate(
        projected[:, query_width : 2 * query_width].reshape(tok_rows, heads_here, HD),
        cosine,
        sine_table,
    )
    key_local = key_local.reshape(tok_rows, query_width).astype(jnp.bfloat16)
    value_local = projected[:, 2 * query_width :].astype(jnp.bfloat16)
    key_flat, value_flat = (
        lax.all_gather(key_local, "row", axis=0, tiled=True),
        lax.all_gather(value_local, "row", axis=0, tiled=True),
    )
    key_rows = key_flat.reshape(group_tokens, heads_here, HD)
    value_rows = value_flat.reshape(group_tokens, heads_here, HD)
    attended, log_total = attend(queries, key_rows, value_rows, segment, row_offset)
    attended_wide = collect(attended.astype(jnp.bfloat16))
    after_attention = hidden + column_product(attended_wide, output_weight, 0)
    normed_two, inverse_two = normalize(after_attention)
    normed_two_wide = widen(normed_two.astype(jnp.bfloat16))
    mlp_weights = jnp.concatenate((gate_weight, up_weight), axis=1)
    gated = project_in(normed_two_wide, mlp_weights)
    gating = gated[:, :unit_width]
    upward = gated[:, unit_width:]
    sigmoid = jax.nn.sigmoid(gating)
    activated = gating * sigmoid
    units_wide = collect((activated * upward).astype(jnp.bfloat16))
    output = after_attention + column_product(units_wide, down_weight, 0)
    differ = output - teacher.astype(jnp.float32)
    local_loss = jnp.sum(counted[:, None] * (differ * differ)) / D
    all_tokens = group_tokens * lax.axis_size("dp")
    out_grad = counted[:, None] * differ * (all_tokens / total_count)
    out_wide = widen(out_grad.astype(jnp.bfloat16))
    units_grad = project_back(out_wide, down_weight)
    down_grad = weight_product(units_wide, out_wide)
    gating_grad = units_grad * upward * sigmoid * (1.0 + gating * (1.0 - sigmoid))
    upward_grad = units_grad * activated
    gated_wide = collect(jnp.concatenate((gating_grad, upward_grad), axis=1).astype(jnp.bfloat16))
    mlp_grads = weight_product(normed_two_wide, gated_wide)
    normed_two_grad = column_product(gated_wide, mlp_weights, 1)
    middle_grad = out_grad + norm_backward(normed_two_grad, normed_two, inverse_two)
    middle_wide = widen(middle_grad.astype(jnp.bfloat16))
    attended_grad = project_back(middle_wide, output_weight).astype(jnp.bfloat16)
    output_grad_sum = weight_product(attended_wide, middle_wide)
    query_grad, key_sum, value_sum = attend_back(
        queries, key_rows, value_rows, segment, row_offset, log_total, attended_grad
    )
    key_grad, value_grad = (
        lax.psum_scatter(
            key_sum.reshape(group_tokens, query_width), "row", scatter_dimension=0, tiled=True
        ),
        lax.psum_scatter(
            value_sum.reshape(group_tokens, query_width), "row", scatter_dimension=0, tiled=True
        ),
    )
    query_pre = unrotate(query_grad, cosine, sine_table).reshape(tok_rows, query_width)
    key_pre = unrotate(key_grad.reshape(tok_rows, heads_here, HD), cosine, sine_table).reshape(
        tok_rows, query_width
    )
    projected_wide = collect(
        jnp.concatenate((query_pre, key_pre, value_grad), axis=1).astype(jnp.bfloat16)
    )
    attn_grads = weight_product(normed_wide, projected_wide)
    normed_grad = column_product(projected_wide, attn_weights, 1)
    input_gradient = middle_grad + norm_backward(normed_grad, normed, inverse_one)
    summed_grads = (
        lax.psum(attn_grads[:, :query_width].astype(jnp.bfloat16), "dp").astype(jnp.float32),
        lax.psum(attn_grads[:, query_width : 2 * query_width].astype(jnp.bfloat16), "dp").astype(
            jnp.float32
        ),
        lax.psum(attn_grads[:, 2 * query_width :].astype(jnp.bfloat16), "dp").astype(jnp.float32),
        lax.psum(output_grad_sum.astype(jnp.bfloat16), "dp").astype(jnp.float32),
        lax.psum(mlp_grads[:, :unit_width].astype(jnp.bfloat16), "dp").astype(jnp.float32),
        lax.psum(mlp_grads[:, unit_width:].astype(jnp.bfloat16), "dp").astype(jnp.float32),
        lax.psum(down_grad.astype(jnp.bfloat16), "dp").astype(jnp.float32),
    )
    mean_loss = lax.psum(local_loss, ("dp", "row", "col")) / total_count
    return (
        output.astype(jnp.bfloat16),
        mean_loss.reshape(1),
        input_gradient,
        summed_grads[0],
        summed_grads[1],
        summed_grads[2],
        summed_grads[3],
        summed_grads[4],
        summed_grads[5],
        summed_grads[6],
    )


BF = jnp.bfloat16
F32 = jnp.float32
LOG2E = 1.4426950408889634
SIDE = 4
HALF = D // 2
PIECE = 256
BLOCK = 512
SLOTS = [(d, h) for h in range(2) for d in range(2)]


def fits_square(mesh):
    return mesh.shape["dp"] == 2 and mesh.shape["row"] == SIDE and mesh.shape["col"] == SIDE


def flip(values, axis, bit):
    return lax.ppermute(values, axis, [(i, i ^ bit) for i in range(SIDE)])


def flip_x(values):
    return flip(values, "row", 1)


def flip_y(values):
    return flip(values, "row", 2)


def flip_far(values):
    return flip(values, "col", 2)


def flip_near(values):
    return flip(values, "col", 1)


def flip_y_near(values):
    pairs = [
        (r * SIDE + c, (r ^ 2) * SIDE + (c ^ 1)) for r in range(SIDE) for c in range(SIDE)
    ]
    return lax.ppermute(values, ("row", "col"), pairs)


def flip_z(values):
    return flip(values, "col", 3)


def flip_dp(values):
    return lax.ppermute(values, "dp", [(0, 1), (1, 0)])


def flip_dp_y(values):
    pairs = [(g * SIDE + r, (1 - g) * SIDE + (r ^ 2)) for g in range(2) for r in range(SIDE)]
    return lax.ppermute(values, ("dp", "row"), pairs)


def near_gather(block, *events):
    half = block.shape[0] // 2
    by_x, by_z = flip_x(block), flip_near(block)
    next_x, next_z = after((by_x, by_z), *events)
    return [block, by_x, by_z, flip_near(next_x[:half]), flip_x(next_z[half:])]


def near_reduce(far, sides, own):
    first = near_reduce_far(far)
    return near_reduce_end(near_reduce_sides(first, sides), own)


def near_reduce_far(far):
    return flip_near(far[0]), flip_x(far[1])


def near_reduce_sides(first, sides):
    far_top, far_bottom = first
    x_top, x_bottom, z_top, z_bottom = sides
    return (
        flip_x((x_top + wide(far_top)).astype(BF)),
        flip_x(x_bottom),
        flip_near(z_top),
        flip_near((z_bottom + wide(far_bottom)).astype(BF)),
    )


def near_reduce_end(got, own):
    x_top, x_bottom, z_top, z_bottom = got
    half = x_top.shape[0]
    top = own[:half] + wide(x_top) + wide(z_top)
    bottom = own[half:] + wide(x_bottom) + wide(z_bottom)
    return jnp.concatenate((top, bottom), axis=0)


def square_gather(block, *events):
    by_z, by_x = flip_far(block), flip_x(block)
    return [block, by_x, by_z, flip_x(after(by_z, *events) if events else by_z)]


def square_reduce(far, by_x, by_z, own, *events):
    got_far = flip_x(far)
    got_far = after(got_far, *events) if events else got_far
    got_x = flip_x(after(by_x, got_far))
    got_z = flip_far((by_z + wide(got_far)).astype(BF))
    return own + wide(got_x) + wide(got_z)


def ordered(flag, own, other, axis):
    return jnp.where(
        flag == 0,
        jnp.concatenate((own, other), axis=axis),
        jnp.concatenate((other, own), axis=axis),
    )


def after(values, *events):
    return lax.optimization_barrier((values, events))[0]


def both_cores(tall, by_y, high, by_y_high, *events):
    own = jnp.stack((tall, by_y, high, by_y_high))
    return own, flip_dp(after(own, *events) if events else own)


def piece(pair, slot, y):
    return pair[slot % 2].at[2 * (slot // 2) + y]


def wide(values):
    return values.astype(F32)


class Spread:
    def __init__(self, grads):
        self.keep, self.send = grads

    def to_core(self, *events):
        self.got = flip_dp(after(self.send, *events))
        return self.got

    def here(self, y, h):
        return wide(self.keep[y, h]) + wide(self.got[y, h])

    def to_y(self, h, *events):
        by_y = flip_dp_y(after(self.here(1, h).astype(BF), *events))
        setattr(self, "by_y%d" % h, by_y)
        return by_y

    def to_high(self, flip_z, *events):
        send = (self.here(0, 1) + wide(self.by_y1)).astype(BF)
        self.high = flip_z(after(send, *events))
        return self.high

    def total(self, *events):
        value = self.here(0, 0) + wide(self.by_y0) + wide(self.high)
        return after(value.astype(BF), *events) if events else value.astype(BF)


def to_x(total, x, axis):
    size = total.shape[axis] // 2
    own = lax.dynamic_slice_in_dim(total, x * size, size, axis)
    return own, lax.dynamic_slice_in_dim(total, (1 - x) * size, size, axis)


def pair_up(own, by_x, x):
    return jnp.where(x == 0, jnp.stack((own, by_x)), jnp.stack((by_x, own)))


def unite(mine, theirs, q, axis):
    parts = []
    for at in range(2):
        parts += [jnp.where(q == 0, mine[at], theirs[at]), jnp.where(q == 0, theirs[at], mine[at])]
    return jnp.concatenate(parts, axis=axis).astype(F32)


def exchanged_sum(value, axes, count):
    tiles = jnp.broadcast_to(value, (count, 8, HD))
    tiles = lax.all_to_all(tiles, axes, split_axis=0, concat_axis=0, tiled=True)
    return jnp.sum(tiles[:, 0, 0]).reshape(1)


def local_norm(values):
    average = jnp.mean(values, axis=1, keepdims=True)
    square = jnp.mean(values * values, axis=1, keepdims=True)
    inverse = lax.rsqrt(square - average * average + EPSILON)
    return ((values - average) * inverse, inverse)


def local_norm_backward(gradient, normed, inverse):
    average = jnp.mean(gradient, axis=1, keepdims=True)
    crossed = jnp.mean(gradient * normed, axis=1, keepdims=True)
    return inverse * (gradient - average - normed * crossed)


def dot(left, right, a, b):
    return lax.dot_general(left, right, (((a,), (b,)), ((), ())), preferred_element_type=F32)


SMEM_SPEC = pl.BlockSpec(memory_space=pltpu.SMEM)
VMEM_SPEC = pl.BlockSpec(memory_space=pltpu.VMEM)


def shape(dims, kind):
    return jax.ShapeDtypeStruct(dims, kind)


def params(megabytes):
    return pltpu.CompilerParams(vmem_limit_bytes=megabytes * 2**20)


def cost(flops, moved, transcendentals=0):
    return pl.CostEstimate(
        flops=int(flops), bytes_accessed=int(moved), transcendentals=int(transcendentals)
    )


def y_half(y):
    return slice(y * HALF, (y + 1) * HALF)


def columns(index, width):
    return slice(index * width, (index + 1) * width)


FAR_SHAPES = [shape((PIECE // 2, D), BF)] * 2
SIDE_SHAPES = [
    shape((PIECE, D), BF),
    shape((PIECE // 2, D), F32),
    shape((PIECE // 2, D), F32),
]
OWN_SHAPES = [shape((PIECE, D), F32)]
NEAR_SHAPES = [
    shape((PIECE // 2, D), F32),
    shape((PIECE // 2, D), BF),
    shape((PIECE // 2, D), BF),
    shape((PIECE // 2, D), F32),
]
SUM_SHAPES = {"far": FAR_SHAPES, "sides": NEAR_SHAPES, "own": OWN_SHAPES}
SUM_BLOCKS = {"far": (3,), "sides": (1, 2), "own": (0,)}


def store_halves(part, value, outs):
    half = PIECE // 2
    for low in range(2):
        rows = value[low * half : (low + 1) * half]
        outs[low][:, y_half(part)] = rows.astype(outs[low].dtype)


def store_sum(kind, index, part, value, outs):
    if kind == "own":
        outs[0][:, y_half(part)] = value
    else:
        store_halves(part, value, outs[2 * index : 2 * index + 2])


ALL_SHAPES = [shape((PIECE, D), kind) for kind in (F32, BF, F32, BF)]


def store_any(a, part, value, outs):
    outs[a][:, y_half(part)] = value.astype(outs[a].dtype)


def qkv_kernel(place_ref, *refs):
    acts, refs = refs[:4], refs[4:]
    weights, refs = refs[:2], refs[2:]
    cos_ref, sin_ref, *refs = refs
    outs, weight_s = refs[:4], refs[4]
    for b in range(4):
        for y in range(2):
            for which in range(3):
                weight_s[y_half(y), columns(which * 4 + b, HD)] = piece(weights, b, y)[which]
    for a in range(4):
        rows = pl.ds(pl.multiple_of(place_ref[a] * PIECE, PIECE), PIECE)
        cos_block, sin_block = cos_ref[rows, :], sin_ref[rows, :]
        act = acts[a][...]
        projected = dot(act, weight_s[...], 1, 0)
        for which in range(3):
            for b in range(4):
                tile = projected[:, columns(which * 4 + b, HD)]
                if which < 2:
                    tile = tile * cos_block + pltpu.roll(tile, HD // 2, 1) * sin_block
                outs[b][which, a] = tile.astype(BF)


def run_qkv(place, acts, weights, cos_wide, sin_wide):
    return pl.pallas_call(
        qkv_kernel,
        out_shape=[shape((3, 4, PIECE, HD), BF)] * 4,
        in_specs=[SMEM_SPEC] + [VMEM_SPEC] * 8,
        out_specs=[VMEM_SPEC] * 4,
        scratch_shapes=[pltpu.VMEM((D, 12 * HD), BF)],
        compiler_params=params(40),
        cost_estimate=cost(2 * 4 * PIECE * D * 12 * HD, 20 * 2**20),
    )(place, *acts, *weights, cos_wide, sin_wide)


def out_kernel(*refs):
    mixed, refs = refs[:4], refs[4:]
    weights, refs = refs[:2], refs[2:]
    outs, weight_s = refs[:4], refs[4]
    for b in range(4):
        for y in range(2):
            weight_s[y_half(y), columns(b, HD)] = piece(weights, b, y)[3]
    for a in range(4):
        act = jnp.concatenate([mixed[b][a] for b in range(4)], axis=1)
        for y in range(2):
            store_any(a, y, dot(act, weight_s[y_half(y), :], 1, 1), outs)


def run_out(mixed, weights):
    outs = pl.pallas_call(
        out_kernel,
        out_shape=ALL_SHAPES,
        in_specs=[VMEM_SPEC] * 6,
        out_specs=[VMEM_SPEC] * 4,
        scratch_shapes=[pltpu.VMEM((D, 4 * HD), BF)],
        compiler_params=params(36),
        cost_estimate=cost(2 * 4 * PIECE * D * 4 * HD, 16 * 2**20),
    )(*mixed, *weights)
    return outs[3], outs[1], outs[2], outs[0]


def input_kernel(*refs):
    back, refs = refs[:4], refs[4:]
    weights, refs = refs[:2], refs[2:]
    outs, weight_s = refs[:4], refs[4]
    for b in range(4):
        for y in range(2):
            for which in range(3):
                weight_s[y_half(y), columns(which * 4 + b, HD)] = piece(weights, b, y)[which]
    for a in range(4):
        act = jnp.concatenate(
            [back[b][which, a] for which in range(3) for b in range(4)], axis=1
        )
        for y in range(2):
            store_any(a, y, dot(act, weight_s[y_half(y), :], 1, 1), outs)


def run_input(back, weights):
    outs = pl.pallas_call(
        input_kernel,
        out_shape=ALL_SHAPES,
        in_specs=[VMEM_SPEC] * 6,
        out_specs=[VMEM_SPEC] * 4,
        scratch_shapes=[pltpu.VMEM((D, 12 * HD), BF)],
        compiler_params=params(40),
        cost_estimate=cost(2 * 4 * PIECE * D * 12 * HD, 20 * 2**20),
    )(*back, *weights)
    return outs[3], outs[1], outs[2], outs[0]


def attended_grad_kernel(*refs):
    acts, refs = refs[:4], refs[4:]
    weights, refs = refs[:2], refs[2:]
    outs, weight_s = refs[:4], refs[4]
    for b in range(4):
        for y in range(2):
            weight_s[y_half(y), columns(b, HD)] = piece(weights, b, y)[3]
    for a in range(4):
        act = acts[a][...]
        value = dot(act, weight_s[...], 1, 0)
        for b in range(4):
            outs[b][a] = value[:, columns(b, HD)].astype(BF)


def run_attended_grad(acts, weights):
    return pl.pallas_call(
        attended_grad_kernel,
        out_shape=[shape((4, PIECE, HD), BF)] * 4,
        in_specs=[VMEM_SPEC] * 6,
        out_specs=[VMEM_SPEC] * 4,
        scratch_shapes=[pltpu.VMEM((D, 4 * HD), BF)],
        compiler_params=params(36),
        cost_estimate=cost(2 * 4 * PIECE * D * 4 * HD, 16 * 2**20),
    )(*acts, *weights)


CHUNK = 256


def up_kernel(count, *refs):
    acts, refs = refs[:count], refs[count:]
    gates, refs = refs[:2], refs[2:]
    ups, refs = refs[:2], refs[2:]
    gating_ref, upward_ref, units_ref = refs
    start = 0
    for act_ref in acts:
        size = act_ref.shape[0]
        rows = slice(start, start + size)
        start += size
        low, high = act_ref[:, y_half(0)], act_ref[:, y_half(1)]
        for b in range(4):
            gate = dot(low, piece(gates, b, 0)[...], 1, 0)
            gate += dot(high, piece(gates, b, 1)[...], 1, 0)
            up = dot(low, piece(ups, b, 0)[...], 1, 0) + dot(high, piece(ups, b, 1)[...], 1, 0)
            gating_ref[b, rows] = gate
            upward_ref[b, rows] = up
            units_ref[b, rows] = (gate * jax.nn.sigmoid(gate) * up).astype(BF)


def run_up(acts, gates, ups):
    rows = sum(act.shape[0] for act in acts)
    width = gates[0].shape[2]
    whole = lambda act: pl.BlockSpec(act.shape, lambda j: (0, 0))
    part = pl.BlockSpec((4, HALF, CHUNK), lambda j: (0, 0, j))
    out = pl.BlockSpec((4, rows, CHUNK), lambda j: (0, 0, j))
    return pl.pallas_call(
        lambda *refs: up_kernel(len(acts), *refs),
        grid=(width // CHUNK,),
        out_shape=[shape((4, rows, width), kind) for kind in (F32, F32, BF)],
        in_specs=[whole(act) for act in acts] + [part] * 4,
        out_specs=[out] * 3,
        compiler_params=params(48),
        cost_estimate=cost(2 * rows * D * 8 * width, 16 * 2**20, 4 * rows * width),
    )(*acts, *gates, *ups)


def down_kernel(kind, units_ref, *refs):
    weights, outs = refs[:2], refs[2:]
    for index in range(len(SUM_BLOCKS[kind])):
        rows = slice(index * PIECE, (index + 1) * PIECE)
        for y in range(2):
            value = dot(units_ref[0, rows], piece(weights, 0, y)[...], 1, 0)
            for b in range(1, 4):
                value += dot(units_ref[b, rows], piece(weights, b, y)[...], 1, 0)
            store_sum(kind, index, y, value, outs)


def run_down(kind, units, weights):
    rows, width = units.shape[1], units.shape[2]
    shapes = SUM_SHAPES[kind]
    return pl.pallas_call(
        lambda *refs: down_kernel(kind, *refs),
        out_shape=shapes,
        in_specs=[VMEM_SPEC] * 3,
        out_specs=[VMEM_SPEC] * len(shapes),
        compiler_params=params(36),
        cost_estimate=cost(2 * rows * D * 4 * width, 12 * 2**20),
    )(units, *weights)


def gated_kernel(count, *refs):
    acts, refs = refs[:count], refs[count:]
    gating_ref, upward_ref, *refs = refs
    weights, refs = refs[:2], refs[2:]
    gate_ref, up_ref = refs
    start = 0
    for act_ref in acts:
        size = act_ref.shape[0]
        rows = slice(start, start + size)
        start += size
        low, high = act_ref[:, y_half(0)], act_ref[:, y_half(1)]
        for b in range(4):
            grad = dot(low, piece(weights, b, 0)[...], 1, 1)
            grad += dot(high, piece(weights, b, 1)[...], 1, 1)
            gate = gating_ref[b, rows]
            sigmoid = jax.nn.sigmoid(gate)
            gate_ref[b, rows] = (
                grad * upward_ref[b, rows] * sigmoid * (1.0 + gate * (1.0 - sigmoid))
            ).astype(BF)
            up_ref[b, rows] = (grad * (gate * sigmoid)).astype(BF)


def run_gated(acts, gating, upward, weights):
    rows, width = gating.shape[1], gating.shape[2]
    return pl.pallas_call(
        lambda *refs: gated_kernel(len(acts), *refs),
        out_shape=[shape((4, rows, width), BF)] * 2,
        in_specs=[VMEM_SPEC] * (len(acts) + 4),
        out_specs=[VMEM_SPEC] * 2,
        compiler_params=params(44),
        cost_estimate=cost(2 * rows * D * 4 * width, 16 * 2**20, 4 * rows * width),
    )(*acts, gating, upward, *weights)


def normed_two_kernel(kind, gate_ref, up_ref, *refs):
    gates, refs = refs[:2], refs[2:]
    ups, refs = refs[:2], refs[2:]
    outs, total_s = refs[:-1], refs[-1]
    step, last = pl.program_id(0), pl.num_programs(0) - 1
    for y in range(2):
        value = dot(gate_ref[0], piece(gates, 0, y)[...], 1, 1)
        for b in range(4):
            if b > 0:
                value += dot(gate_ref[b], piece(gates, b, y)[...], 1, 1)
            value += dot(up_ref[b], piece(ups, b, y)[...], 1, 1)

        @pl.when(step == 0)
        def _():
            total_s[:, y_half(y)] = value

        @pl.when(step == last)
        def _():
            whole = total_s[:, y_half(y)] + value
            for index in range(len(SUM_BLOCKS[kind])):
                rows = slice(index * PIECE, (index + 1) * PIECE)
                store_sum(kind, index, y, whole[rows], outs)


def run_normed_two(kind, gate_low, up_low, gates, ups):
    rows, width = gate_low.shape[1], gate_low.shape[2]
    shapes = SUM_SHAPES[kind]
    low = pl.BlockSpec((4, rows, width // 2), lambda j: (0, 0, j))
    part = pl.BlockSpec((4, HALF, width // 2), lambda j: (0, 0, j))
    return pl.pallas_call(
        lambda *refs: normed_two_kernel(kind, *refs),
        grid=(2,),
        out_shape=shapes,
        in_specs=[low] * 2 + [part] * 4,
        out_specs=[pl.BlockSpec(s.shape, lambda j: (0, 0)) for s in shapes],
        scratch_shapes=[pltpu.VMEM((rows, D), F32)],
        compiler_params=params(48),
        cost_estimate=cost(2 * rows * D * 8 * width, 18 * 2**20),
    )(gate_low, up_low, *gates, *ups)


def wide_grad_kernel(*refs):
    acts, refs = refs[:5], refs[5:]
    lows, refs = refs[:3], refs[3:]
    outs, turned_s = refs[:2], refs[2]

    @pl.when(pl.program_id(1) == 0)
    def _():
        start = 0
        for act_ref in acts:
            size = act_ref.shape[0]
            turned_s[:, start : start + size] = act_ref[...].T
            start += size

    for d in range(2):
        total, start = None, 0
        for low_ref in lows:
            size = low_ref.shape[1]
            value = dot(turned_s[:, start : start + size], low_ref[d], 1, 0)
            total = value if total is None else total + value
            start += size
        outs[d][0, 0] = total.astype(BF)


def run_wide_grad(acts, lows):
    width = lows[0].shape[2]
    return pl.pallas_call(
        wide_grad_kernel,
        grid=(2, 2),
        out_shape=[shape((2, 2, HALF, width), BF)] * 2,
        in_specs=[pl.BlockSpec((act.shape[0], HALF), lambda y, h: (0, y)) for act in acts]
        + [pl.BlockSpec((2, low.shape[1], width), lambda y, h: (h, 0, 0)) for low in lows],
        out_specs=[pl.BlockSpec((1, 1, HALF, width), lambda y, h: (y, h, 0, 0))] * 2,
        scratch_shapes=[pltpu.VMEM((HALF, 4 * PIECE), BF)],
        compiler_params=params(36),
        cost_estimate=cost(2 * 4 * PIECE * D * 4 * width, 16 * 2**20),
    )(*acts, *lows)


def down_grad_kernel(*refs):
    units, refs = refs[:3], refs[3:]
    acts, refs = refs[:5], refs[5:]
    outs, turned_s = refs[:2], refs[2]

    @pl.when(pl.program_id(1) == 0)
    def _():
        start = 0
        for unit_ref in units:
            size = unit_ref.shape[1]
            for d in range(2):
                turned_s[d, :, start : start + size] = unit_ref[d].T
            start += size

    for d in range(2):
        total, start = None, 0
        for act_ref in acts:
            size = act_ref.shape[0]
            value = dot(turned_s[d, :, start : start + size], act_ref[...], 1, 0)
            total = value if total is None else total + value
            start += size
        outs[d][0, 0] = total.astype(BF)


def run_down_grad(units, acts):
    width = units[0].shape[2]
    return pl.pallas_call(
        down_grad_kernel,
        grid=(2, 2),
        out_shape=[shape((2, 2, width, HALF), BF)] * 2,
        in_specs=[pl.BlockSpec((2, unit.shape[1], width), lambda h, y: (h, 0, 0)) for unit in units]
        + [pl.BlockSpec((act.shape[0], HALF), lambda h, y: (0, y)) for act in acts],
        out_specs=[pl.BlockSpec((1, 1, width, HALF), lambda h, y: (y, h, 0, 0))] * 2,
        scratch_shapes=[pltpu.VMEM((2, width, 4 * PIECE), BF)],
        compiler_params=params(36),
        cost_estimate=cost(2 * 4 * PIECE * D * 4 * width, 16 * 2**20),
    )(*units, *acts)


def head_grad_kernel(kinds, *refs):
    acts, refs = refs[:4], refs[4:]
    messages, refs = refs[:4], refs[4:]
    passed, refs = (refs[:2], refs[2:]) if kinds > 1 else (None, refs)
    outs, turned_s, right_s = refs[:2], refs[2], refs[3]
    start = 0
    for act_ref in acts:
        size = act_ref.shape[0]
        turned_s[:, start : start + size] = act_ref[...].T
        start += size

    @pl.when(pl.program_id(0) == 0)
    def _():
        for which in range(kinds):
            for b in range(4):
                for a in range(4):
                    value = messages[b][which, a] if kinds > 1 else messages[b][a]
                    right_s[columns(a, PIECE), columns(which * 4 + b, HD)] = value

    for which in range(kinds):
        value = dot(turned_s[...], right_s[:, columns(which, 4 * HD)], 1, 0)
        for b, (d, h) in enumerate(SLOTS):
            outs[d][0, h, which] = value[:, columns(b, HD)].astype(BF)
    if passed:
        for d in range(2):
            outs[d][0, :, kinds] = passed[d][0, :, 0]


def run_head_grad(kinds, acts, messages, passed=()):
    whole = lambda dims: pl.BlockSpec(dims, lambda y: (0,) * len(dims))
    rows = lambda count: pl.BlockSpec((1, 2, count, HALF, HD), lambda y: (y, 0, 0, 0, 0))
    made = kinds + 1 if passed else kinds
    return pl.pallas_call(
        lambda *refs: head_grad_kernel(kinds, *refs),
        grid=(2,),
        out_shape=[shape((2, 2, made, HALF, HD), BF)] * 2,
        in_specs=[pl.BlockSpec((act.shape[0], HALF), lambda y: (0, y)) for act in acts]
        + [whole(message.shape) for message in messages]
        + [rows(1)] * len(passed),
        out_specs=[rows(made)] * 2,
        scratch_shapes=[
            pltpu.VMEM((HALF, 4 * PIECE), BF),
            pltpu.VMEM((4 * PIECE, kinds * 4 * HD), BF),
        ],
        compiler_params=params(44),
        cost_estimate=cost(2 * 4 * PIECE * D * kinds * 4 * HD, 12 * 2**20),
    )(*acts, *messages, *passed)


def allowed_pairs(starts, query0, key0, shape, query_axis):
    query = query0 + lax.broadcasted_iota(jnp.int32, shape, query_axis)
    key = key0 + lax.broadcasted_iota(jnp.int32, shape, 1 - query_axis)
    first = jnp.zeros(shape, jnp.int32)
    for s in range(CONT):
        first = jnp.where(query >= starts[s], starts[s], first)
    return (key <= query) & ((key < starts[0]) | (key >= first))


def block_bounds(starts, n):
    full = jnp.minimum(n, starts[0] // BLOCK)
    first = jnp.int32(0)
    for s in range(CONT):
        first = jnp.where(n * BLOCK >= starts[s], starts[s], first)
    return full, first


def block_used(starts, first, m):
    return (m * BLOCK < starts[0]) | ((m + 1) * BLOCK > first)


def attention_forward(place_ref, starts_ref, *refs):
    messages, refs = refs[:4], refs[4:]
    outs, refs = refs[:4], refs[4:]
    wide_ref, log_ref, q_s, k_s, v_s, score_s, acc_s, sum_s, max_s = refs
    scale = LOG2E / math.sqrt(HD)
    starts = [starts_ref[s] for s in range(CONT)]
    for b in range(4):
        for a in range(4):
            rows = pl.ds(pl.multiple_of(place_ref[4 * b + a] * PIECE, PIECE), PIECE)
            q_s[rows, :] = messages[b][0, a]
            k_s[rows, :] = messages[b][1, a]
            v_s[rows, :] = messages[b][2, a]

    def one_block(n, carry):
        rows = pl.ds(pl.multiple_of(n * BLOCK, BLOCK), BLOCK)
        full, first = block_bounds(starts, n)
        max_s[...] = jnp.full(max_s.shape, -1e30, F32)
        acc_s[...] = jnp.zeros(acc_s.shape, F32)
        sum_s[...] = jnp.zeros(sum_s.shape, F32)

        def note(scores, m):
            score_s[m] = scores
            top = max_s[...]
            for part in range(BLOCK // HD):
                top = jnp.maximum(top, scores[:, part * HD : (part + 1) * HD])
            max_s[...] = top

        def product(m):
            keys = pl.ds(pl.multiple_of(m * BLOCK, BLOCK), BLOCK)
            return dot(q_s[rows, :], k_s[keys, :], 1, 1)

        @pl.loop(0, full)
        def _(m):
            note(product(m), m)

        @pl.loop(full, n + 1)
        def _(m):
            @pl.when(block_used(starts, first, m))
            def _():
                allowed = allowed_pairs(starts, n * BLOCK, m * BLOCK, (BLOCK, BLOCK), 0)
                note(jnp.where(allowed, product(m), MASKED_SCORE), m)

        highest = jnp.max(max_s[...], axis=1, keepdims=True) * scale

        @pl.loop(0, n + 1)
        def _(m):
            @pl.when(block_used(starts, first, m))
            def _():
                keys = pl.ds(pl.multiple_of(m * BLOCK, BLOCK), BLOCK)
                exponent = jnp.exp2(score_s[m] * scale - highest)
                total = sum_s[...]
                for part in range(BLOCK // HD):
                    total = total + exponent[:, part * HD : (part + 1) * HD]
                sum_s[...] = total
                acc_s[...] += dot(exponent.astype(BF), v_s[keys, :], 1, 0)

        total = jnp.sum(sum_s[...], axis=1, keepdims=True)
        wide_ref[rows, :] = acc_s[...] / total
        log_total = jnp.broadcast_to(highest + jnp.log2(total), (BLOCK, HD))
        log_ref[n] = log_total.T[:8]
        return carry

    lax.fori_loop(0, k_s.shape[0] // BLOCK, one_block, 0)
    for b in range(4):
        for a in range(4):
            rows = pl.ds(pl.multiple_of(place_ref[4 * b + a] * PIECE, PIECE), PIECE)
            outs[b][a] = wide_ref[rows, :].astype(BF)


def attention_backward(place_ref, starts_ref, *refs):
    messages, refs = refs[:4], refs[4:]
    grads, refs = refs[:4], refs[4:]
    wide_ref, log_ref, cos_ref, sin_ref, *refs = refs
    outs, refs = refs[:4], refs[4:]
    q_s, k_s, v_s, g_s, dq_s, dk_s, dv_s = refs
    scale = LOG2E / math.sqrt(HD)
    starts = [starts_ref[s] for s in range(CONT)]
    for b in range(4):
        for a in range(4):
            rows = pl.ds(pl.multiple_of(place_ref[4 * b + a] * PIECE, PIECE), PIECE)
            q_s[rows, :] = messages[b][0, a]
            k_s[rows, :] = messages[b][1, a]
            v_s[rows, :] = messages[b][2, a]
            g_s[rows, :] = grads[b][a]
    dq_s[...] = jnp.zeros(dq_s.shape, F32)
    dk_s[...] = jnp.zeros(dk_s.shape, F32)
    dv_s[...] = jnp.zeros(dv_s.shape, F32)

    def one_block(n, carry):
        rows = pl.ds(pl.multiple_of(n * BLOCK, BLOCK), BLOCK)
        full, first = block_bounds(starts, n)
        crossed = g_s[rows, :].astype(F32) * wide_ref[rows, :]
        row_dot = jnp.sum(crossed.T, axis=0, keepdims=True)
        log_total = log_ref[n][:1]

        def step(m, masked):
            keys = pl.ds(pl.multiple_of(m * BLOCK, BLOCK), BLOCK)
            query, key = q_s[rows, :], k_s[keys, :]
            probability = jnp.exp2(dot(key, query, 1, 1) * scale - log_total)
            if masked:
                allowed = allowed_pairs(starts, n * BLOCK, m * BLOCK, (BLOCK, BLOCK), 1)
                probability = jnp.where(allowed, probability, 0.0)
            prob_grad = dot(v_s[keys, :], g_s[rows, :], 1, 1)
            score_grad = (probability * (prob_grad - row_dot)).astype(BF)
            dv_s[keys, :] += dot(probability.astype(BF), g_s[rows, :], 1, 0)
            dk_s[keys, :] += dot(score_grad, query, 1, 0)
            dq_s[rows, :] += dot(score_grad, key, 0, 0)

        @pl.loop(0, full)
        def _(m):
            step(m, False)

        @pl.loop(full, n + 1)
        def _(m):
            @pl.when(block_used(starts, first, m))
            def _():
                step(m, True)

        return carry

    lax.fori_loop(0, k_s.shape[0] // BLOCK, one_block, 0)
    for b in range(4):
        for a in range(4):
            rows = pl.ds(pl.multiple_of(place_ref[4 * b + a] * PIECE, PIECE), PIECE)
            for which, grad in ((0, dq_s), (1, dk_s)):
                value = grad[rows, :] * (1.0 / math.sqrt(HD))
                turned = value * cos_ref[rows, :] - pltpu.roll(value, HD // 2, 1) * sin_ref[rows, :]
                outs[b][which, a] = turned.astype(BF)
            outs[b][2, a] = dv_s[rows, :].astype(BF)


def run_forward(place, starts, messages):
    tokens = 16 * PIECE
    blocks = tokens // BLOCK
    out_shape = [jax.ShapeDtypeStruct((4, PIECE, HD), BF)] * 4
    out_shape += [
        jax.ShapeDtypeStruct((tokens, HD), F32),
        jax.ShapeDtypeStruct((blocks, 8, BLOCK), F32),
    ]
    return pl.pallas_call(
        attention_forward,
        out_shape=out_shape,
        in_specs=[SMEM_SPEC] * 2 + [VMEM_SPEC] * 4,
        out_specs=[VMEM_SPEC] * 6,
        scratch_shapes=[
            pltpu.VMEM((tokens, HD), BF),
            pltpu.VMEM((tokens, HD), BF),
            pltpu.VMEM((tokens, HD), BF),
            pltpu.VMEM((blocks, BLOCK, BLOCK), F32),
            pltpu.VMEM((BLOCK, HD), F32),
            pltpu.VMEM((BLOCK, HD), F32),
            pltpu.VMEM((BLOCK, HD), F32),
        ],
        compiler_params=pltpu.CompilerParams(vmem_limit_bytes=48 * 2**20),
        cost_estimate=pl.CostEstimate(
            flops=2 * tokens * tokens * HD * 2,
            bytes_accessed=8 * 2**20,
            transcendentals=tokens * tokens // 2,
        ),
    )(place, starts, *messages)


def run_backward(place, starts, messages, grads, wide, log_total, cosine, sine_table):
    tokens = 16 * PIECE
    return pl.pallas_call(
        attention_backward,
        out_shape=[jax.ShapeDtypeStruct((3, 4, PIECE, HD), BF)] * 4,
        in_specs=[SMEM_SPEC] * 2 + [VMEM_SPEC] * 12,
        out_specs=[VMEM_SPEC] * 4,
        scratch_shapes=[pltpu.VMEM((tokens, HD), BF)] * 4 + [pltpu.VMEM((tokens, HD), F32)] * 3,
        compiler_params=pltpu.CompilerParams(vmem_limit_bytes=52 * 2**20),
        cost_estimate=pl.CostEstimate(
            flops=5 * tokens * tokens * HD * 2,
            bytes_accessed=16 * 2**20,
            transcendentals=tokens * tokens // 2,
        ),
    )(place, starts, *messages, *grads, wide, log_total, cosine, sine_table)


def swap_slots(messages):
    return [messages[0], flip_y(messages[1]), flip_near(messages[2]), flip_y_near(messages[3])]


def to_tokens(values):
    return lax.all_to_all(values, "row", split_axis=0, concat_axis=1, tiled=True)


def to_width(values):
    return lax.all_to_all(values, "row", split_axis=1, concat_axis=0, tiled=True)


def square_shards(
    hidden_in,
    teacher,
    valid,
    segment_ids,
    query_weight,
    key_weight,
    value_weight,
    output_weight,
    gate_weight,
    up_weight,
    down_weight,
):
    row, col, dp = lax.axis_index("row"), lax.axis_index("col"), lax.axis_index("dp")
    x, y = row % 2, row // 2
    q = (dp + y) % 2
    own_piece = col * SIDE + row
    segment = segment_ids[0]
    group_tokens = segment.shape[0]
    home_tokens = group_tokens // (SIDE * SIDE)

    def swap_y(values):
        return jnp.where(
            y == 0, values, jnp.concatenate((values[:, HALF:], values[:, :HALF]), axis=1)
        )

    def cut(matrix, at, axis):
        size = matrix.shape[axis] // 4
        return lax.dynamic_slice_in_dim(matrix, (2 * at + q) * size, size, axis)

    def head_cut(at):
        parts = [cut(matrix, at, 1) for matrix in (query_weight, key_weight, value_weight)]
        return jnp.stack(parts + [cut(output_weight, at, 0).T])

    labels = jnp.arange(1, CONT + 1, dtype=jnp.int32)
    starts = jnp.sum((segment[None, :] < labels[:, None]).astype(jnp.int32), axis=1)
    codes = jnp.arange(16, dtype=jnp.int32)
    relative = (
        (codes & 1) + ((codes >> 1) & 1) * 8 + ((codes >> 2) & 1) * 2 + ((codes >> 3) & 1) * 4
    )
    pieces = relative ^ own_piece
    frequency = jnp.power(10000.0, jnp.arange(HD // 2, dtype=F32) * (-2.0 / HD))
    angles = positions(segment).astype(F32)[:, None] * jnp.tile(frequency, 2)[None, :]
    sign = jnp.where(jnp.arange(HD) < HD // 2, -1.0, 1.0)
    cos_wide, sin_wide = jnp.cos(angles), jnp.sin(angles) * sign[None, :]

    heads_x = flip_x(head_cut(1 - x))
    gates_x = flip_x(after(cut(gate_weight, 1 - x, 1), heads_x))
    rows_y = hidden_in.shape[0] // 2
    kept = lax.dynamic_slice_in_dim(hidden_in, y * rows_y, rows_y, 0)
    sent = lax.dynamic_slice_in_dim(hidden_in, (1 - y) * rows_y, rows_y, 0)
    piece_here = jnp.concatenate((kept, flip_y(sent)), axis=1)
    piece_far = flip_far(piece_here)
    piece_x = flip_x(after(piece_here, heads_x))
    piece_far_x = flip_x(piece_far)

    count = after(jnp.sum(valid.astype(F32)), piece_here)
    count = exchanged_sum(count, ("dp", "col"), 2 * SIDE)
    target = to_tokens(after(teacher, piece_x))

    def whole_rows(own, other):
        width = own.shape[1] // 2
        first, second = jnp.where(x == 0, own, other), jnp.where(x == 0, other, own)
        return jnp.concatenate(
            (first[:, :width], second[:, :width], first[:, width:], second[:, width:]), axis=1
        )

    def own_and_x(rows):
        half = rows.shape[0] // 2
        return [lax.dynamic_slice_in_dim(rows, at * half, half, 0) for at in (x, 1 - x)]

    hidden_rows = whole_rows(piece_here, piece_x)
    hidden = own_and_x(hidden_rows)[0].astype(F32)
    acts_here = own_and_x(local_norm(hidden_rows.astype(F32))[0].astype(BF))
    far_rows = whole_rows(piece_far, piece_far_x)
    acts_far = own_and_x(local_norm(far_rows.astype(F32))[0].astype(BF))
    normed_acts = acts_here + acts_far
    heads_tall = ordered(x, head_cut(x), heads_x, 1)
    heads_high = flip_near(heads_tall)
    heads_y = flip_dp_y(heads_tall)
    normed, inverse_one = local_norm(hidden)
    heads_y_high = flip_dp_y(after(heads_high, piece_x, count))
    gates_tall = ordered(x, cut(gate_weight, x, 1), gates_x, 0)
    gates_high = flip_far(after(gates_tall, heads_high, piece_far))
    cos_wide, sin_wide = after((cos_wide, sin_wide), heads_tall)
    heads = both_cores(
        heads_tall, heads_y, heads_high, after(heads_y_high, piece_far, target, cos_wide, sin_wide)
    )
    gates_y = flip_dp_y(after(gates_tall, piece_far_x))

    messages = run_qkv(pieces, normed_acts, heads, cos_wide, sin_wide)
    mlp_x = jnp.stack((cut(up_weight, 1 - x, 1), cut(down_weight, 1 - x, 0)))
    mlp_x = flip_x(after(mlp_x, messages[0]))
    messages = swap_slots(messages)
    messages = after(messages, mlp_x, gates_high, gates_y)

    ups_tall = ordered(x, cut(up_weight, x, 1), after(mlp_x[0], messages), 0)
    ups_high = flip_far(after(ups_tall, gates_high))
    gates_y_high = flip_dp_y(after(gates_high, messages))
    ups_y = flip_dp_y(ups_tall)
    *mixed, wide_mixed, log_total = run_forward(pieces, starts, messages)
    mixed = after(mixed, gates_y_high)
    downs_tall = ordered(x, cut(down_weight, x, 0), after(mlp_x[1], mixed), 1)
    mixed = swap_slots(mixed)
    mixed = after(mixed, ups_high, ups_y)
    gates = both_cores(gates_tall, gates_y, gates_high, gates_y_high, mixed)

    ups_y_high = flip_dp_y(after(ups_high, mixed))
    downs_y = flip_dp_y(after(downs_tall, ups_y_high))
    after_attention = hidden + square_reduce(*run_out(mixed, heads))
    after_attention = after(after_attention, ups_y_high, gates, downs_y)

    normed_two, inverse_two = local_norm(after_attention)
    ups = both_cores(ups_tall, ups_y, ups_high, ups_y_high, normed_two)
    low_two = normed_two.astype(BF)
    up_own = run_up([low_two], gates, ups)
    two_acts = near_gather(low_two, up_own)
    downs_high = flip_far(after(downs_tall, low_two))
    downs_y_high = flip_dp_y(after(downs_high, two_acts[1:3], up_own[2]))
    up_sides = run_up(after(two_acts[1:3], up_own[2]), gates, ups)
    up_far = run_up(after(two_acts[3:], up_sides[2], downs_y_high), gates, ups)
    downs = both_cores(downs_tall, downs_y, downs_high, downs_y_high, two_acts, up_sides[2])
    ups_out = [up_own, up_sides, up_far]
    units = [out[2] for out in ups_out]
    down_far = run_down("far", units[2], downs)
    down_sides = run_down("sides", after(units[1], down_far), downs)
    down_own = run_down("own", after(units[0], down_sides), downs)
    output = after_attention + near_reduce(down_far, down_sides, down_own[0])

    total_count = jnp.maximum(count, 1.0)
    counted_home = lax.dynamic_slice_in_dim(
        valid.astype(F32), row * home_tokens, home_tokens, 0
    )[:, None]
    differ = output - swap_y(target).astype(F32)
    local_loss = jnp.sum(counted_home * (differ * differ)) / D
    all_tokens = group_tokens * lax.axis_size("dp")
    out_grad = counted_home * differ * (all_tokens / total_count)

    low_out = out_grad.astype(BF)
    loss = exchanged_sum(after(local_loss, low_out), ("dp", "row", "col"), 2 * SIDE * SIDE)
    low_own = run_gated([low_out], up_own[0], up_own[1], downs)
    out_acts = near_gather(low_out, low_own)
    low_sides = run_gated(after(out_acts[1:3], low_own), up_sides[0], up_sides[1], downs)
    low_far = run_gated(after(out_acts[3:], low_sides, loss), up_far[0], up_far[1], downs)
    lows = [low_own, low_sides, low_far]
    two_far = run_normed_two("far", *low_far, gates, ups)
    two_sides = run_normed_two("sides", *after(low_sides, two_far), gates, ups)

    first = near_reduce_far(two_far)
    got = near_reduce_sides(first, two_sides)
    two_own = run_normed_two("own", *after(low_own, two_sides, first), gates, ups)
    down_grads = Spread(run_down_grad(after(units, two_own, got[1:3]), out_acts))
    down_core = down_grads.to_core()
    normed_two_grad = near_reduce_end(got, two_own[0])
    middle_grad = out_grad + local_norm_backward(normed_two_grad, normed_two, inverse_two)
    low_middle = middle_grad.astype(BF)
    gate_pair = run_wide_grad(two_acts, after([low[0] for low in lows], low_middle, down_core))
    gate_grads = Spread(gate_pair)
    down_y1 = down_grads.to_y(1)
    layer_output = to_width(swap_y(after(output, low_middle).astype(BF)))
    gate_core = gate_grads.to_core(low_middle)
    down_y0 = down_grads.to_y(0, low_middle)
    up_pair = run_wide_grad(two_acts, after([low[1] for low in lows], gate_pair, down_y1))
    up_grads = Spread(up_pair)
    middle_acts = square_gather(low_middle, gate_pair, up_pair, layer_output)
    middle_acts = after(middle_acts, up_pair, down_y0, layer_output)
    grad_messages = run_attended_grad(middle_acts, heads)
    up_core = up_grads.to_core(grad_messages)
    down_grads.to_high(flip_far, middle_acts[1:3])
    out_pair = run_head_grad(1, after(middle_acts, grad_messages), mixed)
    grad_messages = swap_slots(grad_messages)
    grad_messages = after(grad_messages, up_core, out_pair)
    gate_y1 = gate_grads.to_y(1, grad_messages)
    gate_y0 = gate_grads.to_y(0, grad_messages)
    up_y1 = up_grads.to_y(1, grad_messages)
    back = run_backward(
        pieces, starts, messages, grad_messages, wide_mixed, log_total, cos_wide, sin_wide
    )
    back = after(back, down_grads.high, gate_y1, gate_y0)
    gate_grads.to_high(flip_far, back)
    own_down, send_down = to_x(down_grads.total(back), x, 1)
    down_x = flip_x(send_down)
    back = swap_slots(back)
    back = after(back, down_x, gate_grads.high, up_y1)
    up_y0 = up_grads.to_y(0, back)
    up_grads.to_high(flip_far, back)
    own_gate, send_gate = to_x(gate_grads.total(back), x, 0)
    gate_x = flip_x(send_gate)
    head_pair = run_head_grad(3, normed_acts, back, out_pair)
    head_grads = Spread(head_pair)
    head_core = head_grads.to_core()
    input_sums = run_input(after(back, head_pair), heads)
    input_sums = after(input_sums, head_core)
    head_y1 = head_grads.to_y(1)
    normed_grad = square_reduce(*input_sums, up_grads.high)
    head_y0 = head_grads.to_y(0, head_y1)
    head_grads.to_high(flip_near, head_y1)
    first_mine = jnp.stack((pair_up(own_gate, gate_x, x), pair_up(own_down, down_x, x)))
    first_theirs = flip_dp(after(first_mine, head_y1))
    normed_grad = after(normed_grad, head_y0, head_grads.high, first_theirs)
    input_gradient = middle_grad + local_norm_backward(normed_grad, normed, inverse_one)
    own_head, send_head = to_x(head_grads.total(normed_grad), x, 1)
    own_up, send_up = to_x(up_grads.total(normed_grad), x, 0)
    head_x = flip_x(send_head)
    last_mine = pair_up(own_up, flip_x(send_up), x)
    input_out = to_width(swap_y(input_gradient.astype(BF)))
    last_theirs = flip_dp(after(last_mine, input_out))
    head_mine = pair_up(own_head, head_x, x)
    head_theirs = flip_dp(head_mine)
    mean_loss = loss / total_count

    gate_grad = unite(first_mine[0], first_theirs[0], q, 1)
    down_grad = unite(first_mine[1], first_theirs[1], q, 0)
    up_grad = unite(last_mine, last_theirs, q, 1)
    head_grads = unite(head_mine, head_theirs, q, 2)
    return (
        layer_output,
        mean_loss,
        input_out.astype(F32),
        head_grads[0],
        head_grads[1],
        head_grads[2],
        head_grads[3].T,
        gate_grad,
        up_grad,
        down_grad,
    )


def solution(mesh):
    body = square_shards if fits_square(mesh) else shards
    in_specs = (
        P(("dp", "col"), "row"),
        P(("dp", "col"), "row"),
        P(("dp", "col")),
        P("dp", None),
        P("row", "col"),
        P("row", "col"),
        P("row", "col"),
        P("col", "row"),
        P("row", "col"),
        P("row", "col"),
        P("col", "row"),
    )
    out_specs = (
        P(("dp", "col"), "row"),
        P(),
        P(("dp", "col"), "row"),
        P("row", "col"),
        P("row", "col"),
        P("row", "col"),
        P("col", "row"),
        P("row", "col"),
        P("row", "col"),
        P("col", "row"),
    )
    return jax.shard_map(body, mesh=mesh, in_specs=in_specs, out_specs=out_specs, check_vma=False)
```

```python
import math

import jax
import jax.numpy as jnp
from jax import lax
from jax.experimental import pallas as pl
from jax.experimental.pallas import tpu as pltpu
from jax.sharding import PartitionSpec as P

D = 2048
HD = 128
CONT = 8


EPSILON = 1e-05
MASKED_SCORE = -1e30


def positions(segment):
    labels = jnp.arange(CONT + 1, dtype=jnp.int32)
    onehot = (segment[:, None] == labels[None, :]).astype(jnp.int32)
    counts = jnp.sum(onehot, axis=0)
    starts = jnp.cumsum(counts) - counts
    leading = jnp.sum(onehot * starts[None, :], axis=1)
    indices = jnp.arange(segment.shape[0], dtype=jnp.int32)
    return indices - leading + jnp.where(segment > 0, counts[0], 0)


def rotary(offsets):
    half_width = HD // 2
    frequency = jnp.power(10000.0, jnp.arange(half_width, dtype=jnp.float32) * (-2.0 / HD))
    angles = offsets.astype(jnp.float32)[:, None] * frequency[None, :]
    return (jnp.cos(angles), jnp.sin(angles))


def rotate(values, cosine, sine_table):
    half_width = values.shape[-1] // 2
    leading, trailing = (values[..., :half_width], values[..., half_width:])
    cos_wide = cosine[:, None, :]
    sin_wide = sine_table[:, None, :]
    return jnp.concatenate(
        (leading * cos_wide - trailing * sin_wide, trailing * cos_wide + leading * sin_wide),
        axis=-1,
    )


def unrotate(gradient, cosine, sine_table):
    half_width = gradient.shape[-1] // 2
    leading, trailing = (gradient[..., :half_width], gradient[..., half_width:])
    cos_wide = cosine[:, None, :]
    sin_wide = sine_table[:, None, :]
    return jnp.concatenate(
        (leading * cos_wide + trailing * sin_wide, trailing * cos_wide - leading * sin_wide),
        axis=-1,
    )


def feature_sums(left, right):
    return lax.psum((jnp.sum(left, axis=1), jnp.sum(right, axis=1)), "row")


def normalize(values):
    summed, squared = feature_sums(values, values * values)
    average = (summed / D)[:, None]
    inverse = lax.rsqrt(squared[:, None] / D - average * average + EPSILON)
    return ((values - average) * inverse, inverse)


def norm_backward(gradient, normed, inverse):
    summed, crossed = feature_sums(gradient, gradient * normed)
    return inverse * (gradient - summed[:, None] / D - normed * (crossed[:, None] / D))


def widen(values):
    return lax.all_gather(values, "col", axis=0, tiled=True)


def collect(values):
    return lax.all_gather(values, "row", axis=0, tiled=True)


def row_product(full, matrix, contract):
    return lax.psum_scatter(
        lax.dot_general(
            full, matrix, (((1,), (contract,)), ((), ())), preferred_element_type=jnp.float32
        ),
        "row",
        scatter_dimension=0,
        tiled=True,
    )


def column_product(full, matrix, contract):
    return lax.psum_scatter(
        lax.dot_general(
            full, matrix, (((1,), (contract,)), ((), ())), preferred_element_type=jnp.float32
        ),
        "col",
        scatter_dimension=0,
        tiled=True,
    )


def project_in(gathered, matrix):
    result = row_product(gathered, matrix, 0)
    return result


def project_back(gathered, matrix):
    result = row_product(gathered, matrix, 1)
    return result


def weight_product(left, right):
    return lax.dot_general(
        left, right, (((0,), (0,)), ((), ())), preferred_element_type=jnp.float32
    )


def block_layout(tok_rows):
    blocks = max(1, tok_rows // 512)
    return (blocks, tok_rows // blocks)


def score_maker(key_rows, segment, block):
    key_index = jnp.arange(key_rows.shape[0], dtype=jnp.int32)
    scale = 1.0 / math.sqrt(HD)

    def scores_for(query_block, offset):
        query_index = offset + jnp.arange(block, dtype=jnp.int32)
        query_segment = lax.dynamic_slice_in_dim(segment, offset, block, 0)
        allowed = (key_index[None, :] <= query_index[:, None]) & (
            (segment[None, :] == 0) | (segment[None, :] == query_segment[:, None])
        )
        scores = (
            jnp.einsum("qhd,khd->hqk", query_block, key_rows, preferred_element_type=jnp.float32)
            * scale
        )
        return jnp.where(allowed[None, :, :], scores, MASKED_SCORE)

    return scores_for


def attend(queries, key_rows, value_rows, segment, row_offset):
    tok_rows, heads_here = (queries.shape[0], queries.shape[1])
    blocks, block = block_layout(tok_rows)
    scores_for = score_maker(key_rows, segment, block)
    offsets = row_offset + jnp.arange(blocks, dtype=jnp.int32) * block

    def forward_block(inputs):
        query_block, offset = inputs
        scores = scores_for(query_block, offset)
        highest = jnp.max(scores, axis=-1, keepdims=True)
        exponent = jnp.exp(scores - highest)
        summed = jnp.sum(exponent, axis=-1, keepdims=True)
        probability = (exponent / summed).astype(jnp.bfloat16)
        mixed_block = jnp.einsum(
            "hqk,khd->qhd", probability, value_rows, preferred_element_type=jnp.float32
        )
        return (mixed_block, highest + jnp.log(summed))

    mixed_blocks, log_total = lax.map(
        forward_block, (queries.reshape(blocks, block, heads_here, HD), offsets)
    )
    return (mixed_blocks.reshape(tok_rows, heads_here * HD), log_total)


def attend_back(queries, key_rows, value_rows, segment, row_offset, log_total, attended_grad):
    tok_rows, heads_here = (queries.shape[0], queries.shape[1])
    blocks, block = block_layout(tok_rows)
    scores_for = score_maker(key_rows, segment, block)
    offsets = row_offset + jnp.arange(blocks, dtype=jnp.int32) * block
    scale = 1.0 / math.sqrt(HD)

    def backward_block(carry, inputs):
        key_sum, value_sum = carry
        query_block, grad_block, log_block, offset = inputs
        scores = scores_for(query_block, offset)
        probability = jnp.exp(scores - log_block)
        rounded = probability.astype(jnp.bfloat16)
        prob_grad = jnp.einsum(
            "qhd,khd->hqk", grad_block, value_rows, preferred_element_type=jnp.float32
        )
        row_dot = jnp.sum(probability * prob_grad, axis=-1, keepdims=True)
        score_grad = (probability * (prob_grad - row_dot)).astype(jnp.bfloat16)
        query_grad = (
            jnp.einsum("hqk,khd->qhd", score_grad, key_rows, preferred_element_type=jnp.float32)
            * scale
        )
        key_sum = (
            key_sum
            + jnp.einsum(
                "hqk,qhd->khd", score_grad, query_block, preferred_element_type=jnp.float32
            )
            * scale
        )
        value_sum = value_sum + jnp.einsum(
            "hqk,qhd->khd", rounded, grad_block, preferred_element_type=jnp.float32
        )
        return ((key_sum, value_sum), query_grad)

    empty = jnp.zeros(key_rows.shape, jnp.float32)
    inputs = (
        queries.reshape(blocks, block, heads_here, HD),
        attended_grad.reshape(blocks, block, heads_here, HD),
        log_total,
        offsets,
    )
    (key_sum, value_sum), query_grads = lax.scan(backward_block, (empty, empty), inputs)
    return (query_grads.reshape(tok_rows, heads_here, HD), key_sum, value_sum)


def shards(
    hidden_in,
    teacher,
    valid,
    segment_ids,
    query_weight,
    key_weight,
    value_weight,
    output_weight,
    gate_weight,
    up_weight,
    down_weight,
):
    row_devices = lax.axis_size("row")
    col_devices = lax.axis_size("col")
    tok_cols = hidden_in.shape[0]
    group_tokens = tok_cols * col_devices
    tok_rows = group_tokens // row_devices
    query_width = query_weight.shape[1]
    heads_here = query_width // HD
    unit_width = gate_weight.shape[1]
    segment = segment_ids[0]
    row_offset = lax.axis_index("row") * tok_rows
    cosine_all, sine_all = rotary(positions(segment))
    cosine = lax.dynamic_slice_in_dim(cosine_all, row_offset, tok_rows, 0)
    sine_table = lax.dynamic_slice_in_dim(sine_all, row_offset, tok_rows, 0)
    counted = valid.astype(jnp.float32)
    total_count = jnp.maximum(lax.psum(jnp.sum(counted), ("dp", "col")), 1.0)
    hidden = hidden_in.astype(jnp.float32)
    normed, inverse_one = normalize(hidden)
    normed_wide = widen(normed.astype(jnp.bfloat16))
    attn_weights = jnp.concatenate((query_weight, key_weight, value_weight), axis=1)
    projected = project_in(normed_wide, attn_weights)
    queries = rotate(
        projected[:, :query_width].reshape(tok_rows, heads_here, HD), cosine, sine_table
    ).astype(jnp.bfloat16)
    key_local = rotate(
        projected[:, query_width : 2 * query_width].reshape(tok_rows, heads_here, HD),
        cosine,
        sine_table,
    )
    key_local = key_local.reshape(tok_rows, query_width).astype(jnp.bfloat16)
    value_local = projected[:, 2 * query_width :].astype(jnp.bfloat16)
    key_flat, value_flat = (
        lax.all_gather(key_local, "row", axis=0, tiled=True),
        lax.all_gather(value_local, "row", axis=0, tiled=True),
    )
    key_rows = key_flat.reshape(group_tokens, heads_here, HD)
    value_rows = value_flat.reshape(group_tokens, heads_here, HD)
    attended, log_total = attend(queries, key_rows, value_rows, segment, row_offset)
    attended_wide = collect(attended.astype(jnp.bfloat16))
    after_attention = hidden + column_product(attended_wide, output_weight, 0)
    normed_two, inverse_two = normalize(after_attention)
    normed_two_wide = widen(normed_two.astype(jnp.bfloat16))
    mlp_weights = jnp.concatenate((gate_weight, up_weight), axis=1)
    gated = project_in(normed_two_wide, mlp_weights)
    gating = gated[:, :unit_width]
    upward = gated[:, unit_width:]
    sigmoid = jax.nn.sigmoid(gating)
    activated = gating * sigmoid
    units_wide = collect((activated * upward).astype(jnp.bfloat16))
    output = after_attention + column_product(units_wide, down_weight, 0)
    differ = output - teacher.astype(jnp.float32)
    local_loss = jnp.sum(counted[:, None] * (differ * differ)) / D
    all_tokens = group_tokens * lax.axis_size("dp")
    out_grad = counted[:, None] * differ * (all_tokens / total_count)
    out_wide = widen(out_grad.astype(jnp.bfloat16))
    units_grad = project_back(out_wide, down_weight)
    down_grad = weight_product(units_wide, out_wide)
    gating_grad = units_grad * upward * sigmoid * (1.0 + gating * (1.0 - sigmoid))
    upward_grad = units_grad * activated
    gated_wide = collect(jnp.concatenate((gating_grad, upward_grad), axis=1).astype(jnp.bfloat16))
    mlp_grads = weight_product(normed_two_wide, gated_wide)
    normed_two_grad = column_product(gated_wide, mlp_weights, 1)
    middle_grad = out_grad + norm_backward(normed_two_grad, normed_two, inverse_two)
    middle_wide = widen(middle_grad.astype(jnp.bfloat16))
    attended_grad = project_back(middle_wide, output_weight).astype(jnp.bfloat16)
    output_grad_sum = weight_product(attended_wide, middle_wide)
    query_grad, key_sum, value_sum = attend_back(
        queries, key_rows, value_rows, segment, row_offset, log_total, attended_grad
    )
    key_grad, value_grad = (
        lax.psum_scatter(
            key_sum.reshape(group_tokens, query_width), "row", scatter_dimension=0, tiled=True
        ),
        lax.psum_scatter(
            value_sum.reshape(group_tokens, query_width), "row", scatter_dimension=0, tiled=True
        ),
    )
    query_pre = unrotate(query_grad, cosine, sine_table).reshape(tok_rows, query_width)
    key_pre = unrotate(key_grad.reshape(tok_rows, heads_here, HD), cosine, sine_table).reshape(
        tok_rows, query_width
    )
    projected_wide = collect(
        jnp.concatenate((query_pre, key_pre, value_grad), axis=1).astype(jnp.bfloat16)
    )
    attn_grads = weight_product(normed_wide, projected_wide)
    normed_grad = column_product(projected_wide, attn_weights, 1)
    input_gradient = middle_grad + norm_backward(normed_grad, normed, inverse_one)
    summed_grads = (
        lax.psum(attn_grads[:, :query_width].astype(jnp.bfloat16), "dp").astype(jnp.float32),
        lax.psum(attn_grads[:, query_width : 2 * query_width].astype(jnp.bfloat16), "dp").astype(
            jnp.float32
        ),
        lax.psum(attn_grads[:, 2 * query_width :].astype(jnp.bfloat16), "dp").astype(jnp.float32),
        lax.psum(output_grad_sum.astype(jnp.bfloat16), "dp").astype(jnp.float32),
        lax.psum(mlp_grads[:, :unit_width].astype(jnp.bfloat16), "dp").astype(jnp.float32),
        lax.psum(mlp_grads[:, unit_width:].astype(jnp.bfloat16), "dp").astype(jnp.float32),
        lax.psum(down_grad.astype(jnp.bfloat16), "dp").astype(jnp.float32),
    )
    mean_loss = lax.psum(local_loss, ("dp", "row", "col")) / total_count
    return (
        output.astype(jnp.bfloat16),
        mean_loss.reshape(1),
        input_gradient,
        summed_grads[0],
        summed_grads[1],
        summed_grads[2],
        summed_grads[3],
        summed_grads[4],
        summed_grads[5],
        summed_grads[6],
    )


BF = jnp.bfloat16
F32 = jnp.float32
LOG2E = 1.4426950408889634
SIDE = 4
HALF = D // 2
PIECE = 256
BLOCK = 512
SLOTS = [(d, h) for h in range(2) for d in range(2)]


def fits_square(mesh):
    return mesh.shape["dp"] == 2 and mesh.shape["row"] == SIDE and mesh.shape["col"] == SIDE


def flip(values, axis, bit):
    return lax.ppermute(values, axis, [(i, i ^ bit) for i in range(SIDE)])


def flip_x(values):
    return flip(values, "row", 1)


def flip_y(values):
    return flip(values, "row", 2)


def flip_far(values):
    return flip(values, "col", 2)


def flip_near(values):
    return flip(values, "col", 1)


def flip_y_near(values):
    pairs = [
        (r * SIDE + c, (r ^ 2) * SIDE + (c ^ 1)) for r in range(SIDE) for c in range(SIDE)
    ]
    return lax.ppermute(values, ("row", "col"), pairs)


def flip_z(values):
    return flip(values, "col", 3)


def flip_dp(values):
    return lax.ppermute(values, "dp", [(0, 1), (1, 0)])


def flip_dp_y(values):
    pairs = [(g * SIDE + r, (1 - g) * SIDE + (r ^ 2)) for g in range(2) for r in range(SIDE)]
    return lax.ppermute(values, ("dp", "row"), pairs)


def near_gather(block, *events):
    half = block.shape[0] // 2
    by_x, by_z = flip_x(block), flip_near(block)
    next_x, next_z = after((by_x, by_z), *events)
    return [block, by_x, by_z, flip_near(next_x[:half]), flip_x(next_z[half:])]


def near_reduce(far, sides, own):
    first = near_reduce_far(far)
    return near_reduce_end(near_reduce_sides(first, sides), own)


def near_reduce_far(far):
    return flip_near(far[0]), flip_x(far[1])


def near_reduce_sides(first, sides):
    far_top, far_bottom = first
    x_top, x_bottom, z_top, z_bottom = sides
    return (
        flip_x((x_top + wide(far_top)).astype(BF)),
        flip_x(x_bottom),
        flip_near(z_top),
        flip_near((z_bottom + wide(far_bottom)).astype(BF)),
    )


def near_reduce_end(got, own):
    x_top, x_bottom, z_top, z_bottom = got
    half = x_top.shape[0]
    top = own[:half] + wide(x_top) + wide(z_top)
    bottom = own[half:] + wide(x_bottom) + wide(z_bottom)
    return jnp.concatenate((top, bottom), axis=0)


def square_gather(block, *events):
    by_z, by_x = flip_far(block), flip_x(block)
    return [block, by_x, by_z, flip_x(after(by_z, *events) if events else by_z)]


def square_reduce(far, by_x, by_z, own, *events):
    got_far = flip_x(far)
    got_far = after(got_far, *events) if events else got_far
    got_x = flip_x(after(by_x, got_far))
    got_z = flip_far((by_z + wide(got_far)).astype(BF))
    return own + wide(got_x) + wide(got_z)


def ordered(flag, own, other, axis):
    return jnp.where(
        flag == 0,
        jnp.concatenate((own, other), axis=axis),
        jnp.concatenate((other, own), axis=axis),
    )


def after(values, *events):
    return lax.optimization_barrier((values, events))[0]


def both_cores(tall, by_y, high, by_y_high, *events):
    own = jnp.stack((tall, by_y, high, by_y_high))
    return own, flip_dp(after(own, *events) if events else own)


def piece(pair, slot, y):
    return pair[slot % 2].at[2 * (slot // 2) + y]


def wide(values):
    return values.astype(F32)


class Spread:
    def __init__(self, grads):
        self.keep, self.send = grads

    def to_core(self, *events):
        self.got = flip_dp(after(self.send, *events))
        return self.got

    def here(self, y, h):
        return wide(self.keep[y, h]) + wide(self.got[y, h])

    def to_y(self, h, *events):
        by_y = flip_dp_y(after(self.here(1, h).astype(BF), *events))
        setattr(self, "by_y%d" % h, by_y)
        return by_y

    def to_high(self, flip_z, *events):
        send = (self.here(0, 1) + wide(self.by_y1)).astype(BF)
        self.high = flip_z(after(send, *events))
        return self.high

    def total(self, *events):
        value = self.here(0, 0) + wide(self.by_y0) + wide(self.high)
        return after(value.astype(BF), *events) if events else value.astype(BF)


def to_x(total, x, axis):
    size = total.shape[axis] // 2
    own = lax.dynamic_slice_in_dim(total, x * size, size, axis)
    return own, lax.dynamic_slice_in_dim(total, (1 - x) * size, size, axis)


def pair_up(own, by_x, x):
    return jnp.where(x == 0, jnp.stack((own, by_x)), jnp.stack((by_x, own)))


def unite(mine, theirs, q, axis):
    parts = []
    for at in range(2):
        parts += [jnp.where(q == 0, mine[at], theirs[at]), jnp.where(q == 0, theirs[at], mine[at])]
    return jnp.concatenate(parts, axis=axis).astype(F32)


def exchanged_sum(value, axes, count):
    tiles = jnp.broadcast_to(value, (count, 8, HD))
    tiles = lax.all_to_all(tiles, axes, split_axis=0, concat_axis=0, tiled=True)
    return jnp.sum(tiles[:, 0, 0]).reshape(1)


def local_norm(values):
    average = jnp.mean(values, axis=1, keepdims=True)
    square = jnp.mean(values * values, axis=1, keepdims=True)
    inverse = lax.rsqrt(square - average * average + EPSILON)
    return ((values - average) * inverse, inverse)


def local_norm_backward(gradient, normed, inverse):
    average = jnp.mean(gradient, axis=1, keepdims=True)
    crossed = jnp.mean(gradient * normed, axis=1, keepdims=True)
    return inverse * (gradient - average - normed * crossed)


def dot(left, right, a, b):
    return lax.dot_general(left, right, (((a,), (b,)), ((), ())), preferred_element_type=F32)


SMEM_SPEC = pl.BlockSpec(memory_space=pltpu.SMEM)
VMEM_SPEC = pl.BlockSpec(memory_space=pltpu.VMEM)


def shape(dims, kind):
    return jax.ShapeDtypeStruct(dims, kind)


def params(megabytes):
    return pltpu.CompilerParams(vmem_limit_bytes=megabytes * 2**20)


def cost(flops, moved, transcendentals=0):
    return pl.CostEstimate(
        flops=int(flops), bytes_accessed=int(moved), transcendentals=int(transcendentals)
    )


def y_half(y):
    return slice(y * HALF, (y + 1) * HALF)


def columns(index, width):
    return slice(index * width, (index + 1) * width)


FAR_SHAPES = [shape((PIECE // 2, D), BF)] * 2
SIDE_SHAPES = [
    shape((PIECE, D), BF),
    shape((PIECE // 2, D), F32),
    shape((PIECE // 2, D), F32),
]
OWN_SHAPES = [shape((PIECE, D), F32)]
NEAR_SHAPES = [
    shape((PIECE // 2, D), F32),
    shape((PIECE // 2, D), BF),
    shape((PIECE // 2, D), BF),
    shape((PIECE // 2, D), F32),
]
SUM_SHAPES = {"far": FAR_SHAPES, "sides": NEAR_SHAPES, "own": OWN_SHAPES}
SUM_BLOCKS = {"far": (3,), "sides": (1, 2), "own": (0,)}


def store_halves(part, value, outs):
    half = PIECE // 2
    for low in range(2):
        rows = value[low * half : (low + 1) * half]
        outs[low][:, y_half(part)] = rows.astype(outs[low].dtype)


def store_sum(kind, index, part, value, outs):
    if kind == "own":
        outs[0][:, y_half(part)] = value
    else:
        store_halves(part, value, outs[2 * index : 2 * index + 2])


ALL_SHAPES = [shape((PIECE, D), kind) for kind in (F32, BF, F32, BF)]


def store_any(a, part, value, outs):
    outs[a][:, y_half(part)] = value.astype(outs[a].dtype)


def qkv_kernel(place_ref, *refs):
    acts, refs = refs[:4], refs[4:]
    weights, refs = refs[:2], refs[2:]
    cos_ref, sin_ref, *refs = refs
    outs, weight_s = refs[:4], refs[4]
    for b in range(4):
        for y in range(2):
            for which in range(3):
                weight_s[y_half(y), columns(which * 4 + b, HD)] = piece(weights, b, y)[which]
    for a in range(4):
        rows = pl.ds(pl.multiple_of(place_ref[a] * PIECE, PIECE), PIECE)
        cos_block, sin_block = cos_ref[rows, :], sin_ref[rows, :]
        act = acts[a][...]
        projected = dot(act, weight_s[...], 1, 0)
        for which in range(3):
            for b in range(4):
                tile = projected[:, columns(which * 4 + b, HD)]
                if which < 2:
                    tile = tile * cos_block + pltpu.roll(tile, HD // 2, 1) * sin_block
                outs[b][which, a] = tile.astype(BF)


def run_qkv(place, acts, weights, cos_wide, sin_wide):
    return pl.pallas_call(
        qkv_kernel,
        out_shape=[shape((3, 4, PIECE, HD), BF)] * 4,
        in_specs=[SMEM_SPEC] + [VMEM_SPEC] * 8,
        out_specs=[VMEM_SPEC] * 4,
        scratch_shapes=[pltpu.VMEM((D, 12 * HD), BF)],
        compiler_params=params(40),
        cost_estimate=cost(2 * 4 * PIECE * D * 12 * HD, 20 * 2**20),
    )(place, *acts, *weights, cos_wide, sin_wide)


def out_kernel(*refs):
    mixed, refs = refs[:4], refs[4:]
    weights, refs = refs[:2], refs[2:]
    outs, weight_s = refs[:4], refs[4]
    for b in range(4):
        for y in range(2):
            weight_s[y_half(y), columns(b, HD)] = piece(weights, b, y)[3]
    for a in range(4):
        act = jnp.concatenate([mixed[b][a] for b in range(4)], axis=1)
        for y in range(2):
            store_any(a, y, dot(act, weight_s[y_half(y), :], 1, 1), outs)


def run_out(mixed, weights):
    outs = pl.pallas_call(
        out_kernel,
        out_shape=ALL_SHAPES,
        in_specs=[VMEM_SPEC] * 6,
        out_specs=[VMEM_SPEC] * 4,
        scratch_shapes=[pltpu.VMEM((D, 4 * HD), BF)],
        compiler_params=params(36),
        cost_estimate=cost(2 * 4 * PIECE * D * 4 * HD, 16 * 2**20),
    )(*mixed, *weights)
    return outs[3], outs[1], outs[2], outs[0]


def input_kernel(*refs):
    back, refs = refs[:4], refs[4:]
    weights, refs = refs[:2], refs[2:]
    outs, weight_s = refs[:4], refs[4]
    for b in range(4):
        for y in range(2):
            for which in range(3):
                weight_s[y_half(y), columns(which * 4 + b, HD)] = piece(weights, b, y)[which]
    for a in range(4):
        act = jnp.concatenate(
            [back[b][which, a] for which in range(3) for b in range(4)], axis=1
        )
        for y in range(2):
            store_any(a, y, dot(act, weight_s[y_half(y), :], 1, 1), outs)


def run_input(back, weights):
    outs = pl.pallas_call(
        input_kernel,
        out_shape=ALL_SHAPES,
        in_specs=[VMEM_SPEC] * 6,
        out_specs=[VMEM_SPEC] * 4,
        scratch_shapes=[pltpu.VMEM((D, 12 * HD), BF)],
        compiler_params=params(40),
        cost_estimate=cost(2 * 4 * PIECE * D * 12 * HD, 20 * 2**20),
    )(*back, *weights)
    return outs[3], outs[1], outs[2], outs[0]


def attended_grad_kernel(*refs):
    acts, refs = refs[:4], refs[4:]
    weights, refs = refs[:2], refs[2:]
    outs, weight_s = refs[:4], refs[4]
    for b in range(4):
        for y in range(2):
            weight_s[y_half(y), columns(b, HD)] = piece(weights, b, y)[3]
    for a in range(4):
        act = acts[a][...]
        value = dot(act, weight_s[...], 1, 0)
        for b in range(4):
            outs[b][a] = value[:, columns(b, HD)].astype(BF)


def run_attended_grad(acts, weights):
    return pl.pallas_call(
        attended_grad_kernel,
        out_shape=[shape((4, PIECE, HD), BF)] * 4,
        in_specs=[VMEM_SPEC] * 6,
        out_specs=[VMEM_SPEC] * 4,
        scratch_shapes=[pltpu.VMEM((D, 4 * HD), BF)],
        compiler_params=params(36),
        cost_estimate=cost(2 * 4 * PIECE * D * 4 * HD, 16 * 2**20),
    )(*acts, *weights)


CHUNK = 256


def up_kernel(count, *refs):
    acts, refs = refs[:count], refs[count:]
    gates, refs = refs[:2], refs[2:]
    ups, refs = refs[:2], refs[2:]
    gating_ref, upward_ref, units_ref = refs
    start = 0
    for act_ref in acts:
        size = act_ref.shape[0]
        rows = slice(start, start + size)
        start += size
        low, high = act_ref[:, y_half(0)], act_ref[:, y_half(1)]
        for b in range(4):
            gate = dot(low, piece(gates, b, 0)[...], 1, 0)
            gate += dot(high, piece(gates, b, 1)[...], 1, 0)
            up = dot(low, piece(ups, b, 0)[...], 1, 0) + dot(high, piece(ups, b, 1)[...], 1, 0)
            gating_ref[b, rows] = gate
            upward_ref[b, rows] = up
            units_ref[b, rows] = (gate * jax.nn.sigmoid(gate) * up).astype(BF)


def run_up(acts, gates, ups):
    rows = sum(act.shape[0] for act in acts)
    width = gates[0].shape[2]
    whole = lambda act: pl.BlockSpec(act.shape, lambda j: (0, 0))
    part = pl.BlockSpec((4, HALF, CHUNK), lambda j: (0, 0, j))
    out = pl.BlockSpec((4, rows, CHUNK), lambda j: (0, 0, j))
    return pl.pallas_call(
        lambda *refs: up_kernel(len(acts), *refs),
        grid=(width // CHUNK,),
        out_shape=[shape((4, rows, width), kind) for kind in (F32, F32, BF)],
        in_specs=[whole(act) for act in acts] + [part] * 4,
        out_specs=[out] * 3,
        compiler_params=params(48),
        cost_estimate=cost(2 * rows * D * 8 * width, 16 * 2**20, 4 * rows * width),
    )(*acts, *gates, *ups)


def down_kernel(kind, units_ref, *refs):
    weights, outs = refs[:2], refs[2:]
    for index in range(len(SUM_BLOCKS[kind])):
        rows = slice(index * PIECE, (index + 1) * PIECE)
        for y in range(2):
            value = dot(units_ref[0, rows], piece(weights, 0, y)[...], 1, 0)
            for b in range(1, 4):
                value += dot(units_ref[b, rows], piece(weights, b, y)[...], 1, 0)
            store_sum(kind, index, y, value, outs)


def run_down(kind, units, weights):
    rows, width = units.shape[1], units.shape[2]
    shapes = SUM_SHAPES[kind]
    return pl.pallas_call(
        lambda *refs: down_kernel(kind, *refs),
        out_shape=shapes,
        in_specs=[VMEM_SPEC] * 3,
        out_specs=[VMEM_SPEC] * len(shapes),
        compiler_params=params(36),
        cost_estimate=cost(2 * rows * D * 4 * width, 12 * 2**20),
    )(units, *weights)


def gated_kernel(count, *refs):
    acts, refs = refs[:count], refs[count:]
    gating_ref, upward_ref, *refs = refs
    weights, refs = refs[:2], refs[2:]
    gate_ref, up_ref = refs
    start = 0
    for act_ref in acts:
        size = act_ref.shape[0]
        rows = slice(start, start + size)
        start += size
        low, high = act_ref[:, y_half(0)], act_ref[:, y_half(1)]
        for b in range(4):
            grad = dot(low, piece(weights, b, 0)[...], 1, 1)
            grad += dot(high, piece(weights, b, 1)[...], 1, 1)
            gate = gating_ref[b, rows]
            sigmoid = jax.nn.sigmoid(gate)
            gate_ref[b, rows] = (
                grad * upward_ref[b, rows] * sigmoid * (1.0 + gate * (1.0 - sigmoid))
            ).astype(BF)
            up_ref[b, rows] = (grad * (gate * sigmoid)).astype(BF)


def run_gated(acts, gating, upward, weights):
    rows, width = gating.shape[1], gating.shape[2]
    return pl.pallas_call(
        lambda *refs: gated_kernel(len(acts), *refs),
        out_shape=[shape((4, rows, width), BF)] * 2,
        in_specs=[VMEM_SPEC] * (len(acts) + 4),
        out_specs=[VMEM_SPEC] * 2,
        compiler_params=params(44),
        cost_estimate=cost(2 * rows * D * 4 * width, 16 * 2**20, 4 * rows * width),
    )(*acts, gating, upward, *weights)


def normed_two_kernel(kind, gate_ref, up_ref, *refs):
    gates, refs = refs[:2], refs[2:]
    ups, refs = refs[:2], refs[2:]
    outs, total_s = refs[:-1], refs[-1]
    step, last = pl.program_id(0), pl.num_programs(0) - 1
    for y in range(2):
        value = dot(gate_ref[0], piece(gates, 0, y)[...], 1, 1)
        for b in range(4):
            if b > 0:
                value += dot(gate_ref[b], piece(gates, b, y)[...], 1, 1)
            value += dot(up_ref[b], piece(ups, b, y)[...], 1, 1)

        @pl.when(step == 0)
        def _():
            total_s[:, y_half(y)] = value

        @pl.when(step == last)
        def _():
            whole = total_s[:, y_half(y)] + value
            for index in range(len(SUM_BLOCKS[kind])):
                rows = slice(index * PIECE, (index + 1) * PIECE)
                store_sum(kind, index, y, whole[rows], outs)


def run_normed_two(kind, gate_low, up_low, gates, ups):
    rows, width = gate_low.shape[1], gate_low.shape[2]
    shapes = SUM_SHAPES[kind]
    low = pl.BlockSpec((4, rows, width // 2), lambda j: (0, 0, j))
    part = pl.BlockSpec((4, HALF, width // 2), lambda j: (0, 0, j))
    return pl.pallas_call(
        lambda *refs: normed_two_kernel(kind, *refs),
        grid=(2,),
        out_shape=shapes,
        in_specs=[low] * 2 + [part] * 4,
        out_specs=[pl.BlockSpec(s.shape, lambda j: (0, 0)) for s in shapes],
        scratch_shapes=[pltpu.VMEM((rows, D), F32)],
        compiler_params=params(48),
        cost_estimate=cost(2 * rows * D * 8 * width, 18 * 2**20),
    )(gate_low, up_low, *gates, *ups)


def wide_grad_kernel(*refs):
    acts, refs = refs[:5], refs[5:]
    lows, refs = refs[:3], refs[3:]
    outs, turned_s = refs[:2], refs[2]

    @pl.when(pl.program_id(1) == 0)
    def _():
        start = 0
        for act_ref in acts:
            size = act_ref.shape[0]
            turned_s[:, start : start + size] = act_ref[...].T
            start += size

    for d in range(2):
        total, start = None, 0
        for low_ref in lows:
            size = low_ref.shape[1]
            value = dot(turned_s[:, start : start + size], low_ref[d], 1, 0)
            total = value if total is None else total + value
            start += size
        outs[d][0, 0] = total.astype(BF)


def run_wide_grad(acts, lows):
    width = lows[0].shape[2]
    return pl.pallas_call(
        wide_grad_kernel,
        grid=(2, 2),
        out_shape=[shape((2, 2, HALF, width), BF)] * 2,
        in_specs=[pl.BlockSpec((act.shape[0], HALF), lambda y, h: (0, y)) for act in acts]
        + [pl.BlockSpec((2, low.shape[1], width), lambda y, h: (h, 0, 0)) for low in lows],
        out_specs=[pl.BlockSpec((1, 1, HALF, width), lambda y, h: (y, h, 0, 0))] * 2,
        scratch_shapes=[pltpu.VMEM((HALF, 4 * PIECE), BF)],
        compiler_params=params(36),
        cost_estimate=cost(2 * 4 * PIECE * D * 4 * width, 16 * 2**20),
    )(*acts, *lows)


def down_grad_kernel(*refs):
    units, refs = refs[:3], refs[3:]
    acts, refs = refs[:5], refs[5:]
    outs, turned_s = refs[:2], refs[2]

    @pl.when(pl.program_id(1) == 0)
    def _():
        start = 0
        for unit_ref in units:
            size = unit_ref.shape[1]
            for d in range(2):
                turned_s[d, :, start : start + size] = unit_ref[d].T
            start += size

    for d in range(2):
        total, start = None, 0
        for act_ref in acts:
            size = act_ref.shape[0]
            value = dot(turned_s[d, :, start : start + size], act_ref[...], 1, 0)
            total = value if total is None else total + value
            start += size
        outs[d][0, 0] = total.astype(BF)


def run_down_grad(units, acts):
    width = units[0].shape[2]
    return pl.pallas_call(
        down_grad_kernel,
        grid=(2, 2),
        out_shape=[shape((2, 2, width, HALF), BF)] * 2,
        in_specs=[pl.BlockSpec((2, unit.shape[1], width), lambda h, y: (h, 0, 0)) for unit in units]
        + [pl.BlockSpec((act.shape[0], HALF), lambda h, y: (0, y)) for act in acts],
        out_specs=[pl.BlockSpec((1, 1, width, HALF), lambda h, y: (y, h, 0, 0))] * 2,
        scratch_shapes=[pltpu.VMEM((2, width, 4 * PIECE), BF)],
        compiler_params=params(36),
        cost_estimate=cost(2 * 4 * PIECE * D * 4 * width, 16 * 2**20),
    )(*units, *acts)


def head_grad_kernel(kinds, *refs):
    acts, refs = refs[:4], refs[4:]
    messages, refs = refs[:4], refs[4:]
    passed, refs = (refs[:2], refs[2:]) if kinds > 1 else (None, refs)
    outs, turned_s, right_s = refs[:2], refs[2], refs[3]
    start = 0
    for act_ref in acts:
        size = act_ref.shape[0]
        turned_s[:, start : start + size] = act_ref[...].T
        start += size

    @pl.when(pl.program_id(0) == 0)
    def _():
        for which in range(kinds):
            for b in range(4):
                for a in range(4):
                    value = messages[b][which, a] if kinds > 1 else messages[b][a]
                    right_s[columns(a, PIECE), columns(which * 4 + b, HD)] = value

    for which in range(kinds):
        value = dot(turned_s[...], right_s[:, columns(which, 4 * HD)], 1, 0)
        for b, (d, h) in enumerate(SLOTS):
            outs[d][0, h, which] = value[:, columns(b, HD)].astype(BF)
    if passed:
        for d in range(2):
            outs[d][0, :, kinds] = passed[d][0, :, 0]


def run_head_grad(kinds, acts, messages, passed=()):
    whole = lambda dims: pl.BlockSpec(dims, lambda y: (0,) * len(dims))
    rows = lambda count: pl.BlockSpec((1, 2, count, HALF, HD), lambda y: (y, 0, 0, 0, 0))
    made = kinds + 1 if passed else kinds
    return pl.pallas_call(
        lambda *refs: head_grad_kernel(kinds, *refs),
        grid=(2,),
        out_shape=[shape((2, 2, made, HALF, HD), BF)] * 2,
        in_specs=[pl.BlockSpec((act.shape[0], HALF), lambda y: (0, y)) for act in acts]
        + [whole(message.shape) for message in messages]
        + [rows(1)] * len(passed),
        out_specs=[rows(made)] * 2,
        scratch_shapes=[
            pltpu.VMEM((HALF, 4 * PIECE), BF),
            pltpu.VMEM((4 * PIECE, kinds * 4 * HD), BF),
        ],
        compiler_params=params(44),
        cost_estimate=cost(2 * 4 * PIECE * D * kinds * 4 * HD, 12 * 2**20),
    )(*acts, *messages, *passed)


def allowed_pairs(starts, query0, key0, shape, query_axis):
    query = query0 + lax.broadcasted_iota(jnp.int32, shape, query_axis)
    key = key0 + lax.broadcasted_iota(jnp.int32, shape, 1 - query_axis)
    first = jnp.zeros(shape, jnp.int32)
    for s in range(CONT):
        first = jnp.where(query >= starts[s], starts[s], first)
    return (key <= query) & ((key < starts[0]) | (key >= first))


def block_bounds(starts, n):
    full = jnp.minimum(n, starts[0] // BLOCK)
    first = jnp.int32(0)
    for s in range(CONT):
        first = jnp.where(n * BLOCK >= starts[s], starts[s], first)
    return full, first


def block_used(starts, first, m):
    return (m * BLOCK < starts[0]) | ((m + 1) * BLOCK > first)


def attention_forward(place_ref, starts_ref, *refs):
    messages, refs = refs[:4], refs[4:]
    outs, refs = refs[:4], refs[4:]
    wide_ref, log_ref, q_s, k_s, v_s, score_s, acc_s, sum_s, max_s = refs
    scale = LOG2E / math.sqrt(HD)
    starts = [starts_ref[s] for s in range(CONT)]
    for b in range(4):
        for a in range(4):
            rows = pl.ds(pl.multiple_of(place_ref[4 * b + a] * PIECE, PIECE), PIECE)
            q_s[rows, :] = messages[b][0, a]
            k_s[rows, :] = messages[b][1, a]
            v_s[rows, :] = messages[b][2, a]

    def one_block(n, carry):
        rows = pl.ds(pl.multiple_of(n * BLOCK, BLOCK), BLOCK)
        full, first = block_bounds(starts, n)
        max_s[...] = jnp.full(max_s.shape, -1e30, F32)
        acc_s[...] = jnp.zeros(acc_s.shape, F32)
        sum_s[...] = jnp.zeros(sum_s.shape, F32)

        def note(scores, m):
            score_s[m] = scores
            top = max_s[...]
            for part in range(BLOCK // HD):
                top = jnp.maximum(top, scores[:, part * HD : (part + 1) * HD])
            max_s[...] = top

        def product(m):
            keys = pl.ds(pl.multiple_of(m * BLOCK, BLOCK), BLOCK)
            return dot(q_s[rows, :], k_s[keys, :], 1, 1)

        @pl.loop(0, full)
        def _(m):
            note(product(m), m)

        @pl.loop(full, n + 1)
        def _(m):
            @pl.when(block_used(starts, first, m))
            def _():
                allowed = allowed_pairs(starts, n * BLOCK, m * BLOCK, (BLOCK, BLOCK), 0)
                note(jnp.where(allowed, product(m), MASKED_SCORE), m)

        highest = jnp.max(max_s[...], axis=1, keepdims=True) * scale

        @pl.loop(0, n + 1)
        def _(m):
            @pl.when(block_used(starts, first, m))
            def _():
                keys = pl.ds(pl.multiple_of(m * BLOCK, BLOCK), BLOCK)
                exponent = jnp.exp2(score_s[m] * scale - highest)
                total = sum_s[...]
                for part in range(BLOCK // HD):
                    total = total + exponent[:, part * HD : (part + 1) * HD]
                sum_s[...] = total
                acc_s[...] += dot(exponent.astype(BF), v_s[keys, :], 1, 0)

        total = jnp.sum(sum_s[...], axis=1, keepdims=True)
        wide_ref[rows, :] = acc_s[...] / total
        log_total = jnp.broadcast_to(highest + jnp.log2(total), (BLOCK, HD))
        log_ref[n] = log_total.T[:8]
        return carry

    lax.fori_loop(0, k_s.shape[0] // BLOCK, one_block, 0)
    for b in range(4):
        for a in range(4):
            rows = pl.ds(pl.multiple_of(place_ref[4 * b + a] * PIECE, PIECE), PIECE)
            outs[b][a] = wide_ref[rows, :].astype(BF)


def attention_backward(place_ref, starts_ref, *refs):
    messages, refs = refs[:4], refs[4:]
    grads, refs = refs[:4], refs[4:]
    wide_ref, log_ref, cos_ref, sin_ref, *refs = refs
    outs, refs = refs[:4], refs[4:]
    q_s, k_s, v_s, g_s, dq_s, dk_s, dv_s = refs
    scale = LOG2E / math.sqrt(HD)
    starts = [starts_ref[s] for s in range(CONT)]
    for b in range(4):
        for a in range(4):
            rows = pl.ds(pl.multiple_of(place_ref[4 * b + a] * PIECE, PIECE), PIECE)
            q_s[rows, :] = messages[b][0, a]
            k_s[rows, :] = messages[b][1, a]
            v_s[rows, :] = messages[b][2, a]
            g_s[rows, :] = grads[b][a]
    dq_s[...] = jnp.zeros(dq_s.shape, F32)
    dk_s[...] = jnp.zeros(dk_s.shape, F32)
    dv_s[...] = jnp.zeros(dv_s.shape, F32)

    def one_block(n, carry):
        rows = pl.ds(pl.multiple_of(n * BLOCK, BLOCK), BLOCK)
        full, first = block_bounds(starts, n)
        crossed = g_s[rows, :].astype(F32) * wide_ref[rows, :]
        row_dot = jnp.sum(crossed.T, axis=0, keepdims=True)
        log_total = log_ref[n][:1]

        def step(m, masked):
            keys = pl.ds(pl.multiple_of(m * BLOCK, BLOCK), BLOCK)
            query, key = q_s[rows, :], k_s[keys, :]
            probability = jnp.exp2(dot(key, query, 1, 1) * scale - log_total)
            if masked:
                allowed = allowed_pairs(starts, n * BLOCK, m * BLOCK, (BLOCK, BLOCK), 1)
                probability = jnp.where(allowed, probability, 0.0)
            prob_grad = dot(v_s[keys, :], g_s[rows, :], 1, 1)
            score_grad = (probability * (prob_grad - row_dot)).astype(BF)
            dv_s[keys, :] += dot(probability.astype(BF), g_s[rows, :], 1, 0)
            dk_s[keys, :] += dot(score_grad, query, 1, 0)
            dq_s[rows, :] += dot(score_grad, key, 0, 0)

        @pl.loop(0, full)
        def _(m):
            step(m, False)

        @pl.loop(full, n + 1)
        def _(m):
            @pl.when(block_used(starts, first, m))
            def _():
                step(m, True)

        return carry

    lax.fori_loop(0, k_s.shape[0] // BLOCK, one_block, 0)
    for b in range(4):
        for a in range(4):
            rows = pl.ds(pl.multiple_of(place_ref[4 * b + a] * PIECE, PIECE), PIECE)
            for which, grad in ((0, dq_s), (1, dk_s)):
                value = grad[rows, :] * (1.0 / math.sqrt(HD))
                turned = value * cos_ref[rows, :] - pltpu.roll(value, HD // 2, 1) * sin_ref[rows, :]
                outs[b][which, a] = turned.astype(BF)
            outs[b][2, a] = dv_s[rows, :].astype(BF)


def run_forward(place, starts, messages):
    tokens = 16 * PIECE
    blocks = tokens // BLOCK
    out_shape = [jax.ShapeDtypeStruct((4, PIECE, HD), BF)] * 4
    out_shape += [
        jax.ShapeDtypeStruct((tokens, HD), F32),
        jax.ShapeDtypeStruct((blocks, 8, BLOCK), F32),
    ]
    return pl.pallas_call(
        attention_forward,
        out_shape=out_shape,
        in_specs=[SMEM_SPEC] * 2 + [VMEM_SPEC] * 4,
        out_specs=[VMEM_SPEC] * 6,
        scratch_shapes=[
            pltpu.VMEM((tokens, HD), BF),
            pltpu.VMEM((tokens, HD), BF),
            pltpu.VMEM((tokens, HD), BF),
            pltpu.VMEM((blocks, BLOCK, BLOCK), F32),
            pltpu.VMEM((BLOCK, HD), F32),
            pltpu.VMEM((BLOCK, HD), F32),
            pltpu.VMEM((BLOCK, HD), F32),
        ],
        compiler_params=pltpu.CompilerParams(vmem_limit_bytes=48 * 2**20),
        cost_estimate=pl.CostEstimate(
            flops=2 * tokens * tokens * HD * 2,
            bytes_accessed=8 * 2**20,
            transcendentals=tokens * tokens // 2,
        ),
    )(place, starts, *messages)


def run_backward(place, starts, messages, grads, wide, log_total, cosine, sine_table):
    tokens = 16 * PIECE
    return pl.pallas_call(
        attention_backward,
        out_shape=[jax.ShapeDtypeStruct((3, 4, PIECE, HD), BF)] * 4,
        in_specs=[SMEM_SPEC] * 2 + [VMEM_SPEC] * 12,
        out_specs=[VMEM_SPEC] * 4,
        scratch_shapes=[pltpu.VMEM((tokens, HD), BF)] * 4 + [pltpu.VMEM((tokens, HD), F32)] * 3,
        compiler_params=pltpu.CompilerParams(vmem_limit_bytes=52 * 2**20),
        cost_estimate=pl.CostEstimate(
            flops=5 * tokens * tokens * HD * 2,
            bytes_accessed=16 * 2**20,
            transcendentals=tokens * tokens // 2,
        ),
    )(place, starts, *messages, *grads, wide, log_total, cosine, sine_table)


def swap_slots(messages):
    return [messages[0], flip_y(messages[1]), flip_near(messages[2]), flip_y_near(messages[3])]


def to_tokens(values):
    return lax.all_to_all(values, "row", split_axis=0, concat_axis=1, tiled=True)


def to_width(values):
    return lax.all_to_all(values, "row", split_axis=1, concat_axis=0, tiled=True)


def square_shards(
    hidden_in,
    teacher,
    valid,
    segment_ids,
    query_weight,
    key_weight,
    value_weight,
    output_weight,
    gate_weight,
    up_weight,
    down_weight,
):
    row, col, dp = lax.axis_index("row"), lax.axis_index("col"), lax.axis_index("dp")
    x, y = row % 2, row // 2
    q = (dp + y) % 2
    own_piece = col * SIDE + row
    segment = segment_ids[0]
    group_tokens = segment.shape[0]
    home_tokens = group_tokens // (SIDE * SIDE)

    def swap_y(values):
        return jnp.where(
            y == 0, values, jnp.concatenate((values[:, HALF:], values[:, :HALF]), axis=1)
        )

    def cut(matrix, at, axis):
        size = matrix.shape[axis] // 4
        return lax.dynamic_slice_in_dim(matrix, (2 * at + q) * size, size, axis)

    def head_cut(at):
        parts = [cut(matrix, at, 1) for matrix in (query_weight, key_weight, value_weight)]
        return jnp.stack(parts + [cut(output_weight, at, 0).T])

    labels = jnp.arange(1, CONT + 1, dtype=jnp.int32)
    starts = jnp.sum((segment[None, :] < labels[:, None]).astype(jnp.int32), axis=1)
    codes = jnp.arange(16, dtype=jnp.int32)
    relative = (
        (codes & 1) + ((codes >> 1) & 1) * 8 + ((codes >> 2) & 1) * 2 + ((codes >> 3) & 1) * 4
    )
    pieces = relative ^ own_piece
    frequency = jnp.power(10000.0, jnp.arange(HD // 2, dtype=F32) * (-2.0 / HD))
    angles = positions(segment).astype(F32)[:, None] * jnp.tile(frequency, 2)[None, :]
    sign = jnp.where(jnp.arange(HD) < HD // 2, -1.0, 1.0)
    cos_wide, sin_wide = jnp.cos(angles), jnp.sin(angles) * sign[None, :]

    heads_x = flip_x(head_cut(1 - x))
    gates_x = flip_x(after(cut(gate_weight, 1 - x, 1), heads_x))
    rows_y = hidden_in.shape[0] // 2
    kept = lax.dynamic_slice_in_dim(hidden_in, y * rows_y, rows_y, 0)
    sent = lax.dynamic_slice_in_dim(hidden_in, (1 - y) * rows_y, rows_y, 0)
    piece_here = jnp.concatenate((kept, flip_y(sent)), axis=1)
    piece_far = flip_far(piece_here)
    piece_x = flip_x(after(piece_here, heads_x))
    piece_far_x = flip_x(piece_far)

    count = after(jnp.sum(valid.astype(F32)), piece_here)
    count = exchanged_sum(count, ("dp", "col"), 2 * SIDE)
    target = to_tokens(after(teacher, piece_x))

    def whole_rows(own, other):
        width = own.shape[1] // 2
        first, second = jnp.where(x == 0, own, other), jnp.where(x == 0, other, own)
        return jnp.concatenate(
            (first[:, :width], second[:, :width], first[:, width:], second[:, width:]), axis=1
        )

    def own_and_x(rows):
        half = rows.shape[0] // 2
        return [lax.dynamic_slice_in_dim(rows, at * half, half, 0) for at in (x, 1 - x)]

    hidden_rows = whole_rows(piece_here, piece_x)
    hidden = own_and_x(hidden_rows)[0].astype(F32)
    acts_here = own_and_x(local_norm(hidden_rows.astype(F32))[0].astype(BF))
    far_rows = whole_rows(piece_far, piece_far_x)
    acts_far = own_and_x(local_norm(far_rows.astype(F32))[0].astype(BF))
    normed_acts = acts_here + acts_far
    heads_tall = ordered(x, head_cut(x), heads_x, 1)
    heads_high = flip_near(heads_tall)
    heads_y = flip_dp_y(heads_tall)
    normed, inverse_one = local_norm(hidden)
    heads_y_high = flip_dp_y(after(heads_high, piece_x, count))
    gates_tall = ordered(x, cut(gate_weight, x, 1), gates_x, 0)
    gates_high = flip_far(after(gates_tall, heads_high, piece_far))
    cos_wide, sin_wide = after((cos_wide, sin_wide), heads_tall)
    heads = both_cores(
        heads_tall, heads_y, heads_high, after(heads_y_high, piece_far, target, cos_wide, sin_wide)
    )
    gates_y = flip_dp_y(after(gates_tall, piece_far_x))

    messages = run_qkv(pieces, normed_acts, heads, cos_wide, sin_wide)
    mlp_x = jnp.stack((cut(up_weight, 1 - x, 1), cut(down_weight, 1 - x, 0)))
    mlp_x = flip_x(after(mlp_x, messages[0]))
    messages = swap_slots(messages)
    messages = after(messages, mlp_x, gates_high, gates_y)

    ups_tall = ordered(x, cut(up_weight, x, 1), after(mlp_x[0], messages), 0)
    ups_high = flip_far(after(ups_tall, gates_high))
    gates_y_high = flip_dp_y(after(gates_high, messages))
    ups_y = flip_dp_y(ups_tall)
    *mixed, wide_mixed, log_total = run_forward(pieces, starts, messages)
    mixed = after(mixed, gates_y_high)
    downs_tall = ordered(x, cut(down_weight, x, 0), after(mlp_x[1], mixed), 1)
    mixed = swap_slots(mixed)
    mixed = after(mixed, ups_high, ups_y)
    gates = both_cores(gates_tall, gates_y, gates_high, gates_y_high, mixed)

    ups_y_high = flip_dp_y(after(ups_high, mixed))
    downs_y = flip_dp_y(after(downs_tall, ups_y_high))
    after_attention = hidden + square_reduce(*run_out(mixed, heads))
    after_attention = after(after_attention, ups_y_high, gates, downs_y)

    normed_two, inverse_two = local_norm(after_attention)
    ups = both_cores(ups_tall, ups_y, ups_high, ups_y_high, normed_two)
    low_two = normed_two.astype(BF)
    up_own = run_up([low_two], gates, ups)
    two_acts = near_gather(low_two, up_own)
    downs_high = flip_far(after(downs_tall, low_two))
    downs_y_high = flip_dp_y(after(downs_high, two_acts[1:3], up_own[2]))
    up_sides = run_up(after(two_acts[1:3], up_own[2]), gates, ups)
    up_far = run_up(after(two_acts[3:], up_sides[2], downs_y_high), gates, ups)
    downs = both_cores(downs_tall, downs_y, downs_high, downs_y_high, two_acts, up_sides[2])
    ups_out = [up_own, up_sides, up_far]
    units = [out[2] for out in ups_out]
    down_far = run_down("far", units[2], downs)
    down_sides = run_down("sides", after(units[1], down_far), downs)
    down_own = run_down("own", after(units[0], down_sides), downs)
    output = after_attention + near_reduce(down_far, down_sides, down_own[0])

    total_count = jnp.maximum(count, 1.0)
    counted_home = lax.dynamic_slice_in_dim(
        valid.astype(F32), row * home_tokens, home_tokens, 0
    )[:, None]
    differ = output - swap_y(target).astype(F32)
    local_loss = jnp.sum(counted_home * (differ * differ)) / D
    all_tokens = group_tokens * lax.axis_size("dp")
    out_grad = counted_home * differ * (all_tokens / total_count)

    low_out = out_grad.astype(BF)
    loss = exchanged_sum(after(local_loss, low_out), ("dp", "row", "col"), 2 * SIDE * SIDE)
    low_own = run_gated([low_out], up_own[0], up_own[1], downs)
    out_acts = near_gather(low_out, low_own)
    low_sides = run_gated(after(out_acts[1:3], low_own), up_sides[0], up_sides[1], downs)
    low_far = run_gated(after(out_acts[3:], low_sides, loss), up_far[0], up_far[1], downs)
    lows = [low_own, low_sides, low_far]
    two_far = run_normed_two("far", *low_far, gates, ups)
    two_sides = run_normed_two("sides", *after(low_sides, two_far), gates, ups)

    first = near_reduce_far(two_far)
    got = near_reduce_sides(first, two_sides)
    two_own = run_normed_two("own", *after(low_own, two_sides, first), gates, ups)
    down_grads = Spread(run_down_grad(after(units, two_own, got[1:3]), out_acts))
    down_core = down_grads.to_core()
    normed_two_grad = near_reduce_end(got, two_own[0])
    middle_grad = out_grad + local_norm_backward(normed_two_grad, normed_two, inverse_two)
    low_middle = middle_grad.astype(BF)
    gate_pair = run_wide_grad(two_acts, after([low[0] for low in lows], low_middle, down_core))
    gate_grads = Spread(gate_pair)
    down_y1 = down_grads.to_y(1)
    layer_output = to_width(swap_y(after(output, low_middle).astype(BF)))
    gate_core = gate_grads.to_core(low_middle)
    down_y0 = down_grads.to_y(0, low_middle)
    up_pair = run_wide_grad(two_acts, after([low[1] for low in lows], gate_pair, down_y1))
    up_grads = Spread(up_pair)
    middle_acts = square_gather(low_middle, gate_pair, up_pair, layer_output)
    middle_acts = after(middle_acts, up_pair, down_y0, layer_output)
    grad_messages = run_attended_grad(middle_acts, heads)
    up_core = up_grads.to_core(grad_messages)
    down_grads.to_high(flip_far, middle_acts[1:3])
    out_pair = run_head_grad(1, after(middle_acts, grad_messages), mixed)
    grad_messages = swap_slots(grad_messages)
    grad_messages = after(grad_messages, up_core, out_pair)
    gate_y1 = gate_grads.to_y(1, grad_messages)
    gate_y0 = gate_grads.to_y(0, grad_messages)
    up_y1 = up_grads.to_y(1, grad_messages)
    back = run_backward(
        pieces, starts, messages, grad_messages, wide_mixed, log_total, cos_wide, sin_wide
    )
    back = after(back, down_grads.high, gate_y1, gate_y0)
    gate_grads.to_high(flip_far, back)
    own_down, send_down = to_x(down_grads.total(back), x, 1)
    down_x = flip_x(send_down)
    back = swap_slots(back)
    back = after(back, down_x, gate_grads.high, up_y1)
    up_y0 = up_grads.to_y(0, back)
    up_grads.to_high(flip_far, back)
    own_gate, send_gate = to_x(gate_grads.total(back), x, 0)
    gate_x = flip_x(send_gate)
    head_pair = run_head_grad(3, normed_acts, back, out_pair)
    head_grads = Spread(head_pair)
    head_core = head_grads.to_core()
    input_sums = run_input(after(back, head_pair), heads)
    input_sums = after(input_sums, head_core)
    head_y1 = head_grads.to_y(1)
    normed_grad = square_reduce(*input_sums, up_grads.high)
    head_y0 = head_grads.to_y(0, head_y1)
    head_grads.to_high(flip_near, head_y1)
    first_mine = jnp.stack((pair_up(own_gate, gate_x, x), pair_up(own_down, down_x, x)))
    first_theirs = flip_dp(after(first_mine, head_y1))
    normed_grad = after(normed_grad, head_y0, head_grads.high, first_theirs)
    input_gradient = middle_grad + local_norm_backward(normed_grad, normed, inverse_one)
    own_head, send_head = to_x(head_grads.total(), x, 1)
    own_up, send_up = to_x(up_grads.total(normed_grad), x, 0)
    head_x = flip_x(send_head)
    last_mine = pair_up(own_up, flip_x(send_up), x)
    input_out = to_width(swap_y(input_gradient.astype(BF)))
    last_theirs = flip_dp(after(last_mine, input_out))
    head_mine = pair_up(own_head, head_x, x)
    head_theirs = flip_dp(head_mine)
    mean_loss = loss / total_count

    gate_grad = unite(first_mine[0], first_theirs[0], q, 1)
    down_grad = unite(first_mine[1], first_theirs[1], q, 0)
    up_grad = unite(last_mine, last_theirs, q, 1)
    head_grads = unite(head_mine, head_theirs, q, 2)
    return (
        layer_output,
        mean_loss,
        input_out.astype(F32),
        head_grads[0],
        head_grads[1],
        head_grads[2],
        head_grads[3].T,
        gate_grad,
        up_grad,
        down_grad,
    )


def solution(mesh):
    body = square_shards if fits_square(mesh) else shards
    in_specs = (
        P(("dp", "col"), "row"),
        P(("dp", "col"), "row"),
        P(("dp", "col")),
        P("dp", None),
        P("row", "col"),
        P("row", "col"),
        P("row", "col"),
        P("col", "row"),
        P("row", "col"),
        P("row", "col"),
        P("col", "row"),
    )
    out_specs = (
        P(("dp", "col"), "row"),
        P(),
        P(("dp", "col"), "row"),
        P("row", "col"),
        P("row", "col"),
        P("row", "col"),
        P("col", "row"),
        P("row", "col"),
        P("row", "col"),
        P("col", "row"),
    )
    return jax.shard_map(body, mesh=mesh, in_specs=in_specs, out_specs=out_specs, check_vma=False)
```
